32 devices in a mesh: rows: 16 (over z, y, x), seq: 2 (over core).
Axes of the slice: x: 2, y: 2, z: 4, core: 2. Of those that a mesh axis runs over, the one named last changes fastest.
Arguments:
- tokens: bfloat16 [32, 1024, 1280], P('rows', 'seq'), may hold values from -6 to 6
- segments: int32 [32, 1024], P('rows'), may hold values from 0 to 4, as said below
- gain_attn: float32 [1280], replicated, may hold values from 0.1 to 1.9
- w_query: bfloat16 [1280, 1280], P('rows', 'seq'), may hold values from -0.15625 to 0.15625
- w_key: bfloat16 [1280, 1280], P('rows', 'seq'), may hold values from -0.15625 to 0.15625
- w_value: bfloat16 [1280, 1280], P('rows', 'seq'), may hold values from -0.15625 to 0.15625
- w_out: bfloat16 [1280, 1280], P('rows', 'seq'), may hold values from -6 to 6
- gain_ffn: float32 [1280], replicated, may hold values from 0.1 to 1.9
- w_up: bfloat16 [1280, 5120], P('rows', 'seq'), may hold values from -0.15625 to 0.15625
- w_down: bfloat16 [5120, 1280], P('rows', 'seq'), may hold values from -0.078125 to 0.078125
- cotangent: bfloat16 [32, 1024, 1280], P('rows', 'seq'), may hold values from -6 to 6
Outputs:
- layer_out: bfloat16 [32, 1024, 1280], P('rows', 'seq')
- token_grad: float32 [32, 1024, 1280], P('rows', 'seq')
- gain_attn_grad: float32 [1280], replicated
- query_grad: float32 [1280, 1280], P('rows', 'seq')
- key_grad: float32 [1280, 1280], P('rows', 'seq')
- value_grad: float32 [1280, 1280], P('rows', 'seq')
- out_grad: float32 [1280, 1280], P('rows', 'seq')
- gain_ffn_grad: float32 [1280], replicated
- up_grad: float32 [1280, 5120], P('rows', 'seq')
- down_grad: float32 [5120, 1280], P('rows', 'seq')
The draws below stay inside these ranges and needn't reach their ends.
Inputs may be any that keep to these rules, and one draw needn't show every extreme that they name: `segments`: each row holds five contiguous samples numbered 0 to 4 in order; sample 2 begins within the row's first 512 tokens and ends within its last 512 tokens; every other sample is shorter than 512 tokens.
All inputs are finite; a program needn't handle non-finite values.
Results may differ from the reference program's by a relative error of at most 0.012.
Values may be sent and summed in bfloat16 or wider, within the bound.
A program may use at most 576 MiB of HBM per device.

```python
import jax
import jax.numpy as jnp
from jax import lax

D = 1280
HEADS = 20
HEAD_DIM = 64
FF = 5120
ROW_LEN = 1024
ROWS = 32
SPAN = 512


def draw_segments(key, part):
    key = jax.random.fold_in(key, 7)
    subkeys = jax.random.split(key, 4)
    half_span = SPAN // 2
    row_shape = (ROWS, 1)
    first_cut = jax.random.randint(subkeys[0], row_shape, 1, half_span)
    second_cut = jax.random.randint(subkeys[1], row_shape, half_span, SPAN)
    third_cut = ROW_LEN - SPAN + jax.random.randint(subkeys[2], row_shape, 1, half_span)
    fourth_cut = ROW_LEN - SPAN + jax.random.randint(subkeys[3], row_shape, half_span, SPAN)
    position = jnp.arange(ROW_LEN, dtype=jnp.int32)[None, :]
    return (position >= first_cut).astype(jnp.int32) + (position >= second_cut).astype(jnp.int32) + (position >= third_cut).astype(jnp.int32) + (position >= fourth_cut).astype(jnp.int32)


def block_scale(rng, extent, cuts, least, top_value):
    def one(dim, shards_of):
        steps = jax.random.uniform(jax.random.fold_in(jax.random.fold_in(rng, 6), dim), (shards_of,), jnp.float32, least / len(cuts), top_value / len(cuts))
        return jnp.repeat(jnp.exp(steps), extent[dim] // shards_of).reshape((-1,) + (1,) * (len(extent) - dim - 1))

    loudness = one(*cuts[0])
    for cut in cuts[1:]:
        loudness = loudness * one(*cut)
    return loudness


def gaussian(stream_key, shape, deviation, limit, cuts=(), kind=jnp.bfloat16):
    level = block_scale(stream_key, shape, cuts, -0.22, 0.18) if cuts else 1.0
    result = jax.random.normal(stream_key, shape, jnp.float32) * deviation * level
    return jnp.minimum(jnp.maximum(result, -limit), limit).astype(kind)


def setup_inputs(seed: int = 0) -> dict:
    streams_of = jax.random.split(jax.random.key(seed), 12)
    return {
        "tokens": gaussian(streams_of[0], (ROWS, ROW_LEN, D), 1.0, 6.0, ((0, 16), (1, 2))),
        "segments": draw_segments(jax.random.fold_in(streams_of[11], 71), 0),
        "gain_attn": jnp.clip(1.0 + 0.18 * jax.random.normal(streams_of[2], (D,), jnp.float32), 0.1, 1.9),
        "w_query": gaussian(streams_of[3], (D, D), D ** -0.5, 0.15625, ((0, 16), (1, 2))),
        "w_key": gaussian(streams_of[4], (D, D), D ** -0.5, 0.15625, ((0, 16), (1, 2))),
        "w_value": gaussian(streams_of[5], (D, D), D ** -0.5, 0.15625, ((0, 16), (1, 2))),
        "w_out": gaussian(streams_of[6], (D, D), (max(1, D // ROW_LEN)) ** -0.5, 6.0, ((0, 16), (1, 2))),
        "gain_ffn": jnp.clip(1.0 + 0.18 * jax.random.normal(streams_of[7], (D,), jnp.float32), 0.1, 1.9),
        "w_up": gaussian(streams_of[8], (D, FF), D ** -0.5, 0.15625, ((0, 16), (1, 2))),
        "w_down": gaussian(streams_of[9], (FF, D), FF ** -0.5, 0.078125, ((0, 16), (1, 2))),
        "cotangent": gaussian(streams_of[10], (ROWS, ROW_LEN, D), 1.0, 6.0, ((0, 16), (1, 2))),
    }


@jax.custom_vjp
def low(v):
    return lax.optimization_barrier(v.astype(jnp.bfloat16)).astype(jnp.float32)

@jax.custom_vjp
def low_back(v):
    return v

def low_keep(v):
    return (low(v), None)

def low_pass(kept, grad):
    return (grad,)

def back_keep(v):
    return (v, None)

def back_low(kept, grad):
    return (low(grad),)
low.defvjp(low_keep, low_pass)
low_back.defvjp(back_keep, back_low)
epsilon = 1e-05
root_half = 0.7071067811865476

def norm_rows(values, gain_vec):
    row_mean = lax.optimization_barrier(jnp.mean(values, -1, keepdims=True))
    centred = values - row_mean
    spread = lax.optimization_barrier(jnp.mean(centred * centred, -1, keepdims=True))
    return centred * lax.rsqrt(spread + epsilon) * gain_vec

def gelu_exact(values):
    return 0.5 * values * (1.0 + lax.erf(values * root_half))

def product(left_side, right_side):
    return jnp.dot(left_side, right_side, precision=lax.Precision.HIGHEST)

def layer_row(seg_row, token_row, gain_attn, w_query, w_key, w_value, w_out, gain_ffn, w_up, w_down):
    length = token_row.shape[0]
    lowered = low(norm_rows(token_row, gain_attn))
    queries = low_back(low(product(lowered, w_query))).reshape(length, HEADS, HEAD_DIM)
    key_rows = low_back(low(product(lowered, w_key))).reshape(length, HEADS, HEAD_DIM)
    value_rows = low_back(low(product(lowered, w_value))).reshape(length, HEADS, HEAD_DIM)
    scores = jnp.einsum('qhd,khd->hqk', queries, key_rows, precision=lax.Precision.HIGHEST)
    scores = low_back(scores * HEAD_DIM ** (-0.5))
    allowed = (seg_row[:, None] == seg_row[None, :])[None]
    scores = jnp.where(allowed, scores, -1e+30)
    row_top = lax.optimization_barrier(jnp.max(scores, -1, keepdims=True))
    exponent = jnp.exp(scores - row_top)
    prob_rows = low(exponent / lax.optimization_barrier(jnp.sum(exponent, -1, keepdims=True)))
    mixed = jnp.einsum('hqk,khd->qhd', prob_rows, value_rows, precision=lax.Precision.HIGHEST)
    mixed = low_back(low(mixed.reshape(length, HEADS * HEAD_DIM)))
    residual = token_row + low_back(product(mixed, w_out))
    lowered_two = low(norm_rows(residual, gain_ffn))
    hidden = low(gelu_exact(low_back(product(lowered_two, w_up))))
    return residual + low_back(product(hidden, w_down))

def reference(tokens, segments, gain_attn, w_query, w_key, w_value, w_out, gain_ffn, w_up, w_down, cotangent):
    weights_all = (gain_attn.astype(jnp.float32), w_query.astype(jnp.float32), w_key.astype(jnp.float32), w_value.astype(jnp.float32), w_out.astype(jnp.float32), gain_ffn.astype(jnp.float32), w_up.astype(jnp.float32), w_down.astype(jnp.float32))
    zero_sums = tuple((jnp.zeros_like(weight) for weight in weights_all))

    def row_step(running, row_data):
        seg_row, token_row, cot_row = row_data

        def forward(token_in, *weights):
            return layer_row(seg_row, token_in, *weights)
        row_out, pullback = jax.vjp(forward, token_row.astype(jnp.float32), *weights_all)
        gradients = pullback(cot_row.astype(jnp.float32))
        running = tuple((acc + grad for acc, grad in zip(running, gradients[1:])))
        return (running, (row_out.astype(jnp.bfloat16), gradients[0]))
    totals, (row_outs, token_grads) = lax.scan(row_step, zero_sums, (segments, tokens, cotangent))
    return (row_outs, token_grads, totals[0], totals[1], totals[2], totals[3], totals[4], totals[5], totals[6], totals[7])
```

```python
import functools

import jax
import jax.numpy as jnp
from jax import lax
from jax.experimental import pallas as pl
from jax.experimental.pallas import tpu as pltpu
from jax.sharding import PartitionSpec as P

HEADS = 20
HEAD_DIM = 64


epsilon = 1e-05
root_half = 0.7071067811865476


def norm_rows(values, gain_vec):
    row_mean = jnp.mean(values, -1, keepdims=True)
    centred = values - row_mean
    spread = jnp.mean(centred * centred, -1, keepdims=True)
    return centred * lax.rsqrt(spread + epsilon) * gain_vec


def gelu_exact(values):
    return 0.5 * values * (1.0 + lax.erf(values * root_half))


def times_transposed(left_side, right_side):
    return jnp.einsum("te,de->td", left_side, right_side, preferred_element_type=jnp.float32)


def split_heads(rows_in):
    return rows_in.reshape(rows_in.shape[0], rows_in.shape[1], HEADS, HEAD_DIM)


def join_heads(heads_in):
    return heads_in.reshape(heads_in.shape[0], heads_in.shape[1], HEADS * HEAD_DIM)


def masked_scores(query_heads, key_heads, seg_query, seg_key):
    scores = jnp.einsum(
        "rqhd,rkhd->rhqk", query_heads, key_heads, preferred_element_type=jnp.float32
    )
    scores = scores * HEAD_DIM ** (-0.5)
    allowed = (seg_query[:, :, None] == seg_key[:, None, :])[:, None]
    return (allowed, jnp.where(allowed, scores, -1e30))


def attention_forward(query_rows, key_rows, value_rows, seg_query, seg_key):
    allowed, scores = masked_scores(
        split_heads(query_rows), split_heads(key_rows), seg_query, seg_key
    )
    row_top = jnp.max(scores, -1, keepdims=True)
    exponent = jnp.exp(scores - row_top)
    row_total = jnp.sum(exponent, -1, keepdims=True)
    prob_low = (exponent / row_total).astype(jnp.bfloat16)
    mixed_out = jnp.einsum(
        "rhqk,rkhd->rqhd", prob_low, split_heads(value_rows), preferred_element_type=jnp.float32
    )
    return (join_heads(mixed_out).astype(jnp.bfloat16), row_top + jnp.log(row_total))


def grad_pieces(query_heads, key_heads, value_heads, seg_query, seg_key, log_total, grad_heads):
    allowed, scores = masked_scores(query_heads, key_heads, seg_query, seg_key)
    prob_rows = jnp.where(allowed, jnp.exp(scores - log_total), 0.0)
    grad_probs = jnp.einsum(
        "rqhd,rkhd->rhqk", grad_heads, value_heads, preferred_element_type=jnp.float32
    )
    return (prob_rows, grad_probs)


def attention_grads(query_rows, key_rows, value_rows, seg_query, seg_key, log_total, grad_mixed):
    query_heads = split_heads(query_rows)
    key_heads = split_heads(key_rows)
    grad_heads = split_heads(grad_mixed)
    prob_rows, grad_probs = grad_pieces(
        query_heads, key_heads, split_heads(value_rows), seg_query, seg_key, log_total, grad_heads
    )
    value_part = jnp.einsum(
        "rhqk,rqhd->rkhd",
        prob_rows.astype(jnp.bfloat16),
        grad_heads,
        preferred_element_type=jnp.float32,
    )
    row_inner = jnp.sum(grad_probs * prob_rows, -1, keepdims=True)
    score_grad = (prob_rows * (grad_probs - row_inner)).astype(jnp.bfloat16)
    score_scale = HEAD_DIM ** (-0.5)
    query_part = (
        jnp.einsum("rhqk,rkhd->rqhd", score_grad, key_heads, preferred_element_type=jnp.float32)
        * score_scale
    )
    key_part = (
        jnp.einsum("rhqk,rqhd->rkhd", score_grad, query_heads, preferred_element_type=jnp.float32)
        * score_scale
    )
    return (join_heads(query_part), join_heads(key_part), join_heads(value_part))


def process(token_rows, cot_rows, seg_rows, gain_attn, gain_ffn, weights):
    w_query, w_key, w_value, w_out, w_up, w_down = weights
    row_count, query_count, model_width = token_rows.shape
    offset = lax.axis_index("seq") * query_count
    seg_query = lax.dynamic_slice_in_dim(seg_rows, offset, query_count, 1)

    def shaped(flat_rows):
        return flat_rows.reshape(row_count, query_count, model_width)

    flat_tokens = token_rows.reshape(row_count * query_count, model_width).astype(jnp.float32)
    normed, norm_back = jax.vjp(norm_rows, flat_tokens, gain_attn)
    lowered = normed.astype(jnp.bfloat16)
    queries = jnp.dot(lowered, w_query, preferred_element_type=jnp.float32).astype(jnp.bfloat16)
    key_rows = jnp.dot(lowered, w_key, preferred_element_type=jnp.float32).astype(jnp.bfloat16)
    value_rows = jnp.dot(lowered, w_value, preferred_element_type=jnp.float32).astype(jnp.bfloat16)
    key_whole, value_whole = (
        lax.all_gather(shaped(key_rows), "seq", axis=1, tiled=True),
        lax.all_gather(shaped(value_rows), "seq", axis=1, tiled=True),
    )
    mixed_rows, log_total = attention_forward(
        shaped(queries), key_whole, value_whole, seg_query, seg_rows
    )
    mixed_flat = mixed_rows.reshape(row_count * query_count, model_width)
    residual = flat_tokens + jnp.dot(mixed_flat, w_out, preferred_element_type=jnp.float32)
    normed_two, norm_two_back = jax.vjp(norm_rows, residual, gain_ffn)
    lowered_two = normed_two.astype(jnp.bfloat16)
    hidden_pre = jnp.dot(lowered_two, w_up, preferred_element_type=jnp.float32)
    hidden, gelu_back = jax.vjp(gelu_exact, hidden_pre)
    hidden_low = hidden.astype(jnp.bfloat16)
    layer_rows = (
        residual + jnp.dot(hidden_low, w_down, preferred_element_type=jnp.float32)
    ).astype(jnp.bfloat16)
    grad_out = cot_rows.reshape(row_count * query_count, model_width)
    grad_hidden = times_transposed(grad_out, w_down)
    grad_pre = gelu_back(grad_hidden)[0].astype(jnp.bfloat16)
    grad_normed_two = times_transposed(grad_pre, w_up)
    grad_resid_norm, grad_gain_ffn = norm_two_back(grad_normed_two)
    grad_residual = grad_out.astype(jnp.float32) + grad_resid_norm
    grad_attn = grad_residual.astype(jnp.bfloat16)
    grad_mixed = times_transposed(grad_attn, w_out).astype(jnp.bfloat16)
    query_part, key_part, value_part = attention_grads(
        shaped(queries), key_whole, value_whole, seg_query, seg_rows, log_total, shaped(grad_mixed)
    )
    key_own, value_own = (
        lax.psum_scatter(key_part, "seq", scatter_dimension=1, tiled=True),
        lax.psum_scatter(value_part, "seq", scatter_dimension=1, tiled=True),
    )
    grad_queries = query_part.reshape(row_count * query_count, model_width).astype(jnp.bfloat16)
    grad_keys = key_own.reshape(row_count * query_count, model_width).astype(jnp.bfloat16)
    grad_values = value_own.reshape(row_count * query_count, model_width).astype(jnp.bfloat16)
    grad_normed = (
        times_transposed(grad_queries, w_query)
        + times_transposed(grad_keys, w_key)
        + times_transposed(grad_values, w_value)
    )
    grad_token_norm, grad_gain_attn = norm_back(grad_normed)
    grad_tokens = (grad_residual + grad_token_norm).reshape(row_count, query_count, model_width)
    saved = (
        lowered,
        grad_queries,
        grad_keys,
        grad_values,
        mixed_flat,
        grad_attn,
        lowered_two,
        grad_pre,
        hidden_low,
        grad_out,
    )
    return (
        layer_rows.reshape(row_count, query_count, model_width),
        grad_tokens,
        saved,
        grad_gain_attn,
        grad_gain_ffn,
    )


def body(
    tokens, segments, gain_attn, w_query, w_key, w_value, w_out, gain_ffn, w_up, w_down, cotangent
):
    col_query = lax.all_gather(w_query, "seq", axis=1, tiled=True)
    col_key = lax.all_gather(w_key, "seq", axis=1, tiled=True)
    col_value = lax.all_gather(w_value, "seq", axis=1, tiled=True)
    col_out = lax.all_gather(w_out, "seq", axis=1, tiled=True)
    col_up = lax.all_gather(w_up, "seq", axis=1, tiled=True)
    col_down = lax.all_gather(w_down, "seq", axis=1, tiled=True)
    results = [
        process(
            tokens,
            cotangent,
            segments,
            gain_attn,
            gain_ffn,
            (
                lax.all_gather(col_query, "rows", axis=0, tiled=True),
                lax.all_gather(col_key, "rows", axis=0, tiled=True),
                lax.all_gather(col_value, "rows", axis=0, tiled=True),
                lax.all_gather(col_out, "rows", axis=0, tiled=True),
                lax.all_gather(col_up, "rows", axis=0, tiled=True),
                lax.all_gather(col_down, "rows", axis=0, tiled=True),
            ),
        )
    ]
    layer_out = jnp.concatenate([result_set[0] for result_set in results], 0)
    token_grad = jnp.concatenate([result_set[1] for result_set in results], 0)
    saved = [
        jnp.concatenate([result_set[2][member] for result_set in results], 0)
        for member in range(10)
    ]
    attn_gain_part = sum((result_set[3] for result_set in results))
    ffn_gain_part = sum((result_set[4] for result_set in results))
    gain_attn_grad, gain_ffn_grad = lax.psum((attn_gain_part, ffn_gain_part), ("rows", "seq"))
    (
        lowered,
        grad_queries,
        grad_keys,
        grad_values,
        mixed_flat,
        grad_attn,
        lowered_two,
        grad_pre,
        hidden_low,
        grad_out,
    ) = saved
    splits = lax.axis_size("seq")

    def arrange(grad_block):
        return grad_block.reshape(grad_block.shape[0], splits, grad_block.shape[1] // splits)

    def outer_product(left_side, right_side):
        return jnp.einsum("tc,te->ce", left_side, right_side, preferred_element_type=jnp.float32)

    def input_terms(offset, count):
        blocks = [
            outer_product(lowered, grad_queries),
            outer_product(lowered, grad_keys),
            outer_product(lowered, grad_values),
            outer_product(mixed_flat, grad_attn),
            outer_product(lowered_two, grad_pre),
        ]
        return jnp.concatenate([arrange(grad_block) for grad_block in blocks], 2)

    def hidden_terms(offset, count):
        return arrange(outer_product(hidden_low, grad_out))

    def spread_sum(term_of, shard_rows):
        row_part = lax.psum_scatter(
            term_of(jnp.int32(0), shard_rows * lax.axis_size("rows")),
            "rows",
            scatter_dimension=0,
            tiled=True,
        )
        return lax.psum_scatter(row_part, "seq", scatter_dimension=1, tiled=True)[:, 0, :]

    input_grads = spread_sum(input_terms, w_query.shape[0])
    down_grad = spread_sum(hidden_terms, w_down.shape[0])
    column_width = w_query.shape[1]
    query_grad = input_grads[:, :column_width]
    key_grad = input_grads[:, column_width : 2 * column_width]
    value_grad = input_grads[:, 2 * column_width : 3 * column_width]
    out_grad = input_grads[:, 3 * column_width : 4 * column_width]
    up_grad = input_grads[:, 4 * column_width :]
    return (
        layer_out,
        token_grad,
        gain_attn_grad,
        query_grad,
        key_grad,
        value_grad,
        out_grad,
        gain_ffn_grad,
        up_grad,
        down_grad,
    )


LANES = 128
QUERY_TILE = 256
NEVER = -1e30


def swap_cores(values):
    return lax.ppermute(values, "seq", [(0, 1), (1, 0)])


def both_cores(values, axis):
    other = swap_cores(values)
    first = lax.axis_index("seq") == 0
    return jnp.where(
        first,
        jnp.concatenate([values, other], axis),
        jnp.concatenate([other, values], axis),
    )


def own_half(values, axis, index):
    half = values.shape[axis] // 2
    return lax.dynamic_slice_in_dim(values, index * half, half, axis)


def attend_kernel(start_ref, count_ref, column_ref, line_ref, q_ref, k_ref, v_ref, out_ref):
    row = pl.program_id(0)
    length = k_ref.shape[1]
    lower = lax.broadcasted_iota(jnp.int32, (QUERY_TILE, LANES), 1) < HEAD_DIM

    def tile_step(tile, carry):
        begin = pl.multiple_of(start_ref[row, tile] * LANES, LANES)
        count = count_ref[row, tile]
        queries = pl.ds(pl.multiple_of(tile * QUERY_TILE, QUERY_TILE), QUERY_TILE)

        def window(tiles):
            keys = pl.ds(begin, tiles * LANES)
            query = q_ref[0, queries, :]
            key = k_ref[0, keys, :]
            value = v_ref[0, keys, :]
            allowed = column_ref[0, queries, :1] == line_ref[0, :1, keys]
            mixed = []
            for head in range(2):
                mine = lower if head == 0 else jnp.logical_not(lower)
                masked = jnp.where(mine, query, jnp.zeros_like(query))
                scores = lax.dot_general(
                    masked, key, (((1,), (1,)), ((), ())), preferred_element_type=jnp.float32
                )
                scores = jnp.where(allowed, scores * HEAD_DIM ** (-0.5), NEVER)
                top = jnp.max(scores, -1, keepdims=True)
                exponent = jnp.exp(scores - top)
                total = jnp.sum(exponent, -1, keepdims=True)
                part = jnp.dot(
                    exponent.astype(jnp.bfloat16), value, preferred_element_type=jnp.float32
                )
                mixed.append(part / total)
            out_ref[0, queries, :] = jnp.where(lower, mixed[0], mixed[1]).astype(jnp.bfloat16)

        for tiles in range(1, length // LANES + 1):
            pl.when(count == tiles)(functools.partial(window, tiles))
        return carry

    lax.fori_loop(0, length // QUERY_TILE, tile_step, 0)


def attend_back_kernel(
    start_ref,
    count_ref,
    column_ref,
    line_ref,
    q_ref,
    k_ref,
    v_ref,
    grad_ref,
    dq_ref,
    dk_ref,
    dv_ref,
    dk_sum,
    dv_sum,
):
    row = pl.program_id(0)
    length = k_ref.shape[1]
    lower = lax.broadcasted_iota(jnp.int32, (QUERY_TILE, LANES), 1) < HEAD_DIM
    dk_sum[...] = jnp.zeros_like(dk_sum)
    dv_sum[...] = jnp.zeros_like(dv_sum)
    scale = HEAD_DIM ** (-0.5)

    def tile_step(tile, carry):
        begin = pl.multiple_of(start_ref[row, tile] * LANES, LANES)
        count = count_ref[row, tile]
        queries = pl.ds(pl.multiple_of(tile * QUERY_TILE, QUERY_TILE), QUERY_TILE)

        def window(tiles):
            keys = pl.ds(begin, tiles * LANES)
            query = q_ref[0, queries, :]
            grad = grad_ref[0, queries, :]
            key = k_ref[0, keys, :]
            value = v_ref[0, keys, :]
            allowed = column_ref[0, keys, :1] == line_ref[0, :1, queries]
            query_part = []
            key_part = 0.0
            value_part = 0.0
            for head in range(2):
                mine = lower if head == 0 else jnp.logical_not(lower)
                head_query = jnp.where(mine, query, jnp.zeros_like(query))
                head_grad = jnp.where(mine, grad, jnp.zeros_like(grad))
                scores = lax.dot_general(
                    key, head_query, (((1,), (1,)), ((), ())), preferred_element_type=jnp.float32
                )
                scores = jnp.where(allowed, scores * scale, NEVER)
                top = jnp.max(scores, 0, keepdims=True)
                exponent = jnp.exp(scores - top)
                probs = exponent * (1.0 / jnp.sum(exponent, 0, keepdims=True))
                grad_probs = lax.dot_general(
                    value, head_grad, (((1,), (1,)), ((), ())), preferred_element_type=jnp.float32
                )
                inner = jnp.sum(grad_probs * probs, 0, keepdims=True)
                grad_scores = (probs * (grad_probs - inner)).astype(jnp.bfloat16)
                value_part += jnp.dot(
                    probs.astype(jnp.bfloat16), head_grad, preferred_element_type=jnp.float32
                )
                key_part += jnp.dot(grad_scores, head_query, preferred_element_type=jnp.float32)
                query_part.append(
                    lax.dot_general(
                        grad_scores, key, (((0,), (0,)), ((), ())), preferred_element_type=jnp.float32
                    )
                )
            dq_ref[0, queries, :] = (
                jnp.where(lower, query_part[0], query_part[1]) * scale
            ).astype(jnp.bfloat16)
            dk_sum[keys, :] += key_part
            dv_sum[keys, :] += value_part

        for tiles in range(1, length // LANES + 1):
            pl.when(count == tiles)(functools.partial(window, tiles))
        return carry

    lax.fori_loop(0, length // QUERY_TILE, tile_step, 0)
    dk_ref[0] = (dk_sum[...] * scale).astype(jnp.bfloat16)
    dv_ref[0] = dv_sum[...].astype(jnp.bfloat16)


def windows_of(segments):
    heads = segments[:, ::QUERY_TILE]
    tails = segments[:, QUERY_TILE - 1 :: QUERY_TILE]
    begin = jnp.sum(segments[:, None, :] < heads[:, :, None], -1, dtype=jnp.int32)
    end = jnp.sum(segments[:, None, :] <= tails[:, :, None], -1, dtype=jnp.int32)
    start = begin // LANES
    return start, (end + LANES - 1) // LANES - start


def attention_call(kernel, windows, marks, operands, outputs, scratch):
    rows, length, width = operands[0].shape
    block = pl.BlockSpec((1, length, LANES), lambda row, pair, *_: (row, 0, pair))
    grid = (rows, width // LANES)
    work = rows * width * length * length
    return pl.pallas_call(
        kernel,
        grid_spec=pltpu.PrefetchScalarGridSpec(
            num_scalar_prefetch=2,
            grid=grid,
            in_specs=[
                pl.BlockSpec((1, length, LANES), lambda row, pair, *_: (row, 0, 0)),
                pl.BlockSpec((1, 8, length), lambda row, pair, *_: (row, 0, 0)),
            ]
            + [block] * len(operands),
            out_specs=[block] * outputs,
            scratch_shapes=scratch,
        ),
        out_shape=[jax.ShapeDtypeStruct((rows, length, width), jnp.bfloat16)] * outputs,
        compiler_params=pltpu.CompilerParams(vmem_limit_bytes=48 * 1024 * 1024),
        cost_estimate=pl.CostEstimate(
            flops=4 * len(operands) * work,
            bytes_accessed=2 * (len(operands) + outputs) * rows * length * width,
            transcendentals=work // HEAD_DIM,
        ),
    )(*windows, *marks, *operands)


def norm_stats(values):
    centred = values - jnp.mean(values, -1, keepdims=True)
    scale = lax.rsqrt(jnp.mean(centred * centred, -1, keepdims=True) + epsilon)
    return centred * scale, scale


def norm_back_rows(unit, scale, gain_vec, grad):
    scaled = grad * gain_vec
    inner = jnp.mean(scaled * unit, -1, keepdims=True)
    return scale * (scaled - jnp.mean(scaled, -1, keepdims=True) - unit * inner)


def gather_rows(piece):
    return lax.all_gather(piece, "rows", axis=0, tiled=True)


def scatter_rows(whole):
    return lax.psum_scatter(whole, "rows", scatter_dimension=0, tiled=True).astype(jnp.float32)


def dot_low(left_side, right_side):
    return jnp.dot(left_side, right_side, preferred_element_type=jnp.float32)


def outer_low(left_side, right_side):
    return jnp.einsum(
        "tc,te->ce", left_side, right_side, preferred_element_type=jnp.float32
    ).astype(jnp.bfloat16)


def body_pair(
    tokens, segments, gain_attn, w_query, w_key, w_value, w_out, gain_ffn, w_up, w_down, cotangent
):
    core = lax.axis_index("seq")
    rows, span, width = tokens.shape
    flat = rows * span

    w_q = gather_rows(w_query)
    w_k = gather_rows(w_key)
    w_v = gather_rows(w_value)
    w_o = both_cores(gather_rows(w_out), 1)
    w_u = gather_rows(w_up)
    down_columns = gather_rows(w_down)
    down_other = swap_cores(own_half(down_columns, 0, 1 - core))
    down_mine = own_half(down_columns, 0, core)
    w_d = jnp.where(
        core == 0,
        jnp.concatenate([down_mine, down_other], 1),
        jnp.concatenate([down_other, down_mine], 1),
    )
    w_o_rows = own_half(w_o, 0, core)

    tokens_all = both_cores(tokens, 1).reshape(2 * flat, width).astype(jnp.float32)
    cot_all = both_cores(cotangent, 1).reshape(2 * flat, width)
    tokens_own = tokens.reshape(flat, width).astype(jnp.float32)
    cot_own = cotangent.reshape(flat, width)

    windows = windows_of(segments)
    marks = (
        jnp.broadcast_to(segments[:, :, None], segments.shape + (LANES,)),
        jnp.broadcast_to(segments[:, None, :], (rows, 8, 2 * span)),
    )

    def split(flat_rows, axis_width):
        return flat_rows.reshape(rows, 2 * span, axis_width)

    def share(values):
        wide = split(values, values.shape[-1])
        received = swap_cores(own_half(wide, 1, 1 - core).astype(jnp.bfloat16))
        return (own_half(wide, 1, core) + received.astype(jnp.float32)).reshape(flat, -1)

    normed = (norm_stats(tokens_all)[0] * gain_attn).astype(jnp.bfloat16)
    queries = split(dot_low(normed, w_q).astype(jnp.bfloat16), w_q.shape[1])
    key_rows = split(dot_low(normed, w_k).astype(jnp.bfloat16), w_k.shape[1])
    value_rows = split(dot_low(normed, w_v).astype(jnp.bfloat16), w_v.shape[1])
    (mixed,) = attention_call(
        attend_kernel, windows, marks, (queries, key_rows, value_rows), 1, []
    )
    mixed_other = swap_cores(own_half(mixed, 1, 1 - core))
    mixed_mine = own_half(mixed, 1, core)
    mixed_own = jnp.where(
        core == 0,
        jnp.concatenate([mixed_mine, mixed_other], 2),
        jnp.concatenate([mixed_other, mixed_mine], 2),
    ).reshape(flat, width)
    residual = tokens_own + dot_low(mixed_own, w_o)
    unit_two, scale_two = norm_stats(residual)
    normed_two = (unit_two * gain_ffn).astype(jnp.bfloat16).reshape(rows, span, width)
    normed_two_all = both_cores(normed_two, 1).reshape(2 * flat, width)
    hidden_pre = dot_low(normed_two_all, w_u)
    hidden, gelu_back = jax.vjp(gelu_exact, hidden_pre)
    hidden_low = hidden.astype(jnp.bfloat16)
    layer_out = (residual + share(dot_low(hidden_low, w_d))).astype(jnp.bfloat16)
    grad_pre = gelu_back(times_transposed(cot_all, w_d))[0].astype(jnp.bfloat16)
    grad_normed_two = share(times_transposed(grad_pre, w_u))
    grad_residual = cot_own.astype(jnp.float32) + norm_back_rows(
        unit_two, scale_two, gain_ffn, grad_normed_two
    )
    ffn_gain_part = jnp.sum(grad_normed_two * unit_two, 0)
    grad_attn = grad_residual.astype(jnp.bfloat16).reshape(rows, span, width)
    grad_attn_all = both_cores(grad_attn, 1).reshape(2 * flat, width)
    grad_mixed = split(times_transposed(grad_attn_all, w_o_rows).astype(jnp.bfloat16), width // 2)
    scratch = [pltpu.VMEM((2 * span, LANES), jnp.float32)] * 2
    grad_queries, grad_keys, grad_values = (
        grad.reshape(2 * flat, width // 2)
        for grad in attention_call(
            attend_back_kernel,
            windows,
            marks,
            (queries, key_rows, value_rows, grad_mixed),
            3,
            scratch,
        )
    )
    grad_normed = share(
        times_transposed(grad_queries, w_q)
        + times_transposed(grad_keys, w_k)
        + times_transposed(grad_values, w_v)
    )
    unit_own, scale_own = norm_stats(tokens_own)
    token_grad = grad_residual + norm_back_rows(unit_own, scale_own, gain_attn, grad_normed)
    attn_gain_part = jnp.sum(grad_normed * unit_own, 0)
    gain_attn_grad, gain_ffn_grad = lax.psum((attn_gain_part, ffn_gain_part), ("rows", "seq"))

    def to_columns(row_half):
        received = swap_cores(own_half(row_half, 1, 1 - core))
        kept = own_half(row_half, 1, core)
        return jnp.where(
            core == 0,
            jnp.concatenate([kept, received], 0),
            jnp.concatenate([received, kept], 0),
        )

    down_grad = scatter_rows(to_columns(outer_low(hidden_low, cot_all)))
    up_grad = scatter_rows(outer_low(normed_two_all, grad_pre))
    out_grad = scatter_rows(to_columns(outer_low(mixed.reshape(2 * flat, -1), grad_attn_all)))
    query_grad = scatter_rows(outer_low(normed, grad_queries))
    key_grad = scatter_rows(outer_low(normed, grad_keys))
    value_grad = scatter_rows(outer_low(normed, grad_values))
    return (
        layer_out.reshape(rows, span, width),
        token_grad.reshape(rows, span, width),
        gain_attn_grad,
        query_grad,
        key_grad,
        value_grad,
        out_grad,
        gain_ffn_grad,
        up_grad,
        down_grad,
    )


def solution(mesh):
    paired = mesh.shape["seq"] == 2 and mesh.shape["rows"] == 16
    program = body_pair if paired else body
    return jax.shard_map(
        program,
        mesh=mesh,
        in_specs=(
            P("rows", "seq", None),
            P("rows", None),
            P(),
            P("rows", "seq"),
            P("rows", "seq"),
            P("rows", "seq"),
            P("rows", "seq"),
            P(),
            P("rows", "seq"),
            P("rows", "seq"),
            P("rows", "seq", None),
        ),
        out_specs=(
            P("rows", "seq", None),
            P("rows", "seq", None),
            P(),
            P("rows", "seq"),
            P("rows", "seq"),
            P("rows", "seq"),
            P("rows", "seq"),
            P(),
            P("rows", "seq"),
            P("rows", "seq"),
        ),
        check_vma=False,
    )
```

```python
import functools

import jax
import jax.numpy as jnp
from jax import lax
from jax.experimental import pallas as pl
from jax.experimental.pallas import tpu as pltpu
from jax.sharding import PartitionSpec as P

HEADS = 20
HEAD_DIM = 64


epsilon = 1e-05
root_half = 0.7071067811865476


def norm_rows(values, gain_vec):
    row_mean = jnp.mean(values, -1, keepdims=True)
    centred = values - row_mean
    spread = jnp.mean(centred * centred, -1, keepdims=True)
    return centred * lax.rsqrt(spread + epsilon) * gain_vec


def gelu_exact(values):
    return 0.5 * values * (1.0 + lax.erf(values * root_half))


def times_transposed(left_side, right_side):
    return jnp.einsum("te,de->td", left_side, right_side, preferred_element_type=jnp.float32)


def split_heads(rows_in):
    return rows_in.reshape(rows_in.shape[0], rows_in.shape[1], HEADS, HEAD_DIM)


def join_heads(heads_in):
    return heads_in.reshape(heads_in.shape[0], heads_in.shape[1], HEADS * HEAD_DIM)


def masked_scores(query_heads, key_heads, seg_query, seg_key):
    scores = jnp.einsum(
        "rqhd,rkhd->rhqk", query_heads, key_heads, preferred_element_type=jnp.float32
    )
    scores = scores * HEAD_DIM ** (-0.5)
    allowed = (seg_query[:, :, None] == seg_key[:, None, :])[:, None]
    return (allowed, jnp.where(allowed, scores, -1e30))


def attention_forward(query_rows, key_rows, value_rows, seg_query, seg_key):
    allowed, scores = masked_scores(
        split_heads(query_rows), split_heads(key_rows), seg_query, seg_key
    )
    row_top = jnp.max(scores, -1, keepdims=True)
    exponent = jnp.exp(scores - row_top)
    row_total = jnp.sum(exponent, -1, keepdims=True)
    prob_low = (exponent / row_total).astype(jnp.bfloat16)
    mixed_out = jnp.einsum(
        "rhqk,rkhd->rqhd", prob_low, split_heads(value_rows), preferred_element_type=jnp.float32
    )
    return (join_heads(mixed_out).astype(jnp.bfloat16), row_top + jnp.log(row_total))


def grad_pieces(query_heads, key_heads, value_heads, seg_query, seg_key, log_total, grad_heads):
    allowed, scores = masked_scores(query_heads, key_heads, seg_query, seg_key)
    prob_rows = jnp.where(allowed, jnp.exp(scores - log_total), 0.0)
    grad_probs = jnp.einsum(
        "rqhd,rkhd->rhqk", grad_heads, value_heads, preferred_element_type=jnp.float32
    )
    return (prob_rows, grad_probs)


def attention_grads(query_rows, key_rows, value_rows, seg_query, seg_key, log_total, grad_mixed):
    query_heads = split_heads(query_rows)
    key_heads = split_heads(key_rows)
    grad_heads = split_heads(grad_mixed)
    prob_rows, grad_probs = grad_pieces(
        query_heads, key_heads, split_heads(value_rows), seg_query, seg_key, log_total, grad_heads
    )
    value_part = jnp.einsum(
        "rhqk,rqhd->rkhd",
        prob_rows.astype(jnp.bfloat16),
        grad_heads,
        preferred_element_type=jnp.float32,
    )
    row_inner = jnp.sum(grad_probs * prob_rows, -1, keepdims=True)
    score_grad = (prob_rows * (grad_probs - row_inner)).astype(jnp.bfloat16)
    score_scale = HEAD_DIM ** (-0.5)
    query_part = (
        jnp.einsum("rhqk,rkhd->rqhd", score_grad, key_heads, preferred_element_type=jnp.float32)
        * score_scale
    )
    key_part = (
        jnp.einsum("rhqk,rqhd->rkhd", score_grad, query_heads, preferred_element_type=jnp.float32)
        * score_scale
    )
    return (join_heads(query_part), join_heads(key_part), join_heads(value_part))


def process(token_rows, cot_rows, seg_rows, gain_attn, gain_ffn, weights):
    w_query, w_key, w_value, w_out, w_up, w_down = weights
    row_count, query_count, model_width = token_rows.shape
    offset = lax.axis_index("seq") * query_count
    seg_query = lax.dynamic_slice_in_dim(seg_rows, offset, query_count, 1)

    def shaped(flat_rows):
        return flat_rows.reshape(row_count, query_count, model_width)

    flat_tokens = token_rows.reshape(row_count * query_count, model_width).astype(jnp.float32)
    normed, norm_back = jax.vjp(norm_rows, flat_tokens, gain_attn)
    lowered = normed.astype(jnp.bfloat16)
    queries = jnp.dot(lowered, w_query, preferred_element_type=jnp.float32).astype(jnp.bfloat16)
    key_rows = jnp.dot(lowered, w_key, preferred_element_type=jnp.float32).astype(jnp.bfloat16)
    value_rows = jnp.dot(lowered, w_value, preferred_element_type=jnp.float32).astype(jnp.bfloat16)
    key_whole, value_whole = (
        lax.all_gather(shaped(key_rows), "seq", axis=1, tiled=True),
        lax.all_gather(shaped(value_rows), "seq", axis=1, tiled=True),
    )
    mixed_rows, log_total = attention_forward(
        shaped(queries), key_whole, value_whole, seg_query, seg_rows
    )
    mixed_flat = mixed_rows.reshape(row_count * query_count, model_width)
    residual = flat_tokens + jnp.dot(mixed_flat, w_out, preferred_element_type=jnp.float32)
    normed_two, norm_two_back = jax.vjp(norm_rows, residual, gain_ffn)
    lowered_two = normed_two.astype(jnp.bfloat16)
    hidden_pre = jnp.dot(lowered_two, w_up, preferred_element_type=jnp.float32)
    hidden, gelu_back = jax.vjp(gelu_exact, hidden_pre)
    hidden_low = hidden.astype(jnp.bfloat16)
    layer_rows = (
        residual + jnp.dot(hidden_low, w_down, preferred_element_type=jnp.float32)
    ).astype(jnp.bfloat16)
    grad_out = cot_rows.reshape(row_count * query_count, model_width)
    grad_hidden = times_transposed(grad_out, w_down)
    grad_pre = gelu_back(grad_hidden)[0].astype(jnp.bfloat16)
    grad_normed_two = times_transposed(grad_pre, w_up)
    grad_resid_norm, grad_gain_ffn = norm_two_back(grad_normed_two)
    grad_residual = grad_out.astype(jnp.float32) + grad_resid_norm
    grad_attn = grad_residual.astype(jnp.bfloat16)
    grad_mixed = times_transposed(grad_attn, w_out).astype(jnp.bfloat16)
    query_part, key_part, value_part = attention_grads(
        shaped(queries), key_whole, value_whole, seg_query, seg_rows, log_total, shaped(grad_mixed)
    )
    key_own, value_own = (
        lax.psum_scatter(key_part, "seq", scatter_dimension=1, tiled=True),
        lax.psum_scatter(value_part, "seq", scatter_dimension=1, tiled=True),
    )
    grad_queries = query_part.reshape(row_count * query_count, model_width).astype(jnp.bfloat16)
    grad_keys = key_own.reshape(row_count * query_count, model_width).astype(jnp.bfloat16)
    grad_values = value_own.reshape(row_count * query_count, model_width).astype(jnp.bfloat16)
    grad_normed = (
        times_transposed(grad_queries, w_query)
        + times_transposed(grad_keys, w_key)
        + times_transposed(grad_values, w_value)
    )
    grad_token_norm, grad_gain_attn = norm_back(grad_normed)
    grad_tokens = (grad_residual + grad_token_norm).reshape(row_count, query_count, model_width)
    saved = (
        lowered,
        grad_queries,
        grad_keys,
        grad_values,
        mixed_flat,
        grad_attn,
        lowered_two,
        grad_pre,
        hidden_low,
        grad_out,
    )
    return (
        layer_rows.reshape(row_count, query_count, model_width),
        grad_tokens,
        saved,
        grad_gain_attn,
        grad_gain_ffn,
    )


def body(
    tokens, segments, gain_attn, w_query, w_key, w_value, w_out, gain_ffn, w_up, w_down, cotangent
):
    col_query = lax.all_gather(w_query, "seq", axis=1, tiled=True)
    col_key = lax.all_gather(w_key, "seq", axis=1, tiled=True)
    col_value = lax.all_gather(w_value, "seq", axis=1, tiled=True)
    col_out = lax.all_gather(w_out, "seq", axis=1, tiled=True)
    col_up = lax.all_gather(w_up, "seq", axis=1, tiled=True)
    col_down = lax.all_gather(w_down, "seq", axis=1, tiled=True)
    results = [
        process(
            tokens,
            cotangent,
            segments,
            gain_attn,
            gain_ffn,
            (
                lax.all_gather(col_query, "rows", axis=0, tiled=True),
                lax.all_gather(col_key, "rows", axis=0, tiled=True),
                lax.all_gather(col_value, "rows", axis=0, tiled=True),
                lax.all_gather(col_out, "rows", axis=0, tiled=True),
                lax.all_gather(col_up, "rows", axis=0, tiled=True),
                lax.all_gather(col_down, "rows", axis=0, tiled=True),
            ),
        )
    ]
    layer_out = jnp.concatenate([result_set[0] for result_set in results], 0)
    token_grad = jnp.concatenate([result_set[1] for result_set in results], 0)
    saved = [
        jnp.concatenate([result_set[2][member] for result_set in results], 0)
        for member in range(10)
    ]
    attn_gain_part = sum((result_set[3] for result_set in results))
    ffn_gain_part = sum((result_set[4] for result_set in results))
    gain_attn_grad, gain_ffn_grad = lax.psum((attn_gain_part, ffn_gain_part), ("rows", "seq"))
    (
        lowered,
        grad_queries,
        grad_keys,
        grad_values,
        mixed_flat,
        grad_attn,
        lowered_two,
        grad_pre,
        hidden_low,
        grad_out,
    ) = saved
    splits = lax.axis_size("seq")

    def arrange(grad_block):
        return grad_block.reshape(grad_block.shape[0], splits, grad_block.shape[1] // splits)

    def outer_product(left_side, right_side):
        return jnp.einsum("tc,te->ce", left_side, right_side, preferred_element_type=jnp.float32)

    def input_terms(offset, count):
        blocks = [
            outer_product(lowered, grad_queries),
            outer_product(lowered, grad_keys),
            outer_product(lowered, grad_values),
            outer_product(mixed_flat, grad_attn),
            outer_product(lowered_two, grad_pre),
        ]
        return jnp.concatenate([arrange(grad_block) for grad_block in blocks], 2)

    def hidden_terms(offset, count):
        return arrange(outer_product(hidden_low, grad_out))

    def spread_sum(term_of, shard_rows):
        row_part = lax.psum_scatter(
            term_of(jnp.int32(0), shard_rows * lax.axis_size("rows")),
            "rows",
            scatter_dimension=0,
            tiled=True,
        )
        return lax.psum_scatter(row_part, "seq", scatter_dimension=1, tiled=True)[:, 0, :]

    input_grads = spread_sum(input_terms, w_query.shape[0])
    down_grad = spread_sum(hidden_terms, w_down.shape[0])
    column_width = w_query.shape[1]
    query_grad = input_grads[:, :column_width]
    key_grad = input_grads[:, column_width : 2 * column_width]
    value_grad = input_grads[:, 2 * column_width : 3 * column_width]
    out_grad = input_grads[:, 3 * column_width : 4 * column_width]
    up_grad = input_grads[:, 4 * column_width :]
    return (
        layer_out,
        token_grad,
        gain_attn_grad,
        query_grad,
        key_grad,
        value_grad,
        out_grad,
        gain_ffn_grad,
        up_grad,
        down_grad,
    )


LANES = 128
QUERY_TILE = 256
NEVER = -1e30


def swap_cores(values):
    return lax.ppermute(values, "seq", [(0, 1), (1, 0)])


def both_cores(values, axis):
    other = swap_cores(values)
    first = lax.axis_index("seq") == 0
    return jnp.where(
        first,
        jnp.concatenate([values, other], axis),
        jnp.concatenate([other, values], axis),
    )


def own_half(values, axis, index):
    half = values.shape[axis] // 2
    return lax.dynamic_slice_in_dim(values, index * half, half, axis)


def attend_kernel(start_ref, count_ref, column_ref, line_ref, q_ref, k_ref, v_ref, out_ref):
    row = pl.program_id(0)
    length = k_ref.shape[1]
    lower = lax.broadcasted_iota(jnp.int32, (QUERY_TILE, LANES), 1) < HEAD_DIM

    def tile_step(tile, carry):
        begin = pl.multiple_of(start_ref[row, tile] * LANES, LANES)
        count = count_ref[row, tile]
        queries = pl.ds(pl.multiple_of(tile * QUERY_TILE, QUERY_TILE), QUERY_TILE)

        def window(tiles):
            keys = pl.ds(begin, tiles * LANES)
            query = q_ref[0, queries, :]
            key = k_ref[0, keys, :]
            value = v_ref[0, keys, :]
            allowed = column_ref[0, queries, :1] == line_ref[0, :1, keys]
            mixed = []
            for head in range(2):
                mine = lower if head == 0 else jnp.logical_not(lower)
                masked = jnp.where(mine, query, jnp.zeros_like(query))
                scores = lax.dot_general(
                    masked, key, (((1,), (1,)), ((), ())), preferred_element_type=jnp.float32
                )
                scores = jnp.where(allowed, scores * HEAD_DIM ** (-0.5), NEVER)
                top = jnp.max(scores, -1, keepdims=True)
                exponent = jnp.exp(scores - top)
                total = jnp.sum(exponent, -1, keepdims=True)
                part = jnp.dot(
                    exponent.astype(jnp.bfloat16), value, preferred_element_type=jnp.float32
                )
                mixed.append(part / total)
            out_ref[0, queries, :] = jnp.where(lower, mixed[0], mixed[1]).astype(jnp.bfloat16)

        for tiles in range(1, length // LANES + 1):
            pl.when(count == tiles)(functools.partial(window, tiles))
        return carry

    lax.fori_loop(0, length // QUERY_TILE, tile_step, 0)


def attend_back_kernel(
    start_ref,
    count_ref,
    column_ref,
    line_ref,
    q_ref,
    k_ref,
    v_ref,
    grad_ref,
    dq_ref,
    dk_ref,
    dv_ref,
    dk_sum,
    dv_sum,
):
    row = pl.program_id(0)
    length = k_ref.shape[1]
    lower = lax.broadcasted_iota(jnp.int32, (QUERY_TILE, LANES), 1) < HEAD_DIM
    dk_sum[...] = jnp.zeros_like(dk_sum)
    dv_sum[...] = jnp.zeros_like(dv_sum)
    scale = HEAD_DIM ** (-0.5)

    def tile_step(tile, carry):
        begin = pl.multiple_of(start_ref[row, tile] * LANES, LANES)
        count = count_ref[row, tile]
        queries = pl.ds(pl.multiple_of(tile * QUERY_TILE, QUERY_TILE), QUERY_TILE)

        def window(tiles):
            keys = pl.ds(begin, tiles * LANES)
            query = q_ref[0, queries, :]
            grad = grad_ref[0, queries, :]
            key = k_ref[0, keys, :]
            value = v_ref[0, keys, :]
            allowed = column_ref[0, keys, :1] == line_ref[0, :1, queries]
            query_part = []
            key_part = 0.0
            value_part = 0.0
            for head in range(2):
                mine = lower if head == 0 else jnp.logical_not(lower)
                head_query = jnp.where(mine, query, jnp.zeros_like(query))
                head_grad = jnp.where(mine, grad, jnp.zeros_like(grad))
                scores = lax.dot_general(
                    key, head_query, (((1,), (1,)), ((), ())), preferred_element_type=jnp.float32
                )
                scores = jnp.where(allowed, scores * scale, NEVER)
                top = jnp.max(scores, 0, keepdims=True)
                exponent = jnp.exp(scores - top)
                probs = exponent * (1.0 / jnp.sum(exponent, 0, keepdims=True))
                grad_probs = lax.dot_general(
                    value, head_grad, (((1,), (1,)), ((), ())), preferred_element_type=jnp.float32
                )
                inner = jnp.sum(grad_probs * probs, 0, keepdims=True)
                grad_scores = (probs * (grad_probs - inner)).astype(jnp.bfloat16)
                value_part += jnp.dot(
                    probs.astype(jnp.bfloat16), head_grad, preferred_element_type=jnp.float32
                )
                key_part += jnp.dot(grad_scores, head_query, preferred_element_type=jnp.float32)
                query_part.append(
                    lax.dot_general(
                        grad_scores, key, (((0,), (0,)), ((), ())), preferred_element_type=jnp.float32
                    )
                )
            dq_ref[0, queries, :] = (
                jnp.where(lower, query_part[0], query_part[1]) * scale
            ).astype(jnp.bfloat16)
            dk_sum[keys, :] += key_part
            dv_sum[keys, :] += value_part

        for tiles in range(1, length // LANES + 1):
            pl.when(count == tiles)(functools.partial(window, tiles))
        return carry

    lax.fori_loop(0, length // QUERY_TILE, tile_step, 0)
    dk_ref[0] = (dk_sum[...] * scale).astype(jnp.bfloat16)
    dv_ref[0] = dv_sum[...].astype(jnp.bfloat16)


def windows_of(segments):
    heads = segments[:, ::QUERY_TILE]
    tails = segments[:, QUERY_TILE - 1 :: QUERY_TILE]
    begin = jnp.sum(segments[:, None, :] < heads[:, :, None], -1, dtype=jnp.int32)
    end = jnp.sum(segments[:, None, :] <= tails[:, :, None], -1, dtype=jnp.int32)
    start = begin // LANES
    return start, (end + LANES - 1) // LANES - start


def attention_call(kernel, windows, marks, operands, outputs, scratch):
    rows, length, width = operands[0].shape
    block = pl.BlockSpec((1, length, LANES), lambda row, pair, *_: (row, 0, pair))
    grid = (rows, width // LANES)
    work = rows * width * length * length
    return pl.pallas_call(
        kernel,
        grid_spec=pltpu.PrefetchScalarGridSpec(
            num_scalar_prefetch=2,
            grid=grid,
            in_specs=[
                pl.BlockSpec((1, length, LANES), lambda row, pair, *_: (row, 0, 0)),
                pl.BlockSpec((1, 8, length), lambda row, pair, *_: (row, 0, 0)),
            ]
            + [block] * len(operands),
            out_specs=[block] * outputs,
            scratch_shapes=scratch,
        ),
        out_shape=[jax.ShapeDtypeStruct((rows, length, width), jnp.bfloat16)] * outputs,
        compiler_params=pltpu.CompilerParams(vmem_limit_bytes=48 * 1024 * 1024),
        cost_estimate=pl.CostEstimate(
            flops=4 * len(operands) * work,
            bytes_accessed=2 * (len(operands) + outputs) * rows * length * width,
            transcendentals=work // HEAD_DIM,
        ),
    )(*windows, *marks, *operands)


def norm_stats(values):
    centred = values - jnp.mean(values, -1, keepdims=True)
    scale = lax.rsqrt(jnp.mean(centred * centred, -1, keepdims=True) + epsilon)
    return centred * scale, scale


def norm_back_rows(unit, scale, gain_vec, grad):
    scaled = grad * gain_vec
    inner = jnp.mean(scaled * unit, -1, keepdims=True)
    return scale * (scaled - jnp.mean(scaled, -1, keepdims=True) - unit * inner)


Z_SIZE = 4
RING = (0, 1, 3, 2)
PLACE = (0, 1, 3, 2)


def chip_place():
    index = lax.axis_index("rows")
    return index // 4, (index // 2) % 2, index % 2


def swap_x(values):
    return lax.ppermute(values, "rows", [(row, row ^ 1) for row in range(16)])


def swap_y(values):
    return lax.ppermute(values, "rows", [(row, row ^ 2) for row in range(16)])


def next_z(values):
    pairs = []
    for place in range(Z_SIZE):
        here, there = RING[place], RING[(place + 1) % Z_SIZE]
        pairs += [(here * 4 + rest, there * 4 + rest) for rest in range(4)]
    return lax.ppermute(values, "rows", pairs)


def ring_place():
    zed = chip_place()[0]
    return jnp.where(zed == 2, 3, jnp.where(zed == 3, 2, zed))


def tie(value, *after):
    return lax.optimization_barrier((value, after))[0]


def natural_z(steps):
    place = ring_place()
    stack = jnp.stack(steps)
    return jnp.stack(
        [
            lax.dynamic_index_in_dim(stack, (place - PLACE[zed]) % Z_SIZE, 0, keepdims=False)
            for zed in range(Z_SIZE)
        ]
    )


def load_pieces(place_ref, pieces, target_of, sems):
    copies = []
    for part in range(2):
        for index in range(4):
            piece = pieces[part * 4 + index]
            row_y, row_x = place_ref[1] ^ (index // 2), place_ref[2] ^ (index % 2)
            for zed in range(Z_SIZE):
                target = target_of(part, zed, row_y, row_x, piece)
                copies.append(pltpu.make_async_copy(piece.at[zed], target, sems.at[len(copies)]))
                copies[-1].start()
    return copies


def column_target(whole_ref):
    def target_of(part, zed, row_y, row_x, piece):
        _, depth, wide = piece.shape
        row = pl.multiple_of(((zed * 2 + row_y) * 2 + row_x) * depth, 16)
        left = 0 if part == 0 else whole_ref.shape[1] - wide
        return whole_ref.at[pl.ds(row, depth), pl.ds(left, wide)]

    return target_of


def assemble_columns_kernel(place_ref, *refs):
    *pieces, out_ref, sems = refs
    for copy in load_pieces(place_ref, pieces, column_target(out_ref), sems):
        copy.wait()


def assemble_rows_kernel(place_ref, *refs):
    *pieces, out_ref, sems = refs

    def target_of(part, zed, row_y, row_x, piece):
        depth = piece.shape[1]
        half = (zed // 2) ^ place_ref[3]
        row = (((zed % 2) * 2 + row_y) * 2 + row_x) * 2 * depth + part * depth
        return out_ref.at[half, pl.ds(pl.multiple_of(row, 16), depth), :]

    for copy in load_pieces(place_ref, pieces, target_of, sems):
        copy.wait()


def place_vector():
    return jnp.stack(chip_place() + (lax.axis_index("seq"),)).astype(jnp.int32)


def assemble(kernel, shape, parts):
    return pl.pallas_call(
        kernel,
        grid_spec=pltpu.PrefetchScalarGridSpec(
            num_scalar_prefetch=1,
            grid=(1,),
            in_specs=[pl.BlockSpec(memory_space=pl.ANY)] * 8,
            out_specs=pl.BlockSpec(shape, lambda step, *_: (0,) * len(shape)),
            scratch_shapes=[pltpu.SemaphoreType.DMA((32,))],
        ),
        out_shape=jax.ShapeDtypeStruct(shape, parts[0][0].dtype),
        compiler_params=pltpu.CompilerParams(vmem_limit_bytes=40 * 1024 * 1024),
    )(place_vector(), *parts[0], *parts[1])


FFN_TILE = 256
FFN_CHUNK = 640


def feed_forward_kernel(
    place_ref, normed_ref, cot_ref, *refs, begun
):
    up_pieces, refs = refs[:8], refs[8:]
    down_mine, down_other = refs[:2]
    refs = refs[4:] if begun else refs[2:]
    hidden_ref, grad_pre_ref, y_ref, grad_ref, up_ref, down_ref, up_sems, down_sems = refs
    step = pl.program_id(0)
    wide = down_mine.shape[1]

    def copies():
        down = []
        for index, piece in enumerate((down_mine, down_other)):
            left = pl.multiple_of((place_ref[3] ^ index) * wide, 128)
            target = down_ref.at[:, pl.ds(left, wide)]
            down.append(pltpu.make_async_copy(piece, target, down_sems.at[index]))
        return down

    @pl.when(step == 0)
    def _():
        waits = load_pieces(place_ref, up_pieces, column_target(up_ref), up_sems)
        waits += copies()
        for copy in waits[-2:]:
            copy.start()
        for copy in waits:
            copy.wait()

    normed = normed_ref[...]
    cot = cot_ref[...]
    y_sum = grad_sum = 0.0
    for chunk in range(hidden_ref.shape[1] // FFN_CHUNK):
        units = pl.ds(chunk * FFN_CHUNK, FFN_CHUNK)
        up, down = up_ref[:, units], down_ref[units, :]
        pre = jnp.dot(normed, up, preferred_element_type=jnp.float32)
        grad_hidden = lax.dot_general(
            cot, down, (((1,), (1,)), ((), ())), preferred_element_type=jnp.float32
        )
        phi = 0.5 + 0.5 * lax.erf(pre * root_half)
        hidden = (pre * phi).astype(jnp.bfloat16)
        slope = phi + pre * (jnp.exp(-0.5 * pre * pre) * root_two_pi)
        grad_pre = (grad_hidden * slope).astype(jnp.bfloat16)
        hidden_ref[:, units] = hidden
        grad_pre_ref[:, units] = grad_pre
        y_sum += jnp.dot(hidden, down, preferred_element_type=jnp.float32)
        grad_sum += lax.dot_general(
            grad_pre, up, (((1,), (1,)), ((), ())), preferred_element_type=jnp.float32
        )
    y_ref[...] = y_sum.astype(jnp.bfloat16)
    grad_ref[...] = grad_sum.astype(jnp.bfloat16)


root_two_pi = 0.3989422804014327


def feed_forward(normed, cot, up_parts, down_mine, down_other, begun=()):
    tokens, width = normed.shape
    units = down_mine.shape[0]
    tiles = tokens // FFN_TILE
    offset = tiles if begun else 0
    tile = pl.BlockSpec((FFN_TILE, width), lambda step, *_: (step, 0))
    wide_tile = pl.BlockSpec((FFN_TILE, units), lambda step, *_: (step + offset, 0))
    anywhere = pl.BlockSpec(memory_space=pl.ANY)
    wide_shape = jax.ShapeDtypeStruct((2 * tokens, units), jnp.bfloat16)
    shape = jax.ShapeDtypeStruct((tokens, width), jnp.bfloat16)
    return pl.pallas_call(
        functools.partial(feed_forward_kernel, begun=bool(begun)),
        grid_spec=pltpu.PrefetchScalarGridSpec(
            num_scalar_prefetch=1,
            grid=(tiles,),
            in_specs=[tile, tile] + [anywhere] * (10 + len(begun)),
            out_specs=[wide_tile, wide_tile, tile, tile],
            scratch_shapes=[
                pltpu.VMEM((width, units), jnp.bfloat16),
                pltpu.VMEM((units, width), jnp.bfloat16),
                pltpu.SemaphoreType.DMA((32,)),
                pltpu.SemaphoreType.DMA((2,)),
            ],
        ),
        out_shape=[wide_shape, wide_shape, shape, shape],
        input_output_aliases={13: 0, 14: 1} if begun else {},
        compiler_params=pltpu.CompilerParams(vmem_limit_bytes=56 * 1024 * 1024),
        cost_estimate=pl.CostEstimate(
            flops=8 * tokens * width * units,
            bytes_accessed=4 * width * units + 4 * tokens * (2 * width + units),
            transcendentals=2 * tokens * units,
        ),
    )(place_vector(), normed, cot, *up_parts[0], *up_parts[1], down_mine, down_other, *begun)


def swap_z(values, far):
    pairs = [(row, row ^ (8 if far else 4)) for row in range(16)]
    return lax.ppermute(values, "rows", pairs)


def halves(block):
    depth, wide = block.shape
    if depth > 80:
        return block[: depth // 2], block[depth // 2 :]
    cut = (wide // 128 + 1) // 2 * 128
    return block[:, :cut], block[:, cut:]


def halves_z(stack):
    _, depth, wide = stack.shape
    if depth > 80:
        return stack[:, : depth // 2], stack[:, depth // 2 :]
    cut = (wide // 128 + 1) // 2 * 128
    return stack[:, :, :cut], stack[:, :, cut:]


def start_xy(first, second):
    return (first, swap_x(first), swap_y(first)), (second, swap_x(second), swap_y(second))


def finish_xy(first, second):
    return first + (swap_x(first[2]),), second + (swap_y(second[1]),)


def dot_low(left_side, right_side):
    return jnp.dot(left_side, right_side, preferred_element_type=jnp.float32)


def outer_low(left_side, right_side):
    return jnp.einsum(
        "tc,te->ce", left_side, right_side, preferred_element_type=jnp.float32
    ).astype(jnp.bfloat16)


class Scatter:

    def __init__(self, first, second, by_rows=False):
        self.parts, self.by_rows = (first, second), by_rows

    def pick(self, which, far_y, far_x):
        _, here_y, here_x = chip_place()
        picked = []
        for whole, row, depth, column, wide in self.parts[which]:
            blocks = whole.reshape(Z_SIZE, 2, 2, whole.shape[0] // 16, whole.shape[1])
            picked.append(
                lax.dynamic_slice(
                    blocks,
                    (0, here_y ^ far_y, here_x ^ far_x, row, column),
                    (Z_SIZE, 1, 1, depth, wide),
                ).reshape(Z_SIZE, depth, wide)
            )
        return picked[0] if len(picked) == 1 else jnp.concatenate(picked, 2)

    def spread(self):
        self.first_far = swap_x(self.pick(0, 1, 1))
        self.second_far = swap_y(self.pick(1, 1, 1))
        self.first_near = swap_x(self.pick(0, 0, 1))
        self.second_near = swap_y(self.pick(1, 1, 0))

    def turn(self):
        self.first_turned = swap_y(plus(self.pick(0, 1, 0), self.first_far))
        self.second_turned = swap_x(plus(self.pick(1, 0, 1), self.second_far))

    def gather(self):
        first = plus(self.pick(0, 0, 0), self.first_near, self.first_turned)
        second = plus(self.pick(1, 0, 0), self.second_near, self.second_turned)
        self.sums = jnp.concatenate([first, second], 1 if self.by_rows else 2)
        self.moving = next_z(self.block(1))

    def block(self, back):
        target = (ring_place() - back) % Z_SIZE
        zed = jnp.where(target == 2, 3, jnp.where(target == 3, 2, target))
        return lax.dynamic_index_in_dim(self.sums, zed, 0, keepdims=False)

    def step(self, number):
        self.moving = next_z(plus(self.block(number), self.moving))

    def finish(self):
        return self.block(0).astype(jnp.float32) + self.moving.astype(jnp.float32)

    def hold(self, names, *after):
        for name in names:
            setattr(self, name, tie(getattr(self, name), *after))


def plus_wide(*terms):
    return sum(term.astype(jnp.float32) for term in terms)


def plus(*terms):
    return plus_wide(*terms).astype(jnp.bfloat16)


def body_pair(
    tokens, segments, gain_attn, w_query, w_key, w_value, w_out, gain_ffn, w_up, w_down, cotangent
):
    core = lax.axis_index("seq")
    rows, span, width = tokens.shape
    flat = rows * span

    def split(flat_rows, axis_width):
        return flat_rows.reshape(rows, 2 * span, axis_width)

    def sharing(values):
        wide = split(values, values.shape[-1])
        return swap_cores(own_half(wide, 1, 1 - core).astype(jnp.bfloat16))

    def shared(values, received):
        wide = split(values, values.shape[-1])
        return (own_half(wide, 1, core) + received.astype(jnp.float32)).reshape(flat, -1)

    attn_piece = jnp.concatenate([w_query, w_key, w_value, w_out], 1)
    qkv_wide = 3 * w_query.shape[1]
    tokens_other = swap_cores(tokens)
    attn_steps = [attn_piece]
    for _ in range(2):
        attn_steps.append(next_z(attn_steps[-1]))

    first = core == 0
    tokens_all = jnp.where(
        first,
        jnp.concatenate([tokens, tokens_other], 1),
        jnp.concatenate([tokens_other, tokens], 1),
    )
    tokens_all = tokens_all.reshape(2 * flat, width).astype(jnp.float32)
    tokens_own = tokens.reshape(flat, width).astype(jnp.float32)
    cot_own = cotangent.reshape(flat, width)
    windows = windows_of(segments)
    marks = (
        jnp.broadcast_to(segments[:, :, None], segments.shape + (LANES,)),
        jnp.broadcast_to(segments[:, None, :], (rows, 8, 2 * span)),
    )
    normed = (norm_stats(tokens_all)[0] * gain_attn).astype(jnp.bfloat16)

    attn_steps[2] = tie(attn_steps[2], normed)
    attn_steps.append(next_z(attn_steps[2]))
    attn_stack = natural_z(attn_steps)
    qkv_parts = start_xy(*halves_z(attn_stack[:, :, :qkv_wide]))
    up_steps, down_steps = [tie(w_up, attn_stack)], [tie(w_down, attn_stack)]
    up_steps.append(next_z(up_steps[-1]))
    down_steps.append(next_z(down_steps[-1]))
    qkv_parts = finish_xy(*qkv_parts)
    up_steps[1], down_steps[1] = tie((up_steps[1], down_steps[1]), qkv_parts[0][2], qkv_parts[1][1])
    up_steps.append(next_z(up_steps[-1]))
    down_steps.append(next_z(down_steps[-1]))
    cot_other = swap_cores(cotangent)
    w_qkv = assemble(assemble_columns_kernel, (width, qkv_wide), qkv_parts)
    out_parts = start_xy(*halves_z(tie(attn_stack[:, :, qkv_wide:], qkv_parts)))
    w_qkv, up_steps[2], down_steps[2] = tie((w_qkv, up_steps[2], down_steps[2]))
    up_steps.append(next_z(up_steps[-1]))
    down_steps.append(next_z(down_steps[-1]))
    w_q, w_k, w_v = (w_qkv[:, i * (qkv_wide // 3) : (i + 1) * (qkv_wide // 3)] for i in range(3))

    queries = dot_low(normed, w_q).astype(jnp.bfloat16)
    queries, out_parts = tie((queries, out_parts))
    out_parts = finish_xy(*out_parts)
    normed, up_steps[3], down_steps[3] = tie((normed, up_steps[3], down_steps[3]), queries)
    up_parts = start_xy(*halves_z(natural_z(up_steps)))
    down_stack = natural_z(down_steps)
    key_rows = dot_low(normed, w_k).astype(jnp.bfloat16)
    normed, out_parts = tie((normed, out_parts), key_rows)
    w_o_half = assemble(assemble_columns_kernel, (width, width // 2), out_parts)
    w_o_other = swap_cores(w_o_half)
    value_rows = dot_low(normed, w_v).astype(jnp.bfloat16)

    queries, key_rows, value_rows = (
        split(array, w_q.shape[1]) for array in (queries, key_rows, value_rows)
    )
    queries, w_o_other = tie((queries, w_o_other))

    def attend(row, query_rows):
        return attention_call(
            attend_kernel,
            [array[row : row + 1] for array in windows],
            [array[row : row + 1] for array in marks],
            [array[row : row + 1] for array in (query_rows, key_rows, value_rows)],
            1,
            [],
        )[0]

    mixed_rows = [attend(0, queries)]
    queries, up_parts = tie((queries, up_parts), mixed_rows[0])
    up_parts = finish_xy(*up_parts)
    down_parts = start_xy(*halves_z(tie(down_stack, up_parts[0][2])))
    mixed_rows += [attend(row, queries) for row in range(1, rows)]
    mixed = jnp.concatenate(mixed_rows, 0)
    mixed, up_parts, down_parts = tie((mixed, up_parts, down_parts))
    down_parts = finish_xy(*down_parts)
    w_o = jnp.where(
        first,
        jnp.concatenate([w_o_half, w_o_other], 1),
        jnp.concatenate([w_o_other, w_o_half], 1),
    )
    w_o_rows = own_half(w_o, 0, core)

    mixed_other = swap_cores(own_half(mixed, 1, 1 - core))
    mixed_mine = own_half(mixed, 1, core)
    mixed_own = jnp.where(
        first,
        jnp.concatenate([mixed_mine, mixed_other], 2),
        jnp.concatenate([mixed_other, mixed_mine], 2),
    ).reshape(flat, width)
    residual = tokens_own + dot_low(mixed_own, w_o)
    unit_two, scale_two = norm_stats(residual)
    normed_two = (unit_two * gain_ffn).astype(jnp.bfloat16)
    normed_two, down_parts = tie((normed_two, down_parts))
    normed_two_other = swap_cores(normed_two)
    units = w_up.shape[1]
    down_columns = assemble(assemble_rows_kernel, (2, units, width // 2), down_parts)
    down_mine = down_columns[0]
    down_other = swap_cores(down_columns[1])
    weights = (up_parts, down_mine, down_other)
    cot_other = cot_other.reshape(flat, width)

    hidden_low, grad_pre, y_own, grad_two_own = feed_forward(normed_two, cot_own, *weights)
    (normed_two_other, hidden_low, grad_pre) = tie((normed_two_other, hidden_low, grad_pre))
    hidden_low, grad_pre, y_away, grad_two_away = feed_forward(
        normed_two_other, cot_other, *weights, begun=(hidden_low, grad_pre)
    )
    normed_two_all = jnp.concatenate([normed_two, normed_two_other], 0)
    cot_all = jnp.concatenate([cot_own, cot_other], 0)
    grad_two_came = swap_cores(grad_two_away)
    y_came = swap_cores(y_away)

    hidden_low = tie(hidden_low, grad_two_away, y_away)
    down_half = outer_low(hidden_low, cot_all)
    down_away = swap_cores(own_half(down_half, 1, 1 - core))
    grad_pre, normed_two_all = tie((grad_pre, normed_two_all), down_half)
    up_whole = outer_low(normed_two_all, grad_pre)
    down_away = tie(down_away, up_whole)
    down_kept = own_half(down_half, 1, core)
    down_whole = jnp.where(
        first,
        jnp.concatenate([down_kept, down_away], 0),
        jnp.concatenate([down_away, down_kept], 0),
    )
    depth, wide = w_down.shape
    down_sum = Scatter(
        [(down_whole, 0, depth // 2, 0, wide)],
        [(down_whole, depth // 2, depth // 2, 0, wide)],
        True,
    )
    down_sum.spread()
    depth, wide = w_up.shape
    up_sum = Scatter(
        [(up_whole, 0, depth, 0, wide // 2)], [(up_whole, 0, depth, wide // 2, wide // 2)]
    )
    grad_normed_two = plus_wide(grad_two_own, tie(grad_two_came, up_whole))
    grad_residual = cot_own.astype(jnp.float32) + norm_back_rows(
        unit_two, scale_two, gain_ffn, grad_normed_two
    )
    ffn_gain_part = jnp.sum(grad_normed_two * unit_two, 0)
    grad_attn = grad_residual.astype(jnp.bfloat16).reshape(rows, span, width)
    (grad_attn, down_sum.first_far, down_sum.second_far) = tie(
        (grad_attn, down_sum.first_far, down_sum.second_far)
    )
    down_sum.turn()
    up_sum.spread()
    grad_attn_all = both_cores(grad_attn, 1).reshape(2 * flat, width)
    grad_mixed = split(times_transposed(grad_attn_all, w_o_rows).astype(jnp.bfloat16), width // 2)
    down_names = ("first_near", "second_near", "first_turned", "second_turned")
    down_sum.hold(down_names, grad_mixed)
    grad_mixed = tie(grad_mixed, *(getattr(down_sum, name) for name in down_names))
    down_sum.gather()
    scratch = [pltpu.VMEM((2 * span, LANES), jnp.float32)] * 2

    def attend_back(row, grad_rows):
        return attention_call(
            attend_back_kernel,
            [array[row : row + 1] for array in windows],
            [array[row : row + 1] for array in marks],
            [array[row : row + 1] for array in (queries, key_rows, value_rows, grad_rows)],
            3,
            scratch,
        )

    up_names = ("first_far", "second_far")
    back_rows = []
    for row in range(rows):
        back_rows.append(attend_back(row, grad_mixed))
        if row == 0:
            down_sum.hold(("moving",), *back_rows[-1])
            up_sum.hold(up_names, *back_rows[-1])
            grad_mixed = tie(
                grad_mixed, down_sum.moving, up_sum.first_far, up_sum.second_far, *back_rows[-1]
            )
            down_sum.step(2)
            up_sum.turn()
    grad_queries, grad_keys, grad_values = (
        jnp.concatenate([parts[member] for parts in back_rows], 0).reshape(2 * flat, width // 2)
        for member in range(3)
    )
    down_sum.hold(("moving",), grad_queries)
    up_sum.hold(down_names, grad_queries)
    grad_queries = tie(
        grad_queries, down_sum.moving, *(getattr(up_sum, name) for name in down_names)
    )
    down_sum.step(3)
    up_sum.gather()
    out_half = outer_low(mixed.reshape(2 * flat, -1), tie(grad_attn_all, grad_queries))
    out_away = swap_cores(own_half(out_half, 1, 1 - core))
    query_whole = outer_low(normed, grad_queries)
    key_whole = outer_low(normed, grad_keys)
    value_whole = outer_low(normed, grad_values)
    out_kept = own_half(out_half, 1, core)
    out_whole = jnp.where(
        first,
        jnp.concatenate([out_kept, out_away], 0),
        jnp.concatenate([out_away, out_kept], 0),
    )
    attn_whole = (query_whole, key_whole, value_whole, out_whole)
    up_sum.hold(("moving",), attn_whole)
    attn_whole = tie(attn_whole, up_sum.moving)
    depth, wide = w_query.shape
    attn_sum = Scatter(
        [(whole, 0, depth, 0, wide) for whole in attn_whole[:2]],
        [(whole, 0, depth, 0, wide) for whole in attn_whole[2:]],
    )
    attn_sum.spread()
    up_sum.step(2)
    grad_queries = tie(grad_queries, attn_whole)
    grad_normed_part = (
        times_transposed(grad_queries, w_q)
        + times_transposed(grad_keys, w_k)
        + times_transposed(grad_values, w_v)
    )
    attn_sum.hold(up_names, grad_normed_part)
    up_sum.hold(("moving",), grad_normed_part)
    grad_normed_part = tie(
        grad_normed_part, attn_sum.first_far, attn_sum.second_far, up_sum.moving
    )
    attn_sum.turn()
    up_sum.step(3)
    grad_normed = shared(grad_normed_part, sharing(grad_normed_part))
    y_own, y_came = tie((y_own, y_came), grad_normed_part)
    layer_out = (residual + plus_wide(y_own, y_came)).astype(jnp.bfloat16)
    unit_own, scale_own = norm_stats(tokens_own)
    token_grad = grad_residual + norm_back_rows(unit_own, scale_own, gain_attn, grad_normed)
    attn_gain_part = jnp.sum(grad_normed * unit_own, 0)
    gains = jnp.stack([attn_gain_part, ffn_gain_part])
    gains = gains + swap_cores(gains)
    attn_sum.hold(down_names, token_grad)
    attn_sum.gather()
    gains = gains + swap_x(gains)
    gains = gains + swap_y(gains)
    layer_out, attn_sum.moving = tie((layer_out, attn_sum.moving), gains)
    attn_sum.step(2)
    gains = gains + swap_z(gains, False)
    attn_sum.moving = tie(attn_sum.moving, gains)
    attn_sum.step(3)
    gains = gains + swap_z(gains, True)
    gain_attn_grad, gain_ffn_grad = gains
    down_grad = down_sum.finish()
    up_grad = up_sum.finish()
    attn_grad = attn_sum.finish()
    column_width = w_query.shape[1]
    query_grad, key_grad, value_grad, out_grad = (
        attn_grad[:, index * column_width : (index + 1) * column_width] for index in range(4)
    )
    return (
        layer_out.reshape(rows, span, width),
        token_grad.reshape(rows, span, width),
        gain_attn_grad,
        query_grad,
        key_grad,
        value_grad,
        out_grad,
        gain_ffn_grad,
        up_grad,
        down_grad,
    )


def solution(mesh):
    paired = mesh.shape["seq"] == 2 and mesh.shape["rows"] == 16
    program = body_pair if paired else body
    return jax.shard_map(
        program,
        mesh=mesh,
        in_specs=(
            P("rows", "seq", None),
            P("rows", None),
            P(),
            P("rows", "seq"),
            P("rows", "seq"),
            P("rows", "seq"),
            P("rows", "seq"),
            P(),
            P("rows", "seq"),
            P("rows", "seq"),
            P("rows", "seq", None),
        ),
        out_specs=(
            P("rows", "seq", None),
            P("rows", "seq", None),
            P(),
            P("rows", "seq"),
            P("rows", "seq"),
            P("rows", "seq"),
            P("rows", "seq"),
            P(),
            P("rows", "seq"),
            P("rows", "seq"),
        ),
        check_vma=False,
    )
```

```python
import functools

import jax
import jax.numpy as jnp
from jax import lax
from jax.experimental import pallas as pl
from jax.experimental.pallas import tpu as pltpu
from jax.sharding import PartitionSpec as P

HEADS = 20
HEAD_DIM = 64


epsilon = 1e-05
root_half = 0.7071067811865476


def norm_rows(values, gain_vec):
    row_mean = jnp.mean(values, -1, keepdims=True)
    centred = values - row_mean
    spread = jnp.mean(centred * centred, -1, keepdims=True)
    return centred * lax.rsqrt(spread + epsilon) * gain_vec


def gelu_exact(values):
    return 0.5 * values * (1.0 + lax.erf(values * root_half))


def times_transposed(left_side, right_side):
    return jnp.einsum("te,de->td", left_side, right_side, preferred_element_type=jnp.float32)


def split_heads(rows_in):
    return rows_in.reshape(rows_in.shape[0], rows_in.shape[1], HEADS, HEAD_DIM)


def join_heads(heads_in):
    return heads_in.reshape(heads_in.shape[0], heads_in.shape[1], HEADS * HEAD_DIM)


def masked_scores(query_heads, key_heads, seg_query, seg_key):
    scores = jnp.einsum(
        "rqhd,rkhd->rhqk", query_heads, key_heads, preferred_element_type=jnp.float32
    )
    scores = scores * HEAD_DIM ** (-0.5)
    allowed = (seg_query[:, :, None] == seg_key[:, None, :])[:, None]
    return (allowed, jnp.where(allowed, scores, -1e30))


def attention_forward(query_rows, key_rows, value_rows, seg_query, seg_key):
    allowed, scores = masked_scores(
        split_heads(query_rows), split_heads(key_rows), seg_query, seg_key
    )
    row_top = jnp.max(scores, -1, keepdims=True)
    exponent = jnp.exp(scores - row_top)
    row_total = jnp.sum(exponent, -1, keepdims=True)
    prob_low = (exponent / row_total).astype(jnp.bfloat16)
    mixed_out = jnp.einsum(
        "rhqk,rkhd->rqhd", prob_low, split_heads(value_rows), preferred_element_type=jnp.float32
    )
    return (join_heads(mixed_out).astype(jnp.bfloat16), row_top + jnp.log(row_total))


def grad_pieces(query_heads, key_heads, value_heads, seg_query, seg_key, log_total, grad_heads):
    allowed, scores = masked_scores(query_heads, key_heads, seg_query, seg_key)
    prob_rows = jnp.where(allowed, jnp.exp(scores - log_total), 0.0)
    grad_probs = jnp.einsum(
        "rqhd,rkhd->rhqk", grad_heads, value_heads, preferred_element_type=jnp.float32
    )
    return (prob_rows, grad_probs)


def attention_grads(query_rows, key_rows, value_rows, seg_query, seg_key, log_total, grad_mixed):
    query_heads = split_heads(query_rows)
    key_heads = split_heads(key_rows)
    grad_heads = split_heads(grad_mixed)
    prob_rows, grad_probs = grad_pieces(
        query_heads, key_heads, split_heads(value_rows), seg_query, seg_key, log_total, grad_heads
    )
    value_part = jnp.einsum(
        "rhqk,rqhd->rkhd",
        prob_rows.astype(jnp.bfloat16),
        grad_heads,
        preferred_element_type=jnp.float32,
    )
    row_inner = jnp.sum(grad_probs * prob_rows, -1, keepdims=True)
    score_grad = (prob_rows * (grad_probs - row_inner)).astype(jnp.bfloat16)
    score_scale = HEAD_DIM ** (-0.5)
    query_part = (
        jnp.einsum("rhqk,rkhd->rqhd", score_grad, key_heads, preferred_element_type=jnp.float32)
        * score_scale
    )
    key_part = (
        jnp.einsum("rhqk,rqhd->rkhd", score_grad, query_heads, preferred_element_type=jnp.float32)
        * score_scale
    )
    return (join_heads(query_part), join_heads(key_part), join_heads(value_part))


def process(token_rows, cot_rows, seg_rows, gain_attn, gain_ffn, weights):
    w_query, w_key, w_value, w_out, w_up, w_down = weights
    row_count, query_count, model_width = token_rows.shape
    offset = lax.axis_index("seq") * query_count
    seg_query = lax.dynamic_slice_in_dim(seg_rows, offset, query_count, 1)

    def shaped(flat_rows):
        return flat_rows.reshape(row_count, query_count, model_width)

    flat_tokens = token_rows.reshape(row_count * query_count, model_width).astype(jnp.float32)
    normed, norm_back = jax.vjp(norm_rows, flat_tokens, gain_attn)
    lowered = normed.astype(jnp.bfloat16)
    queries = jnp.dot(lowered, w_query, preferred_element_type=jnp.float32).astype(jnp.bfloat16)
    key_rows = jnp.dot(lowered, w_key, preferred_element_type=jnp.float32).astype(jnp.bfloat16)
    value_rows = jnp.dot(lowered, w_value, preferred_element_type=jnp.float32).astype(jnp.bfloat16)
    key_whole, value_whole = (
        lax.all_gather(shaped(key_rows), "seq", axis=1, tiled=True),
        lax.all_gather(shaped(value_rows), "seq", axis=1, tiled=True),
    )
    mixed_rows, log_total = attention_forward(
        shaped(queries), key_whole, value_whole, seg_query, seg_rows
    )
    mixed_flat = mixed_rows.reshape(row_count * query_count, model_width)
    residual = flat_tokens + jnp.dot(mixed_flat, w_out, preferred_element_type=jnp.float32)
    normed_two, norm_two_back = jax.vjp(norm_rows, residual, gain_ffn)
    lowered_two = normed_two.astype(jnp.bfloat16)
    hidden_pre = jnp.dot(lowered_two, w_up, preferred_element_type=jnp.float32)
    hidden, gelu_back = jax.vjp(gelu_exact, hidden_pre)
    hidden_low = hidden.astype(jnp.bfloat16)
    layer_rows = (
        residual + jnp.dot(hidden_low, w_down, preferred_element_type=jnp.float32)
    ).astype(jnp.bfloat16)
    grad_out = cot_rows.reshape(row_count * query_count, model_width)
    grad_hidden = times_transposed(grad_out, w_down)
    grad_pre = gelu_back(grad_hidden)[0].astype(jnp.bfloat16)
    grad_normed_two = times_transposed(grad_pre, w_up)
    grad_resid_norm, grad_gain_ffn = norm_two_back(grad_normed_two)
    grad_residual = grad_out.astype(jnp.float32) + grad_resid_norm
    grad_attn = grad_residual.astype(jnp.bfloat16)
    grad_mixed = times_transposed(grad_attn, w_out).astype(jnp.bfloat16)
    query_part, key_part, value_part = attention_grads(
        shaped(queries), key_whole, value_whole, seg_query, seg_rows, log_total, shaped(grad_mixed)
    )
    key_own, value_own = (
        lax.psum_scatter(key_part, "seq", scatter_dimension=1, tiled=True),
        lax.psum_scatter(value_part, "seq", scatter_dimension=1, tiled=True),
    )
    grad_queries = query_part.reshape(row_count * query_count, model_width).astype(jnp.bfloat16)
    grad_keys = key_own.reshape(row_count * query_count, model_width).astype(jnp.bfloat16)
    grad_values = value_own.reshape(row_count * query_count, model_width).astype(jnp.bfloat16)
    grad_normed = (
        times_transposed(grad_queries, w_query)
        + times_transposed(grad_keys, w_key)
        + times_transposed(grad_values, w_value)
    )
    grad_token_norm, grad_gain_attn = norm_back(grad_normed)
    grad_tokens = (grad_residual + grad_token_norm).reshape(row_count, query_count, model_width)
    saved = (
        lowered,
        grad_queries,
        grad_keys,
        grad_values,
        mixed_flat,
        grad_attn,
        lowered_two,
        grad_pre,
        hidden_low,
        grad_out,
    )
    return (
        layer_rows.reshape(row_count, query_count, model_width),
        grad_tokens,
        saved,
        grad_gain_attn,
        grad_gain_ffn,
    )


def body(
    tokens, segments, gain_attn, w_query, w_key, w_value, w_out, gain_ffn, w_up, w_down, cotangent
):
    col_query = lax.all_gather(w_query, "seq", axis=1, tiled=True)
    col_key = lax.all_gather(w_key, "seq", axis=1, tiled=True)
    col_value = lax.all_gather(w_value, "seq", axis=1, tiled=True)
    col_out = lax.all_gather(w_out, "seq", axis=1, tiled=True)
    col_up = lax.all_gather(w_up, "seq", axis=1, tiled=True)
    col_down = lax.all_gather(w_down, "seq", axis=1, tiled=True)
    results = [
        process(
            tokens,
            cotangent,
            segments,
            gain_attn,
            gain_ffn,
            (
                lax.all_gather(col_query, "rows", axis=0, tiled=True),
                lax.all_gather(col_key, "rows", axis=0, tiled=True),
                lax.all_gather(col_value, "rows", axis=0, tiled=True),
                lax.all_gather(col_out, "rows", axis=0, tiled=True),
                lax.all_gather(col_up, "rows", axis=0, tiled=True),
                lax.all_gather(col_down, "rows", axis=0, tiled=True),
            ),
        )
    ]
    layer_out = jnp.concatenate([result_set[0] for result_set in results], 0)
    token_grad = jnp.concatenate([result_set[1] for result_set in results], 0)
    saved = [
        jnp.concatenate([result_set[2][member] for result_set in results], 0)
        for member in range(10)
    ]
    attn_gain_part = sum((result_set[3] for result_set in results))
    ffn_gain_part = sum((result_set[4] for result_set in results))
    gain_attn_grad, gain_ffn_grad = lax.psum((attn_gain_part, ffn_gain_part), ("rows", "seq"))
    (
        lowered,
        grad_queries,
        grad_keys,
        grad_values,
        mixed_flat,
        grad_attn,
        lowered_two,
        grad_pre,
        hidden_low,
        grad_out,
    ) = saved
    splits = lax.axis_size("seq")

    def arrange(grad_block):
        return grad_block.reshape(grad_block.shape[0], splits, grad_block.shape[1] // splits)

    def outer_product(left_side, right_side):
        return jnp.einsum("tc,te->ce", left_side, right_side, preferred_element_type=jnp.float32)

    def input_terms(offset, count):
        blocks = [
            outer_product(lowered, grad_queries),
            outer_product(lowered, grad_keys),
            outer_product(lowered, grad_values),
            outer_product(mixed_flat, grad_attn),
            outer_product(lowered_two, grad_pre),
        ]
        return jnp.concatenate([arrange(grad_block) for grad_block in blocks], 2)

    def hidden_terms(offset, count):
        return arrange(outer_product(hidden_low, grad_out))

    def spread_sum(term_of, shard_rows):
        row_part = lax.psum_scatter(
            term_of(jnp.int32(0), shard_rows * lax.axis_size("rows")),
            "rows",
            scatter_dimension=0,
            tiled=True,
        )
        return lax.psum_scatter(row_part, "seq", scatter_dimension=1, tiled=True)[:, 0, :]

    input_grads = spread_sum(input_terms, w_query.shape[0])
    down_grad = spread_sum(hidden_terms, w_down.shape[0])
    column_width = w_query.shape[1]
    query_grad = input_grads[:, :column_width]
    key_grad = input_grads[:, column_width : 2 * column_width]
    value_grad = input_grads[:, 2 * column_width : 3 * column_width]
    out_grad = input_grads[:, 3 * column_width : 4 * column_width]
    up_grad = input_grads[:, 4 * column_width :]
    return (
        layer_out,
        token_grad,
        gain_attn_grad,
        query_grad,
        key_grad,
        value_grad,
        out_grad,
        gain_ffn_grad,
        up_grad,
        down_grad,
    )


LANES = 128
QUERY_TILE = 256
NEVER = -1e30


def swap_cores(values):
    return lax.ppermute(values, "seq", [(0, 1), (1, 0)])


def both_cores(values, axis):
    other = swap_cores(values)
    first = lax.axis_index("seq") == 0
    return jnp.where(
        first,
        jnp.concatenate([values, other], axis),
        jnp.concatenate([other, values], axis),
    )


def own_half(values, axis, index):
    half = values.shape[axis] // 2
    return lax.dynamic_slice_in_dim(values, index * half, half, axis)


def attend_kernel(
    row, begun, start_ref, count_ref, column_ref, line_ref, q_ref, k_ref, v_ref, *rest
):
    (out_ref,) = rest[begun:]
    length = k_ref.shape[1]
    lower = lax.broadcasted_iota(jnp.int32, (QUERY_TILE, LANES), 1) < HEAD_DIM

    def tile_step(tile, carry):
        begin = pl.multiple_of(start_ref[row, tile] * LANES, LANES)
        count = count_ref[row, tile]
        queries = pl.ds(pl.multiple_of(tile * QUERY_TILE, QUERY_TILE), QUERY_TILE)

        def window(tiles):
            keys = pl.ds(begin, tiles * LANES)
            query = q_ref[0, queries, :]
            key = k_ref[0, keys, :]
            value = v_ref[0, keys, :]
            allowed = column_ref[0, queries, :1] == line_ref[0, :1, keys]
            mixed = []
            for head in range(2):
                mine = lower if head == 0 else jnp.logical_not(lower)
                masked = jnp.where(mine, query, jnp.zeros_like(query))
                scores = lax.dot_general(
                    masked, key, (((1,), (1,)), ((), ())), preferred_element_type=jnp.float32
                )
                scores = jnp.where(allowed, scores * HEAD_DIM ** (-0.5), NEVER)
                top = jnp.max(scores, -1, keepdims=True)
                exponent = jnp.exp(scores - top)
                total = jnp.sum(exponent, -1, keepdims=True)
                part = jnp.dot(
                    exponent.astype(jnp.bfloat16), value, preferred_element_type=jnp.float32
                )
                mixed.append(part / total)
            out_ref[0, queries, :] = jnp.where(lower, mixed[0], mixed[1]).astype(jnp.bfloat16)

        for tiles in range(1, length // LANES + 1):
            pl.when(count == tiles)(functools.partial(window, tiles))
        return carry

    lax.fori_loop(0, length // QUERY_TILE, tile_step, 0)


def attend_back_kernel(
    row, begun, start_ref, count_ref, column_ref, line_ref, q_ref, k_ref, v_ref, grad_ref, *rest
):
    dq_ref, dk_ref, dv_ref, dk_sum, dv_sum = rest[begun:]
    length = k_ref.shape[1]
    lower = lax.broadcasted_iota(jnp.int32, (QUERY_TILE, LANES), 1) < HEAD_DIM
    dk_sum[...] = jnp.zeros_like(dk_sum)
    dv_sum[...] = jnp.zeros_like(dv_sum)
    scale = HEAD_DIM ** (-0.5)

    def tile_step(tile, carry):
        begin = pl.multiple_of(start_ref[row, tile] * LANES, LANES)
        count = count_ref[row, tile]
        queries = pl.ds(pl.multiple_of(tile * QUERY_TILE, QUERY_TILE), QUERY_TILE)

        def window(tiles):
            keys = pl.ds(begin, tiles * LANES)
            query = q_ref[0, queries, :]
            grad = grad_ref[0, queries, :]
            key = k_ref[0, keys, :]
            value = v_ref[0, keys, :]
            allowed = column_ref[0, keys, :1] == line_ref[0, :1, queries]
            query_part = []
            key_part = 0.0
            value_part = 0.0
            for head in range(2):
                mine = lower if head == 0 else jnp.logical_not(lower)
                head_query = jnp.where(mine, query, jnp.zeros_like(query))
                head_grad = jnp.where(mine, grad, jnp.zeros_like(grad))
                scores = lax.dot_general(
                    key, head_query, (((1,), (1,)), ((), ())), preferred_element_type=jnp.float32
                )
                scores = jnp.where(allowed, scores * scale, NEVER)
                top = jnp.max(scores, 0, keepdims=True)
                exponent = jnp.exp(scores - top)
                probs = exponent * (1.0 / jnp.sum(exponent, 0, keepdims=True))
                grad_probs = lax.dot_general(
                    value, head_grad, (((1,), (1,)), ((), ())), preferred_element_type=jnp.float32
                )
                inner = jnp.sum(grad_probs * probs, 0, keepdims=True)
                grad_scores = (probs * (grad_probs - inner)).astype(jnp.bfloat16)
                value_part += jnp.dot(
                    probs.astype(jnp.bfloat16), head_grad, preferred_element_type=jnp.float32
                )
                key_part += jnp.dot(grad_scores, head_query, preferred_element_type=jnp.float32)
                query_part.append(
                    lax.dot_general(
                        grad_scores, key, (((0,), (0,)), ((), ())), preferred_element_type=jnp.float32
                    )
                )
            dq_ref[0, queries, :] = (
                jnp.where(lower, query_part[0], query_part[1]) * scale
            ).astype(jnp.bfloat16)
            dk_sum[keys, :] += key_part
            dv_sum[keys, :] += value_part

        for tiles in range(1, length // LANES + 1):
            pl.when(count == tiles)(functools.partial(window, tiles))
        return carry

    lax.fori_loop(0, length // QUERY_TILE, tile_step, 0)
    dk_ref[0] = (dk_sum[...] * scale).astype(jnp.bfloat16)
    dv_ref[0] = dv_sum[...].astype(jnp.bfloat16)


def windows_of(segments):
    heads = segments[:, ::QUERY_TILE]
    tails = segments[:, QUERY_TILE - 1 :: QUERY_TILE]
    begin = jnp.sum(segments[:, None, :] < heads[:, :, None], -1, dtype=jnp.int32)
    end = jnp.sum(segments[:, None, :] <= tails[:, :, None], -1, dtype=jnp.int32)
    start = begin // LANES
    return start, (end + LANES - 1) // LANES - start


def attention_call(kernel, row, windows, marks, operands, outputs, scratch, begun=()):
    rows, length, width = operands[0][0].shape
    wide = outputs[0]
    pairs = wide // LANES

    def block(first):
        return pl.BlockSpec((1, length, LANES), lambda pair, *_: (row, 0, first + pair))

    work = wide * length * length
    shape = jax.ShapeDtypeStruct((rows, length, wide), jnp.bfloat16)
    return pl.pallas_call(
        functools.partial(kernel, row, len(begun)),
        grid_spec=pltpu.PrefetchScalarGridSpec(
            num_scalar_prefetch=2,
            grid=(pairs,),
            in_specs=[
                pl.BlockSpec((1, length, LANES), lambda pair, *_: (row, 0, 0)),
                pl.BlockSpec((1, 8, length), lambda pair, *_: (row, 0, 0)),
            ]
            + [block(first) for _, first in operands]
            + [pl.BlockSpec(memory_space=pl.ANY)] * len(begun),
            out_specs=[block(0)] * len(outputs),
            scratch_shapes=scratch,
        ),
        out_shape=[shape] * len(outputs),
        input_output_aliases={4 + len(operands) + index: index for index in range(len(begun))},
        compiler_params=pltpu.CompilerParams(vmem_limit_bytes=48 * 1024 * 1024),
        cost_estimate=pl.CostEstimate(
            flops=4 * len(operands) * work,
            bytes_accessed=2 * (len(operands) + len(outputs)) * length * wide,
            transcendentals=work // HEAD_DIM,
        ),
    )(*windows, *marks, *(array for array, _ in operands), *begun)


def norm_stats(values):
    centred = values - jnp.mean(values, -1, keepdims=True)
    scale = lax.rsqrt(jnp.mean(centred * centred, -1, keepdims=True) + epsilon)
    return centred * scale, scale


def norm_back_rows(unit, scale, gain_vec, grad):
    scaled = grad * gain_vec
    inner = jnp.mean(scaled * unit, -1, keepdims=True)
    return scale * (scaled - jnp.mean(scaled, -1, keepdims=True) - unit * inner)


Z_SIZE = 4
RING = (0, 1, 3, 2)
PLACE = (0, 1, 3, 2)


def chip_place():
    index = lax.axis_index("rows")
    return index // 4, (index // 2) % 2, index % 2


def swap_x(values):
    return lax.ppermute(values, "rows", [(row, row ^ 1) for row in range(16)])


def swap_y(values):
    return lax.ppermute(values, "rows", [(row, row ^ 2) for row in range(16)])


def next_z(values):
    pairs = []
    for place in range(Z_SIZE):
        here, there = RING[place], RING[(place + 1) % Z_SIZE]
        pairs += [(here * 4 + rest, there * 4 + rest) for rest in range(4)]
    return lax.ppermute(values, "rows", pairs)


def ring_place():
    zed = chip_place()[0]
    return jnp.where(zed == 2, 3, jnp.where(zed == 3, 2, zed))


def tie(value, *after):
    return lax.optimization_barrier((value, after))[0]


def natural_z(steps):
    place = ring_place()
    stack = jnp.stack(steps)
    return jnp.stack(
        [
            lax.dynamic_index_in_dim(stack, (place - PLACE[zed]) % Z_SIZE, 0, keepdims=False)
            for zed in range(Z_SIZE)
        ]
    )


def load_pieces(place_ref, pieces, target_of, sems):
    copies = []
    for part in range(2):
        for index in range(4):
            piece = pieces[part * 4 + index]
            row_y, row_x = place_ref[1] ^ (index // 2), place_ref[2] ^ (index % 2)
            for zed in range(Z_SIZE):
                target = target_of(part, zed, row_y, row_x, piece)
                copies.append(pltpu.make_async_copy(piece.at[zed], target, sems.at[len(copies)]))
                copies[-1].start()
    return copies


def column_target(whole_ref):
    def target_of(part, zed, row_y, row_x, piece):
        _, depth, wide = piece.shape
        row = pl.multiple_of(((zed * 2 + row_y) * 2 + row_x) * depth, 16)
        left = 0 if part == 0 else whole_ref.shape[1] - wide
        return whole_ref.at[pl.ds(row, depth), pl.ds(left, wide)]

    return target_of


def assemble_columns_kernel(place_ref, *refs):
    *pieces, out_ref, sems = refs
    for copy in load_pieces(place_ref, pieces, column_target(out_ref), sems):
        copy.wait()


def assemble_rows_kernel(place_ref, *refs):
    *pieces, out_ref, sems = refs

    def target_of(part, zed, row_y, row_x, piece):
        depth = piece.shape[1]
        half = (zed // 2) ^ place_ref[3]
        row = (((zed % 2) * 2 + row_y) * 2 + row_x) * 2 * depth + part * depth
        return out_ref.at[half, pl.ds(pl.multiple_of(row, 16), depth), :]

    for copy in load_pieces(place_ref, pieces, target_of, sems):
        copy.wait()


def place_vector():
    return jnp.stack(chip_place() + (lax.axis_index("seq"),)).astype(jnp.int32)


def assemble(kernel, shape, parts):
    return pl.pallas_call(
        kernel,
        grid_spec=pltpu.PrefetchScalarGridSpec(
            num_scalar_prefetch=1,
            grid=(1,),
            in_specs=[pl.BlockSpec(memory_space=pl.ANY)] * 8,
            out_specs=pl.BlockSpec(shape, lambda step, *_: (0,) * len(shape)),
            scratch_shapes=[pltpu.SemaphoreType.DMA((32,))],
        ),
        out_shape=jax.ShapeDtypeStruct(shape, parts[0][0].dtype),
        compiler_params=pltpu.CompilerParams(vmem_limit_bytes=40 * 1024 * 1024),
    )(place_vector(), *parts[0], *parts[1])


FFN_TILE = 256
FFN_CHUNK = 640


def feed_forward_kernel(
    place_ref, normed_ref, cot_ref, *refs, begun
):
    up_pieces, refs = refs[:8], refs[8:]
    down_mine, down_other = refs[:2]
    refs = refs[4:] if begun else refs[2:]
    hidden_ref, grad_pre_ref, y_ref, grad_ref, up_ref, down_ref, up_sems, down_sems = refs
    step = pl.program_id(0)
    wide = down_mine.shape[1]

    def copies():
        down = []
        for index, piece in enumerate((down_mine, down_other)):
            left = pl.multiple_of((place_ref[3] ^ index) * wide, 128)
            target = down_ref.at[:, pl.ds(left, wide)]
            down.append(pltpu.make_async_copy(piece, target, down_sems.at[index]))
        return down

    @pl.when(step == 0)
    def _():
        waits = load_pieces(place_ref, up_pieces, column_target(up_ref), up_sems)
        waits += copies()
        for copy in waits[-2:]:
            copy.start()
        for copy in waits:
            copy.wait()

    normed = normed_ref[...]
    cot = cot_ref[...]
    y_sum = grad_sum = 0.0
    for chunk in range(hidden_ref.shape[1] // FFN_CHUNK):
        units = pl.ds(chunk * FFN_CHUNK, FFN_CHUNK)
        up, down = up_ref[:, units], down_ref[units, :]
        pre = jnp.dot(normed, up, preferred_element_type=jnp.float32)
        grad_hidden = lax.dot_general(
            cot, down, (((1,), (1,)), ((), ())), preferred_element_type=jnp.float32
        )
        phi = 0.5 + 0.5 * lax.erf(pre * root_half)
        hidden = (pre * phi).astype(jnp.bfloat16)
        slope = phi + pre * (jnp.exp(-0.5 * pre * pre) * root_two_pi)
        grad_pre = (grad_hidden * slope).astype(jnp.bfloat16)
        hidden_ref[:, units] = hidden
        grad_pre_ref[:, units] = grad_pre
        y_sum += jnp.dot(hidden, down, preferred_element_type=jnp.float32)
        grad_sum += lax.dot_general(
            grad_pre, up, (((1,), (1,)), ((), ())), preferred_element_type=jnp.float32
        )
    y_ref[...] = y_sum.astype(jnp.bfloat16)
    grad_ref[...] = grad_sum.astype(jnp.bfloat16)


root_two_pi = 0.3989422804014327


def feed_forward(normed, cot, up_parts, down_mine, down_other, begun=()):
    tokens, width = normed.shape
    units = down_mine.shape[0]
    tiles = tokens // FFN_TILE
    offset = tiles if begun else 0
    tile = pl.BlockSpec((FFN_TILE, width), lambda step, *_: (step, 0))
    wide_tile = pl.BlockSpec((FFN_TILE, units), lambda step, *_: (step + offset, 0))
    anywhere = pl.BlockSpec(memory_space=pl.ANY)
    wide_shape = jax.ShapeDtypeStruct((2 * tokens, units), jnp.bfloat16)
    shape = jax.ShapeDtypeStruct((tokens, width), jnp.bfloat16)
    return pl.pallas_call(
        functools.partial(feed_forward_kernel, begun=bool(begun)),
        grid_spec=pltpu.PrefetchScalarGridSpec(
            num_scalar_prefetch=1,
            grid=(tiles,),
            in_specs=[tile, tile] + [anywhere] * (10 + len(begun)),
            out_specs=[wide_tile, wide_tile, tile, tile],
            scratch_shapes=[
                pltpu.VMEM((width, units), jnp.bfloat16),
                pltpu.VMEM((units, width), jnp.bfloat16),
                pltpu.SemaphoreType.DMA((32,)),
                pltpu.SemaphoreType.DMA((2,)),
            ],
        ),
        out_shape=[wide_shape, wide_shape, shape, shape],
        input_output_aliases={13: 0, 14: 1} if begun else {},
        compiler_params=pltpu.CompilerParams(vmem_limit_bytes=56 * 1024 * 1024),
        cost_estimate=pl.CostEstimate(
            flops=8 * tokens * width * units,
            bytes_accessed=4 * width * units + 4 * tokens * (2 * width + units),
            transcendentals=2 * tokens * units,
        ),
    )(place_vector(), normed, cot, *up_parts[0], *up_parts[1], down_mine, down_other, *begun)


def following(zed):
    return (2 * zed + 1) % 5


def preceding(zed):
    return (3 * zed + 2) % 5


NORM_TILE = 64


def head_kernel(
    tokens_ref,
    gain_ref,
    cot_ref,
    piece_ref,
    up_ref,
    normed_out,
    cot_out,
    weights_out,
    up_out,
    token_buf,
    normed_buf,
    local_sems,
    send_sems,
    recv_sems,
):
    row, core = lax.axis_index("rows"), lax.axis_index("seq")
    zed, here_y, here_x = row // 4, (row // 2) % 2, row % 2
    rest = row - 4 * zed
    over_x, over_y = row + 1 - 2 * here_x, row + 2 - 4 * here_y
    onward, backward = following(zed) * 4 + rest, preceding(zed) * 4 + rest
    places = [zed]
    for _ in range(3):
        places.append(preceding(places[-1]))
    depth, wide = piece_ref.shape
    half = wide // 2

    barrier = pltpu.get_barrier_semaphore()
    for target in ((onward, core), (backward, core), (over_x, core), (over_y, core), (row, 1 - core)):
        pl.semaphore_signal(
            barrier, inc=1, device_id=target, device_id_type=pl.DeviceIdType.MESH
        )
    load = pltpu.make_async_copy(tokens_ref, token_buf, local_sems.at[0])
    load.start()
    own_rows = pl.ds(pl.multiple_of(row * depth, 16), depth)
    keeps = [
        pltpu.make_async_copy(piece_ref, weights_out.at[own_rows, :], local_sems.at[1]),
        pltpu.make_async_copy(up_ref, up_out.at[zed], local_sems.at[2]),
    ]
    for keep in keeps:
        keep.start()
    pl.semaphore_wait(barrier, 5)

    sent = []

    def send(src, dst, target):
        number = len(sent)
        copy = pltpu.make_async_remote_copy(
            src_ref=src,
            dst_ref=dst,
            send_sem=send_sems.at[number],
            recv_sem=recv_sems.at[number],
            device_id=target,
            device_id_type=pl.DeviceIdType.MESH,
        )
        copy.start()
        sent.append(copy)
        return copy

    def block(place, far_y, far_x, columns):
        at_y = 1 - here_y if far_y else here_y
        at_x = 1 - here_x if far_x else here_x
        index = (place * 2 + at_y) * 2 + at_x
        rows = pl.ds(pl.multiple_of(index * depth, 16), depth)
        return weights_out.at[rows, columns]

    everything, left, right = pl.ds(0, wide), pl.ds(0, half), pl.ds(half, half)

    def source(step, columns):
        if step == 0:
            return piece_ref.at[:, columns]
        return block(places[step], False, False, columns)

    def around(step):
        return send(
            source(step, everything), block(places[step], False, False, everything), (onward, core)
        )

    def around_up(step):
        src = up_ref if step == 0 else up_out.at[places[step]]
        return send(src, up_out.at[places[step]], (onward, core))

    def across(step):
        place = places[step]
        return (
            send(source(step, left), block(place, False, False, left), (over_y, core)),
            send(source(step, right), block(place, False, False, right), (over_x, core)),
            send(source(step, left), block(place, False, False, left), (over_x, core)),
            send(source(step, right), block(place, False, False, right), (over_y, core)),
        )

    def corner(step, crossing):
        place = places[step]
        crossing[0].wait_recv()
        far_left = block(place, True, False, left)
        first = send(far_left, far_left, (over_x, core))
        crossing[1].wait_recv()
        far_right = block(place, False, True, right)
        return first, send(far_right, far_right, (over_y, core))

    ring = around(0)
    crossing = across(0)
    arrivals = [crossing[2], crossing[3]]
    arrivals.append(send(cot_ref, cot_out, (row, 1 - core)))

    load.wait()
    span = token_buf.shape[1]
    for member in range(token_buf.shape[0]):

        def norm_tile(tile, carry, member=member):
            rows = pl.ds(pl.multiple_of(tile * NORM_TILE, NORM_TILE), NORM_TILE)
            unit, _ = norm_stats(token_buf[member, rows, :].astype(jnp.float32))
            normed_buf[member, rows, :] = (unit * gain_ref[...]).astype(jnp.bfloat16)
            return carry

        lax.fori_loop(0, span // NORM_TILE, norm_tile, 0)
    mine = normed_out.at[:, pl.ds(pl.multiple_of(core * span, 16), span), :]
    keeps.append(pltpu.make_async_copy(normed_buf, mine, local_sems.at[3]))
    keeps[-1].start()
    arrivals.append(send(normed_buf, mine, (row, 1 - core)))

    up_ring = None
    for step in range(1, 4):
        ring.wait_recv()
        if step < 3:
            ring = around(step)
        else:
            up_ring = around_up(0)
        arrivals += corner(step - 1, crossing)
        crossing = across(step)
        arrivals += crossing[2:]
    up_ring.wait_recv()
    up_ring = around_up(1)
    arrivals += corner(3, crossing)
    up_ring.wait_recv()
    arrivals.append(around_up(2))
    for copy in arrivals:
        copy.wait_recv()
    for copy in sent:
        copy.wait_send()
    for keep in keeps:
        keep.wait()


def head_call(tokens, gain, cotangent, piece, w_up):
    rows, span, width = tokens.shape
    depth, wide = piece.shape
    anywhere = pl.BlockSpec(memory_space=pl.ANY)
    return pl.pallas_call(
        head_kernel,
        in_specs=[anywhere, pl.BlockSpec(memory_space=pltpu.VMEM)] + [anywhere] * 3,
        out_specs=[anywhere] * 4,
        out_shape=[
            jax.ShapeDtypeStruct((rows, 2 * span, width), jnp.bfloat16),
            jax.ShapeDtypeStruct(cotangent.shape, jnp.bfloat16),
            jax.ShapeDtypeStruct((16 * depth, wide), jnp.bfloat16),
            jax.ShapeDtypeStruct((Z_SIZE,) + w_up.shape, jnp.bfloat16),
        ],
        scratch_shapes=[
            pltpu.VMEM(tokens.shape, jnp.bfloat16),
            pltpu.VMEM(tokens.shape, jnp.bfloat16),
            pltpu.SemaphoreType.DMA((4,)),
            pltpu.SemaphoreType.DMA((32,)),
            pltpu.SemaphoreType.DMA((32,)),
        ],
        compiler_params=pltpu.CompilerParams(
            collective_id=0, has_side_effects=True, vmem_limit_bytes=32 * 1024 * 1024
        ),
    )(tokens, gain.reshape(1, width), cotangent, piece, w_up)


def plus_wide(*terms):
    return sum(term.astype(jnp.float32) for term in terms)


def plus(*terms):
    return plus_wide(*terms).astype(jnp.bfloat16)


TAIL_TILE = 256


def tail_kernel(
    dq_ref,
    dk_ref,
    dv_ref,
    weights_ref,
    query_ref,
    key_ref,
    value_ref,
    tokens_ref,
    residual_ref,
    gain_ref,
    ffn_gain_ref,
    hidden_ref,
    token_out,
    query_out,
    key_out,
    value_out,
    gain_out,
    hidden_out,
    weight_buf,
    dq_buf,
    dk_buf,
    dv_buf,
    own_buf,
    away_buf,
    came_buf,
    token_buf,
    residual_buf,
    far_buf,
    near_buf,
    turned_buf,
    turned_came,
    sum_buf,
    ring_buf,
    ring_came,
    gain_buf,
    gain_came,
    hidden_buf,
    hidden_came,
    local_sems,
    send_sems,
    recv_sems,
):
    row, core = lax.axis_index("rows"), lax.axis_index("seq")
    zed, here_y, here_x = row // 4, (row // 2) % 2, row % 2
    rest = row - 4 * zed
    over_x, over_y = row + 1 - 2 * here_x, row + 2 - 4 * here_y
    onward, backward = following(zed) * 4 + rest, preceding(zed) * 4 + rest
    beside = (zed + 1 - 2 * (zed % 2)) * 4 + rest
    beyond = (zed + 2 - 4 * (zed // 2)) * 4 + rest
    places = [zed]
    for _ in range(3):
        places.append(preceding(places[-1]))
    depth = query_out.shape[0]
    half_wide = query_ref.shape[1]
    span = own_buf.shape[0] // 2

    barrier = pltpu.get_barrier_semaphore()
    for target in ((onward, core), (backward, core), (over_x, core), (over_y, core), (row, 1 - core)):
        pl.semaphore_signal(
            barrier, inc=1, device_id=target, device_id_type=pl.DeviceIdType.MESH
        )
    loads = [
        pltpu.make_async_copy(
            weights_ref.at[:, pl.ds(0, 3 * half_wide)], weight_buf, local_sems.at[0]
        )
    ]
    for index, (source, target) in enumerate(
        (
            (dq_ref, dq_buf),
            (dk_ref, dk_buf),
            (dv_ref, dv_buf),
            (tokens_ref, token_buf),
            (residual_ref, residual_buf),
        )
    ):
        loads.append(pltpu.make_async_copy(source, target, local_sems.at[1 + index]))
    for load in loads:
        load.start()
    pl.semaphore_wait(barrier, 5)

    sent = []

    def send(src, dst, target):
        number = len(sent)
        copy = pltpu.make_async_remote_copy(
            src_ref=src,
            dst_ref=dst,
            send_sem=send_sems.at[number],
            recv_sem=recv_sems.at[number],
            device_id=target,
            device_id_type=pl.DeviceIdType.MESH,
        )
        copy.start()
        sent.append(copy)
        return copy

    cut = (half_wide // 128 + 1) // 2 * 128
    streams = (
        (query_ref, 0, half_wide, 0, False),
        (key_ref, 0, cut, half_wide, False),
        (key_ref, cut, half_wide - cut, half_wide, True),
        (value_ref, 0, half_wide, 2 * half_wide, True),
    )

    def block_of(step, far_y, far_x):
        at_y = 1 - here_y if far_y else here_y
        at_x = 1 - here_x if far_x else here_x
        index = (places[step] * 2 + at_y) * 2 + at_x
        return pl.ds(pl.multiple_of(index * depth, 16), depth)

    far, near, turned = {}, {}, {}

    def issue(step):
        for which, (grad, column, wide, base, flip) in enumerate(streams):
            columns, place = pl.ds(column, wide), pl.ds(base + column, wide)
            target = (over_y if flip else over_x, core)
            far[step, which] = send(
                grad.at[block_of(step, True, True), columns], far_buf.at[step, :, place], target
            )
        for which, (grad, column, wide, base, flip) in enumerate(streams):
            columns, place = pl.ds(column, wide), pl.ds(base + column, wide)
            target = (over_y if flip else over_x, core)
            near[step, which] = send(
                grad.at[block_of(step, flip, not flip), columns],
                near_buf.at[step, :, place],
                target,
            )

    def turn(step):
        for which, (grad, column, wide, base, flip) in enumerate(streams):
            columns, place = pl.ds(column, wide), pl.ds(base + column, wide)
            far[step, which].wait_recv()
            turned_buf[step, :, place] = plus(
                grad[block_of(step, not flip, flip), columns], far_buf[step, :, place]
            )
            target = (over_x if flip else over_y, core)
            turned[step, which] = send(
                turned_buf.at[step, :, place], turned_came.at[step, :, place], target
            )

    def total(step):
        for which, (grad, column, wide, base, _) in enumerate(streams):
            columns, place = pl.ds(column, wide), pl.ds(base + column, wide)
            near[step, which].wait_recv()
            turned[step, which].wait_recv()
            sum_buf[step, :, place] = plus_wide(
                grad[block_of(step, False, False), columns],
                near_buf[step, :, place],
                turned_came[step, :, place],
            )

    ring = []

    def around(step):
        value = sum_buf[step]
        if step > 1:
            ring[-1].wait_recv()
            value = value + ring_came[step - 2].astype(jnp.float32)
        ring_buf[step - 1] = value.astype(jnp.bfloat16)
        ring.append(send(ring_buf.at[step - 1], ring_came.at[step - 1], (onward, core)))

    hidden_ring = []

    def around_hidden(step):
        value = hidden_ref[places[step]].astype(jnp.float32)
        if step > 1:
            hidden_ring[-1].wait_recv()
            value = value + hidden_came[step - 2].astype(jnp.float32)
        hidden_buf[step - 1] = value.astype(jnp.bfloat16)
        hidden_ring.append(
            send(hidden_buf.at[step - 1], hidden_came.at[step - 1], (onward, core))
        )

    def normed_tile(tile, half):
        first = (tile // 2) * 2 * span + half * span + (tile % 2) * TAIL_TILE
        rows = pl.ds(pl.multiple_of(first, TAIL_TILE), TAIL_TILE)
        part = 0.0
        for index, grad in enumerate((dq_buf, dk_buf, dv_buf)):
            part += lax.dot_general(
                grad[rows, :],
                weight_buf[:, pl.ds(index * half_wide, half_wide)],
                (((1,), (1,)), ((), ())),
                preferred_element_type=jnp.float32,
            )
        return pl.ds(pl.multiple_of(tile * TAIL_TILE, TAIL_TILE), TAIL_TILE), part

    def away_tile(tile, carry):
        rows, part = normed_tile(tile, 1 - core)
        away_buf[rows, :] = part.astype(jnp.bfloat16)
        return carry

    def own_tile(tile, carry):
        rows, part = normed_tile(tile, core)
        own_buf[rows, :] = part
        return carry

    def norm_tile(tile, carry):
        rows = pl.ds(pl.multiple_of(tile * NORM_TILE, NORM_TILE), NORM_TILE)
        grad = own_buf[rows, :] + came_buf[rows, :].astype(jnp.float32)
        unit, scale = norm_stats(token_buf[rows, :].astype(jnp.float32))
        residual_buf[rows, :] += norm_back_rows(unit, scale, gain_ref[...], grad)
        return carry + jnp.sum(grad * unit, 0, keepdims=True)

    tiles = own_buf.shape[0] // TAIL_TILE
    norm_tiles = own_buf.shape[0] // NORM_TILE
    issue(1)
    around_hidden(1)
    issue(2)
    for load in loads[:4]:
        load.wait()
    lax.fori_loop(0, tiles, away_tile, 0)
    away = send(away_buf, came_buf, (row, 1 - core))
    turn(1)
    around_hidden(2)
    issue(3)
    lax.fori_loop(0, tiles, own_tile, 0)
    total(1)
    around(1)
    turn(2)
    issue(0)
    for load in loads[4:]:
        load.wait()
    away.wait_recv()
    gain_part = jnp.zeros((1, own_buf.shape[1]), jnp.float32)
    gain_part = lax.fori_loop(0, norm_tiles // 2, norm_tile, gain_part)
    total(2)
    around_hidden(3)
    around(2)
    turn(3)
    gain_part = lax.fori_loop(norm_tiles // 2, norm_tiles, norm_tile, gain_part)
    store = pltpu.make_async_copy(residual_buf, token_out, local_sems.at[6])
    store.start()
    gain_buf[0] = jnp.zeros_like(gain_buf[0])
    gain_buf[0, 0:1] = gain_part
    gain_buf[0, 1:2] = ffn_gain_ref[...]

    def exchange(number, target):
        copy = send(gain_buf.at[number], gain_came.at[number], target)
        copy.wait_recv()
        gain_buf[number + 1] = gain_buf[number] + gain_came[number]

    exchange(0, (row, 1 - core))
    total(3)
    around(3)
    turn(0)
    exchange(1, (over_x, core))
    exchange(2, (over_y, core))
    exchange(3, (beside, core))
    exchange(4, (beyond, core))
    gain_out[...] = gain_buf[5]
    hidden_ring[-1].wait_recv()
    hidden_out[...] = hidden_ref[zed].astype(jnp.float32) + hidden_came[2].astype(jnp.float32)
    total(0)
    ring[-1].wait_recv()
    for index, out in enumerate((query_out, key_out, value_out)):
        columns = pl.ds(index * half_wide, half_wide)
        out[...] = sum_buf[0, :, columns] + ring_came[2, :, columns].astype(jnp.float32)
    for copy in sent:
        copy.wait_send()
    store.wait()


def tail_call(grads, weights, sums, tokens, grad_residual, gain, ffn_gain, hidden_sums):
    flat, width = grad_residual.shape
    half_wide = sums[0].shape[1]
    depth = sums[0].shape[0] // 16
    anywhere, here = pl.BlockSpec(memory_space=pl.ANY), pl.BlockSpec(memory_space=pltpu.VMEM)
    block = pltpu.VMEM((4, depth, 3 * half_wide), jnp.bfloat16)
    moving = pltpu.VMEM((3, depth, 3 * half_wide), jnp.bfloat16)
    gains = pltpu.VMEM((6, 8, width), jnp.float32)
    sum_shape = jax.ShapeDtypeStruct((depth, half_wide), jnp.float32)
    return pl.pallas_call(
        tail_kernel,
        in_specs=[anywhere] * 4 + [here] * 3 + [anywhere] * 2 + [here] * 3,
        out_specs=[anywhere] + [here] * 5,
        out_shape=[
            jax.ShapeDtypeStruct((flat, width), jnp.float32),
            sum_shape,
            sum_shape,
            sum_shape,
            jax.ShapeDtypeStruct((8, width), jnp.float32),
            jax.ShapeDtypeStruct(hidden_sums.shape[1:], jnp.float32),
        ],
        scratch_shapes=[pltpu.VMEM((width, 3 * half_wide), jnp.bfloat16)]
        + [pltpu.VMEM((2 * flat, half_wide), jnp.bfloat16)] * 3
        + [
            pltpu.VMEM((flat, width), jnp.float32),
            pltpu.VMEM((flat, width), jnp.bfloat16),
            pltpu.VMEM((flat, width), jnp.bfloat16),
            pltpu.VMEM((flat, width), jnp.bfloat16),
            pltpu.VMEM((flat, width), jnp.float32),
        ]
        + [block] * 4
        + [pltpu.VMEM((4, depth, 3 * half_wide), jnp.float32), moving, moving, gains, gains]
        + [pltpu.VMEM((3,) + hidden_sums.shape[1:], jnp.bfloat16)] * 2
        + [
            pltpu.SemaphoreType.DMA((7,)),
            pltpu.SemaphoreType.DMA((64,)),
            pltpu.SemaphoreType.DMA((64,)),
        ],
        compiler_params=pltpu.CompilerParams(
            collective_id=1, has_side_effects=True, vmem_limit_bytes=60 * 1024 * 1024
        ),
    )(
        *grads,
        weights,
        *sums,
        tokens,
        grad_residual,
        gain.reshape(1, width),
        ffn_gain.reshape(1, width),
        hidden_sums,
    )


def halves(block):
    depth, wide = block.shape
    if depth > 80:
        return block[: depth // 2], block[depth // 2 :]
    cut = (wide // 128 + 1) // 2 * 128
    return block[:, :cut], block[:, cut:]


def halves_z(stack):
    _, depth, wide = stack.shape
    if depth > 80:
        return stack[:, : depth // 2], stack[:, depth // 2 :]
    cut = (wide // 128 + 1) // 2 * 128
    return stack[:, :, :cut], stack[:, :, cut:]


def start_xy(first, second):
    return (first, swap_x(first), swap_y(first)), (second, swap_x(second), swap_y(second))


def finish_xy(first, second):
    return first + (swap_x(first[2]),), second + (swap_y(second[1]),)


def dot_low(left_side, right_side):
    return jnp.dot(left_side, right_side, preferred_element_type=jnp.float32)


def outer_low(left_side, right_side):
    return jnp.einsum(
        "tc,te->ce", left_side, right_side, preferred_element_type=jnp.float32
    ).astype(jnp.bfloat16)


class Scatter:

    def __init__(self, first, second, by_rows=False):
        self.parts, self.by_rows = (first, second), by_rows

    def pick(self, which, far_y, far_x):
        _, here_y, here_x = chip_place()
        picked = []
        for whole, row, depth, column, wide in self.parts[which]:
            blocks = whole.reshape(Z_SIZE, 2, 2, whole.shape[0] // 16, whole.shape[1])
            picked.append(
                lax.dynamic_slice(
                    blocks,
                    (0, here_y ^ far_y, here_x ^ far_x, row, column),
                    (Z_SIZE, 1, 1, depth, wide),
                ).reshape(Z_SIZE, depth, wide)
            )
        return picked[0] if len(picked) == 1 else jnp.concatenate(picked, 2)

    def spread(self):
        self.first_far = swap_x(self.pick(0, 1, 1))
        self.second_far = swap_y(self.pick(1, 1, 1))
        self.first_near = swap_x(self.pick(0, 0, 1))
        self.second_near = swap_y(self.pick(1, 1, 0))

    def turn(self):
        self.first_turned = swap_y(plus(self.pick(0, 1, 0), self.first_far))
        self.second_turned = swap_x(plus(self.pick(1, 0, 1), self.second_far))

    def near_sums(self):
        first = plus(self.pick(0, 0, 0), self.first_near, self.first_turned)
        second = plus(self.pick(1, 0, 0), self.second_near, self.second_turned)
        return jnp.concatenate([first, second], 1 if self.by_rows else 2)

    def gather(self):
        self.sums = self.near_sums()
        self.moving = next_z(self.block(1))

    def block(self, back):
        target = (ring_place() - back) % Z_SIZE
        zed = jnp.where(target == 2, 3, jnp.where(target == 3, 2, target))
        return lax.dynamic_index_in_dim(self.sums, zed, 0, keepdims=False)

    def step(self, number):
        self.moving = next_z(plus(self.block(number), self.moving))

    def finish(self):
        return self.block(0).astype(jnp.float32) + self.moving.astype(jnp.float32)

    def hold(self, names, *after):
        for name in names:
            setattr(self, name, tie(getattr(self, name), *after))


def body_pair(
    tokens, segments, gain_attn, w_query, w_key, w_value, w_out, gain_ffn, w_up, w_down, cotangent
):
    core = lax.axis_index("seq")
    rows, span, width = tokens.shape
    flat = rows * span

    def split(flat_rows, axis_width):
        return flat_rows.reshape(rows, 2 * span, axis_width)

    def sharing(values):
        wide = split(values, values.shape[-1])
        return swap_cores(own_half(wide, 1, 1 - core).astype(jnp.bfloat16))

    def shared(values, received):
        wide = split(values, values.shape[-1])
        return (own_half(wide, 1, core) + received.astype(jnp.float32)).reshape(flat, -1)

    attn_piece = jnp.concatenate([w_query, w_key, w_value, w_out], 1)
    half_wide = w_query.shape[1]
    normed, cot_other, attn_weights, up_stack = head_call(
        tokens, gain_attn, cotangent, attn_piece, w_up
    )
    first = core == 0
    tokens_own = tokens.reshape(flat, width).astype(jnp.float32)
    cot_own = cotangent.reshape(flat, width)
    windows = windows_of(segments)
    marks = (
        jnp.broadcast_to(segments[:, :, None], segments.shape + (LANES,)),
        jnp.broadcast_to(segments[:, None, :], (rows, 8, 2 * span)),
    )
    normed = normed.reshape(2 * flat, width)
    w_qkv = attn_weights[:, : 3 * half_wide]
    w_q, w_k, w_v = (w_qkv[:, i * half_wide : (i + 1) * half_wide] for i in range(3))

    up_parts = start_xy(*halves_z(up_stack))
    down_steps = [tie(w_down, up_stack)]
    down_steps.append(next_z(down_steps[-1]))
    w_o_half = attn_weights[:, 3 * half_wide :]
    w_o_other = swap_cores(w_o_half)
    qkv = dot_low(normed, w_qkv).astype(jnp.bfloat16)
    qkv, w_o_other, down_steps[1] = tie((qkv, w_o_other, down_steps[1]))
    down_steps.append(next_z(down_steps[-1]))
    qkv = split(qkv, 3 * half_wide)
    pairs = half_wide // LANES
    operands = [(qkv, 0), (qkv, pairs), (qkv, 2 * pairs)]

    def attend(row, operands, begun=()):
        return attention_call(
            attend_kernel, row, windows, marks, operands, [half_wide], [], begun
        )

    mixed = attend(0, operands)
    mixed, up_parts, down_steps[2] = tie((mixed, up_parts, down_steps[2]))
    up_parts = finish_xy(*up_parts)
    down_steps.append(next_z(down_steps[-1]))
    for row in range(1, rows):
        mixed = attend(row, operands, mixed)
    (mixed,) = mixed
    mixed, down_steps[3] = tie((mixed, down_steps[3]))
    down_parts = start_xy(*halves_z(natural_z(down_steps)))
    mixed, up_parts = tie((mixed, up_parts))
    w_o = jnp.where(
        first,
        jnp.concatenate([w_o_half, w_o_other], 1),
        jnp.concatenate([w_o_other, w_o_half], 1),
    )
    w_o_rows = own_half(w_o, 0, core)

    mixed_other = swap_cores(own_half(mixed, 1, 1 - core))
    mixed_mine = own_half(mixed, 1, core)
    mixed_own = jnp.where(
        first,
        jnp.concatenate([mixed_mine, mixed_other], 2),
        jnp.concatenate([mixed_other, mixed_mine], 2),
    ).reshape(flat, width)
    residual = tokens_own + dot_low(mixed_own, w_o)
    unit_two, scale_two = norm_stats(residual)
    normed_two = (unit_two * gain_ffn).astype(jnp.bfloat16)
    normed_two_other = swap_cores(normed_two)
    normed_two, down_parts = tie((normed_two, down_parts))
    down_parts = finish_xy(*down_parts)
    units = w_up.shape[1]
    down_columns = assemble(assemble_rows_kernel, (2, units, width // 2), down_parts)
    down_mine = down_columns[0]
    down_other = swap_cores(down_columns[1])
    weights = (up_parts, down_mine, down_other)
    cot_other = cot_other.reshape(flat, width)

    hidden_low, grad_pre, y_own, grad_two_own = feed_forward(normed_two, cot_own, *weights)
    (normed_two_other, hidden_low, grad_pre) = tie((normed_two_other, hidden_low, grad_pre))
    hidden_low, grad_pre, y_away, grad_two_away = feed_forward(
        normed_two_other, cot_other, *weights, begun=(hidden_low, grad_pre)
    )
    normed_two_all = jnp.concatenate([normed_two, normed_two_other], 0)
    cot_all = jnp.concatenate([cot_own, cot_other], 0)
    grad_two_came = swap_cores(grad_two_away)
    y_came = swap_cores(y_away)

    hidden_low = tie(hidden_low, grad_two_away, y_away)
    down_half = outer_low(hidden_low, cot_all)
    down_away = swap_cores(own_half(down_half, 1, 1 - core))
    grad_pre, normed_two_all = tie((grad_pre, normed_two_all), down_half)
    up_whole = outer_low(normed_two_all, grad_pre)
    down_away = tie(down_away, up_whole)
    down_kept = own_half(down_half, 1, core)
    down_whole = jnp.where(
        first,
        jnp.concatenate([down_kept, down_away], 0),
        jnp.concatenate([down_away, down_kept], 0),
    )
    depth, wide = w_down.shape
    down_sum = Scatter(
        [(down_whole, 0, depth // 2, 0, wide)],
        [(down_whole, depth // 2, depth // 2, 0, wide)],
        True,
    )
    down_sum.spread()
    grad_normed_two = plus_wide(grad_two_own, tie(grad_two_came, up_whole))
    grad_residual = cot_own.astype(jnp.float32) + norm_back_rows(
        unit_two, scale_two, gain_ffn, grad_normed_two
    )
    ffn_gain_part = jnp.sum(grad_normed_two * unit_two, 0)
    grad_attn = grad_residual.astype(jnp.bfloat16).reshape(rows, span, width)
    grad_attn_other = swap_cores(grad_attn)
    grad_attn_all = jnp.where(
        first,
        jnp.concatenate([grad_attn, grad_attn_other], 1),
        jnp.concatenate([grad_attn_other, grad_attn], 1),
    ).reshape(2 * flat, width)
    out_half = outer_low(mixed.reshape(2 * flat, -1), grad_attn_all)
    out_away = swap_cores(own_half(out_half, 1, 1 - core))
    grad_attn_all = tie(grad_attn_all, out_half)
    (grad_attn_all, down_sum.first_far, down_sum.second_far) = tie(
        (grad_attn_all, down_sum.first_far, down_sum.second_far)
    )
    down_sum.turn()
    grad_mixed = split(times_transposed(grad_attn_all, w_o_rows).astype(jnp.bfloat16), width // 2)
    out_kept = own_half(out_half, 1, core)
    out_whole = jnp.where(
        first,
        jnp.concatenate([out_kept, out_away], 0),
        jnp.concatenate([out_away, out_kept], 0),
    )
    depth, wide = w_up.shape
    cut = (wide + half_wide) // 256 * 128
    up_sum = Scatter(
        [(up_whole, 0, depth, 0, cut)],
        [(up_whole, 0, depth, cut, wide - cut), (out_whole, 0, depth, 0, half_wide)],
    )
    up_sum.spread()
    y_own, y_came = tie((y_own, y_came), grad_mixed)
    layer_out = (residual + plus_wide(y_own, y_came)).astype(jnp.bfloat16)
    down_names = ("first_near", "second_near", "first_turned", "second_turned")
    down_sum.hold(down_names, layer_out)
    grad_mixed = tie(grad_mixed, *(getattr(down_sum, name) for name in down_names))
    down_sum.gather()
    scratch = [pltpu.VMEM((2 * span, LANES), jnp.float32)] * 2

    def attend_back(row, grad_rows, begun=()):
        return attention_call(
            attend_back_kernel,
            row,
            windows,
            marks,
            operands + [(grad_rows, 0)],
            [half_wide] * 3,
            scratch,
            begun,
        )

    up_names = ("first_far", "second_far")
    grads = ()
    for row in range(rows):
        grads = attend_back(row, grad_mixed, grads)
        if row == 0:
            down_sum.hold(("moving",), *grads)
            up_sum.hold(up_names, *grads)
            grads = tie(grads, down_sum.moving, up_sum.first_far, up_sum.second_far)
            down_sum.step(2)
            up_sum.turn()
    grad_queries, grad_keys, grad_values = (grad.reshape(2 * flat, half_wide) for grad in grads)
    query_whole = outer_low(normed, grad_queries)
    key_whole = outer_low(normed, grad_keys)
    value_whole = outer_low(normed, grad_values)
    down_sum.hold(("moving",), query_whole)
    key_whole = tie(key_whole, down_sum.moving)
    down_sum.step(3)
    up_sum.hold(down_names, key_whole)
    sums = tie((query_whole, key_whole, value_whole), down_sum.moving)
    token_grad, query_grad, key_grad, value_grad, gains, up_out_grad = tail_call(
        (grad_queries, grad_keys, grad_values),
        attn_weights,
        sums,
        tokens.reshape(flat, width),
        grad_residual,
        gain_attn,
        ffn_gain_part,
        up_sum.near_sums(),
    )
    gain_attn_grad, gain_ffn_grad = gains[0], gains[1]
    down_grad = down_sum.finish()
    up_grad, out_grad = up_out_grad[:, : w_up.shape[1]], up_out_grad[:, w_up.shape[1] :]
    return (
        layer_out.reshape(rows, span, width),
        token_grad.reshape(rows, span, width),
        gain_attn_grad,
        query_grad,
        key_grad,
        value_grad,
        out_grad,
        gain_ffn_grad,
        up_grad,
        down_grad,
    )


def solution(mesh):
    paired = mesh.shape["seq"] == 2 and mesh.shape["rows"] == 16
    program = body_pair if paired else body
    return jax.shard_map(
        program,
        mesh=mesh,
        in_specs=(
            P("rows", "seq", None),
            P("rows", None),
            P(),
            P("rows", "seq"),
            P("rows", "seq"),
            P("rows", "seq"),
            P("rows", "seq"),
            P(),
            P("rows", "seq"),
            P("rows", "seq"),
            P("rows", "seq", None),
        ),
        out_specs=(
            P("rows", "seq", None),
            P("rows", "seq", None),
            P(),
            P("rows", "seq"),
            P("rows", "seq"),
            P("rows", "seq"),
            P("rows", "seq"),
            P(),
            P("rows", "seq"),
            P("rows", "seq"),
        ),
        check_vma=False,
    )
```

```python
import functools

import jax
import jax.numpy as jnp
from jax import lax
from jax.experimental import pallas as pl
from jax.experimental.pallas import tpu as pltpu
from jax.sharding import PartitionSpec as P

HEADS = 20
HEAD_DIM = 64


epsilon = 1e-05
root_half = 0.7071067811865476


def norm_rows(values, gain_vec):
    row_mean = jnp.mean(values, -1, keepdims=True)
    centred = values - row_mean
    spread = jnp.mean(centred * centred, -1, keepdims=True)
    return centred * lax.rsqrt(spread + epsilon) * gain_vec


def gelu_exact(values):
    return 0.5 * values * (1.0 + lax.erf(values * root_half))


def times_transposed(left_side, right_side):
    return jnp.einsum("te,de->td", left_side, right_side, preferred_element_type=jnp.float32)


def split_heads(rows_in):
    return rows_in.reshape(rows_in.shape[0], rows_in.shape[1], HEADS, HEAD_DIM)


def join_heads(heads_in):
    return heads_in.reshape(heads_in.shape[0], heads_in.shape[1], HEADS * HEAD_DIM)


def masked_scores(query_heads, key_heads, seg_query, seg_key):
    scores = jnp.einsum(
        "rqhd,rkhd->rhqk", query_heads, key_heads, preferred_element_type=jnp.float32
    )
    scores = scores * HEAD_DIM ** (-0.5)
    allowed = (seg_query[:, :, None] == seg_key[:, None, :])[:, None]
    return (allowed, jnp.where(allowed, scores, -1e30))


def attention_forward(query_rows, key_rows, value_rows, seg_query, seg_key):
    allowed, scores = masked_scores(
        split_heads(query_rows), split_heads(key_rows), seg_query, seg_key
    )
    row_top = jnp.max(scores, -1, keepdims=True)
    exponent = jnp.exp(scores - row_top)
    row_total = jnp.sum(exponent, -1, keepdims=True)
    prob_low = (exponent / row_total).astype(jnp.bfloat16)
    mixed_out = jnp.einsum(
        "rhqk,rkhd->rqhd", prob_low, split_heads(value_rows), preferred_element_type=jnp.float32
    )
    return (join_heads(mixed_out).astype(jnp.bfloat16), row_top + jnp.log(row_total))


def grad_pieces(query_heads, key_heads, value_heads, seg_query, seg_key, log_total, grad_heads):
    allowed, scores = masked_scores(query_heads, key_heads, seg_query, seg_key)
    prob_rows = jnp.where(allowed, jnp.exp(scores - log_total), 0.0)
    grad_probs = jnp.einsum(
        "rqhd,rkhd->rhqk", grad_heads, value_heads, preferred_element_type=jnp.float32
    )
    return (prob_rows, grad_probs)


def attention_grads(query_rows, key_rows, value_rows, seg_query, seg_key, log_total, grad_mixed):
    query_heads = split_heads(query_rows)
    key_heads = split_heads(key_rows)
    grad_heads = split_heads(grad_mixed)
    prob_rows, grad_probs = grad_pieces(
        query_heads, key_heads, split_heads(value_rows), seg_query, seg_key, log_total, grad_heads
    )
    value_part = jnp.einsum(
        "rhqk,rqhd->rkhd",
        prob_rows.astype(jnp.bfloat16),
        grad_heads,
        preferred_element_type=jnp.float32,
    )
    row_inner = jnp.sum(grad_probs * prob_rows, -1, keepdims=True)
    score_grad = (prob_rows * (grad_probs - row_inner)).astype(jnp.bfloat16)
    score_scale = HEAD_DIM ** (-0.5)
    query_part = (
        jnp.einsum("rhqk,rkhd->rqhd", score_grad, key_heads, preferred_element_type=jnp.float32)
        * score_scale
    )
    key_part = (
        jnp.einsum("rhqk,rqhd->rkhd", score_grad, query_heads, preferred_element_type=jnp.float32)
        * score_scale
    )
    return (join_heads(query_part), join_heads(key_part), join_heads(value_part))


def process(token_rows, cot_rows, seg_rows, gain_attn, gain_ffn, weights):
    w_query, w_key, w_value, w_out, w_up, w_down = weights
    row_count, query_count, model_width = token_rows.shape
    offset = lax.axis_index("seq") * query_count
    seg_query = lax.dynamic_slice_in_dim(seg_rows, offset, query_count, 1)

    def shaped(flat_rows):
        return flat_rows.reshape(row_count, query_count, model_width)

    flat_tokens = token_rows.reshape(row_count * query_count, model_width).astype(jnp.float32)
    normed, norm_back = jax.vjp(norm_rows, flat_tokens, gain_attn)
    lowered = normed.astype(jnp.bfloat16)
    queries = jnp.dot(lowered, w_query, preferred_element_type=jnp.float32).astype(jnp.bfloat16)
    key_rows = jnp.dot(lowered, w_key, preferred_element_type=jnp.float32).astype(jnp.bfloat16)
    value_rows = jnp.dot(lowered, w_value, preferred_element_type=jnp.float32).astype(jnp.bfloat16)
    key_whole, value_whole = (
        lax.all_gather(shaped(key_rows), "seq", axis=1, tiled=True),
        lax.all_gather(shaped(value_rows), "seq", axis=1, tiled=True),
    )
    mixed_rows, log_total = attention_forward(
        shaped(queries), key_whole, value_whole, seg_query, seg_rows
    )
    mixed_flat = mixed_rows.reshape(row_count * query_count, model_width)
    residual = flat_tokens + jnp.dot(mixed_flat, w_out, preferred_element_type=jnp.float32)
    normed_two, norm_two_back = jax.vjp(norm_rows, residual, gain_ffn)
    lowered_two = normed_two.astype(jnp.bfloat16)
    hidden_pre = jnp.dot(lowered_two, w_up, preferred_element_type=jnp.float32)
    hidden, gelu_back = jax.vjp(gelu_exact, hidden_pre)
    hidden_low = hidden.astype(jnp.bfloat16)
    layer_rows = (
        residual + jnp.dot(hidden_low, w_down, preferred_element_type=jnp.float32)
    ).astype(jnp.bfloat16)
    grad_out = cot_rows.reshape(row_count * query_count, model_width)
    grad_hidden = times_transposed(grad_out, w_down)
    grad_pre = gelu_back(grad_hidden)[0].astype(jnp.bfloat16)
    grad_normed_two = times_transposed(grad_pre, w_up)
    grad_resid_norm, grad_gain_ffn = norm_two_back(grad_normed_two)
    grad_residual = grad_out.astype(jnp.float32) + grad_resid_norm
    grad_attn = grad_residual.astype(jnp.bfloat16)
    grad_mixed = times_transposed(grad_attn, w_out).astype(jnp.bfloat16)
    query_part, key_part, value_part = attention_grads(
        shaped(queries), key_whole, value_whole, seg_query, seg_rows, log_total, shaped(grad_mixed)
    )
    key_own, value_own = (
        lax.psum_scatter(key_part, "seq", scatter_dimension=1, tiled=True),
        lax.psum_scatter(value_part, "seq", scatter_dimension=1, tiled=True),
    )
    grad_queries = query_part.reshape(row_count * query_count, model_width).astype(jnp.bfloat16)
    grad_keys = key_own.reshape(row_count * query_count, model_width).astype(jnp.bfloat16)
    grad_values = value_own.reshape(row_count * query_count, model_width).astype(jnp.bfloat16)
    grad_normed = (
        times_transposed(grad_queries, w_query)
        + times_transposed(grad_keys, w_key)
        + times_transposed(grad_values, w_value)
    )
    grad_token_norm, grad_gain_attn = norm_back(grad_normed)
    grad_tokens = (grad_residual + grad_token_norm).reshape(row_count, query_count, model_width)
    saved = (
        lowered,
        grad_queries,
        grad_keys,
        grad_values,
        mixed_flat,
        grad_attn,
        lowered_two,
        grad_pre,
        hidden_low,
        grad_out,
    )
    return (
        layer_rows.reshape(row_count, query_count, model_width),
        grad_tokens,
        saved,
        grad_gain_attn,
        grad_gain_ffn,
    )


def body(
    tokens, segments, gain_attn, w_query, w_key, w_value, w_out, gain_ffn, w_up, w_down, cotangent
):
    col_query = lax.all_gather(w_query, "seq", axis=1, tiled=True)
    col_key = lax.all_gather(w_key, "seq", axis=1, tiled=True)
    col_value = lax.all_gather(w_value, "seq", axis=1, tiled=True)
    col_out = lax.all_gather(w_out, "seq", axis=1, tiled=True)
    col_up = lax.all_gather(w_up, "seq", axis=1, tiled=True)
    col_down = lax.all_gather(w_down, "seq", axis=1, tiled=True)
    results = [
        process(
            tokens,
            cotangent,
            segments,
            gain_attn,
            gain_ffn,
            (
                lax.all_gather(col_query, "rows", axis=0, tiled=True),
                lax.all_gather(col_key, "rows", axis=0, tiled=True),
                lax.all_gather(col_value, "rows", axis=0, tiled=True),
                lax.all_gather(col_out, "rows", axis=0, tiled=True),
                lax.all_gather(col_up, "rows", axis=0, tiled=True),
                lax.all_gather(col_down, "rows", axis=0, tiled=True),
            ),
        )
    ]
    layer_out = jnp.concatenate([result_set[0] for result_set in results], 0)
    token_grad = jnp.concatenate([result_set[1] for result_set in results], 0)
    saved = [
        jnp.concatenate([result_set[2][member] for result_set in results], 0)
        for member in range(10)
    ]
    attn_gain_part = sum((result_set[3] for result_set in results))
    ffn_gain_part = sum((result_set[4] for result_set in results))
    gain_attn_grad, gain_ffn_grad = lax.psum((attn_gain_part, ffn_gain_part), ("rows", "seq"))
    (
        lowered,
        grad_queries,
        grad_keys,
        grad_values,
        mixed_flat,
        grad_attn,
        lowered_two,
        grad_pre,
        hidden_low,
        grad_out,
    ) = saved
    splits = lax.axis_size("seq")

    def arrange(grad_block):
        return grad_block.reshape(grad_block.shape[0], splits, grad_block.shape[1] // splits)

    def outer_product(left_side, right_side):
        return jnp.einsum("tc,te->ce", left_side, right_side, preferred_element_type=jnp.float32)

    def input_terms(offset, count):
        blocks = [
            outer_product(lowered, grad_queries),
            outer_product(lowered, grad_keys),
            outer_product(lowered, grad_values),
            outer_product(mixed_flat, grad_attn),
            outer_product(lowered_two, grad_pre),
        ]
        return jnp.concatenate([arrange(grad_block) for grad_block in blocks], 2)

    def hidden_terms(offset, count):
        return arrange(outer_product(hidden_low, grad_out))

    def spread_sum(term_of, shard_rows):
        row_part = lax.psum_scatter(
            term_of(jnp.int32(0), shard_rows * lax.axis_size("rows")),
            "rows",
            scatter_dimension=0,
            tiled=True,
        )
        return lax.psum_scatter(row_part, "seq", scatter_dimension=1, tiled=True)[:, 0, :]

    input_grads = spread_sum(input_terms, w_query.shape[0])
    down_grad = spread_sum(hidden_terms, w_down.shape[0])
    column_width = w_query.shape[1]
    query_grad = input_grads[:, :column_width]
    key_grad = input_grads[:, column_width : 2 * column_width]
    value_grad = input_grads[:, 2 * column_width : 3 * column_width]
    out_grad = input_grads[:, 3 * column_width : 4 * column_width]
    up_grad = input_grads[:, 4 * column_width :]
    return (
        layer_out,
        token_grad,
        gain_attn_grad,
        query_grad,
        key_grad,
        value_grad,
        out_grad,
        gain_ffn_grad,
        up_grad,
        down_grad,
    )


LANES = 128
QUERY_TILE = 128
BACK_TILE = 256
NEVER = -1e30


def swap_cores(values):
    return lax.ppermute(values, "seq", [(0, 1), (1, 0)])


def both_cores(values, axis):
    other = swap_cores(values)
    first = lax.axis_index("seq") == 0
    return jnp.where(
        first,
        jnp.concatenate([values, other], axis),
        jnp.concatenate([other, values], axis),
    )


def own_half(values, axis, index):
    half = values.shape[axis] // 2
    return lax.dynamic_slice_in_dim(values, index * half, half, axis)


def two_heads(ref, rows, columns):
    values = ref[0, rows, columns]
    lower = lax.broadcasted_iota(jnp.int32, values.shape, 1) < HEAD_DIM
    zero = jnp.zeros_like(values)
    return jnp.concatenate([jnp.where(lower, values, zero), jnp.where(lower, zero, values)], 0)


def merge_heads(values):
    half = values.shape[0] // 2
    lower = lax.broadcasted_iota(jnp.int32, (half, LANES), 1) < HEAD_DIM
    return jnp.where(lower, values[:half], values[half:])


def over_windows(first_row, query_tile, start_ref, count_ref, length, window):
    row = first_row + pl.program_id(0)

    def tile_step(tile, carry):
        begin = pl.multiple_of(start_ref[row, tile] * LANES, LANES)
        count = count_ref[row, tile]
        queries = pl.ds(pl.multiple_of(tile * query_tile, query_tile), query_tile)
        for tiles in range(1, length // LANES + 1):
            keys = pl.ds(begin, tiles * LANES)
            pl.when(count == tiles)(functools.partial(window, queries, keys))
        return carry

    lax.fori_loop(0, length // query_tile, tile_step, 0)


last_dims = (((1,), (1,)), ((), ()))
first_dims = (((0,), (0,)), ((), ()))
exponent_scale = HEAD_DIM ** (-0.5) * 1.4426950408889634


def attend_kernel(
    row, begun, start_ref, count_ref, column_ref, line_ref, q_ref, k_ref, v_ref, *rest
):
    (out_ref,) = rest[begun:]
    _, length, wide = q_ref.shape

    def window(queries, keys):
        allowed = column_ref[0, queries, :1] == line_ref[0, :1, keys]
        bias = jnp.where(allowed, 0.0, NEVER)[None]

        def scores_of(pair):
            columns = pl.ds(pair * LANES, LANES)
            return lax.dot_general(
                two_heads(q_ref, queries, columns),
                k_ref[0, keys, columns],
                last_dims,
                preferred_element_type=jnp.float32,
            )

        ahead = scores_of(0)
        for pair in range(wide // LANES):
            scores = ahead
            if (pair + 1) * LANES < wide:
                ahead = scores_of(pair + 1)
            shape = scores.shape
            scores = (scores.reshape((2, QUERY_TILE) + shape[1:]) + bias).reshape(shape)
            top = jnp.max(scores, -1, keepdims=True)
            exponent = jnp.exp2((scores - top) * exponent_scale)
            columns = pl.ds(pair * LANES, LANES)
            part = jnp.dot(
                exponent.astype(jnp.bfloat16),
                v_ref[0, keys, columns],
                preferred_element_type=jnp.float32,
            )
            part = part / jnp.sum(exponent, -1, keepdims=True)
            out_ref[0, queries, columns] = merge_heads(part).astype(jnp.bfloat16)

    over_windows(row, QUERY_TILE, start_ref, count_ref, length, window)


def attend_back_kernel(
    row, begun, start_ref, count_ref, column_ref, line_ref, q_ref, k_ref, v_ref, grad_ref, *rest
):
    dq_ref, dk_ref, dv_ref, dk_sum, dv_sum = rest[begun:]
    dk_sum[...] = jnp.zeros_like(dk_sum)
    dv_sum[...] = jnp.zeros_like(dv_sum)
    scale = HEAD_DIM ** (-0.5)
    columns = pl.ds(0, LANES)

    def window(queries, keys):
        query, grad = two_heads(q_ref, queries, columns), two_heads(grad_ref, queries, columns)
        key, value = k_ref[0, keys, :], v_ref[0, keys, :]
        bias = jnp.where(column_ref[0, keys, :1] == line_ref[0, :1, queries], 0.0, NEVER)
        scores = lax.dot_general(key, query, last_dims, preferred_element_type=jnp.float32)
        scores = scores + jnp.concatenate([bias, bias], 1)
        top = jnp.max(scores, 0, keepdims=True)
        exponent = jnp.exp2((scores - top) * exponent_scale)
        probs = exponent * (1.0 / jnp.sum(exponent, 0, keepdims=True))
        grad_probs = lax.dot_general(value, grad, last_dims, preferred_element_type=jnp.float32)
        inner = jnp.sum(grad_probs * probs, 0, keepdims=True)
        grad_scores = (probs * (grad_probs - inner)).astype(jnp.bfloat16)
        dv_sum[keys, :] += jnp.dot(
            probs.astype(jnp.bfloat16), grad, preferred_element_type=jnp.float32
        )
        dk_sum[keys, :] += jnp.dot(grad_scores, query, preferred_element_type=jnp.float32)
        query_part = lax.dot_general(
            grad_scores, key, first_dims, preferred_element_type=jnp.float32
        )
        dq_ref[0, queries, :] = (merge_heads(query_part) * scale).astype(jnp.bfloat16)

    over_windows(row, BACK_TILE, start_ref, count_ref, k_ref.shape[1], window)
    dk_ref[0] = (dk_sum[...] * scale).astype(jnp.bfloat16)
    dv_ref[0] = dv_sum[...].astype(jnp.bfloat16)


def windows_of(segments, query_tile):
    heads = segments[:, ::query_tile]
    tails = segments[:, query_tile - 1 :: query_tile]
    begin = jnp.sum(segments[:, None, :] < heads[:, :, None], -1, dtype=jnp.int32)
    end = jnp.sum(segments[:, None, :] <= tails[:, :, None], -1, dtype=jnp.int32)
    start = begin // LANES
    return start, (end + LANES - 1) // LANES - start


def attention_call(
    kernel, row, rows, windows, marks, operands, outputs, scratch, block_wide, begun=()
):
    all_rows, length, _ = operands[0][0].shape
    wide = outputs[0]
    steps = wide // block_wide

    def block(part):
        return pl.BlockSpec(
            (1, length, block_wide), lambda at, step, *_: (row + at, 0, part * steps + step)
        )

    work = rows * wide * length * length
    shape = jax.ShapeDtypeStruct((all_rows, length, wide), jnp.bfloat16)
    return pl.pallas_call(
        functools.partial(kernel, row, len(begun)),
        grid_spec=pltpu.PrefetchScalarGridSpec(
            num_scalar_prefetch=2,
            grid=(rows, steps),
            in_specs=[
                pl.BlockSpec((1, length, LANES), lambda at, *_: (row + at, 0, 0)),
                pl.BlockSpec((1, 8, length), lambda at, *_: (row + at, 0, 0)),
            ]
            + [block(first) for _, first in operands]
            + [pl.BlockSpec(memory_space=pl.ANY)] * len(begun),
            out_specs=[block(0)] * len(outputs),
            scratch_shapes=scratch,
        ),
        out_shape=[shape] * len(outputs),
        input_output_aliases={4 + len(operands) + index: index for index in range(len(begun))},
        compiler_params=pltpu.CompilerParams(vmem_limit_bytes=48 * 1024 * 1024),
        cost_estimate=pl.CostEstimate(
            flops=4 * len(operands) * work,
            bytes_accessed=2 * (len(operands) + len(outputs)) * rows * length * wide,
            transcendentals=work // HEAD_DIM,
        ),
    )(*windows, *marks, *(array for array, _ in operands), *begun)


def norm_stats(values):
    centred = values - jnp.mean(values, -1, keepdims=True)
    scale = lax.rsqrt(jnp.mean(centred * centred, -1, keepdims=True) + epsilon)
    return centred * scale, scale


def norm_back_rows(unit, scale, gain_vec, grad):
    scaled = grad * gain_vec
    inner = jnp.mean(scaled * unit, -1, keepdims=True)
    return scale * (scaled - jnp.mean(scaled, -1, keepdims=True) - unit * inner)


Z_SIZE = 4
RING = (0, 1, 3, 2)
PLACE = (0, 1, 3, 2)


def chip_place():
    index = lax.axis_index("rows")
    return index // 4, (index // 2) % 2, index % 2


def swap_x(values):
    return lax.ppermute(values, "rows", [(row, row ^ 1) for row in range(16)])


def swap_y(values):
    return lax.ppermute(values, "rows", [(row, row ^ 2) for row in range(16)])


def next_z(values):
    pairs = []
    for place in range(Z_SIZE):
        here, there = RING[place], RING[(place + 1) % Z_SIZE]
        pairs += [(here * 4 + rest, there * 4 + rest) for rest in range(4)]
    return lax.ppermute(values, "rows", pairs)


def ring_place():
    zed = chip_place()[0]
    return jnp.where(zed == 2, 3, jnp.where(zed == 3, 2, zed))


def tie(value, *after):
    return lax.optimization_barrier((value, after))[0]


def natural_z(steps):
    place = ring_place()
    stack = jnp.stack(steps)
    return jnp.stack(
        [
            lax.dynamic_index_in_dim(stack, (place - PLACE[zed]) % Z_SIZE, 0, keepdims=False)
            for zed in range(Z_SIZE)
        ]
    )


def load_pieces(place_ref, pieces, target_of, sems):
    copies = []
    for part in range(2):
        for across in range(2):
            for along in range(2):
                far_y, far_x = (along, across) if part == 0 else (across, along)
                row_y, row_x = place_ref[1] ^ far_y, place_ref[2] ^ far_x
                piece = pieces[part * 2 + across].at[along]
                for zed in range(Z_SIZE):
                    target = target_of(part, zed, row_y, row_x, piece)
                    copies.append(
                        pltpu.make_async_copy(piece.at[zed], target, sems.at[len(copies)])
                    )
                    copies[-1].start()
    return copies


def column_target(whole_ref):
    def target_of(part, zed, row_y, row_x, piece):
        _, depth, wide = piece.shape
        row = pl.multiple_of(((zed * 2 + row_y) * 2 + row_x) * depth, 16)
        left = 0 if part == 0 else whole_ref.shape[1] - wide
        return whole_ref.at[pl.ds(row, depth), pl.ds(left, wide)]

    return target_of


def assemble_columns_kernel(place_ref, *refs):
    *pieces, out_ref, sems = refs
    for copy in load_pieces(place_ref, pieces, column_target(out_ref), sems):
        copy.wait()


def place_vector():
    return jnp.stack(chip_place() + (lax.axis_index("seq"),)).astype(jnp.int32)


def assemble(kernel, shape, parts):
    return pl.pallas_call(
        kernel,
        grid_spec=pltpu.PrefetchScalarGridSpec(
            num_scalar_prefetch=1,
            grid=(1,),
            in_specs=[pl.BlockSpec(memory_space=pl.ANY)] * 4,
            out_specs=pl.BlockSpec(shape, lambda step, *_: (0,) * len(shape)),
            scratch_shapes=[pltpu.SemaphoreType.DMA((32,))],
        ),
        out_shape=jax.ShapeDtypeStruct(shape, parts[0][0].dtype),
        compiler_params=pltpu.CompilerParams(vmem_limit_bytes=40 * 1024 * 1024),
    )(place_vector(), *parts[0], *parts[1])


FFN_TILE = 256
FFN_CHUNK = 512
root_two_pi = 0.3989422804014327


def feed_forward_kernel(*refs):
    normed_ref, cot_ref, *refs = refs
    up_pieces, down_pieces, refs = refs[:4], refs[4:8], refs[8:]
    hidden_ref, grad_pre_ref, y_ref, grad_ref, normed_out, y_came, grad_came, *refs = refs
    up_ref, down_ref, normed_buf, y_away, grad_away, *refs = refs
    up_sems, down_sems, sent_sems, came_sems, normed_sems, away_sends, away_recvs = refs
    step = pl.program_id(0)
    row, core = lax.axis_index("rows"), lax.axis_index("seq")
    here_y, here_x = (row // 2) % 2, row % 2
    twin = (row, 1 - core)
    span = normed_ref.shape[0]
    tiles = span // FFN_TILE

    def remote(src, dst, send_sem, recv_sem):
        return pltpu.make_async_remote_copy(
            src_ref=src,
            dst_ref=dst,
            send_sem=send_sem,
            recv_sem=recv_sem,
            device_id=twin,
            device_id_type=pl.DeviceIdType.MESH,
        )

    def normed_copies():
        own, others = normed_buf.at[pl.ds(0, span), :], normed_buf.at[pl.ds(span, span), :]
        return (
            pltpu.make_async_copy(normed_ref, own, normed_sems.at[0]),
            remote(normed_ref, others, normed_sems.at[1], normed_sems.at[2]),
        )

    def up_copies():
        copies = []
        for part in range(2):
            for across in range(2):
                for along in range(2):
                    far_y, far_x = (along, across) if part == 0 else (across, along)
                    row_y = 1 - here_y if far_y else here_y
                    row_x = 1 - here_x if far_x else here_x
                    for zed in range(Z_SIZE):
                        piece = up_pieces[part * 2 + across].at[along, zed]
                        depth, wide = piece.shape
                        first = pl.multiple_of(((zed * 2 + row_y) * 2 + row_x) * depth, 16)
                        left = 0 if part == 0 else up_ref.shape[1] - wide
                        target = up_ref.at[pl.ds(first, depth), pl.ds(left, wide)]
                        copies.append(pltpu.make_async_copy(piece, target, up_sems.at[len(copies)]))
        return copies

    def down_copies():
        kept, given = [], []
        for part in range(2):
            for across in range(2):
                for along in range(2):
                    far_y, far_x = (along, across) if part == 0 else (across, along)
                    row_y = 1 - here_y if far_y else here_y
                    row_x = 1 - here_x if far_x else here_x
                    for lower in range(2):
                        pieces = down_pieces[part * 2 + across]
                        depth, wide = pieces.shape[2:]
                        first = (((lower * 2 + row_y) * 2 + row_x) * 2 + part) * depth
                        rows = pl.ds(pl.multiple_of(first, 16), depth)
                        target = down_ref.at[rows, pl.ds(pl.multiple_of(core * wide, 128), wide)]
                        number = len(kept)
                        kept.append(
                            pltpu.make_async_copy(
                                pieces.at[along, 2 * core + lower], target, down_sems.at[number]
                            )
                        )
                        given.append(
                            remote(
                                pieces.at[along, 2 * (1 - core) + lower],
                                target,
                                sent_sems.at[number],
                                came_sems.at[number],
                            )
                        )
        return kept, given

    def away_copies(tile):
        rows = pl.ds(pl.multiple_of(tile * FFN_TILE, FFN_TILE), FFN_TILE)
        return [
            remote(buf.at[tile], out.at[rows, :], away_sends.at[which, tile], away_recvs.at[which, tile])
            for which, (buf, out) in enumerate(((y_away, y_came), (grad_away, grad_came)))
        ]

    @pl.when(step == 0)
    def _():
        barrier = pltpu.get_barrier_semaphore()
        pl.semaphore_signal(barrier, inc=1, device_id=twin, device_id_type=pl.DeviceIdType.MESH)
        kept, given = down_copies()
        own, others = normed_copies()
        ups = up_copies()
        for copy in [own] + ups + kept:
            copy.start()
        pl.semaphore_wait(barrier, 1)
        for copy in given:
            copy.start()
        others.start()
        for copy in [own] + ups + kept:
            copy.wait()
        for copy in given:
            copy.wait_recv()

    @pl.when(step == tiles)
    def _():
        normed_copies()[1].wait_recv()

    normed = normed_buf[pl.ds(pl.multiple_of(step * FFN_TILE, FFN_TILE), FFN_TILE), :]
    cot = cot_ref[...]
    y_sum = grad_sum = 0.0
    for chunk in range(hidden_ref.shape[1] // FFN_CHUNK):
        units = pl.ds(chunk * FFN_CHUNK, FFN_CHUNK)
        up, down = up_ref[:, units], down_ref[units, :]
        pre = jnp.dot(normed, up, preferred_element_type=jnp.float32)
        grad_hidden = lax.dot_general(cot, down, last_dims, preferred_element_type=jnp.float32)
        phi = 0.5 + 0.5 * lax.erf(pre * root_half)
        hidden = (pre * phi).astype(jnp.bfloat16)
        slope = phi + pre * (jnp.exp(-0.5 * pre * pre) * root_two_pi)
        grad_pre = (grad_hidden * slope).astype(jnp.bfloat16)
        hidden_ref[:, units] = hidden
        grad_pre_ref[:, units] = grad_pre
        y_sum += jnp.dot(hidden, down, preferred_element_type=jnp.float32)
        grad_sum += lax.dot_general(grad_pre, up, last_dims, preferred_element_type=jnp.float32)

    @pl.when(step < tiles)
    def _():
        y_ref[...] = y_sum.astype(jnp.bfloat16)
        grad_ref[...] = grad_sum.astype(jnp.bfloat16)

    for tile in range(tiles):

        @pl.when(step == tiles + tile)
        def _(tile=tile):
            y_away[tile] = y_sum.astype(jnp.bfloat16)
            grad_away[tile] = grad_sum.astype(jnp.bfloat16)
            for copy in away_copies(tile):
                copy.start()

    @pl.when(step == 2 * tiles - 1)
    def _():
        store = pltpu.make_async_copy(normed_buf, normed_out, normed_sems.at[0])
        store.start()
        for copy in (*down_copies()[1], normed_copies()[1]):
            copy.wait_send()
        for tile in range(tiles):
            for copy in away_copies(tile):
                copy.wait()
        store.wait()


def feed_forward(normed, cot_all, up_parts, down_parts):
    tokens, width = normed.shape
    units = up_parts[0][0].shape[3] + up_parts[1][0].shape[3]
    tiles = tokens // FFN_TILE
    tile = pl.BlockSpec((FFN_TILE, width), lambda step: (step, 0))
    own_tile = pl.BlockSpec((FFN_TILE, width), lambda step: (jnp.minimum(step, tiles - 1), 0))
    wide_tile = pl.BlockSpec((FFN_TILE, units), lambda step: (step, 0))
    anywhere = pl.BlockSpec(memory_space=pl.ANY)
    wide_shape = jax.ShapeDtypeStruct((2 * tokens, units), jnp.bfloat16)
    shape = jax.ShapeDtypeStruct((tokens, width), jnp.bfloat16)
    away = pltpu.VMEM((tiles, FFN_TILE, width), jnp.bfloat16)
    sems = pltpu.SemaphoreType.DMA
    return pl.pallas_call(
        feed_forward_kernel,
        grid=(2 * tiles,),
        in_specs=[anywhere, tile] + [anywhere] * 8,
        out_specs=[wide_tile, wide_tile, own_tile, own_tile] + [anywhere] * 3,
        out_shape=[
            wide_shape,
            wide_shape,
            shape,
            shape,
            jax.ShapeDtypeStruct((2 * tokens, width), jnp.bfloat16),
            shape,
            shape,
        ],
        scratch_shapes=[
            pltpu.VMEM((width, units), jnp.bfloat16),
            pltpu.VMEM((units, width), jnp.bfloat16),
            pltpu.VMEM((2 * tokens, width), jnp.bfloat16),
            away,
            away,
            sems((32,)),
            sems((16,)),
            sems((16,)),
            sems((16,)),
            sems((3,)),
            sems((2, tiles)),
            sems((2, tiles)),
        ],
        compiler_params=pltpu.CompilerParams(
            collective_id=2, has_side_effects=True, vmem_limit_bytes=60 * 1024 * 1024
        ),
        cost_estimate=pl.CostEstimate(
            flops=16 * tokens * width * units,
            bytes_accessed=4 * width * units + 8 * tokens * (2 * width + units),
            transcendentals=4 * tokens * units,
        ),
    )(normed, cot_all, *up_parts[0], *up_parts[1], *down_parts[0], *down_parts[1])


def following(zed):
    return (2 * zed + 1) % 5


def preceding(zed):
    return (3 * zed + 2) % 5


NORM_TILE = 64


def head_kernel(
    tokens_ref,
    gain_ref,
    cot_ref,
    piece_ref,
    up_ref,
    normed_out,
    cot_out,
    weights_out,
    up_out,
    token_buf,
    normed_buf,
    local_sems,
    send_sems,
    recv_sems,
):
    row, core = lax.axis_index("rows"), lax.axis_index("seq")
    zed, here_y, here_x = row // 4, (row // 2) % 2, row % 2
    rest = row - 4 * zed
    over_x, over_y = row + 1 - 2 * here_x, row + 2 - 4 * here_y
    onward, backward = following(zed) * 4 + rest, preceding(zed) * 4 + rest
    places = [zed]
    for _ in range(3):
        places.append(preceding(places[-1]))
    depth, wide = piece_ref.shape
    half = wide // 2

    barrier = pltpu.get_barrier_semaphore()
    for target in ((onward, core), (backward, core), (over_x, core), (over_y, core), (row, 1 - core)):
        pl.semaphore_signal(
            barrier, inc=1, device_id=target, device_id_type=pl.DeviceIdType.MESH
        )
    load = pltpu.make_async_copy(tokens_ref, token_buf, local_sems.at[0])
    load.start()
    own_rows = pl.ds(pl.multiple_of(row * depth, 16), depth)
    keeps = [
        pltpu.make_async_copy(piece_ref, weights_out.at[own_rows, :], local_sems.at[1]),
        pltpu.make_async_copy(up_ref, up_out.at[zed], local_sems.at[2]),
    ]
    for keep in keeps:
        keep.start()
    pl.semaphore_wait(barrier, 5)

    sent = []

    def send(src, dst, target):
        number = len(sent)
        copy = pltpu.make_async_remote_copy(
            src_ref=src,
            dst_ref=dst,
            send_sem=send_sems.at[number],
            recv_sem=recv_sems.at[number],
            device_id=target,
            device_id_type=pl.DeviceIdType.MESH,
        )
        copy.start()
        sent.append(copy)
        return copy

    def block(place, far_y, far_x, columns):
        at_y = 1 - here_y if far_y else here_y
        at_x = 1 - here_x if far_x else here_x
        index = (place * 2 + at_y) * 2 + at_x
        rows = pl.ds(pl.multiple_of(index * depth, 16), depth)
        return weights_out.at[rows, columns]

    everything, left, right = pl.ds(0, wide), pl.ds(0, half), pl.ds(half, half)

    def source(step, columns):
        if step == 0:
            return piece_ref.at[:, columns]
        return block(places[step], False, False, columns)

    def around(step):
        return send(
            source(step, everything), block(places[step], False, False, everything), (onward, core)
        )

    def around_up(step):
        src = up_ref if step == 0 else up_out.at[places[step]]
        return send(src, up_out.at[places[step]], (onward, core))

    def across(step):
        place = places[step]
        return (
            send(source(step, left), block(place, False, False, left), (over_y, core)),
            send(source(step, right), block(place, False, False, right), (over_x, core)),
            send(source(step, left), block(place, False, False, left), (over_x, core)),
            send(source(step, right), block(place, False, False, right), (over_y, core)),
        )

    def corner(step, crossing):
        place = places[step]
        crossing[0].wait_recv()
        far_left = block(place, True, False, left)
        first = send(far_left, far_left, (over_x, core))
        crossing[1].wait_recv()
        far_right = block(place, False, True, right)
        return first, send(far_right, far_right, (over_y, core))

    ring = around(0)
    crossing = across(0)
    arrivals = [crossing[2], crossing[3]]
    arrivals.append(send(cot_ref, cot_out, (row, 1 - core)))

    load.wait()
    span = token_buf.shape[1]
    for member in range(token_buf.shape[0]):

        def norm_tile(tile, carry, member=member):
            rows = pl.ds(pl.multiple_of(tile * NORM_TILE, NORM_TILE), NORM_TILE)
            unit, _ = norm_stats(token_buf[member, rows, :].astype(jnp.float32))
            normed_buf[member, rows, :] = (unit * gain_ref[...]).astype(jnp.bfloat16)
            return carry

        lax.fori_loop(0, span // NORM_TILE, norm_tile, 0)
    mine = normed_out.at[:, pl.ds(pl.multiple_of(core * span, 16), span), :]
    keeps.append(pltpu.make_async_copy(normed_buf, mine, local_sems.at[3]))
    keeps[-1].start()
    arrivals.append(send(normed_buf, mine, (row, 1 - core)))

    up_ring = None
    for step in range(1, 4):
        ring.wait_recv()
        if step < 3:
            ring = around(step)
        else:
            up_ring = around_up(0)
        arrivals += corner(step - 1, crossing)
        crossing = across(step)
        arrivals += crossing[2:]
    up_ring.wait_recv()
    up_ring = around_up(1)
    arrivals += corner(3, crossing)
    up_ring.wait_recv()
    arrivals.append(around_up(2))
    for copy in arrivals:
        copy.wait_recv()
    for copy in sent:
        copy.wait_send()
    for keep in keeps:
        keep.wait()


def head_call(tokens, gain, cotangent, piece, w_up):
    rows, span, width = tokens.shape
    depth, wide = piece.shape
    anywhere = pl.BlockSpec(memory_space=pl.ANY)
    return pl.pallas_call(
        head_kernel,
        in_specs=[anywhere, pl.BlockSpec(memory_space=pltpu.VMEM)] + [anywhere] * 3,
        out_specs=[anywhere] * 4,
        out_shape=[
            jax.ShapeDtypeStruct((rows, 2 * span, width), jnp.bfloat16),
            jax.ShapeDtypeStruct(cotangent.shape, jnp.bfloat16),
            jax.ShapeDtypeStruct((16 * depth, wide), jnp.bfloat16),
            jax.ShapeDtypeStruct((Z_SIZE,) + w_up.shape, jnp.bfloat16),
        ],
        scratch_shapes=[
            pltpu.VMEM(tokens.shape, jnp.bfloat16),
            pltpu.VMEM(tokens.shape, jnp.bfloat16),
            pltpu.SemaphoreType.DMA((4,)),
            pltpu.SemaphoreType.DMA((32,)),
            pltpu.SemaphoreType.DMA((32,)),
        ],
        compiler_params=pltpu.CompilerParams(
            collective_id=0, has_side_effects=True, vmem_limit_bytes=32 * 1024 * 1024
        ),
    )(tokens, gain.reshape(1, width), cotangent, piece, w_up)


def plus_wide(*terms):
    return sum(term.astype(jnp.float32) for term in terms)


def plus(*terms):
    return plus_wide(*terms).astype(jnp.bfloat16)


TAIL_TILE = 256


def tail_kernel(
    dq_ref,
    dk_ref,
    dv_ref,
    weights_ref,
    query_ref,
    key_ref,
    value_ref,
    tokens_ref,
    residual_ref,
    gain_ref,
    ffn_gain_ref,
    hidden_ref,
    token_out,
    query_out,
    key_out,
    value_out,
    gain_out,
    up_out,
    out_out,
    weight_buf,
    dq_buf,
    dk_buf,
    dv_buf,
    own_buf,
    away_buf,
    came_buf,
    token_buf,
    residual_buf,
    far_buf,
    near_buf,
    turned_buf,
    turned_came,
    sum_buf,
    ring_buf,
    ring_came,
    gain_buf,
    gain_came,
    hidden_buf,
    hidden_came,
    local_sems,
    send_sems,
    recv_sems,
):
    row, core = lax.axis_index("rows"), lax.axis_index("seq")
    zed, here_y, here_x = row // 4, (row // 2) % 2, row % 2
    rest = row - 4 * zed
    over_x, over_y = row + 1 - 2 * here_x, row + 2 - 4 * here_y
    onward, backward = following(zed) * 4 + rest, preceding(zed) * 4 + rest
    beside = (zed + 1 - 2 * (zed % 2)) * 4 + rest
    beyond = (zed + 2 - 4 * (zed // 2)) * 4 + rest
    places = [zed]
    for _ in range(3):
        places.append(preceding(places[-1]))
    depth = query_out.shape[0]
    half_wide = query_ref.shape[1]
    span = own_buf.shape[0] // 2

    barrier = pltpu.get_barrier_semaphore()
    for target in ((onward, core), (backward, core), (over_x, core), (over_y, core), (row, 1 - core)):
        pl.semaphore_signal(
            barrier, inc=1, device_id=target, device_id_type=pl.DeviceIdType.MESH
        )
    loads = [
        pltpu.make_async_copy(
            weights_ref.at[:, pl.ds(0, 3 * half_wide)], weight_buf, local_sems.at[0]
        )
    ]
    for index, (source, target) in enumerate(
        (
            (dq_ref, dq_buf),
            (dk_ref, dk_buf),
            (dv_ref, dv_buf),
            (tokens_ref, token_buf),
            (residual_ref, residual_buf),
        )
    ):
        loads.append(pltpu.make_async_copy(source, target, local_sems.at[1 + index]))
    for load in loads:
        load.start()
    pl.semaphore_wait(barrier, 5)

    sent = []

    def send(src, dst, target):
        number = len(sent)
        copy = pltpu.make_async_remote_copy(
            src_ref=src,
            dst_ref=dst,
            send_sem=send_sems.at[number],
            recv_sem=recv_sems.at[number],
            device_id=target,
            device_id_type=pl.DeviceIdType.MESH,
        )
        copy.start()
        sent.append(copy)
        return copy

    cut = (half_wide // 128 + 1) // 2 * 128
    streams = (
        (query_ref, 0, half_wide, 0, False),
        (key_ref, 0, cut, half_wide, False),
        (key_ref, cut, half_wide - cut, half_wide, True),
        (value_ref, 0, half_wide, 2 * half_wide, True),
    )

    def block_of(step, far_y, far_x):
        at_y = 1 - here_y if far_y else here_y
        at_x = 1 - here_x if far_x else here_x
        index = (places[step] * 2 + at_y) * 2 + at_x
        return pl.ds(pl.multiple_of(index * depth, 16), depth)

    far, near, turned = {}, {}, {}

    def issue(step):
        for which, (grad, column, wide, base, flip) in enumerate(streams):
            columns, place = pl.ds(column, wide), pl.ds(base + column, wide)
            target = (over_y if flip else over_x, core)
            far[step, which] = send(
                grad.at[block_of(step, True, True), columns], far_buf.at[step, :, place], target
            )
        for which, (grad, column, wide, base, flip) in enumerate(streams):
            columns, place = pl.ds(column, wide), pl.ds(base + column, wide)
            target = (over_y if flip else over_x, core)
            near[step, which] = send(
                grad.at[block_of(step, flip, not flip), columns],
                near_buf.at[step, :, place],
                target,
            )

    def turn(step):
        for which, (grad, column, wide, base, flip) in enumerate(streams):
            columns, place = pl.ds(column, wide), pl.ds(base + column, wide)
            far[step, which].wait_recv()
            turned_buf[step, :, place] = plus(
                grad[block_of(step, not flip, flip), columns], far_buf[step, :, place]
            )
            target = (over_x if flip else over_y, core)
            turned[step, which] = send(
                turned_buf.at[step, :, place], turned_came.at[step, :, place], target
            )

    def total(step):
        for which, (grad, column, wide, base, _) in enumerate(streams):
            columns, place = pl.ds(column, wide), pl.ds(base + column, wide)
            near[step, which].wait_recv()
            turned[step, which].wait_recv()
            sum_buf[step, :, place] = plus_wide(
                grad[block_of(step, False, False), columns],
                near_buf[step, :, place],
                turned_came[step, :, place],
            )

    ring = []

    def around(step):
        value = sum_buf[step]
        if step > 1:
            ring[-1].wait_recv()
            value = value + ring_came[step - 2].astype(jnp.float32)
        ring_buf[step - 1] = value.astype(jnp.bfloat16)
        ring.append(send(ring_buf.at[step - 1], ring_came.at[step - 1], (onward, core)))

    hidden_ring = []

    def around_hidden(step):
        value = hidden_ref[places[step]].astype(jnp.float32)
        if step > 1:
            hidden_ring[-1].wait_recv()
            value = value + hidden_came[step - 2].astype(jnp.float32)
        hidden_buf[step - 1] = value.astype(jnp.bfloat16)
        hidden_ring.append(
            send(hidden_buf.at[step - 1], hidden_came.at[step - 1], (onward, core))
        )

    def normed_tile(tile, half):
        first = (tile // 2) * 2 * span + half * span + (tile % 2) * TAIL_TILE
        rows = pl.ds(pl.multiple_of(first, TAIL_TILE), TAIL_TILE)
        part = 0.0
        for index, grad in enumerate((dq_buf, dk_buf, dv_buf)):
            part += lax.dot_general(
                grad[rows, :],
                weight_buf[:, pl.ds(index * half_wide, half_wide)],
                (((1,), (1,)), ((), ())),
                preferred_element_type=jnp.float32,
            )
        return pl.ds(pl.multiple_of(tile * TAIL_TILE, TAIL_TILE), TAIL_TILE), part

    def away_tile(tile, carry):
        rows, part = normed_tile(tile, 1 - core)
        away_buf[rows, :] = part.astype(jnp.bfloat16)
        return carry

    def own_tile(tile, carry):
        rows, part = normed_tile(tile, core)
        own_buf[rows, :] = part
        return carry

    def norm_tile(tile, carry):
        rows = pl.ds(pl.multiple_of(tile * NORM_TILE, NORM_TILE), NORM_TILE)
        grad = own_buf[rows, :] + came_buf[rows, :].astype(jnp.float32)
        unit, scale = norm_stats(token_buf[rows, :].astype(jnp.float32))
        residual_buf[rows, :] += norm_back_rows(unit, scale, gain_ref[...], grad)
        return carry + jnp.sum(grad * unit, 0, keepdims=True)

    tiles = own_buf.shape[0] // TAIL_TILE
    norm_tiles = own_buf.shape[0] // NORM_TILE
    middle, quarter = tiles // 2, norm_tiles // 4
    issue(1)
    around_hidden(1)
    issue(2)
    for load in loads[:4]:
        load.wait()
    lax.fori_loop(0, middle, away_tile, 0)
    turn(1)
    issue(3)
    lax.fori_loop(middle, tiles, away_tile, 0)
    away = send(away_buf, came_buf, (row, 1 - core))
    around_hidden(2)
    lax.fori_loop(0, middle, own_tile, 0)
    turn(2)
    total(1)
    around(1)
    issue(0)
    lax.fori_loop(middle, tiles, own_tile, 0)
    for load in loads[4:]:
        load.wait()
    away.wait_recv()
    gain_part = jnp.zeros((1, own_buf.shape[1]), jnp.float32)
    gain_part = lax.fori_loop(0, quarter, norm_tile, gain_part)
    turn(3)
    around_hidden(3)
    gain_part = lax.fori_loop(quarter, 2 * quarter, norm_tile, gain_part)
    total(2)
    around(2)
    gain_part = lax.fori_loop(2 * quarter, 3 * quarter, norm_tile, gain_part)
    turn(0)
    gain_part = lax.fori_loop(3 * quarter, norm_tiles, norm_tile, gain_part)
    store = pltpu.make_async_copy(residual_buf, token_out, local_sems.at[6])
    store.start()
    gain_buf[0] = jnp.zeros_like(gain_buf[0])
    gain_buf[0, 0:1] = gain_part
    gain_buf[0, 1:2] = ffn_gain_ref[...]

    def exchange(number, target):
        copy = send(gain_buf.at[number], gain_came.at[number], target)
        copy.wait_recv()
        gain_buf[number + 1] = gain_buf[number] + gain_came[number]

    exchange(0, (row, 1 - core))
    exchange(1, (over_x, core))
    total(3)
    around(3)
    exchange(2, (over_y, core))
    exchange(3, (beside, core))
    exchange(4, (beyond, core))
    gain_out[...] = gain_buf[5]
    hidden_ring[-1].wait_recv()
    up_wide = up_out.shape[1]
    for out, columns in ((up_out, pl.ds(0, up_wide)), (out_out, pl.ds(up_wide, half_wide))):
        out[...] = plus_wide(hidden_ref[zed, :, columns], hidden_came[2, :, columns])
    total(0)
    ring[-1].wait_recv()
    for index, out in enumerate((query_out, key_out, value_out)):
        columns = pl.ds(index * half_wide, half_wide)
        out[...] = sum_buf[0, :, columns] + ring_came[2, :, columns].astype(jnp.float32)
    for copy in sent:
        copy.wait_send()
    store.wait()


def tail_call(grads, weights, sums, tokens, grad_residual, gain, ffn_gain, hidden_sums):
    flat, width = grad_residual.shape
    half_wide = sums[0].shape[1]
    depth = sums[0].shape[0] // 16
    anywhere, here = pl.BlockSpec(memory_space=pl.ANY), pl.BlockSpec(memory_space=pltpu.VMEM)
    block = pltpu.VMEM((4, depth, 3 * half_wide), jnp.bfloat16)
    moving = pltpu.VMEM((3, depth, 3 * half_wide), jnp.bfloat16)
    gains = pltpu.VMEM((6, 8, width), jnp.float32)
    sum_shape = jax.ShapeDtypeStruct((depth, half_wide), jnp.float32)
    return pl.pallas_call(
        tail_kernel,
        in_specs=[anywhere] * 4 + [here] * 3 + [anywhere] * 2 + [here] * 3,
        out_specs=[anywhere] + [here] * 6,
        out_shape=[
            jax.ShapeDtypeStruct((flat, width), jnp.float32),
            sum_shape,
            sum_shape,
            sum_shape,
            jax.ShapeDtypeStruct((8, width), jnp.float32),
            jax.ShapeDtypeStruct((depth, hidden_sums.shape[2] - half_wide), jnp.float32),
            sum_shape,
        ],
        scratch_shapes=[pltpu.VMEM((width, 3 * half_wide), jnp.bfloat16)]
        + [pltpu.VMEM((2 * flat, half_wide), jnp.bfloat16)] * 3
        + [
            pltpu.VMEM((flat, width), jnp.float32),
            pltpu.VMEM((flat, width), jnp.bfloat16),
            pltpu.VMEM((flat, width), jnp.bfloat16),
            pltpu.VMEM((flat, width), jnp.bfloat16),
            pltpu.VMEM((flat, width), jnp.float32),
        ]
        + [block] * 4
        + [pltpu.VMEM((4, depth, 3 * half_wide), jnp.float32), moving, moving, gains, gains]
        + [pltpu.VMEM((3,) + hidden_sums.shape[1:], jnp.bfloat16)] * 2
        + [
            pltpu.SemaphoreType.DMA((7,)),
            pltpu.SemaphoreType.DMA((64,)),
            pltpu.SemaphoreType.DMA((64,)),
        ],
        compiler_params=pltpu.CompilerParams(
            collective_id=1, has_side_effects=True, vmem_limit_bytes=60 * 1024 * 1024
        ),
    )(
        *grads,
        weights,
        *sums,
        tokens,
        grad_residual,
        gain.reshape(1, width),
        ffn_gain.reshape(1, width),
        hidden_sums,
    )


def halves_z(stack):
    _, depth, wide = stack.shape
    if depth > 80:
        return stack[:, : depth // 2], stack[:, depth // 2 :]
    cut = (wide // 128 + 1) // 2 * 128
    return stack[:, :, :cut], stack[:, :, cut:]


def gather_first(first, second):
    return jnp.stack([first, swap_y(first)]), jnp.stack([second, swap_x(second)])


def gather_second(first, second):
    return (first, swap_x(first)), (second, swap_y(second))


def dot_low(left_side, right_side):
    return jnp.dot(left_side, right_side, preferred_element_type=jnp.float32)


def outer_low(left_side, right_side):
    return jnp.einsum(
        "tc,te->ce", left_side, right_side, preferred_element_type=jnp.float32
    ).astype(jnp.bfloat16)


class Scatter:

    def __init__(self, first, second, by_rows=False):
        self.parts, self.by_rows = (first, second), by_rows

    def pick(self, which, start_y, start_x, count_y=1, count_x=1):
        picked = []
        for whole, row, depth, column, wide in self.parts[which]:
            blocks = whole.reshape(Z_SIZE, 2, 2, whole.shape[0] // 16, whole.shape[1])
            picked.append(
                lax.dynamic_slice(
                    blocks,
                    (0, start_y, start_x, row, column),
                    (Z_SIZE, count_y, count_x, depth, wide),
                ).reshape(Z_SIZE, count_y * count_x, depth, wide)
            )
        return picked[0] if len(picked) == 1 else jnp.concatenate(picked, 3)

    def prepare(self, *after):
        _, here_y, here_x = chip_place()
        here_x, here_y = tie((here_x, here_y), *after)
        self.away = (self.pick(0, 0, 1 - here_x, 2, 1), self.pick(1, 1 - here_y, 0, 1, 2))

    def spread(self):
        self.came = (swap_x(self.away[0]), swap_y(self.away[1]))

    def of_came(self, which, far):
        _, here_y, here_x = chip_place()
        here = here_x if which else here_y
        return lax.dynamic_slice_in_dim(self.came[which], here ^ far, 1, 1)

    def turn(self):
        _, here_y, here_x = chip_place()
        first = plus(self.pick(0, 1 - here_y, here_x), self.of_came(0, 1))
        second = plus(self.pick(1, here_y, 1 - here_x), self.of_came(1, 1))
        self.turning = (first, second)
        self.turned = (swap_y(first), swap_x(second))

    def near_sums(self):
        _, here_y, here_x = chip_place()
        first, second = (
            plus(
                self.pick(which, here_y, here_x), self.of_came(which, 0), self.turned[which]
            ).reshape((Z_SIZE,) + self.turned[which].shape[2:])
            for which in range(2)
        )
        return jnp.concatenate([first, second], 1 if self.by_rows else 2)

    def gather(self):
        self.sums = self.near_sums()
        self.moving = next_z(self.block(1))

    def block(self, back):
        target = (ring_place() - back) % Z_SIZE
        zed = jnp.where(target == 2, 3, jnp.where(target == 3, 2, target))
        return lax.dynamic_index_in_dim(self.sums, zed, 0, keepdims=False)

    def step(self, number):
        self.moving = next_z(plus(self.block(number), self.moving))

    def finish(self):
        return self.block(0).astype(jnp.float32) + self.moving.astype(jnp.float32)

    def hold(self, names, *after):
        for name in names:
            setattr(self, name, tie(getattr(self, name), *after))


def body_pair(
    tokens, segments, gain_attn, w_query, w_key, w_value, w_out, gain_ffn, w_up, w_down, cotangent
):
    core = lax.axis_index("seq")
    rows, span, width = tokens.shape
    flat = rows * span

    def split(flat_rows, axis_width):
        return flat_rows.reshape(rows, 2 * span, axis_width)

    def sharing(values):
        wide = split(values, values.shape[-1])
        return swap_cores(own_half(wide, 1, 1 - core).astype(jnp.bfloat16))

    def shared(values, received):
        wide = split(values, values.shape[-1])
        return (own_half(wide, 1, core) + received.astype(jnp.float32)).reshape(flat, -1)

    attn_piece = jnp.concatenate([w_query, w_key, w_value, w_out], 1)
    half_wide = w_query.shape[1]
    normed, cot_other, attn_weights, up_stack = head_call(
        tokens, gain_attn, cotangent, attn_piece, w_up
    )
    first = core == 0
    tokens_own = tokens.reshape(flat, width).astype(jnp.float32)
    cot_own = cotangent.reshape(flat, width)
    windows = windows_of(segments, QUERY_TILE)
    back_windows = windows_of(segments, BACK_TILE)
    marks = (
        jnp.broadcast_to(segments[:, :, None], segments.shape + (LANES,)),
        jnp.broadcast_to(segments[:, None, :], (rows, 8, 2 * span)),
    )
    normed = normed.reshape(2 * flat, width)
    w_qkv = attn_weights[:, : 3 * half_wide]
    w_q, w_k, w_v = (w_qkv[:, i * half_wide : (i + 1) * half_wide] for i in range(3))

    up_parts = gather_first(*halves_z(up_stack))
    down_steps = [tie(w_down, up_stack)]
    down_steps.append(next_z(down_steps[-1]))
    w_o_half = attn_weights[:, 3 * half_wide :]
    w_o_other = swap_cores(w_o_half)
    qk_rows = dot_low(normed, w_qkv[:, : 2 * half_wide]).astype(jnp.bfloat16)
    normed, w_o_other, down_steps[1], up_parts = tie(
        (normed, w_o_other, down_steps[1], up_parts), qk_rows
    )
    down_steps.append(next_z(down_steps[-1]))
    up_near = up_parts
    up_parts = gather_second(*up_parts)
    normed = tie(normed, up_near)
    value_rows = dot_low(normed, w_qkv[:, 2 * half_wide :]).astype(jnp.bfloat16)
    value_rows, down_steps[2] = tie((value_rows, down_steps[2]))
    down_steps.append(next_z(down_steps[-1]))
    qk_rows, value_rows = split(qk_rows, 2 * half_wide), split(value_rows, half_wide)
    qk_rows = tie(qk_rows, up_near)
    operands = [(qk_rows, 0), (qk_rows, 1), (value_rows, 0)]
    (mixed,) = attention_call(
        attend_kernel, 0, rows, windows, marks, operands, [half_wide], [], half_wide
    )
    mixed, down_steps[3], up_parts = tie((mixed, down_steps[3], up_parts))
    down_parts = gather_first(*halves_z(natural_z(down_steps)))
    w_o = jnp.where(
        first,
        jnp.concatenate([w_o_half, w_o_other], 1),
        jnp.concatenate([w_o_other, w_o_half], 1),
    )
    w_o_rows = own_half(w_o, 0, core)

    mixed_other = swap_cores(own_half(mixed, 1, 1 - core))
    mixed_mine = own_half(mixed, 1, core)
    mixed_own = jnp.where(
        first,
        jnp.concatenate([mixed_mine, mixed_other], 2),
        jnp.concatenate([mixed_other, mixed_mine], 2),
    ).reshape(flat, width)
    mixed_own, down_parts = tie((mixed_own, down_parts))
    mixed_own = tie(mixed_own, down_parts)
    down_parts = gather_second(*down_parts)
    residual = tokens_own + dot_low(mixed_own, w_o)
    unit_two, scale_two = norm_stats(residual)
    normed_two = (unit_two * gain_ffn).astype(jnp.bfloat16)
    cot_all = jnp.concatenate([cot_own, cot_other.reshape(flat, width)], 0)
    hidden_low, grad_pre, y_own, grad_two_own, normed_two_all, y_came, grad_two_came = feed_forward(
        normed_two, cot_all, up_parts, down_parts
    )

    down_half = outer_low(hidden_low, cot_all)
    down_away = swap_cores(own_half(down_half, 1, 1 - core))
    grad_normed_two = plus_wide(grad_two_own, tie(grad_two_came, down_half))
    grad_residual = cot_own.astype(jnp.float32) + norm_back_rows(
        unit_two, scale_two, gain_ffn, grad_normed_two
    )
    ffn_gain_part = jnp.sum(grad_normed_two * unit_two, 0)
    grad_attn = grad_residual.astype(jnp.bfloat16).reshape(rows, span, width)
    grad_attn_other = swap_cores(grad_attn)
    down_away = tie(down_away, grad_attn, ffn_gain_part)
    down_kept = own_half(down_half, 1, core)
    down_whole = jnp.where(
        first,
        jnp.concatenate([down_kept, down_away], 0),
        jnp.concatenate([down_away, down_kept], 0),
    )
    depth, wide = w_down.shape
    down_sum = Scatter(
        [(down_whole, 0, depth // 2, 0, wide)],
        [(down_whole, depth // 2, depth // 2, 0, wide)],
        True,
    )
    down_sum.prepare()
    down_sum.spread()
    up_whole = outer_low(normed_two_all, tie(grad_pre, *down_sum.away))
    grad_attn_other = tie(grad_attn_other, up_whole)
    grad_attn_all = jnp.where(
        first,
        jnp.concatenate([grad_attn, grad_attn_other], 1),
        jnp.concatenate([grad_attn_other, grad_attn], 1),
    ).reshape(2 * flat, width)
    out_half = outer_low(mixed.reshape(2 * flat, -1), grad_attn_all)
    out_away = swap_cores(own_half(out_half, 1, 1 - core))
    grad_mixed = split(times_transposed(grad_attn_all, w_o_rows).astype(jnp.bfloat16), width // 2)
    out_away = tie(out_away, grad_mixed)
    out_kept = own_half(out_half, 1, core)
    out_whole = jnp.where(
        first,
        jnp.concatenate([out_kept, out_away], 0),
        jnp.concatenate([out_away, out_kept], 0),
    )
    depth, wide = w_up.shape
    cut = (wide + half_wide) // 256 * 128
    up_sum = Scatter(
        [(up_whole, 0, depth, 0, cut)],
        [(up_whole, 0, depth, cut, wide - cut), (out_whole, 0, depth, 0, half_wide)],
    )
    down_sum.hold(("came",), grad_mixed)
    down_sum.turn()
    y_own, y_came = tie((y_own, y_came), *down_sum.turning)
    layer_out = (residual + plus_wide(y_own, y_came)).astype(jnp.bfloat16)
    up_sum.prepare(*down_sum.turning)
    up_sum.spread()
    grad_mixed = tie(grad_mixed, layer_out, *up_sum.away, *down_sum.turning)
    scratch = [pltpu.VMEM((2 * span, LANES), jnp.float32)] * 2

    def attend_back(row, grad_rows, begun=()):
        return attention_call(
            attend_back_kernel,
            row,
            1,
            back_windows,
            marks,
            operands + [(grad_rows, 0)],
            [half_wide] * 3,
            scratch,
            LANES,
            begun,
        )

    grads = attend_back(0, grad_mixed)
    down_sum.hold(("turned",), *grads)
    down_sum.gather()
    grads = tie(grads, down_sum.sums)
    for row in range(1, rows):
        grads = attend_back(row, grad_mixed, grads)
    down_sum.hold(("moving",), *grads)
    up_sum.hold(("came",), *grads)
    grads = tie(grads, down_sum.moving, up_sum.came)
    up_sum.turn()
    down_sum.step(2)
    grads = tie(grads, *up_sum.turning)
    grad_queries, grad_keys, grad_values = (grad.reshape(2 * flat, half_wide) for grad in grads)
    query_whole = outer_low(normed, grad_queries)
    key_whole = outer_low(normed, grad_keys)
    down_sum.hold(("moving",), query_whole, key_whole)
    grad_values = tie(grad_values, down_sum.moving)
    down_sum.step(3)
    value_whole = outer_low(normed, grad_values)
    up_sum.hold(("turned",), value_whole)
    sums = tie((query_whole, key_whole, value_whole), down_sum.moving)
    token_grad, query_grad, key_grad, value_grad, gains, up_grad, out_grad = tail_call(
        (grad_queries, grad_keys, grad_values),
        attn_weights,
        sums,
        tokens.reshape(flat, width),
        grad_residual,
        gain_attn,
        ffn_gain_part,
        up_sum.near_sums(),
    )
    gain_attn_grad, gain_ffn_grad = gains[0], gains[1]
    down_grad = down_sum.finish()
    return (
        layer_out.reshape(rows, span, width),
        token_grad.reshape(rows, span, width),
        gain_attn_grad,
        query_grad,
        key_grad,
        value_grad,
        out_grad,
        gain_ffn_grad,
        up_grad,
        down_grad,
    )


def solution(mesh):
    paired = mesh.shape["seq"] == 2 and mesh.shape["rows"] == 16
    program = body_pair if paired else body
    return jax.shard_map(
        program,
        mesh=mesh,
        in_specs=(
            P("rows", "seq", None),
            P("rows", None),
            P(),
            P("rows", "seq"),
            P("rows", "seq"),
            P("rows", "seq"),
            P("rows", "seq"),
            P(),
            P("rows", "seq"),
            P("rows", "seq"),
            P("rows", "seq", None),
        ),
        out_specs=(
            P("rows", "seq", None),
            P("rows", "seq", None),
            P(),
            P("rows", "seq"),
            P("rows", "seq"),
            P("rows", "seq"),
            P("rows", "seq"),
            P(),
            P("rows", "seq"),
            P("rows", "seq"),
        ),
        check_vma=False,
    )
```

```python
import functools

import jax
import jax.numpy as jnp
from jax import lax
from jax.experimental import pallas as pl
from jax.experimental.pallas import tpu as pltpu
from jax.sharding import PartitionSpec as P

HEADS = 20
HEAD_DIM = 64


epsilon = 1e-05
root_half = 0.7071067811865476


def norm_rows(values, gain_vec):
    row_mean = jnp.mean(values, -1, keepdims=True)
    centred = values - row_mean
    spread = jnp.mean(centred * centred, -1, keepdims=True)
    return centred * lax.rsqrt(spread + epsilon) * gain_vec


def gelu_exact(values):
    return 0.5 * values * (1.0 + lax.erf(values * root_half))


def times_transposed(left_side, right_side):
    return jnp.einsum("te,de->td", left_side, right_side, preferred_element_type=jnp.float32)


def split_heads(rows_in):
    return rows_in.reshape(rows_in.shape[0], rows_in.shape[1], HEADS, HEAD_DIM)


def join_heads(heads_in):
    return heads_in.reshape(heads_in.shape[0], heads_in.shape[1], HEADS * HEAD_DIM)


def masked_scores(query_heads, key_heads, seg_query, seg_key):
    scores = jnp.einsum(
        "rqhd,rkhd->rhqk", query_heads, key_heads, preferred_element_type=jnp.float32
    )
    scores = scores * HEAD_DIM ** (-0.5)
    allowed = (seg_query[:, :, None] == seg_key[:, None, :])[:, None]
    return (allowed, jnp.where(allowed, scores, -1e30))


def attention_forward(query_rows, key_rows, value_rows, seg_query, seg_key):
    allowed, scores = masked_scores(
        split_heads(query_rows), split_heads(key_rows), seg_query, seg_key
    )
    row_top = jnp.max(scores, -1, keepdims=True)
    exponent = jnp.exp(scores - row_top)
    row_total = jnp.sum(exponent, -1, keepdims=True)
    prob_low = (exponent / row_total).astype(jnp.bfloat16)
    mixed_out = jnp.einsum(
        "rhqk,rkhd->rqhd", prob_low, split_heads(value_rows), preferred_element_type=jnp.float32
    )
    return (join_heads(mixed_out).astype(jnp.bfloat16), row_top + jnp.log(row_total))


def grad_pieces(query_heads, key_heads, value_heads, seg_query, seg_key, log_total, grad_heads):
    allowed, scores = masked_scores(query_heads, key_heads, seg_query, seg_key)
    prob_rows = jnp.where(allowed, jnp.exp(scores - log_total), 0.0)
    grad_probs = jnp.einsum(
        "rqhd,rkhd->rhqk", grad_heads, value_heads, preferred_element_type=jnp.float32
    )
    return (prob_rows, grad_probs)


def attention_grads(query_rows, key_rows, value_rows, seg_query, seg_key, log_total, grad_mixed):
    query_heads = split_heads(query_rows)
    key_heads = split_heads(key_rows)
    grad_heads = split_heads(grad_mixed)
    prob_rows, grad_probs = grad_pieces(
        query_heads, key_heads, split_heads(value_rows), seg_query, seg_key, log_total, grad_heads
    )
    value_part = jnp.einsum(
        "rhqk,rqhd->rkhd",
        prob_rows.astype(jnp.bfloat16),
        grad_heads,
        preferred_element_type=jnp.float32,
    )
    row_inner = jnp.sum(grad_probs * prob_rows, -1, keepdims=True)
    score_grad = (prob_rows * (grad_probs - row_inner)).astype(jnp.bfloat16)
    score_scale = HEAD_DIM ** (-0.5)
    query_part = (
        jnp.einsum("rhqk,rkhd->rqhd", score_grad, key_heads, preferred_element_type=jnp.float32)
        * score_scale
    )
    key_part = (
        jnp.einsum("rhqk,rqhd->rkhd", score_grad, query_heads, preferred_element_type=jnp.float32)
        * score_scale
    )
    return (join_heads(query_part), join_heads(key_part), join_heads(value_part))


def process(token_rows, cot_rows, seg_rows, gain_attn, gain_ffn, weights):
    w_query, w_key, w_value, w_out, w_up, w_down = weights
    row_count, query_count, model_width = token_rows.shape
    offset = lax.axis_index("seq") * query_count
    seg_query = lax.dynamic_slice_in_dim(seg_rows, offset, query_count, 1)

    def shaped(flat_rows):
        return flat_rows.reshape(row_count, query_count, model_width)

    flat_tokens = token_rows.reshape(row_count * query_count, model_width).astype(jnp.float32)
    normed, norm_back = jax.vjp(norm_rows, flat_tokens, gain_attn)
    lowered = normed.astype(jnp.bfloat16)
    queries = jnp.dot(lowered, w_query, preferred_element_type=jnp.float32).astype(jnp.bfloat16)
    key_rows = jnp.dot(lowered, w_key, preferred_element_type=jnp.float32).astype(jnp.bfloat16)
    value_rows = jnp.dot(lowered, w_value, preferred_element_type=jnp.float32).astype(jnp.bfloat16)
    key_whole, value_whole = (
        lax.all_gather(shaped(key_rows), "seq", axis=1, tiled=True),
        lax.all_gather(shaped(value_rows), "seq", axis=1, tiled=True),
    )
    mixed_rows, log_total = attention_forward(
        shaped(queries), key_whole, value_whole, seg_query, seg_rows
    )
    mixed_flat = mixed_rows.reshape(row_count * query_count, model_width)
    residual = flat_tokens + jnp.dot(mixed_flat, w_out, preferred_element_type=jnp.float32)
    normed_two, norm_two_back = jax.vjp(norm_rows, residual, gain_ffn)
    lowered_two = normed_two.astype(jnp.bfloat16)
    hidden_pre = jnp.dot(lowered_two, w_up, preferred_element_type=jnp.float32)
    hidden, gelu_back = jax.vjp(gelu_exact, hidden_pre)
    hidden_low = hidden.astype(jnp.bfloat16)
    layer_rows = (
        residual + jnp.dot(hidden_low, w_down, preferred_element_type=jnp.float32)
    ).astype(jnp.bfloat16)
    grad_out = cot_rows.reshape(row_count * query_count, model_width)
    grad_hidden = times_transposed(grad_out, w_down)
    grad_pre = gelu_back(grad_hidden)[0].astype(jnp.bfloat16)
    grad_normed_two = times_transposed(grad_pre, w_up)
    grad_resid_norm, grad_gain_ffn = norm_two_back(grad_normed_two)
    grad_residual = grad_out.astype(jnp.float32) + grad_resid_norm
    grad_attn = grad_residual.astype(jnp.bfloat16)
    grad_mixed = times_transposed(grad_attn, w_out).astype(jnp.bfloat16)
    query_part, key_part, value_part = attention_grads(
        shaped(queries), key_whole, value_whole, seg_query, seg_rows, log_total, shaped(grad_mixed)
    )
    key_own, value_own = (
        lax.psum_scatter(key_part, "seq", scatter_dimension=1, tiled=True),
        lax.psum_scatter(value_part, "seq", scatter_dimension=1, tiled=True),
    )
    grad_queries = query_part.reshape(row_count * query_count, model_width).astype(jnp.bfloat16)
    grad_keys = key_own.reshape(row_count * query_count, model_width).astype(jnp.bfloat16)
    grad_values = value_own.reshape(row_count * query_count, model_width).astype(jnp.bfloat16)
    grad_normed = (
        times_transposed(grad_queries, w_query)
        + times_transposed(grad_keys, w_key)
        + times_transposed(grad_values, w_value)
    )
    grad_token_norm, grad_gain_attn = norm_back(grad_normed)
    grad_tokens = (grad_residual + grad_token_norm).reshape(row_count, query_count, model_width)
    saved = (
        lowered,
        grad_queries,
        grad_keys,
        grad_values,
        mixed_flat,
        grad_attn,
        lowered_two,
        grad_pre,
        hidden_low,
        grad_out,
    )
    return (
        layer_rows.reshape(row_count, query_count, model_width),
        grad_tokens,
        saved,
        grad_gain_attn,
        grad_gain_ffn,
    )


def body(
    tokens, segments, gain_attn, w_query, w_key, w_value, w_out, gain_ffn, w_up, w_down, cotangent
):
    col_query = lax.all_gather(w_query, "seq", axis=1, tiled=True)
    col_key = lax.all_gather(w_key, "seq", axis=1, tiled=True)
    col_value = lax.all_gather(w_value, "seq", axis=1, tiled=True)
    col_out = lax.all_gather(w_out, "seq", axis=1, tiled=True)
    col_up = lax.all_gather(w_up, "seq", axis=1, tiled=True)
    col_down = lax.all_gather(w_down, "seq", axis=1, tiled=True)
    results = [
        process(
            tokens,
            cotangent,
            segments,
            gain_attn,
            gain_ffn,
            (
                lax.all_gather(col_query, "rows", axis=0, tiled=True),
                lax.all_gather(col_key, "rows", axis=0, tiled=True),
                lax.all_gather(col_value, "rows", axis=0, tiled=True),
                lax.all_gather(col_out, "rows", axis=0, tiled=True),
                lax.all_gather(col_up, "rows", axis=0, tiled=True),
                lax.all_gather(col_down, "rows", axis=0, tiled=True),
            ),
        )
    ]
    layer_out = jnp.concatenate([result_set[0] for result_set in results], 0)
    token_grad = jnp.concatenate([result_set[1] for result_set in results], 0)
    saved = [
        jnp.concatenate([result_set[2][member] for result_set in results], 0)
        for member in range(10)
    ]
    attn_gain_part = sum((result_set[3] for result_set in results))
    ffn_gain_part = sum((result_set[4] for result_set in results))
    gain_attn_grad, gain_ffn_grad = lax.psum((attn_gain_part, ffn_gain_part), ("rows", "seq"))
    (
        lowered,
        grad_queries,
        grad_keys,
        grad_values,
        mixed_flat,
        grad_attn,
        lowered_two,
        grad_pre,
        hidden_low,
        grad_out,
    ) = saved
    splits = lax.axis_size("seq")

    def arrange(grad_block):
        return grad_block.reshape(grad_block.shape[0], splits, grad_block.shape[1] // splits)

    def outer_product(left_side, right_side):
        return jnp.einsum("tc,te->ce", left_side, right_side, preferred_element_type=jnp.float32)

    def input_terms(offset, count):
        blocks = [
            outer_product(lowered, grad_queries),
            outer_product(lowered, grad_keys),
            outer_product(lowered, grad_values),
            outer_product(mixed_flat, grad_attn),
            outer_product(lowered_two, grad_pre),
        ]
        return jnp.concatenate([arrange(grad_block) for grad_block in blocks], 2)

    def hidden_terms(offset, count):
        return arrange(outer_product(hidden_low, grad_out))

    def spread_sum(term_of, shard_rows):
        row_part = lax.psum_scatter(
            term_of(jnp.int32(0), shard_rows * lax.axis_size("rows")),
            "rows",
            scatter_dimension=0,
            tiled=True,
        )
        return lax.psum_scatter(row_part, "seq", scatter_dimension=1, tiled=True)[:, 0, :]

    input_grads = spread_sum(input_terms, w_query.shape[0])
    down_grad = spread_sum(hidden_terms, w_down.shape[0])
    column_width = w_query.shape[1]
    query_grad = input_grads[:, :column_width]
    key_grad = input_grads[:, column_width : 2 * column_width]
    value_grad = input_grads[:, 2 * column_width : 3 * column_width]
    out_grad = input_grads[:, 3 * column_width : 4 * column_width]
    up_grad = input_grads[:, 4 * column_width :]
    return (
        layer_out,
        token_grad,
        gain_attn_grad,
        query_grad,
        key_grad,
        value_grad,
        out_grad,
        gain_ffn_grad,
        up_grad,
        down_grad,
    )


LANES = 128
QUERY_TILE = 128
BACK_TILE = 256
NEVER = -1e30


def swap_cores(values):
    return lax.ppermute(values, "seq", [(0, 1), (1, 0)])


def both_cores(values, axis):
    other = swap_cores(values)
    first = lax.axis_index("seq") == 0
    return jnp.where(
        first,
        jnp.concatenate([values, other], axis),
        jnp.concatenate([other, values], axis),
    )


def own_half(values, axis, index):
    half = values.shape[axis] // 2
    return lax.dynamic_slice_in_dim(values, index * half, half, axis)


def two_heads(ref, rows, columns):
    values = ref[0, rows, columns]
    lower = lax.broadcasted_iota(jnp.int32, values.shape, 1) < HEAD_DIM
    zero = jnp.zeros_like(values)
    return jnp.concatenate([jnp.where(lower, values, zero), jnp.where(lower, zero, values)], 0)


def merge_heads(values):
    half = values.shape[0] // 2
    lower = lax.broadcasted_iota(jnp.int32, (half, LANES), 1) < HEAD_DIM
    return jnp.where(lower, values[:half], values[half:])


def over_windows(first_row, query_tile, start_ref, count_ref, length, window):
    row = first_row + pl.program_id(0)

    def tile_step(tile, carry):
        begin = pl.multiple_of(start_ref[row, tile] * LANES, LANES)
        count = count_ref[row, tile]
        queries = pl.ds(pl.multiple_of(tile * query_tile, query_tile), query_tile)
        for tiles in range(1, length // LANES + 1):
            keys = pl.ds(begin, tiles * LANES)
            pl.when(count == tiles)(functools.partial(window, queries, keys))
        return carry

    lax.fori_loop(0, length // query_tile, tile_step, 0)


last_dims = (((1,), (1,)), ((), ()))
first_dims = (((0,), (0,)), ((), ()))
exponent_scale = HEAD_DIM ** (-0.5) * 1.4426950408889634


def attend_kernel(
    row, begun, start_ref, count_ref, column_ref, line_ref, q_ref, k_ref, v_ref, *rest
):
    (out_ref,) = rest[begun:]
    _, length, wide = q_ref.shape

    def window(queries, keys):
        allowed = column_ref[0, queries, :1] == line_ref[0, :1, keys]
        bias = jnp.where(allowed, 0.0, NEVER)[None]

        def scores_of(pair):
            columns = pl.ds(pair * LANES, LANES)
            return lax.dot_general(
                two_heads(q_ref, queries, columns),
                k_ref[0, keys, columns],
                last_dims,
                preferred_element_type=jnp.float32,
            )

        ahead = scores_of(0)
        for pair in range(wide // LANES):
            scores = ahead
            if (pair + 1) * LANES < wide:
                ahead = scores_of(pair + 1)
            shape = scores.shape
            scores = (scores.reshape((2, QUERY_TILE) + shape[1:]) + bias).reshape(shape)
            top = jnp.max(scores, -1, keepdims=True)
            exponent = jnp.exp2((scores - top) * exponent_scale)
            columns = pl.ds(pair * LANES, LANES)
            part = jnp.dot(
                exponent.astype(jnp.bfloat16),
                v_ref[0, keys, columns],
                preferred_element_type=jnp.float32,
            )
            part = part / jnp.sum(exponent, -1, keepdims=True)
            out_ref[0, queries, columns] = merge_heads(part).astype(jnp.bfloat16)

    over_windows(row, QUERY_TILE, start_ref, count_ref, length, window)


def attend_back_kernel(
    row, begun, start_ref, count_ref, column_ref, line_ref, q_ref, k_ref, v_ref, grad_ref, *rest
):
    dq_ref, dk_ref, dv_ref, dk_sum, dv_sum = rest[begun:]
    dk_sum[...] = jnp.zeros_like(dk_sum)
    dv_sum[...] = jnp.zeros_like(dv_sum)
    scale = HEAD_DIM ** (-0.5)
    columns = pl.ds(0, LANES)

    def window(queries, keys):
        query, grad = two_heads(q_ref, queries, columns), two_heads(grad_ref, queries, columns)
        key, value = k_ref[0, keys, :], v_ref[0, keys, :]
        bias = jnp.where(column_ref[0, keys, :1] == line_ref[0, :1, queries], 0.0, NEVER)
        scores = lax.dot_general(key, query, last_dims, preferred_element_type=jnp.float32)
        scores = scores + jnp.concatenate([bias, bias], 1)
        top = jnp.max(scores, 0, keepdims=True)
        exponent = jnp.exp2((scores - top) * exponent_scale)
        probs = exponent * (1.0 / jnp.sum(exponent, 0, keepdims=True))
        grad_probs = lax.dot_general(value, grad, last_dims, preferred_element_type=jnp.float32)
        inner = jnp.sum(grad_probs * probs, 0, keepdims=True)
        grad_scores = (probs * (grad_probs - inner)).astype(jnp.bfloat16)
        dv_sum[keys, :] += jnp.dot(
            probs.astype(jnp.bfloat16), grad, preferred_element_type=jnp.float32
        )
        dk_sum[keys, :] += jnp.dot(grad_scores, query, preferred_element_type=jnp.float32)
        query_part = lax.dot_general(
            grad_scores, key, first_dims, preferred_element_type=jnp.float32
        )
        dq_ref[0, queries, :] = (merge_heads(query_part) * scale).astype(jnp.bfloat16)

    over_windows(row, BACK_TILE, start_ref, count_ref, k_ref.shape[1], window)
    dk_ref[0] = (dk_sum[...] * scale).astype(jnp.bfloat16)
    dv_ref[0] = dv_sum[...].astype(jnp.bfloat16)


def windows_of(segments, query_tile):
    heads = segments[:, ::query_tile]
    tails = segments[:, query_tile - 1 :: query_tile]
    begin = jnp.sum(segments[:, None, :] < heads[:, :, None], -1, dtype=jnp.int32)
    end = jnp.sum(segments[:, None, :] <= tails[:, :, None], -1, dtype=jnp.int32)
    start = begin // LANES
    return start, (end + LANES - 1) // LANES - start


def attention_call(
    kernel, row, rows, windows, marks, operands, outputs, scratch, block_wide, begun=()
):
    all_rows, length, _ = operands[0][0].shape
    wide = outputs[0]
    steps = wide // block_wide

    def block(part):
        return pl.BlockSpec(
            (1, length, block_wide), lambda at, step, *_: (row + at, 0, part * steps + step)
        )

    work = rows * wide * length * length
    shape = jax.ShapeDtypeStruct((all_rows, length, wide), jnp.bfloat16)
    return pl.pallas_call(
        functools.partial(kernel, row, len(begun)),
        grid_spec=pltpu.PrefetchScalarGridSpec(
            num_scalar_prefetch=2,
            grid=(rows, steps),
            in_specs=[
                pl.BlockSpec((1, length, LANES), lambda at, *_: (row + at, 0, 0)),
                pl.BlockSpec((1, 8, length), lambda at, *_: (row + at, 0, 0)),
            ]
            + [block(first) for _, first in operands]
            + [pl.BlockSpec(memory_space=pl.ANY)] * len(begun),
            out_specs=[block(0)] * len(outputs),
            scratch_shapes=scratch,
        ),
        out_shape=[shape] * len(outputs),
        input_output_aliases={4 + len(operands) + index: index for index in range(len(begun))},
        compiler_params=pltpu.CompilerParams(vmem_limit_bytes=48 * 1024 * 1024),
        cost_estimate=pl.CostEstimate(
            flops=4 * len(operands) * work,
            bytes_accessed=2 * (len(operands) + len(outputs)) * rows * length * wide,
            transcendentals=work // HEAD_DIM,
        ),
    )(*windows, *marks, *(array for array, _ in operands), *begun)


def norm_stats(values):
    centred = values - jnp.mean(values, -1, keepdims=True)
    scale = lax.rsqrt(jnp.mean(centred * centred, -1, keepdims=True) + epsilon)
    return centred * scale, scale


def norm_back_rows(unit, scale, gain_vec, grad):
    scaled = grad * gain_vec
    inner = jnp.mean(scaled * unit, -1, keepdims=True)
    return scale * (scaled - jnp.mean(scaled, -1, keepdims=True) - unit * inner)


Z_SIZE = 4
RING = (0, 1, 3, 2)
PLACE = (0, 1, 3, 2)


def chip_place():
    index = lax.axis_index("rows")
    return index // 4, (index // 2) % 2, index % 2


def swap_x(values):
    return lax.ppermute(values, "rows", [(row, row ^ 1) for row in range(16)])


def swap_y(values):
    return lax.ppermute(values, "rows", [(row, row ^ 2) for row in range(16)])


def next_z(values):
    pairs = []
    for place in range(Z_SIZE):
        here, there = RING[place], RING[(place + 1) % Z_SIZE]
        pairs += [(here * 4 + rest, there * 4 + rest) for rest in range(4)]
    return lax.ppermute(values, "rows", pairs)


def ring_place():
    zed = chip_place()[0]
    return jnp.where(zed == 2, 3, jnp.where(zed == 3, 2, zed))


def tie(value, *after):
    return lax.optimization_barrier((value, after))[0]


def natural_z(steps):
    place = ring_place()
    stack = jnp.stack(steps)
    return jnp.stack(
        [
            lax.dynamic_index_in_dim(stack, (place - PLACE[zed]) % Z_SIZE, 0, keepdims=False)
            for zed in range(Z_SIZE)
        ]
    )


def load_pieces(place_ref, pieces, target_of, sems):
    copies = []
    for part in range(2):
        for across in range(2):
            for along in range(2):
                far_y, far_x = (along, across) if part == 0 else (across, along)
                row_y, row_x = place_ref[1] ^ far_y, place_ref[2] ^ far_x
                piece = pieces[part * 2 + across].at[along]
                for zed in range(Z_SIZE):
                    target = target_of(part, zed, row_y, row_x, piece)
                    copies.append(
                        pltpu.make_async_copy(piece.at[zed], target, sems.at[len(copies)])
                    )
                    copies[-1].start()
    return copies


def column_target(whole_ref):
    def target_of(part, zed, row_y, row_x, piece):
        _, depth, wide = piece.shape
        row = pl.multiple_of(((zed * 2 + row_y) * 2 + row_x) * depth, 16)
        left = 0 if part == 0 else whole_ref.shape[1] - wide
        return whole_ref.at[pl.ds(row, depth), pl.ds(left, wide)]

    return target_of


def assemble_columns_kernel(place_ref, *refs):
    *pieces, out_ref, sems = refs
    for copy in load_pieces(place_ref, pieces, column_target(out_ref), sems):
        copy.wait()


def place_vector():
    return jnp.stack(chip_place() + (lax.axis_index("seq"),)).astype(jnp.int32)


def assemble(kernel, shape, parts):
    return pl.pallas_call(
        kernel,
        grid_spec=pltpu.PrefetchScalarGridSpec(
            num_scalar_prefetch=1,
            grid=(1,),
            in_specs=[pl.BlockSpec(memory_space=pl.ANY)] * 4,
            out_specs=pl.BlockSpec(shape, lambda step, *_: (0,) * len(shape)),
            scratch_shapes=[pltpu.SemaphoreType.DMA((32,))],
        ),
        out_shape=jax.ShapeDtypeStruct(shape, parts[0][0].dtype),
        compiler_params=pltpu.CompilerParams(vmem_limit_bytes=40 * 1024 * 1024),
    )(place_vector(), *parts[0], *parts[1])


FFN_TILE = 256
FFN_CHUNK = 512
root_two_pi = 0.3989422804014327


def feed_forward_kernel(*refs):
    normed_ref, cot_ref, *refs = refs
    up_pieces, down_pieces, refs = refs[:4], refs[4:10], refs[10:]
    hidden_ref, grad_pre_ref, y_ref, grad_ref, normed_out, y_came, grad_came, *refs = refs
    up_ref, down_ref, normed_buf, y_away, grad_away, *refs = refs
    up_sems, down_sems, sent_sems, came_sems, normed_sems, away_sends, away_recvs, *refs = refs
    corner_sends, corner_recvs = refs
    step = pl.program_id(0)
    row, core = lax.axis_index("rows"), lax.axis_index("seq")
    here_y, here_x = (row // 2) % 2, row % 2
    twin = (row, 1 - core)
    over_x, over_y = row + 1 - 2 * here_x, row + 2 - 4 * here_y
    span = normed_ref.shape[0]
    tiles = span // FFN_TILE

    def remote(src, dst, send_sem, recv_sem):
        return pltpu.make_async_remote_copy(
            src_ref=src,
            dst_ref=dst,
            send_sem=send_sem,
            recv_sem=recv_sem,
            device_id=twin,
            device_id_type=pl.DeviceIdType.MESH,
        )

    def normed_copies():
        own, others = normed_buf.at[pl.ds(0, span), :], normed_buf.at[pl.ds(span, span), :]
        return (
            pltpu.make_async_copy(normed_ref, own, normed_sems.at[0]),
            remote(normed_ref, others, normed_sems.at[1], normed_sems.at[2]),
        )

    def up_copies():
        copies = []
        for part in range(2):
            for across in range(2):
                for along in range(2):
                    far_y, far_x = (along, across) if part == 0 else (across, along)
                    row_y = 1 - here_y if far_y else here_y
                    row_x = 1 - here_x if far_x else here_x
                    for zed in range(Z_SIZE):
                        piece = up_pieces[part * 2 + across].at[along, zed]
                        depth, wide = piece.shape
                        first = pl.multiple_of(((zed * 2 + row_y) * 2 + row_x) * depth, 16)
                        left = 0 if part == 0 else up_ref.shape[1] - wide
                        target = up_ref.at[pl.ds(first, depth), pl.ds(left, wide)]
                        copies.append(pltpu.make_async_copy(piece, target, up_sems.at[len(copies)]))
        return copies

    def down_rows(part, lower, row_y, row_x, depth):
        first = (((lower * 2 + row_y) * 2 + row_x) * 2 + part) * depth
        return pl.ds(pl.multiple_of(first, 16), depth)

    def down_copies():
        kept, given = [], []
        for part in range(2):
            for which, (far_y, far_x) in enumerate(
                ((0, 0), (1, 0), (0, 1)) if part == 0 else ((0, 0), (0, 1), (1, 0))
            ):
                row_y = 1 - here_y if far_y else here_y
                row_x = 1 - here_x if far_x else here_x
                for lower in range(2):
                    pieces = down_pieces[part * 3 + which]
                    depth, wide = pieces.shape[1:]
                    rows = down_rows(part, lower, row_y, row_x, depth)
                    target = down_ref.at[rows, pl.ds(pl.multiple_of(core * wide, 128), wide)]
                    number = len(kept)
                    kept.append(
                        pltpu.make_async_copy(
                            pieces.at[2 * core + lower], target, down_sems.at[number]
                        )
                    )
                    given.append(
                        remote(
                            pieces.at[2 * (1 - core) + lower],
                            target,
                            sent_sems.at[number],
                            came_sems.at[number],
                        )
                    )
        return kept, given

    def corner_copies():
        sends, arrivals = [], []
        for part in range(2):
            pieces = down_pieces[part * 3 + 1]
            depth, wide = pieces.shape[1:]
            row_y, row_x = (1 - here_y, here_x) if part == 0 else (here_y, 1 - here_x)
            for other in range(2):
                for lower in range(2):
                    number = len(sends)
                    rows = down_rows(part, lower, row_y, row_x, depth)
                    target = down_ref.at[rows, pl.ds(pl.multiple_of(core * wide, 128), wide)]
                    sends.append(
                        pltpu.make_async_remote_copy(
                            src_ref=pieces.at[2 * other + lower],
                            dst_ref=target,
                            send_sem=corner_sends.at[number],
                            recv_sem=corner_recvs.at[part, core, lower],
                            device_id=(over_x if part == 0 else over_y, other),
                            device_id_type=pl.DeviceIdType.MESH,
                        )
                    )
                    rows = down_rows(part, lower, 1 - here_y, 1 - here_x, depth)
                    target = down_ref.at[rows, pl.ds(other * wide, wide)]
                    arrivals.append(
                        pltpu.make_async_remote_copy(
                            src_ref=target,
                            dst_ref=target,
                            send_sem=corner_sends.at[number],
                            recv_sem=corner_recvs.at[part, other, lower],
                            device_id=(over_x if part == 0 else over_y, other),
                            device_id_type=pl.DeviceIdType.MESH,
                        )
                    )
        return sends, arrivals

    def away_copies(tile):
        rows = pl.ds(pl.multiple_of(tile * FFN_TILE, FFN_TILE), FFN_TILE)
        return [
            remote(buf.at[tile], out.at[rows, :], away_sends.at[which, tile], away_recvs.at[which, tile])
            for which, (buf, out) in enumerate(((y_away, y_came), (grad_away, grad_came)))
        ]

    @pl.when(step == 0)
    def _():
        barrier = pltpu.get_barrier_semaphore()
        for target in (twin, (over_x, 0), (over_x, 1), (over_y, 0), (over_y, 1)):
            pl.semaphore_signal(
                barrier, inc=1, device_id=target, device_id_type=pl.DeviceIdType.MESH
            )
        kept, given = down_copies()
        corners, arrivals = corner_copies()
        own, others = normed_copies()
        ups = up_copies()
        pl.semaphore_wait(barrier, 5)
        for copy in corners + [own] + ups + kept + given + [others]:
            copy.start()
        for copy in [own] + ups + kept:
            copy.wait()
        for copy in given + arrivals:
            copy.wait_recv()

    @pl.when(step == tiles)
    def _():
        normed_copies()[1].wait_recv()

    normed = normed_buf[pl.ds(pl.multiple_of(step * FFN_TILE, FFN_TILE), FFN_TILE), :]
    cot = cot_ref[...]
    y_sum = grad_sum = 0.0
    for chunk in range(hidden_ref.shape[1] // FFN_CHUNK):
        units = pl.ds(chunk * FFN_CHUNK, FFN_CHUNK)
        up, down = up_ref[:, units], down_ref[units, :]
        pre = jnp.dot(normed, up, preferred_element_type=jnp.float32)
        grad_hidden = lax.dot_general(cot, down, last_dims, preferred_element_type=jnp.float32)
        phi = 0.5 + 0.5 * lax.erf(pre * root_half)
        hidden = (pre * phi).astype(jnp.bfloat16)
        slope = phi + pre * (jnp.exp(-0.5 * pre * pre) * root_two_pi)
        grad_pre = (grad_hidden * slope).astype(jnp.bfloat16)
        hidden_ref[:, units] = hidden
        grad_pre_ref[:, units] = grad_pre
        y_sum += jnp.dot(hidden, down, preferred_element_type=jnp.float32)
        grad_sum += lax.dot_general(grad_pre, up, last_dims, preferred_element_type=jnp.float32)

    @pl.when(step < tiles)
    def _():
        y_ref[...] = y_sum.astype(jnp.bfloat16)
        grad_ref[...] = grad_sum.astype(jnp.bfloat16)

    for tile in range(tiles):

        @pl.when(step == tiles + tile)
        def _(tile=tile):
            y_away[tile] = y_sum.astype(jnp.bfloat16)
            grad_away[tile] = grad_sum.astype(jnp.bfloat16)
            for copy in away_copies(tile):
                copy.start()

    @pl.when(step == 2 * tiles - 1)
    def _():
        store = pltpu.make_async_copy(normed_buf, normed_out, normed_sems.at[0])
        store.start()
        for copy in (*down_copies()[1], *corner_copies()[0], normed_copies()[1]):
            copy.wait_send()
        for tile in range(tiles):
            for copy in away_copies(tile):
                copy.wait()
        store.wait()


def feed_forward(normed, cot_all, up_parts, down_parts):
    tokens, width = normed.shape
    units = up_parts[0][0].shape[3] + up_parts[1][0].shape[3]
    tiles = tokens // FFN_TILE
    tile = pl.BlockSpec((FFN_TILE, width), lambda step: (step, 0))
    own_tile = pl.BlockSpec((FFN_TILE, width), lambda step: (jnp.minimum(step, tiles - 1), 0))
    wide_tile = pl.BlockSpec((FFN_TILE, units), lambda step: (step, 0))
    anywhere = pl.BlockSpec(memory_space=pl.ANY)
    wide_shape = jax.ShapeDtypeStruct((2 * tokens, units), jnp.bfloat16)
    shape = jax.ShapeDtypeStruct((tokens, width), jnp.bfloat16)
    away = pltpu.VMEM((tiles, FFN_TILE, width), jnp.bfloat16)
    sems = pltpu.SemaphoreType.DMA
    return pl.pallas_call(
        feed_forward_kernel,
        grid=(2 * tiles,),
        in_specs=[anywhere, tile] + [anywhere] * 10,
        out_specs=[wide_tile, wide_tile, own_tile, own_tile] + [anywhere] * 3,
        out_shape=[
            wide_shape,
            wide_shape,
            shape,
            shape,
            jax.ShapeDtypeStruct((2 * tokens, width), jnp.bfloat16),
            shape,
            shape,
        ],
        scratch_shapes=[
            pltpu.VMEM((width, units), jnp.bfloat16),
            pltpu.VMEM((units, width), jnp.bfloat16),
            pltpu.VMEM((2 * tokens, width), jnp.bfloat16),
            away,
            away,
            sems((32,)),
            sems((16,)),
            sems((16,)),
            sems((16,)),
            sems((3,)),
            sems((2, tiles)),
            sems((2, tiles)),
            sems((8,)),
            sems((2, 2, 2)),
        ],
        compiler_params=pltpu.CompilerParams(
            collective_id=2, has_side_effects=True, vmem_limit_bytes=60 * 1024 * 1024
        ),
        cost_estimate=pl.CostEstimate(
            flops=16 * tokens * width * units,
            bytes_accessed=4 * width * units + 8 * tokens * (2 * width + units),
            transcendentals=4 * tokens * units,
        ),
    )(normed, cot_all, *up_parts[0], *up_parts[1], *down_parts)


RESIDUAL_TILE = 128


def residual_kernel(*refs):
    residual_ref, cot_ref, y_ref, y_came, grad_ref, grad_came, gain_ref, *refs = refs
    layer_ref, out_ref, gain_out, both_out, buf, local_sems, send_sems, recv_sems = refs
    step = pl.program_id(0)
    steps = buf.shape[0]
    row, core = lax.axis_index("rows"), lax.axis_index("seq")
    twin = (row, 1 - core)
    span = both_out.shape[1] // 2

    def copies(tile):
        each = span // RESIDUAL_TILE
        first = core * span + (tile % each) * RESIDUAL_TILE
        rows = pl.ds(pl.multiple_of(first, RESIDUAL_TILE), RESIDUAL_TILE)
        target = both_out.at[tile // each, rows, :]
        return (
            pltpu.make_async_copy(buf.at[tile], target, local_sems.at[tile]),
            pltpu.make_async_remote_copy(
                src_ref=buf.at[tile],
                dst_ref=target,
                send_sem=send_sems.at[tile],
                recv_sem=recv_sems.at[tile],
                device_id=twin,
                device_id_type=pl.DeviceIdType.MESH,
            ),
        )

    @pl.when(step == 0)
    def _():
        barrier = pltpu.get_barrier_semaphore()
        pl.semaphore_signal(barrier, inc=1, device_id=twin, device_id_type=pl.DeviceIdType.MESH)
        pl.semaphore_wait(barrier, 1)
        gain_out[...] = jnp.zeros_like(gain_out)

    residual = residual_ref[...]
    layer_ref[...] = plus(residual, y_ref[...], y_came[...])
    unit, scale = norm_stats(residual)
    grad = plus_wide(grad_ref[...], grad_came[...])
    grad_residual = cot_ref[...].astype(jnp.float32) + norm_back_rows(
        unit, scale, gain_ref[...], grad
    )
    out_ref[...] = grad_residual
    gain_out[0:1, :] += jnp.sum(grad * unit, 0, keepdims=True)
    for tile in range(steps):

        @pl.when(step == tile)
        def _(tile=tile):
            buf[tile] = grad_residual.astype(jnp.bfloat16)
            for copy in copies(tile):
                copy.start()

    @pl.when(step == steps - 1)
    def _():
        for tile in range(steps):
            for copy in copies(tile):
                copy.wait()


def residual_call(rows, residual, cot, y_own, y_came, grad_own, grad_came, gain):
    flat, width = residual.shape
    steps = flat // RESIDUAL_TILE
    tile = pl.BlockSpec((RESIDUAL_TILE, width), lambda step: (step, 0))
    sems = pltpu.SemaphoreType.DMA((steps,))
    return pl.pallas_call(
        residual_kernel,
        grid=(steps,),
        in_specs=[tile] * 6 + [pl.BlockSpec((1, width), lambda step: (0, 0))],
        out_specs=[
            tile,
            tile,
            pl.BlockSpec((8, width), lambda step: (0, 0)),
            pl.BlockSpec(memory_space=pl.ANY),
        ],
        out_shape=[
            jax.ShapeDtypeStruct((flat, width), jnp.bfloat16),
            jax.ShapeDtypeStruct((flat, width), jnp.float32),
            jax.ShapeDtypeStruct((8, width), jnp.float32),
            jax.ShapeDtypeStruct((rows, 2 * flat // rows, width), jnp.bfloat16),
        ],
        scratch_shapes=[
            pltpu.VMEM((steps, RESIDUAL_TILE, width), jnp.bfloat16),
            sems,
            sems,
            sems,
        ],
        compiler_params=pltpu.CompilerParams(
            collective_id=3, has_side_effects=True, vmem_limit_bytes=32 * 1024 * 1024
        ),
    )(residual, cot, y_own, y_came, grad_own, grad_came, gain.reshape(1, width))


def following(zed):
    return (2 * zed + 1) % 5


def preceding(zed):
    return (3 * zed + 2) % 5


NORM_TILE = 64


def head_kernel(
    tokens_ref,
    gain_ref,
    cot_ref,
    piece_ref,
    up_ref,
    normed_out,
    cot_out,
    weights_out,
    up_out,
    token_buf,
    normed_buf,
    local_sems,
    send_sems,
    recv_sems,
):
    row, core = lax.axis_index("rows"), lax.axis_index("seq")
    zed, here_y, here_x = row // 4, (row // 2) % 2, row % 2
    rest = row - 4 * zed
    over_x, over_y = row + 1 - 2 * here_x, row + 2 - 4 * here_y
    onward, backward = following(zed) * 4 + rest, preceding(zed) * 4 + rest
    places = [zed]
    for _ in range(3):
        places.append(preceding(places[-1]))
    depth, wide = piece_ref.shape
    half = wide // 2

    barrier = pltpu.get_barrier_semaphore()
    for target in ((onward, core), (backward, core), (over_x, core), (over_y, core), (row, 1 - core)):
        pl.semaphore_signal(
            barrier, inc=1, device_id=target, device_id_type=pl.DeviceIdType.MESH
        )
    load = pltpu.make_async_copy(tokens_ref, token_buf, local_sems.at[0])
    load.start()
    own_rows = pl.ds(pl.multiple_of(row * depth, 16), depth)
    keeps = [
        pltpu.make_async_copy(piece_ref, weights_out.at[own_rows, :], local_sems.at[1]),
        pltpu.make_async_copy(up_ref, up_out.at[zed], local_sems.at[2]),
    ]
    for keep in keeps:
        keep.start()
    pl.semaphore_wait(barrier, 5)

    sent = []

    def send(src, dst, target):
        number = len(sent)
        copy = pltpu.make_async_remote_copy(
            src_ref=src,
            dst_ref=dst,
            send_sem=send_sems.at[number],
            recv_sem=recv_sems.at[number],
            device_id=target,
            device_id_type=pl.DeviceIdType.MESH,
        )
        copy.start()
        sent.append(copy)
        return copy

    def block(place, far_y, far_x, columns):
        at_y = 1 - here_y if far_y else here_y
        at_x = 1 - here_x if far_x else here_x
        index = (place * 2 + at_y) * 2 + at_x
        rows = pl.ds(pl.multiple_of(index * depth, 16), depth)
        return weights_out.at[rows, columns]

    everything, left, right = pl.ds(0, wide), pl.ds(0, half), pl.ds(half, half)

    def source(step, columns):
        if step == 0:
            return piece_ref.at[:, columns]
        return block(places[step], False, False, columns)

    def around(step):
        return send(
            source(step, everything), block(places[step], False, False, everything), (onward, core)
        )

    def around_up(step):
        src = up_ref if step == 0 else up_out.at[places[step]]
        return send(src, up_out.at[places[step]], (onward, core))

    def across(step):
        place = places[step]
        return (
            send(source(step, left), block(place, False, False, left), (over_y, core)),
            send(source(step, right), block(place, False, False, right), (over_x, core)),
            send(source(step, left), block(place, False, False, left), (over_x, core)),
            send(source(step, right), block(place, False, False, right), (over_y, core)),
        )

    def corner(step, crossing):
        place = places[step]
        crossing[0].wait_recv()
        far_left = block(place, True, False, left)
        first = send(far_left, far_left, (over_x, core))
        crossing[1].wait_recv()
        far_right = block(place, False, True, right)
        return first, send(far_right, far_right, (over_y, core))

    ring = around(0)
    crossing = across(0)
    arrivals = [crossing[2], crossing[3]]
    arrivals.append(send(cot_ref, cot_out, (row, 1 - core)))

    load.wait()
    span = token_buf.shape[1]
    for member in range(token_buf.shape[0]):

        def norm_tile(tile, carry, member=member):
            rows = pl.ds(pl.multiple_of(tile * NORM_TILE, NORM_TILE), NORM_TILE)
            unit, _ = norm_stats(token_buf[member, rows, :].astype(jnp.float32))
            normed_buf[member, rows, :] = (unit * gain_ref[...]).astype(jnp.bfloat16)
            return carry

        lax.fori_loop(0, span // NORM_TILE, norm_tile, 0)
    mine = normed_out.at[:, pl.ds(pl.multiple_of(core * span, 16), span), :]
    keeps.append(pltpu.make_async_copy(normed_buf, mine, local_sems.at[3]))
    keeps[-1].start()
    arrivals.append(send(normed_buf, mine, (row, 1 - core)))

    up_ring = None
    for step in range(1, 4):
        ring.wait_recv()
        if step < 3:
            ring = around(step)
        if step == 2:
            up_ring = around_up(0)
        arrivals += corner(step - 1, crossing)
        crossing = across(step)
        arrivals += crossing[2:]
        if step == 3:
            up_ring.wait_recv()
            up_ring = around_up(1)
    arrivals += corner(3, crossing)
    up_ring.wait_recv()
    arrivals.append(around_up(2))
    for copy in arrivals:
        copy.wait_recv()
    for copy in sent:
        copy.wait_send()
    for keep in keeps:
        keep.wait()


def head_call(tokens, gain, cotangent, piece, w_up):
    rows, span, width = tokens.shape
    depth, wide = piece.shape
    anywhere = pl.BlockSpec(memory_space=pl.ANY)
    return pl.pallas_call(
        head_kernel,
        in_specs=[anywhere, pl.BlockSpec(memory_space=pltpu.VMEM)] + [anywhere] * 3,
        out_specs=[anywhere] * 4,
        out_shape=[
            jax.ShapeDtypeStruct((rows, 2 * span, width), jnp.bfloat16),
            jax.ShapeDtypeStruct(cotangent.shape, jnp.bfloat16),
            jax.ShapeDtypeStruct((16 * depth, wide), jnp.bfloat16),
            jax.ShapeDtypeStruct((Z_SIZE,) + w_up.shape, jnp.bfloat16),
        ],
        scratch_shapes=[
            pltpu.VMEM(tokens.shape, jnp.bfloat16),
            pltpu.VMEM(tokens.shape, jnp.bfloat16),
            pltpu.SemaphoreType.DMA((4,)),
            pltpu.SemaphoreType.DMA((32,)),
            pltpu.SemaphoreType.DMA((32,)),
        ],
        compiler_params=pltpu.CompilerParams(
            collective_id=0, has_side_effects=True, vmem_limit_bytes=32 * 1024 * 1024
        ),
    )(tokens, gain.reshape(1, width), cotangent, piece, w_up)


def plus_wide(*terms):
    return sum(term.astype(jnp.float32) for term in terms)


def plus(*terms):
    return plus_wide(*terms).astype(jnp.bfloat16)


TAIL_TILE = 256


def tail_kernel(
    dq_ref,
    dk_ref,
    dv_ref,
    weights_ref,
    query_ref,
    key_ref,
    value_ref,
    tokens_ref,
    residual_ref,
    gain_ref,
    ffn_gain_ref,
    hidden_ref,
    token_out,
    query_out,
    key_out,
    value_out,
    gain_out,
    up_out,
    out_out,
    weight_buf,
    dq_buf,
    dk_buf,
    dv_buf,
    own_buf,
    away_buf,
    came_buf,
    token_buf,
    residual_buf,
    far_buf,
    near_buf,
    turned_buf,
    turned_came,
    sum_buf,
    ring_buf,
    ring_came,
    gain_buf,
    gain_came,
    hidden_buf,
    hidden_came,
    local_sems,
    send_sems,
    recv_sems,
):
    row, core = lax.axis_index("rows"), lax.axis_index("seq")
    zed, here_y, here_x = row // 4, (row // 2) % 2, row % 2
    rest = row - 4 * zed
    over_x, over_y = row + 1 - 2 * here_x, row + 2 - 4 * here_y
    onward, backward = following(zed) * 4 + rest, preceding(zed) * 4 + rest
    beside = (zed + 1 - 2 * (zed % 2)) * 4 + rest
    beyond = (zed + 2 - 4 * (zed // 2)) * 4 + rest
    places = [zed]
    for _ in range(3):
        places.append(preceding(places[-1]))
    depth = query_out.shape[0]
    half_wide = query_ref.shape[1]
    span = own_buf.shape[0] // 2

    barrier = pltpu.get_barrier_semaphore()
    for target in ((onward, core), (backward, core), (over_x, core), (over_y, core), (row, 1 - core)):
        pl.semaphore_signal(
            barrier, inc=1, device_id=target, device_id_type=pl.DeviceIdType.MESH
        )
    loads = [
        pltpu.make_async_copy(
            weights_ref.at[:, pl.ds(0, 3 * half_wide)], weight_buf, local_sems.at[0]
        )
    ]
    for index, (source, target) in enumerate(
        (
            (dq_ref, dq_buf),
            (dk_ref, dk_buf),
            (dv_ref, dv_buf),
            (tokens_ref, token_buf),
            (residual_ref, residual_buf),
        )
    ):
        loads.append(pltpu.make_async_copy(source, target, local_sems.at[1 + index]))
    for load in loads:
        load.start()
    pl.semaphore_wait(barrier, 5)

    sent = []

    def send(src, dst, target):
        number = len(sent)
        copy = pltpu.make_async_remote_copy(
            src_ref=src,
            dst_ref=dst,
            send_sem=send_sems.at[number],
            recv_sem=recv_sems.at[number],
            device_id=target,
            device_id_type=pl.DeviceIdType.MESH,
        )
        copy.start()
        sent.append(copy)
        return copy

    cut = (half_wide // 128 + 1) // 2 * 128
    streams = (
        (query_ref, 0, half_wide, 0, False),
        (key_ref, 0, cut, half_wide, False),
        (key_ref, cut, half_wide - cut, half_wide, True),
        (value_ref, 0, half_wide, 2 * half_wide, True),
    )

    def block_of(step, far_y, far_x):
        at_y = 1 - here_y if far_y else here_y
        at_x = 1 - here_x if far_x else here_x
        index = (places[step] * 2 + at_y) * 2 + at_x
        return pl.ds(pl.multiple_of(index * depth, 16), depth)

    far, near, turned = {}, {}, {}

    def issue(step):
        for which, (grad, column, wide, base, flip) in enumerate(streams):
            columns, place = pl.ds(column, wide), pl.ds(base + column, wide)
            target = (over_y if flip else over_x, core)
            far[step, which] = send(
                grad.at[block_of(step, True, True), columns], far_buf.at[step, :, place], target
            )
        for which, (grad, column, wide, base, flip) in enumerate(streams):
            columns, place = pl.ds(column, wide), pl.ds(base + column, wide)
            target = (over_y if flip else over_x, core)
            near[step, which] = send(
                grad.at[block_of(step, flip, not flip), columns],
                near_buf.at[step, :, place],
                target,
            )

    def turn(step):
        for which, (grad, column, wide, base, flip) in enumerate(streams):
            columns, place = pl.ds(column, wide), pl.ds(base + column, wide)
            far[step, which].wait_recv()
            turned_buf[step, :, place] = plus(
                grad[block_of(step, not flip, flip), columns], far_buf[step, :, place]
            )
            target = (over_x if flip else over_y, core)
            turned[step, which] = send(
                turned_buf.at[step, :, place], turned_came.at[step, :, place], target
            )

    def total(step):
        for which, (grad, column, wide, base, _) in enumerate(streams):
            columns, place = pl.ds(column, wide), pl.ds(base + column, wide)
            near[step, which].wait_recv()
            turned[step, which].wait_recv()
            sum_buf[step, :, place] = plus_wide(
                grad[block_of(step, False, False), columns],
                near_buf[step, :, place],
                turned_came[step, :, place],
            )

    ring = []

    def around(step):
        value = sum_buf[step]
        if step > 1:
            ring[-1].wait_recv()
            value = value + ring_came[step - 2].astype(jnp.float32)
        ring_buf[step - 1] = value.astype(jnp.bfloat16)
        ring.append(send(ring_buf.at[step - 1], ring_came.at[step - 1], (onward, core)))

    hidden_ring = []

    def around_hidden(step):
        value = hidden_ref[places[step]].astype(jnp.float32)
        if step > 1:
            hidden_ring[-1].wait_recv()
            value = value + hidden_came[step - 2].astype(jnp.float32)
        hidden_buf[step - 1] = value.astype(jnp.bfloat16)
        hidden_ring.append(
            send(hidden_buf.at[step - 1], hidden_came.at[step - 1], (onward, core))
        )

    def normed_tile(tile, half):
        first = (tile // 2) * 2 * span + half * span + (tile % 2) * TAIL_TILE
        rows = pl.ds(pl.multiple_of(first, TAIL_TILE), TAIL_TILE)
        part = 0.0
        for index, grad in enumerate((dq_buf, dk_buf, dv_buf)):
            part += lax.dot_general(
                grad[rows, :],
                weight_buf[:, pl.ds(index * half_wide, half_wide)],
                (((1,), (1,)), ((), ())),
                preferred_element_type=jnp.float32,
            )
        return pl.ds(pl.multiple_of(tile * TAIL_TILE, TAIL_TILE), TAIL_TILE), part

    def away_tile(tile, carry):
        rows, part = normed_tile(tile, 1 - core)
        away_buf[rows, :] = part.astype(jnp.bfloat16)
        return carry

    def own_tile(tile, carry):
        rows, part = normed_tile(tile, core)
        own_buf[rows, :] = part
        return carry

    def norm_tile(tile, carry):
        rows = pl.ds(pl.multiple_of(tile * NORM_TILE, NORM_TILE), NORM_TILE)
        grad = own_buf[rows, :] + came_buf[rows, :].astype(jnp.float32)
        unit, scale = norm_stats(token_buf[rows, :].astype(jnp.float32))
        residual_buf[rows, :] += norm_back_rows(unit, scale, gain_ref[...], grad)
        return carry + jnp.sum(grad * unit, 0, keepdims=True)

    tiles = own_buf.shape[0] // TAIL_TILE
    norm_tiles = own_buf.shape[0] // NORM_TILE
    middle, quarter = tiles // 2, norm_tiles // 4
    issue(1)
    around_hidden(1)
    issue(2)
    for load in loads[:4]:
        load.wait()
    lax.fori_loop(0, middle, away_tile, 0)
    turn(1)
    issue(3)
    lax.fori_loop(middle, tiles, away_tile, 0)
    away = send(away_buf, came_buf, (row, 1 - core))
    around_hidden(2)
    lax.fori_loop(0, middle, own_tile, 0)
    turn(2)
    total(1)
    around(1)
    issue(0)
    lax.fori_loop(middle, tiles, own_tile, 0)
    for load in loads[4:]:
        load.wait()
    away.wait_recv()
    gain_part = jnp.zeros((1, own_buf.shape[1]), jnp.float32)
    gain_part = lax.fori_loop(0, quarter, norm_tile, gain_part)
    turn(3)
    around_hidden(3)
    gain_part = lax.fori_loop(quarter, 2 * quarter, norm_tile, gain_part)
    total(2)
    around(2)
    gain_part = lax.fori_loop(2 * quarter, 3 * quarter, norm_tile, gain_part)
    turn(0)
    gain_part = lax.fori_loop(3 * quarter, norm_tiles, norm_tile, gain_part)
    store = pltpu.make_async_copy(residual_buf, token_out, local_sems.at[6])
    store.start()
    gain_buf[0] = jnp.zeros_like(gain_buf[0])
    gain_buf[0, 0:1] = gain_part
    gain_buf[0, 1:2] = ffn_gain_ref[...]

    def exchange(number, target):
        copy = send(gain_buf.at[number], gain_came.at[number], target)
        copy.wait_recv()
        gain_buf[number + 1] = gain_buf[number] + gain_came[number]

    exchange(0, (row, 1 - core))
    exchange(1, (over_x, core))
    total(3)
    around(3)
    exchange(2, (over_y, core))
    exchange(3, (beside, core))
    exchange(4, (beyond, core))
    gain_out[...] = gain_buf[5]
    hidden_ring[-1].wait_recv()
    up_wide = up_out.shape[1]
    for out, columns in ((up_out, pl.ds(0, up_wide)), (out_out, pl.ds(up_wide, half_wide))):
        out[...] = plus_wide(hidden_ref[zed, :, columns], hidden_came[2, :, columns])
    total(0)
    ring[-1].wait_recv()
    for index, out in enumerate((query_out, key_out, value_out)):
        columns = pl.ds(index * half_wide, half_wide)
        out[...] = sum_buf[0, :, columns] + ring_came[2, :, columns].astype(jnp.float32)
    for copy in sent:
        copy.wait_send()
    store.wait()


def tail_call(grads, weights, sums, tokens, grad_residual, gain, ffn_gain, hidden_sums):
    flat, width = grad_residual.shape
    half_wide = sums[0].shape[1]
    depth = sums[0].shape[0] // 16
    anywhere, here = pl.BlockSpec(memory_space=pl.ANY), pl.BlockSpec(memory_space=pltpu.VMEM)
    block = pltpu.VMEM((4, depth, 3 * half_wide), jnp.bfloat16)
    moving = pltpu.VMEM((3, depth, 3 * half_wide), jnp.bfloat16)
    gains = pltpu.VMEM((6, 8, width), jnp.float32)
    sum_shape = jax.ShapeDtypeStruct((depth, half_wide), jnp.float32)
    return pl.pallas_call(
        tail_kernel,
        in_specs=[anywhere] * 4 + [here] * 3 + [anywhere] * 2 + [here] * 3,
        out_specs=[anywhere] + [here] * 6,
        out_shape=[
            jax.ShapeDtypeStruct((flat, width), jnp.float32),
            sum_shape,
            sum_shape,
            sum_shape,
            jax.ShapeDtypeStruct((8, width), jnp.float32),
            jax.ShapeDtypeStruct((depth, hidden_sums.shape[2] - half_wide), jnp.float32),
            sum_shape,
        ],
        scratch_shapes=[pltpu.VMEM((width, 3 * half_wide), jnp.bfloat16)]
        + [pltpu.VMEM((2 * flat, half_wide), jnp.bfloat16)] * 3
        + [
            pltpu.VMEM((flat, width), jnp.float32),
            pltpu.VMEM((flat, width), jnp.bfloat16),
            pltpu.VMEM((flat, width), jnp.bfloat16),
            pltpu.VMEM((flat, width), jnp.bfloat16),
            pltpu.VMEM((flat, width), jnp.float32),
        ]
        + [block] * 4
        + [pltpu.VMEM((4, depth, 3 * half_wide), jnp.float32), moving, moving, gains, gains]
        + [pltpu.VMEM((3,) + hidden_sums.shape[1:], jnp.bfloat16)] * 2
        + [
            pltpu.SemaphoreType.DMA((7,)),
            pltpu.SemaphoreType.DMA((64,)),
            pltpu.SemaphoreType.DMA((64,)),
        ],
        compiler_params=pltpu.CompilerParams(
            collective_id=1, has_side_effects=True, vmem_limit_bytes=60 * 1024 * 1024
        ),
    )(
        *grads,
        weights,
        *sums,
        tokens,
        grad_residual,
        gain.reshape(1, width),
        ffn_gain.reshape(1, width),
        hidden_sums,
    )


def halves_z(stack):
    _, depth, wide = stack.shape
    if depth > 80:
        return stack[:, : depth // 2], stack[:, depth // 2 :]
    cut = (wide // 128 + 1) // 2 * 128
    return stack[:, :, :cut], stack[:, :, cut:]


def gather_first(first, second):
    return jnp.stack([first, swap_y(first)]), jnp.stack([second, swap_x(second)])


def gather_second(first, second):
    return (first, swap_x(first)), (second, swap_y(second))


def dot_low(left_side, right_side):
    return jnp.dot(left_side, right_side, preferred_element_type=jnp.float32)


def outer_low(left_side, right_side):
    return jnp.einsum(
        "tc,te->ce", left_side, right_side, preferred_element_type=jnp.float32
    ).astype(jnp.bfloat16)


class Scatter:

    def __init__(self, first, second, by_rows=False):
        self.parts, self.by_rows = (first, second), by_rows

    def pick(self, which, start_y, start_x, count_y=1, count_x=1):
        picked = []
        for whole, row, depth, column, wide in self.parts[which]:
            planes = Z_SIZE // len(self.parts[which]) if self.by_rows else Z_SIZE
            blocks = whole.reshape(planes, 2, 2, whole.shape[0] // planes // 4, whole.shape[1])
            picked.append(
                lax.dynamic_slice(
                    blocks,
                    (0, start_y, start_x, row, column),
                    (planes, count_y, count_x, depth, wide),
                ).reshape(planes, count_y * count_x, depth, wide)
            )
        axis = 0 if self.by_rows else 3
        return picked[0] if len(picked) == 1 else jnp.concatenate(picked, axis)

    def prepare(self, *after):
        _, here_y, here_x = chip_place()
        here_x, here_y = tie((here_x, here_y), *after)
        self.away = (self.pick(0, 0, 1 - here_x, 2, 1), self.pick(1, 1 - here_y, 0, 1, 2))

    def spread(self):
        self.came = (swap_x(self.away[0]), swap_y(self.away[1]))

    def of_came(self, which, far):
        _, here_y, here_x = chip_place()
        here = here_x if which else here_y
        return lax.dynamic_slice_in_dim(self.came[which], here ^ far, 1, 1)

    def turn(self):
        _, here_y, here_x = chip_place()
        first = plus(self.pick(0, 1 - here_y, here_x), self.of_came(0, 1))
        second = plus(self.pick(1, here_y, 1 - here_x), self.of_came(1, 1))
        self.turning = (first, second)
        self.turned = (swap_y(first), swap_x(second))

    def near_sums(self):
        _, here_y, here_x = chip_place()
        first, second = (
            plus(
                self.pick(which, here_y, here_x), self.of_came(which, 0), self.turned[which]
            ).reshape((Z_SIZE,) + self.turned[which].shape[2:])
            for which in range(2)
        )
        return jnp.concatenate([first, second], 1 if self.by_rows else 2)

    def gather(self):
        self.sums = self.near_sums()
        self.moving = next_z(self.block(1))

    def block(self, back):
        target = (ring_place() - back) % Z_SIZE
        zed = jnp.where(target == 2, 3, jnp.where(target == 3, 2, target))
        if self.by_rows:
            zed = zed ^ (2 * lax.axis_index("seq"))
        return lax.dynamic_index_in_dim(self.sums, zed, 0, keepdims=False)

    def step(self, number):
        self.moving = next_z(plus(self.block(number), self.moving))

    def finish(self):
        return self.block(0).astype(jnp.float32) + self.moving.astype(jnp.float32)

    def hold(self, names, *after):
        for name in names:
            setattr(self, name, tie(getattr(self, name), *after))


def body_pair(
    tokens, segments, gain_attn, w_query, w_key, w_value, w_out, gain_ffn, w_up, w_down, cotangent
):
    core = lax.axis_index("seq")
    rows, span, width = tokens.shape
    flat = rows * span

    def split(flat_rows, axis_width):
        return flat_rows.reshape(rows, 2 * span, axis_width)

    def sharing(values):
        wide = split(values, values.shape[-1])
        return swap_cores(own_half(wide, 1, 1 - core).astype(jnp.bfloat16))

    def shared(values, received):
        wide = split(values, values.shape[-1])
        return (own_half(wide, 1, core) + received.astype(jnp.float32)).reshape(flat, -1)

    attn_piece = jnp.concatenate([w_query, w_key, w_value, w_out], 1)
    half_wide = w_query.shape[1]
    normed, cot_other, attn_weights, up_stack = head_call(
        tokens, gain_attn, cotangent, attn_piece, w_up
    )
    first = core == 0
    tokens_own = tokens.reshape(flat, width).astype(jnp.float32)
    cot_own = cotangent.reshape(flat, width)
    windows = windows_of(segments, QUERY_TILE)
    back_windows = windows_of(segments, BACK_TILE)
    marks = (
        jnp.broadcast_to(segments[:, :, None], segments.shape + (LANES,)),
        jnp.broadcast_to(segments[:, None, :], (rows, 8, 2 * span)),
    )
    normed = normed.reshape(2 * flat, width)
    w_qkv = attn_weights[:, : 3 * half_wide]
    w_q, w_k, w_v = (w_qkv[:, i * half_wide : (i + 1) * half_wide] for i in range(3))

    up_parts = gather_first(*halves_z(up_stack))
    down_steps = [tie(w_down, up_stack)]
    down_steps.append(next_z(down_steps[-1]))
    w_o_half = attn_weights[:, 3 * half_wide :]
    w_o_other = swap_cores(w_o_half)
    qk_rows = dot_low(normed, w_qkv[:, : 2 * half_wide]).astype(jnp.bfloat16)
    normed, w_o_other, down_steps[1], up_parts = tie(
        (normed, w_o_other, down_steps[1], up_parts), qk_rows
    )
    down_steps.append(next_z(down_steps[-1]))
    up_near = up_parts
    up_parts = gather_second(*up_parts)
    normed = tie(normed, up_near)
    value_rows = dot_low(normed, w_qkv[:, 2 * half_wide :]).astype(jnp.bfloat16)
    value_rows, down_steps[2] = tie((value_rows, down_steps[2]))
    down_steps.append(next_z(down_steps[-1]))
    qk_rows, value_rows = split(qk_rows, 2 * half_wide), split(value_rows, half_wide)
    qk_rows = tie(qk_rows, up_near)
    operands = [(qk_rows, 0), (qk_rows, 1), (value_rows, 0)]
    (mixed,) = attention_call(
        attend_kernel, 0, rows, windows, marks, operands, [half_wide], [], half_wide
    )
    mixed, down_steps[3], up_parts = tie((mixed, down_steps[3], up_parts))
    down_first, down_second = halves_z(natural_z(down_steps))
    down_came = swap_y(down_first), swap_x(down_second), swap_x(down_first), swap_y(down_second)
    w_o = jnp.where(
        first,
        jnp.concatenate([w_o_half, w_o_other], 1),
        jnp.concatenate([w_o_other, w_o_half], 1),
    )
    w_o_rows = own_half(w_o, 0, core)

    mixed_other = swap_cores(own_half(mixed, 1, 1 - core))
    mixed_mine = own_half(mixed, 1, core)
    mixed_own = jnp.where(
        first,
        jnp.concatenate([mixed_mine, mixed_other], 2),
        jnp.concatenate([mixed_other, mixed_mine], 2),
    ).reshape(flat, width)
    mixed_own, w_o, w_o_rows = tie((mixed_own, w_o, w_o_rows))
    residual = tokens_own + dot_low(mixed_own, w_o)
    unit_two, _ = norm_stats(residual)
    normed_two = (unit_two * gain_ffn).astype(jnp.bfloat16)
    normed_two, down_came = tie((normed_two, down_came))
    first_y, second_x, first_x, second_y = down_came
    down_parts = (down_first, first_y, first_x, down_second, second_x, second_y)
    cot_other = tie(cot_other, mixed_own)
    cot_all = jnp.concatenate([cot_own, cot_other.reshape(flat, width)], 0)
    hidden_low, grad_pre, y_own, grad_two_own, normed_two_all, y_came, grad_two_came = feed_forward(
        normed_two, cot_all, up_parts, down_parts
    )

    down_half = outer_low(hidden_low, cot_all)
    down_away = swap_cores(own_half(down_half, 1, 1 - core))
    layer_out, grad_residual, ffn_gain_rows, grad_attn_all = residual_call(
        rows, residual, cot_own, y_own, y_came, grad_two_own, tie(grad_two_came, down_half), gain_ffn
    )
    ffn_gain_part = ffn_gain_rows[0]
    grad_attn_all = grad_attn_all.reshape(2 * flat, width)
    down_away = tie(down_away, grad_residual)
    depth, wide = w_down.shape
    down_halves = ((down_half, core * wide), (down_away, 0))
    down_sum = Scatter(
        *(
            [(whole, row, depth // 2, column, wide) for whole, column in down_halves]
            for row in (0, depth // 2)
        ),
        True,
    )
    down_sum.prepare()
    down_sum.spread()
    up_whole = outer_low(normed_two_all, tie(grad_pre, *down_sum.away))
    grad_attn_all = tie(grad_attn_all, up_whole)
    out_half = outer_low(mixed.reshape(2 * flat, -1), grad_attn_all)
    out_away = swap_cores(own_half(out_half, 1, 1 - core))
    grad_mixed = split(times_transposed(grad_attn_all, w_o_rows).astype(jnp.bfloat16), width // 2)
    out_away = tie(out_away, grad_mixed)
    out_kept = own_half(out_half, 1, core)
    out_whole = jnp.where(
        first,
        jnp.concatenate([out_kept, out_away], 0),
        jnp.concatenate([out_away, out_kept], 0),
    )
    depth, wide = w_up.shape
    cut = (wide + half_wide) // 256 * 128
    up_sum = Scatter(
        [(up_whole, 0, depth, 0, cut)],
        [(up_whole, 0, depth, cut, wide - cut), (out_whole, 0, depth, 0, half_wide)],
    )
    down_sum.hold(("came",), grad_mixed)
    down_sum.turn()
    up_sum.prepare(*down_sum.turning)
    up_sum.spread()
    grad_mixed = tie(grad_mixed, *up_sum.away, *down_sum.turning)
    scratch = [pltpu.VMEM((2 * span, LANES), jnp.float32)] * 2

    def attend_back(row, grad_rows, begun=()):
        return attention_call(
            attend_back_kernel,
            row,
            1,
            back_windows,
            marks,
            operands + [(grad_rows, 0)],
            [half_wide] * 3,
            scratch,
            LANES,
            begun,
        )

    grads = attend_back(0, grad_mixed)
    down_sum.hold(("turned",), *grads)
    down_sum.gather()
    grads = tie(grads, down_sum.sums)
    for row in range(1, rows):
        grads = attend_back(row, grad_mixed, grads)
    down_sum.hold(("moving",), *grads)
    up_sum.hold(("came",), *grads)
    grads = tie(grads, down_sum.moving, up_sum.came)
    up_sum.turn()
    down_sum.step(2)
    grads = tie(grads, *up_sum.turning)
    grad_queries, grad_keys, grad_values = (grad.reshape(2 * flat, half_wide) for grad in grads)
    query_whole = outer_low(normed, grad_queries)
    key_whole = outer_low(normed, grad_keys)
    down_sum.hold(("moving",), query_whole, key_whole)
    grad_values = tie(grad_values, down_sum.moving)
    down_sum.step(3)
    value_whole = outer_low(normed, grad_values)
    up_sum.hold(("turned",), value_whole)
    sums = tie((query_whole, key_whole, value_whole), down_sum.moving)
    token_grad, query_grad, key_grad, value_grad, gains, up_grad, out_grad = tail_call(
        (grad_queries, grad_keys, grad_values),
        attn_weights,
        sums,
        tokens.reshape(flat, width),
        grad_residual,
        gain_attn,
        ffn_gain_part,
        up_sum.near_sums(),
    )
    gain_attn_grad, gain_ffn_grad = gains[0], gains[1]
    down_grad = down_sum.finish()
    return (
        layer_out.reshape(rows, span, width),
        token_grad.reshape(rows, span, width),
        gain_attn_grad,
        query_grad,
        key_grad,
        value_grad,
        out_grad,
        gain_ffn_grad,
        up_grad,
        down_grad,
    )


def solution(mesh):
    paired = mesh.shape["seq"] == 2 and mesh.shape["rows"] == 16
    program = body_pair if paired else body
    return jax.shard_map(
        program,
        mesh=mesh,
        in_specs=(
            P("rows", "seq", None),
            P("rows", None),
            P(),
            P("rows", "seq"),
            P("rows", "seq"),
            P("rows", "seq"),
            P("rows", "seq"),
            P(),
            P("rows", "seq"),
            P("rows", "seq"),
            P("rows", "seq", None),
        ),
        out_specs=(
            P("rows", "seq", None),
            P("rows", "seq", None),
            P(),
            P("rows", "seq"),
            P("rows", "seq"),
            P("rows", "seq"),
            P("rows", "seq"),
            P(),
            P("rows", "seq"),
            P("rows", "seq"),
        ),
        check_vma=False,
    )
```

```python
import functools

import jax
import jax.numpy as jnp
from jax import lax
from jax.experimental import pallas as pl
from jax.experimental.pallas import tpu as pltpu
from jax.sharding import PartitionSpec as P

HEADS = 20
HEAD_DIM = 64


epsilon = 1e-05
root_half = 0.7071067811865476


def norm_rows(values, gain_vec):
    row_mean = jnp.mean(values, -1, keepdims=True)
    centred = values - row_mean
    spread = jnp.mean(centred * centred, -1, keepdims=True)
    return centred * lax.rsqrt(spread + epsilon) * gain_vec


def gelu_exact(values):
    return 0.5 * values * (1.0 + lax.erf(values * root_half))


def times_transposed(left_side, right_side):
    return jnp.einsum("te,de->td", left_side, right_side, preferred_element_type=jnp.float32)


def split_heads(rows_in):
    return rows_in.reshape(rows_in.shape[0], rows_in.shape[1], HEADS, HEAD_DIM)


def join_heads(heads_in):
    return heads_in.reshape(heads_in.shape[0], heads_in.shape[1], HEADS * HEAD_DIM)


def masked_scores(query_heads, key_heads, seg_query, seg_key):
    scores = jnp.einsum(
        "rqhd,rkhd->rhqk", query_heads, key_heads, preferred_element_type=jnp.float32
    )
    scores = scores * HEAD_DIM ** (-0.5)
    allowed = (seg_query[:, :, None] == seg_key[:, None, :])[:, None]
    return (allowed, jnp.where(allowed, scores, -1e30))


def attention_forward(query_rows, key_rows, value_rows, seg_query, seg_key):
    allowed, scores = masked_scores(
        split_heads(query_rows), split_heads(key_rows), seg_query, seg_key
    )
    row_top = jnp.max(scores, -1, keepdims=True)
    exponent = jnp.exp(scores - row_top)
    row_total = jnp.sum(exponent, -1, keepdims=True)
    prob_low = (exponent / row_total).astype(jnp.bfloat16)
    mixed_out = jnp.einsum(
        "rhqk,rkhd->rqhd", prob_low, split_heads(value_rows), preferred_element_type=jnp.float32
    )
    return (join_heads(mixed_out).astype(jnp.bfloat16), row_top + jnp.log(row_total))


def grad_pieces(query_heads, key_heads, value_heads, seg_query, seg_key, log_total, grad_heads):
    allowed, scores = masked_scores(query_heads, key_heads, seg_query, seg_key)
    prob_rows = jnp.where(allowed, jnp.exp(scores - log_total), 0.0)
    grad_probs = jnp.einsum(
        "rqhd,rkhd->rhqk", grad_heads, value_heads, preferred_element_type=jnp.float32
    )
    return (prob_rows, grad_probs)


def attention_grads(query_rows, key_rows, value_rows, seg_query, seg_key, log_total, grad_mixed):
    query_heads = split_heads(query_rows)
    key_heads = split_heads(key_rows)
    grad_heads = split_heads(grad_mixed)
    prob_rows, grad_probs = grad_pieces(
        query_heads, key_heads, split_heads(value_rows), seg_query, seg_key, log_total, grad_heads
    )
    value_part = jnp.einsum(
        "rhqk,rqhd->rkhd",
        prob_rows.astype(jnp.bfloat16),
        grad_heads,
        preferred_element_type=jnp.float32,
    )
    row_inner = jnp.sum(grad_probs * prob_rows, -1, keepdims=True)
    score_grad = (prob_rows * (grad_probs - row_inner)).astype(jnp.bfloat16)
    score_scale = HEAD_DIM ** (-0.5)
    query_part = (
        jnp.einsum("rhqk,rkhd->rqhd", score_grad, key_heads, preferred_element_type=jnp.float32)
        * score_scale
    )
    key_part = (
        jnp.einsum("rhqk,rqhd->rkhd", score_grad, query_heads, preferred_element_type=jnp.float32)
        * score_scale
    )
    return (join_heads(query_part), join_heads(key_part), join_heads(value_part))


def process(token_rows, cot_rows, seg_rows, gain_attn, gain_ffn, weights):
    w_query, w_key, w_value, w_out, w_up, w_down = weights
    row_count, query_count, model_width = token_rows.shape
    offset = lax.axis_index("seq") * query_count
    seg_query = lax.dynamic_slice_in_dim(seg_rows, offset, query_count, 1)

    def shaped(flat_rows):
        return flat_rows.reshape(row_count, query_count, model_width)

    flat_tokens = token_rows.reshape(row_count * query_count, model_width).astype(jnp.float32)
    normed, norm_back = jax.vjp(norm_rows, flat_tokens, gain_attn)
    lowered = normed.astype(jnp.bfloat16)
    queries = jnp.dot(lowered, w_query, preferred_element_type=jnp.float32).astype(jnp.bfloat16)
    key_rows = jnp.dot(lowered, w_key, preferred_element_type=jnp.float32).astype(jnp.bfloat16)
    value_rows = jnp.dot(lowered, w_value, preferred_element_type=jnp.float32).astype(jnp.bfloat16)
    key_whole, value_whole = (
        lax.all_gather(shaped(key_rows), "seq", axis=1, tiled=True),
        lax.all_gather(shaped(value_rows), "seq", axis=1, tiled=True),
    )
    mixed_rows, log_total = attention_forward(
        shaped(queries), key_whole, value_whole, seg_query, seg_rows
    )
    mixed_flat = mixed_rows.reshape(row_count * query_count, model_width)
    residual = flat_tokens + jnp.dot(mixed_flat, w_out, preferred_element_type=jnp.float32)
    normed_two, norm_two_back = jax.vjp(norm_rows, residual, gain_ffn)
    lowered_two = normed_two.astype(jnp.bfloat16)
    hidden_pre = jnp.dot(lowered_two, w_up, preferred_element_type=jnp.float32)
    hidden, gelu_back = jax.vjp(gelu_exact, hidden_pre)
    hidden_low = hidden.astype(jnp.bfloat16)
    layer_rows = (
        residual + jnp.dot(hidden_low, w_down, preferred_element_type=jnp.float32)
    ).astype(jnp.bfloat16)
    grad_out = cot_rows.reshape(row_count * query_count, model_width)
    grad_hidden = times_transposed(grad_out, w_down)
    grad_pre = gelu_back(grad_hidden)[0].astype(jnp.bfloat16)
    grad_normed_two = times_transposed(grad_pre, w_up)
    grad_resid_norm, grad_gain_ffn = norm_two_back(grad_normed_two)
    grad_residual = grad_out.astype(jnp.float32) + grad_resid_norm
    grad_attn = grad_residual.astype(jnp.bfloat16)
    grad_mixed = times_transposed(grad_attn, w_out).astype(jnp.bfloat16)
    query_part, key_part, value_part = attention_grads(
        shaped(queries), key_whole, value_whole, seg_query, seg_rows, log_total, shaped(grad_mixed)
    )
    key_own, value_own = (
        lax.psum_scatter(key_part, "seq", scatter_dimension=1, tiled=True),
        lax.psum_scatter(value_part, "seq", scatter_dimension=1, tiled=True),
    )
    grad_queries = query_part.reshape(row_count * query_count, model_width).astype(jnp.bfloat16)
    grad_keys = key_own.reshape(row_count * query_count, model_width).astype(jnp.bfloat16)
    grad_values = value_own.reshape(row_count * query_count, model_width).astype(jnp.bfloat16)
    grad_normed = (
        times_transposed(grad_queries, w_query)
        + times_transposed(grad_keys, w_key)
        + times_transposed(grad_values, w_value)
    )
    grad_token_norm, grad_gain_attn = norm_back(grad_normed)
    grad_tokens = (grad_residual + grad_token_norm).reshape(row_count, query_count, model_width)
    saved = (
        lowered,
        grad_queries,
        grad_keys,
        grad_values,
        mixed_flat,
        grad_attn,
        lowered_two,
        grad_pre,
        hidden_low,
        grad_out,
    )
    return (
        layer_rows.reshape(row_count, query_count, model_width),
        grad_tokens,
        saved,
        grad_gain_attn,
        grad_gain_ffn,
    )


def body(
    tokens, segments, gain_attn, w_query, w_key, w_value, w_out, gain_ffn, w_up, w_down, cotangent
):
    col_query = lax.all_gather(w_query, "seq", axis=1, tiled=True)
    col_key = lax.all_gather(w_key, "seq", axis=1, tiled=True)
    col_value = lax.all_gather(w_value, "seq", axis=1, tiled=True)
    col_out = lax.all_gather(w_out, "seq", axis=1, tiled=True)
    col_up = lax.all_gather(w_up, "seq", axis=1, tiled=True)
    col_down = lax.all_gather(w_down, "seq", axis=1, tiled=True)
    results = [
        process(
            tokens,
            cotangent,
            segments,
            gain_attn,
            gain_ffn,
            (
                lax.all_gather(col_query, "rows", axis=0, tiled=True),
                lax.all_gather(col_key, "rows", axis=0, tiled=True),
                lax.all_gather(col_value, "rows", axis=0, tiled=True),
                lax.all_gather(col_out, "rows", axis=0, tiled=True),
                lax.all_gather(col_up, "rows", axis=0, tiled=True),
                lax.all_gather(col_down, "rows", axis=0, tiled=True),
            ),
        )
    ]
    layer_out = jnp.concatenate([result_set[0] for result_set in results], 0)
    token_grad = jnp.concatenate([result_set[1] for result_set in results], 0)
    saved = [
        jnp.concatenate([result_set[2][member] for result_set in results], 0)
        for member in range(10)
    ]
    attn_gain_part = sum((result_set[3] for result_set in results))
    ffn_gain_part = sum((result_set[4] for result_set in results))
    gain_attn_grad, gain_ffn_grad = lax.psum((attn_gain_part, ffn_gain_part), ("rows", "seq"))
    (
        lowered,
        grad_queries,
        grad_keys,
        grad_values,
        mixed_flat,
        grad_attn,
        lowered_two,
        grad_pre,
        hidden_low,
        grad_out,
    ) = saved
    splits = lax.axis_size("seq")

    def arrange(grad_block):
        return grad_block.reshape(grad_block.shape[0], splits, grad_block.shape[1] // splits)

    def outer_product(left_side, right_side):
        return jnp.einsum("tc,te->ce", left_side, right_side, preferred_element_type=jnp.float32)

    def input_terms(offset, count):
        blocks = [
            outer_product(lowered, grad_queries),
            outer_product(lowered, grad_keys),
            outer_product(lowered, grad_values),
            outer_product(mixed_flat, grad_attn),
            outer_product(lowered_two, grad_pre),
        ]
        return jnp.concatenate([arrange(grad_block) for grad_block in blocks], 2)

    def hidden_terms(offset, count):
        return arrange(outer_product(hidden_low, grad_out))

    def spread_sum(term_of, shard_rows):
        row_part = lax.psum_scatter(
            term_of(jnp.int32(0), shard_rows * lax.axis_size("rows")),
            "rows",
            scatter_dimension=0,
            tiled=True,
        )
        return lax.psum_scatter(row_part, "seq", scatter_dimension=1, tiled=True)[:, 0, :]

    input_grads = spread_sum(input_terms, w_query.shape[0])
    down_grad = spread_sum(hidden_terms, w_down.shape[0])
    column_width = w_query.shape[1]
    query_grad = input_grads[:, :column_width]
    key_grad = input_grads[:, column_width : 2 * column_width]
    value_grad = input_grads[:, 2 * column_width : 3 * column_width]
    out_grad = input_grads[:, 3 * column_width : 4 * column_width]
    up_grad = input_grads[:, 4 * column_width :]
    return (
        layer_out,
        token_grad,
        gain_attn_grad,
        query_grad,
        key_grad,
        value_grad,
        out_grad,
        gain_ffn_grad,
        up_grad,
        down_grad,
    )


LANES = 128
QUERY_TILE = 128
BACK_TILE = 256
NEVER = -1e30


def swap_cores(values):
    return lax.ppermute(values, "seq", [(0, 1), (1, 0)])


def both_cores(values, axis):
    other = swap_cores(values)
    first = lax.axis_index("seq") == 0
    return jnp.where(
        first,
        jnp.concatenate([values, other], axis),
        jnp.concatenate([other, values], axis),
    )


def own_half(values, axis, index):
    half = values.shape[axis] // 2
    return lax.dynamic_slice_in_dim(values, index * half, half, axis)


def two_heads(ref, rows, columns):
    values = ref[0, rows, columns]
    lower = lax.broadcasted_iota(jnp.int32, values.shape, 1) < HEAD_DIM
    zero = jnp.zeros_like(values)
    return jnp.concatenate([jnp.where(lower, values, zero), jnp.where(lower, zero, values)], 0)


def merge_heads(values):
    half = values.shape[0] // 2
    lower = lax.broadcasted_iota(jnp.int32, (half, LANES), 1) < HEAD_DIM
    return jnp.where(lower, values[:half], values[half:])


def over_windows(first_row, query_tile, start_ref, count_ref, length, window):
    row = first_row + pl.program_id(0)

    def tile_step(tile, carry):
        begin = pl.multiple_of(start_ref[row, tile] * LANES, LANES)
        count = count_ref[row, tile]
        queries = pl.ds(pl.multiple_of(tile * query_tile, query_tile), query_tile)
        for tiles in range(1, length // LANES + 1):
            keys = pl.ds(begin, tiles * LANES)
            pl.when(count == tiles)(functools.partial(window, queries, keys))
        return carry

    lax.fori_loop(0, length // query_tile, tile_step, 0)


last_dims = (((1,), (1,)), ((), ()))
first_dims = (((0,), (0,)), ((), ()))
exponent_scale = HEAD_DIM ** (-0.5) * 1.4426950408889634


def attend_kernel(
    row, begun, start_ref, count_ref, column_ref, line_ref, q_ref, k_ref, v_ref, *rest
):
    (out_ref,) = rest[begun:]
    _, length, wide = q_ref.shape

    def window(queries, keys):
        allowed = column_ref[0, queries, :1] == line_ref[0, :1, keys]
        bias = jnp.where(allowed, 0.0, NEVER)[None]

        def scores_of(pair):
            columns = pl.ds(pair * LANES, LANES)
            return lax.dot_general(
                two_heads(q_ref, queries, columns),
                k_ref[0, keys, columns],
                last_dims,
                preferred_element_type=jnp.float32,
            )

        ahead = scores_of(0)
        for pair in range(wide // LANES):
            scores = ahead
            if (pair + 1) * LANES < wide:
                ahead = scores_of(pair + 1)
            shape = scores.shape
            scores = (scores.reshape((2, QUERY_TILE) + shape[1:]) + bias).reshape(shape)
            top = jnp.max(scores, -1, keepdims=True)
            exponent = jnp.exp2((scores - top) * exponent_scale)
            columns = pl.ds(pair * LANES, LANES)
            part = jnp.dot(
                exponent.astype(jnp.bfloat16),
                v_ref[0, keys, columns],
                preferred_element_type=jnp.float32,
            )
            part = part / jnp.sum(exponent, -1, keepdims=True)
            out_ref[0, queries, columns] = merge_heads(part).astype(jnp.bfloat16)

    over_windows(row, QUERY_TILE, start_ref, count_ref, length, window)


def attend_back_kernel(
    row, begun, start_ref, count_ref, column_ref, line_ref, q_ref, k_ref, v_ref, grad_ref, *rest
):
    dq_ref, dk_ref, dv_ref, dk_sum, dv_sum = rest[begun:]
    dk_sum[...] = jnp.zeros_like(dk_sum)
    dv_sum[...] = jnp.zeros_like(dv_sum)
    scale = HEAD_DIM ** (-0.5)
    columns = pl.ds(0, LANES)

    def window(queries, keys):
        query, grad = two_heads(q_ref, queries, columns), two_heads(grad_ref, queries, columns)
        key, value = k_ref[0, keys, :], v_ref[0, keys, :]
        bias = jnp.where(column_ref[0, keys, :1] == line_ref[0, :1, queries], 0.0, NEVER)
        scores = lax.dot_general(key, query, last_dims, preferred_element_type=jnp.float32)
        scores = scores + jnp.concatenate([bias, bias], 1)
        top = jnp.max(scores, 0, keepdims=True)
        exponent = jnp.exp2((scores - top) * exponent_scale)
        probs = exponent * (1.0 / jnp.sum(exponent, 0, keepdims=True))
        grad_probs = lax.dot_general(value, grad, last_dims, preferred_element_type=jnp.float32)
        inner = jnp.sum(grad_probs * probs, 0, keepdims=True)
        grad_scores = (probs * (grad_probs - inner)).astype(jnp.bfloat16)
        dv_sum[keys, :] += jnp.dot(
            probs.astype(jnp.bfloat16), grad, preferred_element_type=jnp.float32
        )
        dk_sum[keys, :] += jnp.dot(grad_scores, query, preferred_element_type=jnp.float32)
        query_part = lax.dot_general(
            grad_scores, key, first_dims, preferred_element_type=jnp.float32
        )
        dq_ref[0, queries, :] = (merge_heads(query_part) * scale).astype(jnp.bfloat16)

    over_windows(row, BACK_TILE, start_ref, count_ref, k_ref.shape[1], window)
    dk_ref[0] = (dk_sum[...] * scale).astype(jnp.bfloat16)
    dv_ref[0] = dv_sum[...].astype(jnp.bfloat16)


def windows_of(segments, query_tile):
    heads = segments[:, ::query_tile]
    tails = segments[:, query_tile - 1 :: query_tile]
    begin = jnp.sum(segments[:, None, :] < heads[:, :, None], -1, dtype=jnp.int32)
    end = jnp.sum(segments[:, None, :] <= tails[:, :, None], -1, dtype=jnp.int32)
    start = begin // LANES
    return start, (end + LANES - 1) // LANES - start


def attention_call(
    kernel, row, rows, windows, marks, operands, outputs, scratch, block_wide, begun=()
):
    all_rows, length, _ = operands[0][0].shape
    wide = outputs[0]
    steps = wide // block_wide

    def block(part):
        return pl.BlockSpec(
            (1, length, block_wide), lambda at, step, *_: (row + at, 0, part * steps + step)
        )

    work = rows * wide * length * length
    shape = jax.ShapeDtypeStruct((all_rows, length, wide), jnp.bfloat16)
    return pl.pallas_call(
        functools.partial(kernel, row, len(begun)),
        grid_spec=pltpu.PrefetchScalarGridSpec(
            num_scalar_prefetch=2,
            grid=(rows, steps),
            in_specs=[
                pl.BlockSpec((1, length, LANES), lambda at, *_: (row + at, 0, 0)),
                pl.BlockSpec((1, 8, length), lambda at, *_: (row + at, 0, 0)),
            ]
            + [block(first) for _, first in operands]
            + [pl.BlockSpec(memory_space=pl.ANY)] * len(begun),
            out_specs=[block(0)] * len(outputs),
            scratch_shapes=scratch,
        ),
        out_shape=[shape] * len(outputs),
        input_output_aliases={4 + len(operands) + index: index for index in range(len(begun))},
        compiler_params=pltpu.CompilerParams(vmem_limit_bytes=48 * 1024 * 1024),
        cost_estimate=pl.CostEstimate(
            flops=4 * len(operands) * work,
            bytes_accessed=2 * (len(operands) + len(outputs)) * rows * length * wide,
            transcendentals=work // HEAD_DIM,
        ),
    )(*windows, *marks, *(array for array, _ in operands), *begun)


def norm_stats(values):
    centred = values - jnp.mean(values, -1, keepdims=True)
    scale = lax.rsqrt(jnp.mean(centred * centred, -1, keepdims=True) + epsilon)
    return centred * scale, scale


def norm_back_rows(unit, scale, gain_vec, grad):
    scaled = grad * gain_vec
    inner = jnp.mean(scaled * unit, -1, keepdims=True)
    return scale * (scaled - jnp.mean(scaled, -1, keepdims=True) - unit * inner)


Z_SIZE = 4
RING = (0, 1, 3, 2)
PLACE = (0, 1, 3, 2)


def chip_place():
    index = lax.axis_index("rows")
    return index // 4, (index // 2) % 2, index % 2


def swap_x(values):
    return lax.ppermute(values, "rows", [(row, row ^ 1) for row in range(16)])


def swap_y(values):
    return lax.ppermute(values, "rows", [(row, row ^ 2) for row in range(16)])


def next_z(values):
    pairs = []
    for place in range(Z_SIZE):
        here, there = RING[place], RING[(place + 1) % Z_SIZE]
        pairs += [(here * 4 + rest, there * 4 + rest) for rest in range(4)]
    return lax.ppermute(values, "rows", pairs)


def ring_place():
    zed = chip_place()[0]
    return jnp.where(zed == 2, 3, jnp.where(zed == 3, 2, zed))


def tie(value, *after):
    return lax.optimization_barrier((value, after))[0]


def natural_z(steps):
    place = ring_place()
    stack = jnp.stack(steps)
    return jnp.stack(
        [
            lax.dynamic_index_in_dim(stack, (place - PLACE[zed]) % Z_SIZE, 0, keepdims=False)
            for zed in range(Z_SIZE)
        ]
    )


def load_pieces(place_ref, pieces, target_of, sems):
    copies = []
    for part in range(2):
        for across in range(2):
            for along in range(2):
                far_y, far_x = (along, across) if part == 0 else (across, along)
                row_y, row_x = place_ref[1] ^ far_y, place_ref[2] ^ far_x
                piece = pieces[part * 2 + across].at[along]
                for zed in range(Z_SIZE):
                    target = target_of(part, zed, row_y, row_x, piece)
                    copies.append(
                        pltpu.make_async_copy(piece.at[zed], target, sems.at[len(copies)])
                    )
                    copies[-1].start()
    return copies


def column_target(whole_ref):
    def target_of(part, zed, row_y, row_x, piece):
        _, depth, wide = piece.shape
        row = pl.multiple_of(((zed * 2 + row_y) * 2 + row_x) * depth, 16)
        left = 0 if part == 0 else whole_ref.shape[1] - wide
        return whole_ref.at[pl.ds(row, depth), pl.ds(left, wide)]

    return target_of


def assemble_columns_kernel(place_ref, *refs):
    *pieces, out_ref, sems = refs
    for copy in load_pieces(place_ref, pieces, column_target(out_ref), sems):
        copy.wait()


def place_vector():
    return jnp.stack(chip_place() + (lax.axis_index("seq"),)).astype(jnp.int32)


def assemble(kernel, shape, parts):
    return pl.pallas_call(
        kernel,
        grid_spec=pltpu.PrefetchScalarGridSpec(
            num_scalar_prefetch=1,
            grid=(1,),
            in_specs=[pl.BlockSpec(memory_space=pl.ANY)] * 4,
            out_specs=pl.BlockSpec(shape, lambda step, *_: (0,) * len(shape)),
            scratch_shapes=[pltpu.SemaphoreType.DMA((32,))],
        ),
        out_shape=jax.ShapeDtypeStruct(shape, parts[0][0].dtype),
        compiler_params=pltpu.CompilerParams(vmem_limit_bytes=40 * 1024 * 1024),
    )(place_vector(), *parts[0], *parts[1])


FFN_TILE = 256
FFN_CHUNK = 512
root_two_pi = 0.3989422804014327


def feed_forward_kernel(*refs):
    normed_ref, cot_ref, *refs = refs
    up_pieces, down_pieces, refs = refs[:4], refs[4:10], refs[10:]
    hidden_ref, grad_pre_ref, y_ref, grad_ref, normed_out, y_came, grad_came, *refs = refs
    up_ref, down_ref, normed_buf, y_away, grad_away, *refs = refs
    up_sems, down_sems, sent_sems, came_sems, normed_sems, away_sends, away_recvs, *refs = refs
    corner_sends, corner_recvs = refs
    step = pl.program_id(0)
    row, core = lax.axis_index("rows"), lax.axis_index("seq")
    here_y, here_x = (row // 2) % 2, row % 2
    twin = (row, 1 - core)
    over_x, over_y = row + 1 - 2 * here_x, row + 2 - 4 * here_y
    span = normed_ref.shape[0]
    tiles = span // FFN_TILE

    def remote(src, dst, send_sem, recv_sem):
        return pltpu.make_async_remote_copy(
            src_ref=src,
            dst_ref=dst,
            send_sem=send_sem,
            recv_sem=recv_sem,
            device_id=twin,
            device_id_type=pl.DeviceIdType.MESH,
        )

    def normed_copies():
        own, others = normed_buf.at[pl.ds(0, span), :], normed_buf.at[pl.ds(span, span), :]
        return (
            pltpu.make_async_copy(normed_ref, own, normed_sems.at[0]),
            remote(normed_ref, others, normed_sems.at[1], normed_sems.at[2]),
        )

    def up_copies():
        copies = []
        for part in range(2):
            for across in range(2):
                for along in range(2):
                    far_y, far_x = (along, across) if part == 0 else (across, along)
                    row_y = 1 - here_y if far_y else here_y
                    row_x = 1 - here_x if far_x else here_x
                    for zed in range(Z_SIZE):
                        piece = up_pieces[part * 2 + across].at[along, zed]
                        depth, wide = piece.shape
                        first = pl.multiple_of(((zed * 2 + row_y) * 2 + row_x) * depth, 16)
                        left = 0 if part == 0 else up_ref.shape[1] - wide
                        target = up_ref.at[pl.ds(first, depth), pl.ds(left, wide)]
                        copies.append(pltpu.make_async_copy(piece, target, up_sems.at[len(copies)]))
        return copies

    def down_rows(part, lower, row_y, row_x, depth):
        first = (((lower * 2 + row_y) * 2 + row_x) * 2 + part) * depth
        return pl.ds(pl.multiple_of(first, 16), depth)

    def down_copies():
        kept, given = [], []
        for part in range(2):
            for which, (far_y, far_x) in enumerate(
                ((0, 0), (1, 0), (0, 1)) if part == 0 else ((0, 0), (0, 1), (1, 0))
            ):
                row_y = 1 - here_y if far_y else here_y
                row_x = 1 - here_x if far_x else here_x
                for lower in range(2):
                    pieces = down_pieces[part * 3 + which]
                    depth, wide = pieces.shape[1:]
                    rows = down_rows(part, lower, row_y, row_x, depth)
                    target = down_ref.at[rows, pl.ds(pl.multiple_of(core * wide, 128), wide)]
                    number = len(kept)
                    kept.append(
                        pltpu.make_async_copy(
                            pieces.at[2 * core + lower], target, down_sems.at[number]
                        )
                    )
                    given.append(
                        remote(
                            pieces.at[2 * (1 - core) + lower],
                            target,
                            sent_sems.at[number],
                            came_sems.at[number],
                        )
                    )
        return kept, given

    def corner_copies():
        sends, arrivals = [], []
        for part in range(2):
            pieces = down_pieces[part * 3 + 1]
            depth, wide = pieces.shape[1:]
            row_y, row_x = (1 - here_y, here_x) if part == 0 else (here_y, 1 - here_x)
            for other in range(2):
                for lower in range(2):
                    number = len(sends)
                    rows = down_rows(part, lower, row_y, row_x, depth)
                    target = down_ref.at[rows, pl.ds(pl.multiple_of(core * wide, 128), wide)]
                    sends.append(
                        pltpu.make_async_remote_copy(
                            src_ref=pieces.at[2 * other + lower],
                            dst_ref=target,
                            send_sem=corner_sends.at[number],
                            recv_sem=corner_recvs.at[part, core, lower],
                            device_id=(over_x if part == 0 else over_y, other),
                            device_id_type=pl.DeviceIdType.MESH,
                        )
                    )
                    rows = down_rows(part, lower, 1 - here_y, 1 - here_x, depth)
                    target = down_ref.at[rows, pl.ds(other * wide, wide)]
                    arrivals.append(
                        pltpu.make_async_remote_copy(
                            src_ref=target,
                            dst_ref=target,
                            send_sem=corner_sends.at[number],
                            recv_sem=corner_recvs.at[part, other, lower],
                            device_id=(over_x if part == 0 else over_y, other),
                            device_id_type=pl.DeviceIdType.MESH,
                        )
                    )
        return sends, arrivals

    def away_copies(tile):
        rows = pl.ds(pl.multiple_of(tile * FFN_TILE, FFN_TILE), FFN_TILE)
        return [
            remote(buf.at[tile], out.at[rows, :], away_sends.at[which, tile], away_recvs.at[which, tile])
            for which, (buf, out) in enumerate(((y_away, y_came), (grad_away, grad_came)))
        ]

    @pl.when(step == 0)
    def _():
        barrier = pltpu.get_barrier_semaphore()
        for target in (twin, (over_x, 0), (over_x, 1), (over_y, 0), (over_y, 1)):
            pl.semaphore_signal(
                barrier, inc=1, device_id=target, device_id_type=pl.DeviceIdType.MESH
            )
        kept, given = down_copies()
        corners, arrivals = corner_copies()
        own, others = normed_copies()
        ups = up_copies()
        pl.semaphore_wait(barrier, 5)
        for copy in corners + [own] + ups + kept + given + [others]:
            copy.start()
        for copy in [own] + ups + kept:
            copy.wait()
        for copy in given + arrivals:
            copy.wait_recv()

    @pl.when(step == tiles)
    def _():
        normed_copies()[1].wait_recv()

    normed = normed_buf[pl.ds(pl.multiple_of(step * FFN_TILE, FFN_TILE), FFN_TILE), :]
    cot = cot_ref[...]
    y_sum = grad_sum = 0.0
    for chunk in range(hidden_ref.shape[1] // FFN_CHUNK):
        units = pl.ds(chunk * FFN_CHUNK, FFN_CHUNK)
        up, down = up_ref[:, units], down_ref[units, :]
        pre = jnp.dot(normed, up, preferred_element_type=jnp.float32)
        grad_hidden = lax.dot_general(cot, down, last_dims, preferred_element_type=jnp.float32)
        phi = 0.5 + 0.5 * lax.erf(pre * root_half)
        hidden = (pre * phi).astype(jnp.bfloat16)
        slope = phi + pre * (jnp.exp(-0.5 * pre * pre) * root_two_pi)
        grad_pre = (grad_hidden * slope).astype(jnp.bfloat16)
        hidden_ref[:, units] = hidden
        grad_pre_ref[:, units] = grad_pre
        y_sum += jnp.dot(hidden, down, preferred_element_type=jnp.float32)
        grad_sum += lax.dot_general(grad_pre, up, last_dims, preferred_element_type=jnp.float32)

    @pl.when(step < tiles)
    def _():
        y_ref[...] = y_sum.astype(jnp.bfloat16)
        grad_ref[...] = grad_sum.astype(jnp.bfloat16)

    for tile in range(tiles):

        @pl.when(step == tiles + tile)
        def _(tile=tile):
            y_away[tile] = y_sum.astype(jnp.bfloat16)
            grad_away[tile] = grad_sum.astype(jnp.bfloat16)
            for copy in away_copies(tile):
                copy.start()

    @pl.when(step == 2 * tiles - 1)
    def _():
        store = pltpu.make_async_copy(normed_buf, normed_out, normed_sems.at[0])
        store.start()
        for copy in (*down_copies()[1], *corner_copies()[0], normed_copies()[1]):
            copy.wait_send()
        for tile in range(tiles):
            for copy in away_copies(tile):
                copy.wait()
        store.wait()


def feed_forward(normed, cot_all, up_parts, down_parts):
    tokens, width = normed.shape
    units = up_parts[0][0].shape[3] + up_parts[1][0].shape[3]
    tiles = tokens // FFN_TILE
    tile = pl.BlockSpec((FFN_TILE, width), lambda step: (step, 0))
    own_tile = pl.BlockSpec((FFN_TILE, width), lambda step: (jnp.minimum(step, tiles - 1), 0))
    wide_tile = pl.BlockSpec((FFN_TILE, units), lambda step: (step, 0))
    anywhere = pl.BlockSpec(memory_space=pl.ANY)
    wide_shape = jax.ShapeDtypeStruct((2 * tokens, units), jnp.bfloat16)
    shape = jax.ShapeDtypeStruct((tokens, width), jnp.bfloat16)
    away = pltpu.VMEM((tiles, FFN_TILE, width), jnp.bfloat16)
    sems = pltpu.SemaphoreType.DMA
    return pl.pallas_call(
        feed_forward_kernel,
        grid=(2 * tiles,),
        in_specs=[anywhere, tile] + [anywhere] * 10,
        out_specs=[wide_tile, wide_tile, own_tile, own_tile] + [anywhere] * 3,
        out_shape=[
            wide_shape,
            wide_shape,
            shape,
            shape,
            jax.ShapeDtypeStruct((2 * tokens, width), jnp.bfloat16),
            shape,
            shape,
        ],
        scratch_shapes=[
            pltpu.VMEM((width, units), jnp.bfloat16),
            pltpu.VMEM((units, width), jnp.bfloat16),
            pltpu.VMEM((2 * tokens, width), jnp.bfloat16),
            away,
            away,
            sems((32,)),
            sems((16,)),
            sems((16,)),
            sems((16,)),
            sems((3,)),
            sems((2, tiles)),
            sems((2, tiles)),
            sems((8,)),
            sems((2, 2, 2)),
        ],
        compiler_params=pltpu.CompilerParams(
            collective_id=2, has_side_effects=True, vmem_limit_bytes=60 * 1024 * 1024
        ),
        cost_estimate=pl.CostEstimate(
            flops=16 * tokens * width * units,
            bytes_accessed=4 * width * units + 8 * tokens * (2 * width + units),
            transcendentals=4 * tokens * units,
        ),
    )(normed, cot_all, *up_parts[0], *up_parts[1], *down_parts)


RESIDUAL_TILE = 128


def residual_kernel(*refs):
    residual_ref, cot_ref, y_ref, y_came, grad_ref, grad_came, gain_ref, *refs = refs
    layer_ref, out_ref, gain_out, both_out, buf, local_sems, send_sems, recv_sems = refs
    step = pl.program_id(0)
    steps = buf.shape[0]
    row, core = lax.axis_index("rows"), lax.axis_index("seq")
    twin = (row, 1 - core)
    span = both_out.shape[1] // 2

    def copies(tile):
        each = span // RESIDUAL_TILE
        first = core * span + (tile % each) * RESIDUAL_TILE
        rows = pl.ds(pl.multiple_of(first, RESIDUAL_TILE), RESIDUAL_TILE)
        target = both_out.at[tile // each, rows, :]
        return (
            pltpu.make_async_copy(buf.at[tile], target, local_sems.at[tile]),
            pltpu.make_async_remote_copy(
                src_ref=buf.at[tile],
                dst_ref=target,
                send_sem=send_sems.at[tile],
                recv_sem=recv_sems.at[tile],
                device_id=twin,
                device_id_type=pl.DeviceIdType.MESH,
            ),
        )

    @pl.when(step == 0)
    def _():
        barrier = pltpu.get_barrier_semaphore()
        pl.semaphore_signal(barrier, inc=1, device_id=twin, device_id_type=pl.DeviceIdType.MESH)
        pl.semaphore_wait(barrier, 1)
        gain_out[...] = jnp.zeros_like(gain_out)

    residual = residual_ref[...]
    layer_ref[...] = plus(residual, y_ref[...], y_came[...])
    unit, scale = norm_stats(residual)
    grad = plus_wide(grad_ref[...], grad_came[...])
    grad_residual = cot_ref[...].astype(jnp.float32) + norm_back_rows(
        unit, scale, gain_ref[...], grad
    )
    out_ref[...] = grad_residual
    gain_out[0:1, :] += jnp.sum(grad * unit, 0, keepdims=True)
    for tile in range(steps):

        @pl.when(step == tile)
        def _(tile=tile):
            buf[tile] = grad_residual.astype(jnp.bfloat16)
            for copy in copies(tile):
                copy.start()

    @pl.when(step == steps - 1)
    def _():
        for tile in range(steps):
            for copy in copies(tile):
                copy.wait()


def residual_call(rows, residual, cot, y_own, y_came, grad_own, grad_came, gain):
    flat, width = residual.shape
    steps = flat // RESIDUAL_TILE
    tile = pl.BlockSpec((RESIDUAL_TILE, width), lambda step: (step, 0))
    sems = pltpu.SemaphoreType.DMA((steps,))
    return pl.pallas_call(
        residual_kernel,
        grid=(steps,),
        in_specs=[tile] * 6 + [pl.BlockSpec((1, width), lambda step: (0, 0))],
        out_specs=[
            tile,
            tile,
            pl.BlockSpec((8, width), lambda step: (0, 0)),
            pl.BlockSpec(memory_space=pl.ANY),
        ],
        out_shape=[
            jax.ShapeDtypeStruct((flat, width), jnp.bfloat16),
            jax.ShapeDtypeStruct((flat, width), jnp.float32),
            jax.ShapeDtypeStruct((8, width), jnp.float32),
            jax.ShapeDtypeStruct((rows, 2 * flat // rows, width), jnp.bfloat16),
        ],
        scratch_shapes=[
            pltpu.VMEM((steps, RESIDUAL_TILE, width), jnp.bfloat16),
            sems,
            sems,
            sems,
        ],
        compiler_params=pltpu.CompilerParams(
            collective_id=3, has_side_effects=True, vmem_limit_bytes=32 * 1024 * 1024
        ),
    )(residual, cot, y_own, y_came, grad_own, grad_came, gain.reshape(1, width))


def following(zed):
    return (2 * zed + 1) % 5


def preceding(zed):
    return (3 * zed + 2) % 5


NORM_TILE = 64


def head_kernel(
    tokens_ref,
    gain_ref,
    cot_ref,
    piece_ref,
    up_ref,
    normed_out,
    cot_out,
    weights_out,
    up_out,
    token_buf,
    normed_buf,
    local_sems,
    send_sems,
    recv_sems,
):
    row, core = lax.axis_index("rows"), lax.axis_index("seq")
    zed, here_y, here_x = row // 4, (row // 2) % 2, row % 2
    rest = row - 4 * zed
    over_x, over_y = row + 1 - 2 * here_x, row + 2 - 4 * here_y
    onward, backward = following(zed) * 4 + rest, preceding(zed) * 4 + rest
    places = [zed]
    for _ in range(3):
        places.append(preceding(places[-1]))
    depth, wide = piece_ref.shape
    half = wide // 2

    barrier = pltpu.get_barrier_semaphore()
    for target in ((onward, core), (backward, core), (over_x, core), (over_y, core), (row, 1 - core)):
        pl.semaphore_signal(
            barrier, inc=1, device_id=target, device_id_type=pl.DeviceIdType.MESH
        )
    load = pltpu.make_async_copy(tokens_ref, token_buf, local_sems.at[0])
    load.start()
    own_rows = pl.ds(pl.multiple_of(row * depth, 16), depth)
    keeps = [
        pltpu.make_async_copy(piece_ref, weights_out.at[own_rows, :], local_sems.at[1]),
        pltpu.make_async_copy(up_ref, up_out.at[zed], local_sems.at[2]),
    ]
    for keep in keeps:
        keep.start()
    pl.semaphore_wait(barrier, 5)

    sent = []

    def send(src, dst, target):
        number = len(sent)
        copy = pltpu.make_async_remote_copy(
            src_ref=src,
            dst_ref=dst,
            send_sem=send_sems.at[number],
            recv_sem=recv_sems.at[number],
            device_id=target,
            device_id_type=pl.DeviceIdType.MESH,
        )
        copy.start()
        sent.append(copy)
        return copy

    def block(place, far_y, far_x, columns):
        at_y = 1 - here_y if far_y else here_y
        at_x = 1 - here_x if far_x else here_x
        index = (place * 2 + at_y) * 2 + at_x
        rows = pl.ds(pl.multiple_of(index * depth, 16), depth)
        return weights_out.at[rows, columns]

    everything, left, right = pl.ds(0, wide), pl.ds(0, half), pl.ds(half, half)

    def source(step, columns):
        if step == 0:
            return piece_ref.at[:, columns]
        return block(places[step], False, False, columns)

    def around(step):
        return send(
            source(step, everything), block(places[step], False, False, everything), (onward, core)
        )

    def around_up(step):
        src = up_ref if step == 0 else up_out.at[places[step]]
        return send(src, up_out.at[places[step]], (onward, core))

    def across(step):
        place = places[step]
        return (
            send(source(step, left), block(place, False, False, left), (over_y, core)),
            send(source(step, right), block(place, False, False, right), (over_x, core)),
            send(source(step, left), block(place, False, False, left), (over_x, core)),
            send(source(step, right), block(place, False, False, right), (over_y, core)),
        )

    def corner(step, crossing):
        place = places[step]
        crossing[0].wait_recv()
        far_left = block(place, True, False, left)
        first = send(far_left, far_left, (over_x, core))
        crossing[1].wait_recv()
        far_right = block(place, False, True, right)
        return first, send(far_right, far_right, (over_y, core))

    ring = around(0)
    crossing = across(0)
    arrivals = [crossing[2], crossing[3]]
    arrivals.append(send(cot_ref, cot_out, (row, 1 - core)))

    load.wait()
    span = token_buf.shape[1]
    for member in range(token_buf.shape[0]):

        def norm_tile(tile, carry, member=member):
            rows = pl.ds(pl.multiple_of(tile * NORM_TILE, NORM_TILE), NORM_TILE)
            unit, _ = norm_stats(token_buf[member, rows, :].astype(jnp.float32))
            normed_buf[member, rows, :] = (unit * gain_ref[...]).astype(jnp.bfloat16)
            return carry

        lax.fori_loop(0, span // NORM_TILE, norm_tile, 0)
    mine = normed_out.at[:, pl.ds(pl.multiple_of(core * span, 16), span), :]
    keeps.append(pltpu.make_async_copy(normed_buf, mine, local_sems.at[3]))
    keeps[-1].start()
    arrivals.append(send(normed_buf, mine, (row, 1 - core)))

    up_ring = None
    for step in range(1, 4):
        ring.wait_recv()
        if step < 3:
            ring = around(step)
        if step == 2:
            up_ring = around_up(0)
        arrivals += corner(step - 1, crossing)
        crossing = across(step)
        arrivals += crossing[2:]
        if step == 3:
            up_ring.wait_recv()
            up_ring = around_up(1)
    arrivals += corner(3, crossing)
    up_ring.wait_recv()
    arrivals.append(around_up(2))
    for copy in arrivals:
        copy.wait_recv()
    for copy in sent:
        copy.wait_send()
    for keep in keeps:
        keep.wait()


def head_call(tokens, gain, cotangent, piece, w_up):
    rows, span, width = tokens.shape
    depth, wide = piece.shape
    anywhere = pl.BlockSpec(memory_space=pl.ANY)
    return pl.pallas_call(
        head_kernel,
        in_specs=[anywhere, pl.BlockSpec(memory_space=pltpu.VMEM)] + [anywhere] * 3,
        out_specs=[anywhere] * 4,
        out_shape=[
            jax.ShapeDtypeStruct((rows, 2 * span, width), jnp.bfloat16),
            jax.ShapeDtypeStruct(cotangent.shape, jnp.bfloat16),
            jax.ShapeDtypeStruct((16 * depth, wide), jnp.bfloat16),
            jax.ShapeDtypeStruct((Z_SIZE,) + w_up.shape, jnp.bfloat16),
        ],
        scratch_shapes=[
            pltpu.VMEM(tokens.shape, jnp.bfloat16),
            pltpu.VMEM(tokens.shape, jnp.bfloat16),
            pltpu.SemaphoreType.DMA((4,)),
            pltpu.SemaphoreType.DMA((32,)),
            pltpu.SemaphoreType.DMA((32,)),
        ],
        compiler_params=pltpu.CompilerParams(
            collective_id=0, has_side_effects=True, vmem_limit_bytes=32 * 1024 * 1024
        ),
    )(tokens, gain.reshape(1, width), cotangent, piece, w_up)


def plus_wide(*terms):
    return sum(term.astype(jnp.float32) for term in terms)


def plus(*terms):
    return plus_wide(*terms).astype(jnp.bfloat16)


TAIL_TILE = 256


def tail_kernel(
    dq_ref,
    dk_ref,
    dv_ref,
    weights_ref,
    query_ref,
    key_ref,
    value_ref,
    tokens_ref,
    residual_ref,
    gain_ref,
    ffn_gain_ref,
    hidden_ref,
    token_out,
    query_out,
    key_out,
    value_out,
    gain_out,
    up_out,
    out_out,
    weight_buf,
    dq_buf,
    dk_buf,
    dv_buf,
    own_buf,
    away_buf,
    came_buf,
    token_buf,
    residual_buf,
    far_buf,
    near_buf,
    turned_buf,
    turned_came,
    sum_buf,
    ring_buf,
    ring_came,
    gain_buf,
    gain_came,
    hidden_buf,
    hidden_came,
    local_sems,
    send_sems,
    recv_sems,
):
    row, core = lax.axis_index("rows"), lax.axis_index("seq")
    zed, here_y, here_x = row // 4, (row // 2) % 2, row % 2
    rest = row - 4 * zed
    over_x, over_y = row + 1 - 2 * here_x, row + 2 - 4 * here_y
    onward, backward = following(zed) * 4 + rest, preceding(zed) * 4 + rest
    beside = (zed + 1 - 2 * (zed % 2)) * 4 + rest
    beyond = (zed + 2 - 4 * (zed // 2)) * 4 + rest
    places = [zed]
    for _ in range(3):
        places.append(preceding(places[-1]))
    depth = query_out.shape[0]
    half_wide = query_ref.shape[1]
    span = own_buf.shape[0] // 2

    barrier = pltpu.get_barrier_semaphore()
    for target in ((onward, core), (backward, core), (over_x, core), (over_y, core), (row, 1 - core)):
        pl.semaphore_signal(
            barrier, inc=1, device_id=target, device_id_type=pl.DeviceIdType.MESH
        )
    loads = [
        pltpu.make_async_copy(
            weights_ref.at[:, pl.ds(0, 3 * half_wide)], weight_buf, local_sems.at[0]
        )
    ]
    for index, (source, target) in enumerate(
        (
            (dq_ref, dq_buf),
            (dk_ref, dk_buf),
            (dv_ref, dv_buf),
            (tokens_ref, token_buf),
            (residual_ref, residual_buf),
        )
    ):
        loads.append(pltpu.make_async_copy(source, target, local_sems.at[1 + index]))
    for load in loads:
        load.start()
    pl.semaphore_wait(barrier, 5)

    sent = []

    def send(src, dst, target):
        number = len(sent)
        copy = pltpu.make_async_remote_copy(
            src_ref=src,
            dst_ref=dst,
            send_sem=send_sems.at[number],
            recv_sem=recv_sems.at[number],
            device_id=target,
            device_id_type=pl.DeviceIdType.MESH,
        )
        copy.start()
        sent.append(copy)
        return copy

    cut = (half_wide // 128 + 1) // 2 * 128
    streams = (
        (query_ref, 0, half_wide, 0, False),
        (key_ref, 0, cut, half_wide, False),
        (key_ref, cut, half_wide - cut, half_wide, True),
        (value_ref, 0, half_wide, 2 * half_wide, True),
    )

    def block_of(step, far_y, far_x):
        at_y = 1 - here_y if far_y else here_y
        at_x = 1 - here_x if far_x else here_x
        index = (places[step] * 2 + at_y) * 2 + at_x
        return pl.ds(pl.multiple_of(index * depth, 16), depth)

    far, near, turned = {}, {}, {}

    def issue(step):
        for which, (grad, column, wide, base, flip) in enumerate(streams):
            columns, place = pl.ds(column, wide), pl.ds(base + column, wide)
            target = (over_y if flip else over_x, core)
            far[step, which] = send(
                grad.at[block_of(step, True, True), columns], far_buf.at[step, :, place], target
            )
        for which, (grad, column, wide, base, flip) in enumerate(streams):
            columns, place = pl.ds(column, wide), pl.ds(base + column, wide)
            target = (over_y if flip else over_x, core)
            near[step, which] = send(
                grad.at[block_of(step, flip, not flip), columns],
                near_buf.at[step, :, place],
                target,
            )

    def turn(step):
        for which, (grad, column, wide, base, flip) in enumerate(streams):
            columns, place = pl.ds(column, wide), pl.ds(base + column, wide)
            far[step, which].wait_recv()
            turned_buf[step, :, place] = plus(
                grad[block_of(step, not flip, flip), columns], far_buf[step, :, place]
            )
            target = (over_x if flip else over_y, core)
            turned[step, which] = send(
                turned_buf.at[step, :, place], turned_came.at[step, :, place], target
            )

    def total(step):
        for which, (grad, column, wide, base, _) in enumerate(streams):
            columns, place = pl.ds(column, wide), pl.ds(base + column, wide)
            near[step, which].wait_recv()
            turned[step, which].wait_recv()
            sum_buf[step, :, place] = plus_wide(
                grad[block_of(step, False, False), columns],
                near_buf[step, :, place],
                turned_came[step, :, place],
            )

    ring = []

    def around(step):
        value = sum_buf[step]
        if step > 1:
            ring[-1].wait_recv()
            value = value + ring_came[step - 2].astype(jnp.float32)
        ring_buf[step - 1] = value.astype(jnp.bfloat16)
        ring.append(send(ring_buf.at[step - 1], ring_came.at[step - 1], (onward, core)))

    hidden_ring = []

    def around_hidden(step):
        value = hidden_ref[places[step]].astype(jnp.float32)
        if step > 1:
            hidden_ring[-1].wait_recv()
            value = value + hidden_came[step - 2].astype(jnp.float32)
        hidden_buf[step - 1] = value.astype(jnp.bfloat16)
        hidden_ring.append(
            send(hidden_buf.at[step - 1], hidden_came.at[step - 1], (onward, core))
        )

    def normed_tile(tile, half):
        first = (tile // 2) * 2 * span + half * span + (tile % 2) * TAIL_TILE
        rows = pl.ds(pl.multiple_of(first, TAIL_TILE), TAIL_TILE)
        part = 0.0
        for index, grad in enumerate((dq_buf, dk_buf, dv_buf)):
            part += lax.dot_general(
                grad[rows, :],
                weight_buf[:, pl.ds(index * half_wide, half_wide)],
                (((1,), (1,)), ((), ())),
                preferred_element_type=jnp.float32,
            )
        return pl.ds(pl.multiple_of(tile * TAIL_TILE, TAIL_TILE), TAIL_TILE), part

    def away_tile(tile, carry):
        rows, part = normed_tile(tile, 1 - core)
        away_buf[rows, :] = part.astype(jnp.bfloat16)
        return carry

    def own_tile(tile, carry):
        rows, part = normed_tile(tile, core)
        own_buf[rows, :] = part
        return carry

    def norm_tile(tile, carry):
        rows = pl.ds(pl.multiple_of(tile * NORM_TILE, NORM_TILE), NORM_TILE)
        grad = own_buf[rows, :] + came_buf[rows, :].astype(jnp.float32)
        unit, scale = norm_stats(token_buf[rows, :].astype(jnp.float32))
        residual_buf[rows, :] += norm_back_rows(unit, scale, gain_ref[...], grad)
        return carry + jnp.sum(grad * unit, 0, keepdims=True)

    tiles = own_buf.shape[0] // TAIL_TILE
    norm_tiles = own_buf.shape[0] // NORM_TILE
    middle, quarter = tiles // 2, norm_tiles // 4
    issue(1)
    around_hidden(1)
    issue(2)
    for load in loads[:4]:
        load.wait()
    lax.fori_loop(0, middle, away_tile, 0)
    turn(1)
    issue(3)
    lax.fori_loop(middle, tiles, away_tile, 0)
    away = send(away_buf, came_buf, (row, 1 - core))
    around_hidden(2)
    lax.fori_loop(0, middle, own_tile, 0)
    turn(2)
    total(1)
    around(1)
    issue(0)
    lax.fori_loop(middle, tiles, own_tile, 0)
    for load in loads[4:]:
        load.wait()
    away.wait_recv()
    gain_part = jnp.zeros((1, own_buf.shape[1]), jnp.float32)
    gain_part = lax.fori_loop(0, quarter, norm_tile, gain_part)
    turn(3)
    around_hidden(3)
    gain_part = lax.fori_loop(quarter, 2 * quarter, norm_tile, gain_part)
    total(2)
    around(2)
    gain_part = lax.fori_loop(2 * quarter, 3 * quarter, norm_tile, gain_part)
    turn(0)
    gain_part = lax.fori_loop(3 * quarter, norm_tiles, norm_tile, gain_part)
    store = pltpu.make_async_copy(residual_buf, token_out, local_sems.at[6])
    store.start()
    gain_buf[0] = jnp.zeros_like(gain_buf[0])
    gain_buf[0, 0:1] = gain_part
    gain_buf[0, 1:2] = ffn_gain_ref[...]

    def exchange(number, target):
        copy = send(gain_buf.at[number], gain_came.at[number], target)
        copy.wait_recv()
        gain_buf[number + 1] = gain_buf[number] + gain_came[number]

    exchange(0, (row, 1 - core))
    exchange(1, (over_x, core))
    total(3)
    around(3)
    exchange(2, (over_y, core))
    exchange(3, (beside, core))
    exchange(4, (beyond, core))
    gain_out[...] = gain_buf[5]
    hidden_ring[-1].wait_recv()
    up_wide = up_out.shape[1]
    for out, columns in ((up_out, pl.ds(0, up_wide)), (out_out, pl.ds(up_wide, half_wide))):
        out[...] = plus_wide(hidden_ref[zed, :, columns], hidden_came[2, :, columns])
    total(0)
    ring[-1].wait_recv()
    for index, out in enumerate((query_out, key_out, value_out)):
        columns = pl.ds(index * half_wide, half_wide)
        out[...] = sum_buf[0, :, columns] + ring_came[2, :, columns].astype(jnp.float32)
    for copy in sent:
        copy.wait_send()
    store.wait()


def tail_call(grads, weights, sums, tokens, grad_residual, gain, ffn_gain, hidden_sums):
    flat, width = grad_residual.shape
    half_wide = sums[0].shape[1]
    depth = sums[0].shape[0] // 16
    anywhere, here = pl.BlockSpec(memory_space=pl.ANY), pl.BlockSpec(memory_space=pltpu.VMEM)
    block = pltpu.VMEM((4, depth, 3 * half_wide), jnp.bfloat16)
    moving = pltpu.VMEM((3, depth, 3 * half_wide), jnp.bfloat16)
    gains = pltpu.VMEM((6, 8, width), jnp.float32)
    sum_shape = jax.ShapeDtypeStruct((depth, half_wide), jnp.float32)
    return pl.pallas_call(
        tail_kernel,
        in_specs=[anywhere] * 4 + [here] * 3 + [anywhere] * 2 + [here] * 3,
        out_specs=[anywhere] + [here] * 6,
        out_shape=[
            jax.ShapeDtypeStruct((flat, width), jnp.float32),
            sum_shape,
            sum_shape,
            sum_shape,
            jax.ShapeDtypeStruct((8, width), jnp.float32),
            jax.ShapeDtypeStruct((depth, hidden_sums.shape[2] - half_wide), jnp.float32),
            sum_shape,
        ],
        scratch_shapes=[pltpu.VMEM((width, 3 * half_wide), jnp.bfloat16)]
        + [pltpu.VMEM((2 * flat, half_wide), jnp.bfloat16)] * 3
        + [
            pltpu.VMEM((flat, width), jnp.float32),
            pltpu.VMEM((flat, width), jnp.bfloat16),
            pltpu.VMEM((flat, width), jnp.bfloat16),
            pltpu.VMEM((flat, width), jnp.bfloat16),
            pltpu.VMEM((flat, width), jnp.float32),
        ]
        + [block] * 4
        + [pltpu.VMEM((4, depth, 3 * half_wide), jnp.float32), moving, moving, gains, gains]
        + [pltpu.VMEM((3,) + hidden_sums.shape[1:], jnp.bfloat16)] * 2
        + [
            pltpu.SemaphoreType.DMA((7,)),
            pltpu.SemaphoreType.DMA((64,)),
            pltpu.SemaphoreType.DMA((64,)),
        ],
        compiler_params=pltpu.CompilerParams(
            collective_id=1, has_side_effects=True, vmem_limit_bytes=60 * 1024 * 1024
        ),
    )(
        *grads,
        weights,
        *sums,
        tokens,
        grad_residual,
        gain.reshape(1, width),
        ffn_gain.reshape(1, width),
        hidden_sums,
    )


def halves_z(stack):
    _, depth, wide = stack.shape
    if depth > 80:
        return stack[:, : depth // 2], stack[:, depth // 2 :]
    cut = (wide // 128 + 1) // 2 * 128
    return stack[:, :, :cut], stack[:, :, cut:]


def gather_first(first, second):
    return jnp.stack([first, swap_y(first)]), jnp.stack([second, swap_x(second)])


def gather_second(first, second):
    return (first, swap_x(first)), (second, swap_y(second))


def dot_low(left_side, right_side):
    return jnp.dot(left_side, right_side, preferred_element_type=jnp.float32)


def outer_low(left_side, right_side):
    return jnp.einsum(
        "tc,te->ce", left_side, right_side, preferred_element_type=jnp.float32
    ).astype(jnp.bfloat16)


class Scatter:

    def __init__(self, first, second, by_rows=False):
        self.parts, self.by_rows = (first, second), by_rows

    def pick(self, which, start_y, start_x, count_y=1, count_x=1):
        picked = []
        for whole, row, depth, column, wide in self.parts[which]:
            planes = Z_SIZE // len(self.parts[which]) if self.by_rows else Z_SIZE
            blocks = whole.reshape(planes, 2, 2, whole.shape[0] // planes // 4, whole.shape[1])
            picked.append(
                lax.dynamic_slice(
                    blocks,
                    (0, start_y, start_x, row, column),
                    (planes, count_y, count_x, depth, wide),
                ).reshape(planes, count_y * count_x, depth, wide)
            )
        axis = 0 if self.by_rows else 3
        return picked[0] if len(picked) == 1 else jnp.concatenate(picked, axis)

    def prepare(self, *after):
        _, here_y, here_x = chip_place()
        here_x, here_y = tie((here_x, here_y), *after)
        self.away = (self.pick(0, 0, 1 - here_x, 2, 1), self.pick(1, 1 - here_y, 0, 1, 2))

    def spread(self):
        self.came = (swap_x(self.away[0]), swap_y(self.away[1]))

    def of_came(self, which, far):
        _, here_y, here_x = chip_place()
        here = here_x if which else here_y
        return lax.dynamic_slice_in_dim(self.came[which], here ^ far, 1, 1)

    def turn(self):
        _, here_y, here_x = chip_place()
        first = plus(self.pick(0, 1 - here_y, here_x), self.of_came(0, 1))
        second = plus(self.pick(1, here_y, 1 - here_x), self.of_came(1, 1))
        self.turning = (first, second)
        self.turned = (swap_y(first), swap_x(second))

    def near_sums(self):
        _, here_y, here_x = chip_place()
        first, second = (
            plus(
                self.pick(which, here_y, here_x), self.of_came(which, 0), self.turned[which]
            ).reshape((Z_SIZE,) + self.turned[which].shape[2:])
            for which in range(2)
        )
        return jnp.concatenate([first, second], 1 if self.by_rows else 2)

    def gather(self):
        self.sums = self.near_sums()
        self.moving = next_z(self.block(1))

    def block(self, back):
        target = (ring_place() - back) % Z_SIZE
        zed = jnp.where(target == 2, 3, jnp.where(target == 3, 2, target))
        if self.by_rows:
            zed = zed ^ (2 * lax.axis_index("seq"))
        return lax.dynamic_index_in_dim(self.sums, zed, 0, keepdims=False)

    def step(self, number):
        self.moving = next_z(plus(self.block(number), self.moving))

    def finish(self):
        return self.block(0).astype(jnp.float32) + self.moving.astype(jnp.float32)

    def hold(self, names, *after):
        for name in names:
            setattr(self, name, tie(getattr(self, name), *after))


def body_pair(
    tokens, segments, gain_attn, w_query, w_key, w_value, w_out, gain_ffn, w_up, w_down, cotangent
):
    core = lax.axis_index("seq")
    rows, span, width = tokens.shape
    flat = rows * span

    def split(flat_rows, axis_width):
        return flat_rows.reshape(rows, 2 * span, axis_width)

    def sharing(values):
        wide = split(values, values.shape[-1])
        return swap_cores(own_half(wide, 1, 1 - core).astype(jnp.bfloat16))

    def shared(values, received):
        wide = split(values, values.shape[-1])
        return (own_half(wide, 1, core) + received.astype(jnp.float32)).reshape(flat, -1)

    attn_piece = jnp.concatenate([w_query, w_key, w_value, w_out], 1)
    half_wide = w_query.shape[1]
    normed, cot_other, attn_weights, up_stack = head_call(
        tokens, gain_attn, cotangent, attn_piece, w_up
    )
    first = core == 0
    tokens_own = tokens.reshape(flat, width).astype(jnp.float32)
    cot_own = cotangent.reshape(flat, width)
    windows = windows_of(segments, QUERY_TILE)
    back_windows = windows_of(segments, BACK_TILE)
    marks = (
        jnp.broadcast_to(segments[:, :, None], segments.shape + (LANES,)),
        jnp.broadcast_to(segments[:, None, :], (rows, 8, 2 * span)),
    )
    normed = normed.reshape(2 * flat, width)
    w_qkv = attn_weights[:, : 3 * half_wide]
    w_q, w_k, w_v = (w_qkv[:, i * half_wide : (i + 1) * half_wide] for i in range(3))

    up_parts = gather_first(*halves_z(up_stack))
    down_steps = [tie(w_down, up_stack)]
    down_steps.append(next_z(down_steps[-1]))
    w_o_half = attn_weights[:, 3 * half_wide :]
    w_o_other = swap_cores(w_o_half)
    qk_rows = dot_low(normed, w_qkv[:, : 2 * half_wide]).astype(jnp.bfloat16)
    normed, w_o_other, down_steps[1], up_parts = tie(
        (normed, w_o_other, down_steps[1], up_parts), qk_rows
    )
    down_steps.append(next_z(down_steps[-1]))
    up_near = up_parts
    up_parts = gather_second(*up_parts)
    normed = tie(normed, up_near)
    value_rows = dot_low(normed, w_qkv[:, 2 * half_wide :]).astype(jnp.bfloat16)
    value_rows, down_steps[2] = tie((value_rows, down_steps[2]))
    down_steps.append(next_z(down_steps[-1]))
    qk_rows, value_rows = split(qk_rows, 2 * half_wide), split(value_rows, half_wide)
    qk_rows = tie(qk_rows, up_near)
    operands = [(qk_rows, 0), (qk_rows, 1), (value_rows, 0)]
    (mixed,) = attention_call(
        attend_kernel, 0, rows, windows, marks, operands, [half_wide], [], half_wide
    )
    mixed, down_steps[3], up_parts = tie((mixed, down_steps[3], up_parts))
    down_first, down_second = halves_z(natural_z(down_steps))
    down_came = swap_y(down_first), swap_x(down_second), swap_x(down_first), swap_y(down_second)
    w_o_other = tie(w_o_other, down_first, down_second)
    w_o = jnp.where(
        first,
        jnp.concatenate([w_o_half, w_o_other], 1),
        jnp.concatenate([w_o_other, w_o_half], 1),
    )
    w_o_rows = own_half(w_o, 0, core)

    mixed_other = swap_cores(own_half(mixed, 1, 1 - core))
    mixed_mine = own_half(mixed, 1, core)
    mixed_own = jnp.where(
        first,
        jnp.concatenate([mixed_mine, mixed_other], 2),
        jnp.concatenate([mixed_other, mixed_mine], 2),
    ).reshape(flat, width)
    mixed_own, w_o, w_o_rows = tie((mixed_own, w_o, w_o_rows))
    residual = tokens_own + dot_low(mixed_own, w_o)
    unit_two, _ = norm_stats(residual)
    normed_two = (unit_two * gain_ffn).astype(jnp.bfloat16)
    cot_other = tie(cot_other, mixed_own)
    cot_all = jnp.concatenate([cot_own, cot_other.reshape(flat, width)], 0)
    normed_two, cot_all, down_came = tie((normed_two, cot_all, down_came))
    first_y, second_x, first_x, second_y = down_came
    down_parts = (down_first, first_y, first_x, down_second, second_x, second_y)
    hidden_low, grad_pre, y_own, grad_two_own, normed_two_all, y_came, grad_two_came = feed_forward(
        normed_two, cot_all, up_parts, down_parts
    )

    down_half = outer_low(hidden_low, cot_all)
    down_away = swap_cores(own_half(down_half, 1, 1 - core))
    layer_out, grad_residual, ffn_gain_rows, grad_attn_all = residual_call(
        rows, residual, cot_own, y_own, y_came, grad_two_own, tie(grad_two_came, down_half), gain_ffn
    )
    ffn_gain_part = ffn_gain_rows[0]
    grad_attn_all = grad_attn_all.reshape(2 * flat, width)
    down_away = tie(down_away, grad_residual)
    depth, wide = w_down.shape
    down_halves = ((down_half, core * wide), (down_away, 0))
    down_sum = Scatter(
        *(
            [(whole, row, depth // 2, column, wide) for whole, column in down_halves]
            for row in (0, depth // 2)
        ),
        True,
    )
    down_sum.prepare()
    down_sum.spread()
    up_whole = outer_low(normed_two_all, tie(grad_pre, *down_sum.away))
    grad_attn_all = tie(grad_attn_all, up_whole)
    out_half = outer_low(mixed.reshape(2 * flat, -1), grad_attn_all)
    out_away = swap_cores(own_half(out_half, 1, 1 - core))
    grad_mixed = split(times_transposed(grad_attn_all, w_o_rows).astype(jnp.bfloat16), width // 2)
    out_away = tie(out_away, grad_mixed)
    out_kept = own_half(out_half, 1, core)
    out_whole = jnp.where(
        first,
        jnp.concatenate([out_kept, out_away], 0),
        jnp.concatenate([out_away, out_kept], 0),
    )
    depth, wide = w_up.shape
    cut = (wide + half_wide) // 256 * 128
    up_sum = Scatter(
        [(up_whole, 0, depth, 0, cut)],
        [(up_whole, 0, depth, cut, wide - cut), (out_whole, 0, depth, 0, half_wide)],
    )
    down_sum.hold(("came",), grad_mixed)
    down_sum.turn()
    up_sum.prepare(*down_sum.turning)
    up_sum.spread()
    grad_mixed = tie(grad_mixed, *up_sum.away, *down_sum.turning)
    scratch = [pltpu.VMEM((2 * span, LANES), jnp.float32)] * 2

    def attend_back(row, grad_rows, begun=()):
        return attention_call(
            attend_back_kernel,
            row,
            1,
            back_windows,
            marks,
            operands + [(grad_rows, 0)],
            [half_wide] * 3,
            scratch,
            LANES,
            begun,
        )

    grads = attend_back(0, grad_mixed)
    down_sum.hold(("turned",), *grads)
    down_sum.gather()
    grads = tie(grads, down_sum.sums)
    for row in range(1, rows):
        grads = attend_back(row, grad_mixed, grads)
    down_sum.hold(("moving",), *grads)
    up_sum.hold(("came",), *grads)
    grads = tie(grads, down_sum.moving, up_sum.came)
    up_sum.turn()
    down_sum.step(2)
    grads = tie(grads, *up_sum.turning)
    grad_queries, grad_keys, grad_values = (grad.reshape(2 * flat, half_wide) for grad in grads)
    query_whole = outer_low(normed, grad_queries)
    key_whole = outer_low(normed, grad_keys)
    down_sum.hold(("moving",), query_whole, key_whole)
    grad_values = tie(grad_values, down_sum.moving)
    down_sum.step(3)
    value_whole = outer_low(normed, grad_values)
    up_sum.hold(("turned",), value_whole)
    sums = tie((query_whole, key_whole, value_whole), down_sum.moving)
    token_grad, query_grad, key_grad, value_grad, gains, up_grad, out_grad = tail_call(
        (grad_queries, grad_keys, grad_values),
        attn_weights,
        sums,
        tokens.reshape(flat, width),
        grad_residual,
        gain_attn,
        ffn_gain_part,
        up_sum.near_sums(),
    )
    gain_attn_grad, gain_ffn_grad = gains[0], gains[1]
    down_grad = down_sum.finish()
    return (
        layer_out.reshape(rows, span, width),
        token_grad.reshape(rows, span, width),
        gain_attn_grad,
        query_grad,
        key_grad,
        value_grad,
        out_grad,
        gain_ffn_grad,
        up_grad,
        down_grad,
    )


def solution(mesh):
    paired = mesh.shape["seq"] == 2 and mesh.shape["rows"] == 16
    program = body_pair if paired else body
    return jax.shard_map(
        program,
        mesh=mesh,
        in_specs=(
            P("rows", "seq", None),
            P("rows", None),
            P(),
            P("rows", "seq"),
            P("rows", "seq"),
            P("rows", "seq"),
            P("rows", "seq"),
            P(),
            P("rows", "seq"),
            P("rows", "seq"),
            P("rows", "seq", None),
        ),
        out_specs=(
            P("rows", "seq", None),
            P("rows", "seq", None),
            P(),
            P("rows", "seq"),
            P("rows", "seq"),
            P("rows", "seq"),
            P("rows", "seq"),
            P(),
            P("rows", "seq"),
            P("rows", "seq"),
        ),
        check_vma=False,
    )
```

```python
import functools

import jax
import jax.numpy as jnp
from jax import lax
from jax.experimental import pallas as pl
from jax.experimental.pallas import tpu as pltpu
from jax.sharding import PartitionSpec as P

HEADS = 20
HEAD_DIM = 64


epsilon = 1e-05
root_half = 0.7071067811865476


def norm_rows(values, gain_vec):
    row_mean = jnp.mean(values, -1, keepdims=True)
    centred = values - row_mean
    spread = jnp.mean(centred * centred, -1, keepdims=True)
    return centred * lax.rsqrt(spread + epsilon) * gain_vec


def gelu_exact(values):
    return 0.5 * values * (1.0 + lax.erf(values * root_half))


def times_transposed(left_side, right_side):
    return jnp.einsum("te,de->td", left_side, right_side, preferred_element_type=jnp.float32)


def split_heads(rows_in):
    return rows_in.reshape(rows_in.shape[0], rows_in.shape[1], HEADS, HEAD_DIM)


def join_heads(heads_in):
    return heads_in.reshape(heads_in.shape[0], heads_in.shape[1], HEADS * HEAD_DIM)


def masked_scores(query_heads, key_heads, seg_query, seg_key):
    scores = jnp.einsum(
        "rqhd,rkhd->rhqk", query_heads, key_heads, preferred_element_type=jnp.float32
    )
    scores = scores * HEAD_DIM ** (-0.5)
    allowed = (seg_query[:, :, None] == seg_key[:, None, :])[:, None]
    return (allowed, jnp.where(allowed, scores, -1e30))


def attention_forward(query_rows, key_rows, value_rows, seg_query, seg_key):
    allowed, scores = masked_scores(
        split_heads(query_rows), split_heads(key_rows), seg_query, seg_key
    )
    row_top = jnp.max(scores, -1, keepdims=True)
    exponent = jnp.exp(scores - row_top)
    row_total = jnp.sum(exponent, -1, keepdims=True)
    prob_low = (exponent / row_total).astype(jnp.bfloat16)
    mixed_out = jnp.einsum(
        "rhqk,rkhd->rqhd", prob_low, split_heads(value_rows), preferred_element_type=jnp.float32
    )
    return (join_heads(mixed_out).astype(jnp.bfloat16), row_top + jnp.log(row_total))


def grad_pieces(query_heads, key_heads, value_heads, seg_query, seg_key, log_total, grad_heads):
    allowed, scores = masked_scores(query_heads, key_heads, seg_query, seg_key)
    prob_rows = jnp.where(allowed, jnp.exp(scores - log_total), 0.0)
    grad_probs = jnp.einsum(
        "rqhd,rkhd->rhqk", grad_heads, value_heads, preferred_element_type=jnp.float32
    )
    return (prob_rows, grad_probs)


def attention_grads(query_rows, key_rows, value_rows, seg_query, seg_key, log_total, grad_mixed):
    query_heads = split_heads(query_rows)
    key_heads = split_heads(key_rows)
    grad_heads = split_heads(grad_mixed)
    prob_rows, grad_probs = grad_pieces(
        query_heads, key_heads, split_heads(value_rows), seg_query, seg_key, log_total, grad_heads
    )
    value_part = jnp.einsum(
        "rhqk,rqhd->rkhd",
        prob_rows.astype(jnp.bfloat16),
        grad_heads,
        preferred_element_type=jnp.float32,
    )
    row_inner = jnp.sum(grad_probs * prob_rows, -1, keepdims=True)
    score_grad = (prob_rows * (grad_probs - row_inner)).astype(jnp.bfloat16)
    score_scale = HEAD_DIM ** (-0.5)
    query_part = (
        jnp.einsum("rhqk,rkhd->rqhd", score_grad, key_heads, preferred_element_type=jnp.float32)
        * score_scale
    )
    key_part = (
        jnp.einsum("rhqk,rqhd->rkhd", score_grad, query_heads, preferred_element_type=jnp.float32)
        * score_scale
    )
    return (join_heads(query_part), join_heads(key_part), join_heads(value_part))


def process(token_rows, cot_rows, seg_rows, gain_attn, gain_ffn, weights):
    w_query, w_key, w_value, w_out, w_up, w_down = weights
    row_count, query_count, model_width = token_rows.shape
    offset = lax.axis_index("seq") * query_count
    seg_query = lax.dynamic_slice_in_dim(seg_rows, offset, query_count, 1)

    def shaped(flat_rows):
        return flat_rows.reshape(row_count, query_count, model_width)

    flat_tokens = token_rows.reshape(row_count * query_count, model_width).astype(jnp.float32)
    normed, norm_back = jax.vjp(norm_rows, flat_tokens, gain_attn)
    lowered = normed.astype(jnp.bfloat16)
    queries = jnp.dot(lowered, w_query, preferred_element_type=jnp.float32).astype(jnp.bfloat16)
    key_rows = jnp.dot(lowered, w_key, preferred_element_type=jnp.float32).astype(jnp.bfloat16)
    value_rows = jnp.dot(lowered, w_value, preferred_element_type=jnp.float32).astype(jnp.bfloat16)
    key_whole, value_whole = (
        lax.all_gather(shaped(key_rows), "seq", axis=1, tiled=True),
        lax.all_gather(shaped(value_rows), "seq", axis=1, tiled=True),
    )
    mixed_rows, log_total = attention_forward(
        shaped(queries), key_whole, value_whole, seg_query, seg_rows
    )
    mixed_flat = mixed_rows.reshape(row_count * query_count, model_width)
    residual = flat_tokens + jnp.dot(mixed_flat, w_out, preferred_element_type=jnp.float32)
    normed_two, norm_two_back = jax.vjp(norm_rows, residual, gain_ffn)
    lowered_two = normed_two.astype(jnp.bfloat16)
    hidden_pre = jnp.dot(lowered_two, w_up, preferred_element_type=jnp.float32)
    hidden, gelu_back = jax.vjp(gelu_exact, hidden_pre)
    hidden_low = hidden.astype(jnp.bfloat16)
    layer_rows = (
        residual + jnp.dot(hidden_low, w_down, preferred_element_type=jnp.float32)
    ).astype(jnp.bfloat16)
    grad_out = cot_rows.reshape(row_count * query_count, model_width)
    grad_hidden = times_transposed(grad_out, w_down)
    grad_pre = gelu_back(grad_hidden)[0].astype(jnp.bfloat16)
    grad_normed_two = times_transposed(grad_pre, w_up)
    grad_resid_norm, grad_gain_ffn = norm_two_back(grad_normed_two)
    grad_residual = grad_out.astype(jnp.float32) + grad_resid_norm
    grad_attn = grad_residual.astype(jnp.bfloat16)
    grad_mixed = times_transposed(grad_attn, w_out).astype(jnp.bfloat16)
    query_part, key_part, value_part = attention_grads(
        shaped(queries), key_whole, value_whole, seg_query, seg_rows, log_total, shaped(grad_mixed)
    )
    key_own, value_own = (
        lax.psum_scatter(key_part, "seq", scatter_dimension=1, tiled=True),
        lax.psum_scatter(value_part, "seq", scatter_dimension=1, tiled=True),
    )
    grad_queries = query_part.reshape(row_count * query_count, model_width).astype(jnp.bfloat16)
    grad_keys = key_own.reshape(row_count * query_count, model_width).astype(jnp.bfloat16)
    grad_values = value_own.reshape(row_count * query_count, model_width).astype(jnp.bfloat16)
    grad_normed = (
        times_transposed(grad_queries, w_query)
        + times_transposed(grad_keys, w_key)
        + times_transposed(grad_values, w_value)
    )
    grad_token_norm, grad_gain_attn = norm_back(grad_normed)
    grad_tokens = (grad_residual + grad_token_norm).reshape(row_count, query_count, model_width)
    saved = (
        lowered,
        grad_queries,
        grad_keys,
        grad_values,
        mixed_flat,
        grad_attn,
        lowered_two,
        grad_pre,
        hidden_low,
        grad_out,
    )
    return (
        layer_rows.reshape(row_count, query_count, model_width),
        grad_tokens,
        saved,
        grad_gain_attn,
        grad_gain_ffn,
    )


def body(
    tokens, segments, gain_attn, w_query, w_key, w_value, w_out, gain_ffn, w_up, w_down, cotangent
):
    col_query = lax.all_gather(w_query, "seq", axis=1, tiled=True)
    col_key = lax.all_gather(w_key, "seq", axis=1, tiled=True)
    col_value = lax.all_gather(w_value, "seq", axis=1, tiled=True)
    col_out = lax.all_gather(w_out, "seq", axis=1, tiled=True)
    col_up = lax.all_gather(w_up, "seq", axis=1, tiled=True)
    col_down = lax.all_gather(w_down, "seq", axis=1, tiled=True)
    results = [
        process(
            tokens,
            cotangent,
            segments,
            gain_attn,
            gain_ffn,
            (
                lax.all_gather(col_query, "rows", axis=0, tiled=True),
                lax.all_gather(col_key, "rows", axis=0, tiled=True),
                lax.all_gather(col_value, "rows", axis=0, tiled=True),
                lax.all_gather(col_out, "rows", axis=0, tiled=True),
                lax.all_gather(col_up, "rows", axis=0, tiled=True),
                lax.all_gather(col_down, "rows", axis=0, tiled=True),
            ),
        )
    ]
    layer_out = jnp.concatenate([result_set[0] for result_set in results], 0)
    token_grad = jnp.concatenate([result_set[1] for result_set in results], 0)
    saved = [
        jnp.concatenate([result_set[2][member] for result_set in results], 0)
        for member in range(10)
    ]
    attn_gain_part = sum((result_set[3] for result_set in results))
    ffn_gain_part = sum((result_set[4] for result_set in results))
    gain_attn_grad, gain_ffn_grad = lax.psum((attn_gain_part, ffn_gain_part), ("rows", "seq"))
    (
        lowered,
        grad_queries,
        grad_keys,
        grad_values,
        mixed_flat,
        grad_attn,
        lowered_two,
        grad_pre,
        hidden_low,
        grad_out,
    ) = saved
    splits = lax.axis_size("seq")

    def arrange(grad_block):
        return grad_block.reshape(grad_block.shape[0], splits, grad_block.shape[1] // splits)

    def outer_product(left_side, right_side):
        return jnp.einsum("tc,te->ce", left_side, right_side, preferred_element_type=jnp.float32)

    def input_terms(offset, count):
        blocks = [
            outer_product(lowered, grad_queries),
            outer_product(lowered, grad_keys),
            outer_product(lowered, grad_values),
            outer_product(mixed_flat, grad_attn),
            outer_product(lowered_two, grad_pre),
        ]
        return jnp.concatenate([arrange(grad_block) for grad_block in blocks], 2)

    def hidden_terms(offset, count):
        return arrange(outer_product(hidden_low, grad_out))

    def spread_sum(term_of, shard_rows):
        row_part = lax.psum_scatter(
            term_of(jnp.int32(0), shard_rows * lax.axis_size("rows")),
            "rows",
            scatter_dimension=0,
            tiled=True,
        )
        return lax.psum_scatter(row_part, "seq", scatter_dimension=1, tiled=True)[:, 0, :]

    input_grads = spread_sum(input_terms, w_query.shape[0])
    down_grad = spread_sum(hidden_terms, w_down.shape[0])
    column_width = w_query.shape[1]
    query_grad = input_grads[:, :column_width]
    key_grad = input_grads[:, column_width : 2 * column_width]
    value_grad = input_grads[:, 2 * column_width : 3 * column_width]
    out_grad = input_grads[:, 3 * column_width : 4 * column_width]
    up_grad = input_grads[:, 4 * column_width :]
    return (
        layer_out,
        token_grad,
        gain_attn_grad,
        query_grad,
        key_grad,
        value_grad,
        out_grad,
        gain_ffn_grad,
        up_grad,
        down_grad,
    )


LANES = 128
QUERY_TILE = 128
BACK_TILE = 256
NEVER = -1e30


def swap_cores(values):
    return lax.ppermute(values, "seq", [(0, 1), (1, 0)])


def both_cores(values, axis):
    other = swap_cores(values)
    first = lax.axis_index("seq") == 0
    return jnp.where(
        first,
        jnp.concatenate([values, other], axis),
        jnp.concatenate([other, values], axis),
    )


def own_half(values, axis, index):
    half = values.shape[axis] // 2
    return lax.dynamic_slice_in_dim(values, index * half, half, axis)


def two_heads(ref, rows, columns):
    values = ref[0, rows, columns]
    lower = lax.broadcasted_iota(jnp.int32, values.shape, 1) < HEAD_DIM
    zero = jnp.zeros_like(values)
    return jnp.concatenate([jnp.where(lower, values, zero), jnp.where(lower, zero, values)], 0)


def merge_heads(values):
    half = values.shape[0] // 2
    lower = lax.broadcasted_iota(jnp.int32, (half, LANES), 1) < HEAD_DIM
    return jnp.where(lower, values[:half], values[half:])


def over_windows(first_row, query_tile, start_ref, count_ref, length, window):
    row = first_row + pl.program_id(0)

    def tile_step(tile, carry):
        begin = pl.multiple_of(start_ref[row, tile] * LANES, LANES)
        count = count_ref[row, tile]
        queries = pl.ds(pl.multiple_of(tile * query_tile, query_tile), query_tile)
        for tiles in range(1, length // LANES + 1):
            keys = pl.ds(begin, tiles * LANES)
            pl.when(count == tiles)(functools.partial(window, queries, keys))
        return carry

    lax.fori_loop(0, length // query_tile, tile_step, 0)


last_dims = (((1,), (1,)), ((), ()))
first_dims = (((0,), (0,)), ((), ()))
exponent_scale = HEAD_DIM ** (-0.5) * 1.4426950408889634


def attend_kernel(
    row, begun, start_ref, count_ref, column_ref, line_ref, q_ref, k_ref, v_ref, *rest
):
    (out_ref,) = rest[begun:]
    _, length, wide = q_ref.shape

    def window(queries, keys):
        allowed = column_ref[0, queries, :1] == line_ref[0, :1, keys]
        bias = jnp.where(allowed, 0.0, NEVER)[None]

        def scores_of(pair):
            columns = pl.ds(pair * LANES, LANES)
            return lax.dot_general(
                two_heads(q_ref, queries, columns),
                k_ref[0, keys, columns],
                last_dims,
                preferred_element_type=jnp.float32,
            )

        ahead = scores_of(0)
        for pair in range(wide // LANES):
            scores = ahead
            if (pair + 1) * LANES < wide:
                ahead = scores_of(pair + 1)
            shape = scores.shape
            scores = (scores.reshape((2, QUERY_TILE) + shape[1:]) + bias).reshape(shape)
            top = jnp.max(scores, -1, keepdims=True)
            exponent = jnp.exp2((scores - top) * exponent_scale)
            columns = pl.ds(pair * LANES, LANES)
            part = jnp.dot(
                exponent.astype(jnp.bfloat16),
                v_ref[0, keys, columns],
                preferred_element_type=jnp.float32,
            )
            part = part / jnp.sum(exponent, -1, keepdims=True)
            out_ref[0, queries, columns] = merge_heads(part).astype(jnp.bfloat16)

    over_windows(row, QUERY_TILE, start_ref, count_ref, length, window)


def attend_back_kernel(
    row, begun, start_ref, count_ref, column_ref, line_ref, q_ref, k_ref, v_ref, grad_ref, *rest
):
    dq_ref, dk_ref, dv_ref, dk_sum, dv_sum = rest[begun:]
    dk_sum[...] = jnp.zeros_like(dk_sum)
    dv_sum[...] = jnp.zeros_like(dv_sum)
    scale = HEAD_DIM ** (-0.5)
    columns = pl.ds(0, LANES)

    def window(queries, keys):
        query, grad = two_heads(q_ref, queries, columns), two_heads(grad_ref, queries, columns)
        key, value = k_ref[0, keys, :], v_ref[0, keys, :]
        bias = jnp.where(column_ref[0, keys, :1] == line_ref[0, :1, queries], 0.0, NEVER)
        scores = lax.dot_general(key, query, last_dims, preferred_element_type=jnp.float32)
        scores = scores + jnp.concatenate([bias, bias], 1)
        top = jnp.max(scores, 0, keepdims=True)
        exponent = jnp.exp2((scores - top) * exponent_scale)
        probs = exponent * (1.0 / jnp.sum(exponent, 0, keepdims=True))
        grad_probs = lax.dot_general(value, grad, last_dims, preferred_element_type=jnp.float32)
        inner = jnp.sum(grad_probs * probs, 0, keepdims=True)
        grad_scores = (probs * (grad_probs - inner)).astype(jnp.bfloat16)
        dv_sum[keys, :] += jnp.dot(
            probs.astype(jnp.bfloat16), grad, preferred_element_type=jnp.float32
        )
        dk_sum[keys, :] += jnp.dot(grad_scores, query, preferred_element_type=jnp.float32)
        query_part = lax.dot_general(
            grad_scores, key, first_dims, preferred_element_type=jnp.float32
        )
        dq_ref[0, queries, :] = (merge_heads(query_part) * scale).astype(jnp.bfloat16)

    over_windows(row, BACK_TILE, start_ref, count_ref, k_ref.shape[1], window)
    dk_ref[0] = (dk_sum[...] * scale).astype(jnp.bfloat16)
    dv_ref[0] = dv_sum[...].astype(jnp.bfloat16)


def windows_of(segments, query_tile):
    heads = segments[:, ::query_tile]
    tails = segments[:, query_tile - 1 :: query_tile]
    begin = jnp.sum(segments[:, None, :] < heads[:, :, None], -1, dtype=jnp.int32)
    end = jnp.sum(segments[:, None, :] <= tails[:, :, None], -1, dtype=jnp.int32)
    start = begin // LANES
    return start, (end + LANES - 1) // LANES - start


def attention_call(
    kernel, row, rows, windows, marks, operands, outputs, scratch, block_wide, begun=()
):
    all_rows, length, _ = operands[0][0].shape
    wide = outputs[0]
    steps = wide // block_wide

    def block(part):
        return pl.BlockSpec(
            (1, length, block_wide), lambda at, step, *_: (row + at, 0, part * steps + step)
        )

    work = rows * wide * length * length
    shape = jax.ShapeDtypeStruct((all_rows, length, wide), jnp.bfloat16)
    return pl.pallas_call(
        functools.partial(kernel, row, len(begun)),
        grid_spec=pltpu.PrefetchScalarGridSpec(
            num_scalar_prefetch=2,
            grid=(rows, steps),
            in_specs=[
                pl.BlockSpec((1, length, LANES), lambda at, *_: (row + at, 0, 0)),
                pl.BlockSpec((1, 8, length), lambda at, *_: (row + at, 0, 0)),
            ]
            + [block(first) for _, first in operands]
            + [pl.BlockSpec(memory_space=pl.ANY)] * len(begun),
            out_specs=[block(0)] * len(outputs),
            scratch_shapes=scratch,
        ),
        out_shape=[shape] * len(outputs),
        input_output_aliases={4 + len(operands) + index: index for index in range(len(begun))},
        compiler_params=pltpu.CompilerParams(vmem_limit_bytes=48 * 1024 * 1024),
        cost_estimate=pl.CostEstimate(
            flops=4 * len(operands) * work,
            bytes_accessed=2 * (len(operands) + len(outputs)) * rows * length * wide,
            transcendentals=work // HEAD_DIM,
        ),
    )(*windows, *marks, *(array for array, _ in operands), *begun)


def norm_stats(values):
    centred = values - jnp.mean(values, -1, keepdims=True)
    scale = lax.rsqrt(jnp.mean(centred * centred, -1, keepdims=True) + epsilon)
    return centred * scale, scale


def norm_back_rows(unit, scale, gain_vec, grad):
    scaled = grad * gain_vec
    inner = jnp.mean(scaled * unit, -1, keepdims=True)
    return scale * (scaled - jnp.mean(scaled, -1, keepdims=True) - unit * inner)


Z_SIZE = 4
RING = (0, 1, 3, 2)
PLACE = (0, 1, 3, 2)


def chip_place():
    index = lax.axis_index("rows")
    return index // 4, (index // 2) % 2, index % 2


def swap_x(values):
    return lax.ppermute(values, "rows", [(row, row ^ 1) for row in range(16)])


def swap_y(values):
    return lax.ppermute(values, "rows", [(row, row ^ 2) for row in range(16)])


def next_z(values):
    pairs = []
    for place in range(Z_SIZE):
        here, there = RING[place], RING[(place + 1) % Z_SIZE]
        pairs += [(here * 4 + rest, there * 4 + rest) for rest in range(4)]
    return lax.ppermute(values, "rows", pairs)


def ring_place():
    zed = chip_place()[0]
    return jnp.where(zed == 2, 3, jnp.where(zed == 3, 2, zed))


def tie(value, *after):
    return lax.optimization_barrier((value, after))[0]


def natural_z(steps):
    place = ring_place()
    stack = jnp.stack(steps)
    return jnp.stack(
        [
            lax.dynamic_index_in_dim(stack, (place - PLACE[zed]) % Z_SIZE, 0, keepdims=False)
            for zed in range(Z_SIZE)
        ]
    )


def load_pieces(place_ref, pieces, target_of, sems):
    copies = []
    for part in range(2):
        for across in range(2):
            for along in range(2):
                far_y, far_x = (along, across) if part == 0 else (across, along)
                row_y, row_x = place_ref[1] ^ far_y, place_ref[2] ^ far_x
                piece = pieces[part * 2 + across].at[along]
                for zed in range(Z_SIZE):
                    target = target_of(part, zed, row_y, row_x, piece)
                    copies.append(
                        pltpu.make_async_copy(piece.at[zed], target, sems.at[len(copies)])
                    )
                    copies[-1].start()
    return copies


def column_target(whole_ref):
    def target_of(part, zed, row_y, row_x, piece):
        _, depth, wide = piece.shape
        row = pl.multiple_of(((zed * 2 + row_y) * 2 + row_x) * depth, 16)
        left = 0 if part == 0 else whole_ref.shape[1] - wide
        return whole_ref.at[pl.ds(row, depth), pl.ds(left, wide)]

    return target_of


def assemble_columns_kernel(place_ref, *refs):
    *pieces, out_ref, sems = refs
    for copy in load_pieces(place_ref, pieces, column_target(out_ref), sems):
        copy.wait()


def place_vector():
    return jnp.stack(chip_place() + (lax.axis_index("seq"),)).astype(jnp.int32)


def assemble(kernel, shape, parts):
    return pl.pallas_call(
        kernel,
        grid_spec=pltpu.PrefetchScalarGridSpec(
            num_scalar_prefetch=1,
            grid=(1,),
            in_specs=[pl.BlockSpec(memory_space=pl.ANY)] * 4,
            out_specs=pl.BlockSpec(shape, lambda step, *_: (0,) * len(shape)),
            scratch_shapes=[pltpu.SemaphoreType.DMA((32,))],
        ),
        out_shape=jax.ShapeDtypeStruct(shape, parts[0][0].dtype),
        compiler_params=pltpu.CompilerParams(vmem_limit_bytes=40 * 1024 * 1024),
    )(place_vector(), *parts[0], *parts[1])


FFN_TILE = 256
FFN_CHUNK = 512
root_two_pi = 0.3989422804014327


def feed_forward_kernel(*refs):
    normed_ref, cot_ref, *refs = refs
    up_pieces, down_pieces, refs = refs[:4], refs[4:10], refs[10:]
    hidden_ref, grad_pre_ref, y_ref, grad_ref, normed_out, y_came, grad_came, *refs = refs
    up_ref, down_ref, normed_buf, y_away, grad_away, *refs = refs
    up_sems, down_sems, sent_sems, came_sems, normed_sems, away_sends, away_recvs, *refs = refs
    corner_sends, corner_recvs = refs
    step = pl.program_id(0)
    row, core = lax.axis_index("rows"), lax.axis_index("seq")
    here_y, here_x = (row // 2) % 2, row % 2
    twin = (row, 1 - core)
    over_x, over_y = row + 1 - 2 * here_x, row + 2 - 4 * here_y
    span = normed_ref.shape[0]
    tiles = span // FFN_TILE

    def remote(src, dst, send_sem, recv_sem):
        return pltpu.make_async_remote_copy(
            src_ref=src,
            dst_ref=dst,
            send_sem=send_sem,
            recv_sem=recv_sem,
            device_id=twin,
            device_id_type=pl.DeviceIdType.MESH,
        )

    def normed_copies():
        own, others = normed_buf.at[pl.ds(0, span), :], normed_buf.at[pl.ds(span, span), :]
        return (
            pltpu.make_async_copy(normed_ref, own, normed_sems.at[0]),
            remote(normed_ref, others, normed_sems.at[1], normed_sems.at[2]),
        )

    def up_copies():
        copies = []
        for part in range(2):
            for across in range(2):
                for along in range(2):
                    far_y, far_x = (along, across) if part == 0 else (across, along)
                    row_y = 1 - here_y if far_y else here_y
                    row_x = 1 - here_x if far_x else here_x
                    for zed in range(Z_SIZE):
                        piece = up_pieces[part * 2 + across].at[along, zed]
                        depth, wide = piece.shape
                        first = pl.multiple_of(((zed * 2 + row_y) * 2 + row_x) * depth, 16)
                        left = 0 if part == 0 else up_ref.shape[1] - wide
                        target = up_ref.at[pl.ds(first, depth), pl.ds(left, wide)]
                        copies.append(pltpu.make_async_copy(piece, target, up_sems.at[len(copies)]))
        return copies

    def down_rows(part, lower, row_y, row_x, depth):
        first = (((lower * 2 + row_y) * 2 + row_x) * 2 + part) * depth
        return pl.ds(pl.multiple_of(first, 16), depth)

    def down_copies():
        kept, given = [], []
        for part in range(2):
            for which, (far_y, far_x) in enumerate(
                ((0, 0), (1, 0), (0, 1)) if part == 0 else ((0, 0), (0, 1), (1, 0))
            ):
                row_y = 1 - here_y if far_y else here_y
                row_x = 1 - here_x if far_x else here_x
                for lower in range(2):
                    pieces = down_pieces[part * 3 + which]
                    depth, wide = pieces.shape[1:]
                    rows = down_rows(part, lower, row_y, row_x, depth)
                    target = down_ref.at[rows, pl.ds(pl.multiple_of(core * wide, 128), wide)]
                    number = len(kept)
                    kept.append(
                        pltpu.make_async_copy(
                            pieces.at[2 * core + lower], target, down_sems.at[number]
                        )
                    )
                    given.append(
                        remote(
                            pieces.at[2 * (1 - core) + lower],
                            target,
                            sent_sems.at[number],
                            came_sems.at[number],
                        )
                    )
        return kept, given

    def corner_copies():
        sends, arrivals = [], []
        for part in range(2):
            pieces = down_pieces[part * 3 + 1]
            depth, wide = pieces.shape[1:]
            row_y, row_x = (1 - here_y, here_x) if part == 0 else (here_y, 1 - here_x)
            for other in range(2):
                for lower in range(2):
                    number = len(sends)
                    rows = down_rows(part, lower, row_y, row_x, depth)
                    target = down_ref.at[rows, pl.ds(pl.multiple_of(core * wide, 128), wide)]
                    sends.append(
                        pltpu.make_async_remote_copy(
                            src_ref=pieces.at[2 * other + lower],
                            dst_ref=target,
                            send_sem=corner_sends.at[number],
                            recv_sem=corner_recvs.at[part, core, lower],
                            device_id=(over_x if part == 0 else over_y, other),
                            device_id_type=pl.DeviceIdType.MESH,
                        )
                    )
                    rows = down_rows(part, lower, 1 - here_y, 1 - here_x, depth)
                    target = down_ref.at[rows, pl.ds(other * wide, wide)]
                    arrivals.append(
                        pltpu.make_async_remote_copy(
                            src_ref=target,
                            dst_ref=target,
                            send_sem=corner_sends.at[number],
                            recv_sem=corner_recvs.at[part, other, lower],
                            device_id=(over_x if part == 0 else over_y, other),
                            device_id_type=pl.DeviceIdType.MESH,
                        )
                    )
        return sends, arrivals

    def away_copies(tile):
        rows = pl.ds(pl.multiple_of(tile * FFN_TILE, FFN_TILE), FFN_TILE)
        return [
            remote(buf.at[tile], out.at[rows, :], away_sends.at[which, tile], away_recvs.at[which, tile])
            for which, (buf, out) in enumerate(((y_away, y_came), (grad_away, grad_came)))
        ]

    @pl.when(step == 0)
    def _():
        barrier = pltpu.get_barrier_semaphore()
        for target in (twin, (over_x, 0), (over_x, 1), (over_y, 0), (over_y, 1)):
            pl.semaphore_signal(
                barrier, inc=1, device_id=target, device_id_type=pl.DeviceIdType.MESH
            )
        kept, given = down_copies()
        corners, arrivals = corner_copies()
        own, others = normed_copies()
        ups = up_copies()
        pl.semaphore_wait(barrier, 5)
        for copy in corners + [own] + ups + kept + given + [others]:
            copy.start()
        for copy in [own] + ups + kept:
            copy.wait()
        for copy in given + arrivals:
            copy.wait_recv()

    @pl.when(step == tiles)
    def _():
        normed_copies()[1].wait_recv()

    normed = normed_buf[pl.ds(pl.multiple_of(step * FFN_TILE, FFN_TILE), FFN_TILE), :]
    cot = cot_ref[...]
    y_sum = grad_sum = 0.0
    for chunk in range(hidden_ref.shape[1] // FFN_CHUNK):
        units = pl.ds(chunk * FFN_CHUNK, FFN_CHUNK)
        up, down = up_ref[:, units], down_ref[units, :]
        pre = jnp.dot(normed, up, preferred_element_type=jnp.float32)
        grad_hidden = lax.dot_general(cot, down, last_dims, preferred_element_type=jnp.float32)
        phi = 0.5 + 0.5 * lax.erf(pre * root_half)
        hidden = (pre * phi).astype(jnp.bfloat16)
        slope = phi + pre * (jnp.exp(-0.5 * pre * pre) * root_two_pi)
        grad_pre = (grad_hidden * slope).astype(jnp.bfloat16)
        hidden_ref[:, units] = hidden
        grad_pre_ref[:, units] = grad_pre
        y_sum += jnp.dot(hidden, down, preferred_element_type=jnp.float32)
        grad_sum += lax.dot_general(grad_pre, up, last_dims, preferred_element_type=jnp.float32)

    @pl.when(step < tiles)
    def _():
        y_ref[...] = y_sum.astype(jnp.bfloat16)
        grad_ref[...] = grad_sum.astype(jnp.bfloat16)

    for tile in range(tiles):

        @pl.when(step == tiles + tile)
        def _(tile=tile):
            y_away[tile] = y_sum.astype(jnp.bfloat16)
            grad_away[tile] = grad_sum.astype(jnp.bfloat16)
            for copy in away_copies(tile):
                copy.start()

    @pl.when(step == 2 * tiles - 1)
    def _():
        store = pltpu.make_async_copy(normed_buf, normed_out, normed_sems.at[0])
        store.start()
        for copy in (*down_copies()[1], *corner_copies()[0], normed_copies()[1]):
            copy.wait_send()
        for tile in range(tiles):
            for copy in away_copies(tile):
                copy.wait()
        store.wait()


def feed_forward(normed, cot_all, up_parts, down_parts):
    tokens, width = normed.shape
    units = up_parts[0][0].shape[3] + up_parts[1][0].shape[3]
    tiles = tokens // FFN_TILE
    tile = pl.BlockSpec((FFN_TILE, width), lambda step: (step, 0))
    own_tile = pl.BlockSpec((FFN_TILE, width), lambda step: (jnp.minimum(step, tiles - 1), 0))
    wide_tile = pl.BlockSpec((FFN_TILE, units), lambda step: (step, 0))
    anywhere = pl.BlockSpec(memory_space=pl.ANY)
    wide_shape = jax.ShapeDtypeStruct((2 * tokens, units), jnp.bfloat16)
    shape = jax.ShapeDtypeStruct((tokens, width), jnp.bfloat16)
    away = pltpu.VMEM((tiles, FFN_TILE, width), jnp.bfloat16)
    sems = pltpu.SemaphoreType.DMA
    return pl.pallas_call(
        feed_forward_kernel,
        grid=(2 * tiles,),
        in_specs=[anywhere, tile] + [anywhere] * 10,
        out_specs=[wide_tile, wide_tile, own_tile, own_tile] + [anywhere] * 3,
        out_shape=[
            wide_shape,
            wide_shape,
            shape,
            shape,
            jax.ShapeDtypeStruct((2 * tokens, width), jnp.bfloat16),
            shape,
            shape,
        ],
        scratch_shapes=[
            pltpu.VMEM((width, units), jnp.bfloat16),
            pltpu.VMEM((units, width), jnp.bfloat16),
            pltpu.VMEM((2 * tokens, width), jnp.bfloat16),
            away,
            away,
            sems((32,)),
            sems((16,)),
            sems((16,)),
            sems((16,)),
            sems((3,)),
            sems((2, tiles)),
            sems((2, tiles)),
            sems((8,)),
            sems((2, 2, 2)),
        ],
        compiler_params=pltpu.CompilerParams(
            collective_id=2, has_side_effects=True, vmem_limit_bytes=60 * 1024 * 1024
        ),
        cost_estimate=pl.CostEstimate(
            flops=16 * tokens * width * units,
            bytes_accessed=4 * width * units + 8 * tokens * (2 * width + units),
            transcendentals=4 * tokens * units,
        ),
    )(normed, cot_all, *up_parts[0], *up_parts[1], *down_parts)


RESIDUAL_TILE = 128


def residual_kernel(*refs):
    residual_ref, cot_ref, y_ref, y_came, grad_ref, grad_came, gain_ref, *refs = refs
    layer_ref, out_ref, gain_out, both_out, buf, local_sems, send_sems, recv_sems = refs
    step = pl.program_id(0)
    steps = buf.shape[0]
    row, core = lax.axis_index("rows"), lax.axis_index("seq")
    twin = (row, 1 - core)
    span = both_out.shape[1] // 2

    def copies(tile):
        each = span // RESIDUAL_TILE
        first = core * span + (tile % each) * RESIDUAL_TILE
        rows = pl.ds(pl.multiple_of(first, RESIDUAL_TILE), RESIDUAL_TILE)
        target = both_out.at[tile // each, rows, :]
        return (
            pltpu.make_async_copy(buf.at[tile], target, local_sems.at[tile]),
            pltpu.make_async_remote_copy(
                src_ref=buf.at[tile],
                dst_ref=target,
                send_sem=send_sems.at[tile],
                recv_sem=recv_sems.at[tile],
                device_id=twin,
                device_id_type=pl.DeviceIdType.MESH,
            ),
        )

    @pl.when(step == 0)
    def _():
        barrier = pltpu.get_barrier_semaphore()
        pl.semaphore_signal(barrier, inc=1, device_id=twin, device_id_type=pl.DeviceIdType.MESH)
        pl.semaphore_wait(barrier, 1)
        gain_out[...] = jnp.zeros_like(gain_out)

    residual = residual_ref[...]
    layer_ref[...] = plus(residual, y_ref[...], y_came[...])
    unit, scale = norm_stats(residual)
    grad = plus_wide(grad_ref[...], grad_came[...])
    grad_residual = cot_ref[...].astype(jnp.float32) + norm_back_rows(
        unit, scale, gain_ref[...], grad
    )
    out_ref[...] = grad_residual
    gain_out[0:1, :] += jnp.sum(grad * unit, 0, keepdims=True)
    for tile in range(steps):

        @pl.when(step == tile)
        def _(tile=tile):
            buf[tile] = grad_residual.astype(jnp.bfloat16)
            for copy in copies(tile):
                copy.start()

    @pl.when(step == steps - 1)
    def _():
        for tile in range(steps):
            for copy in copies(tile):
                copy.wait()


def residual_call(rows, residual, cot, y_own, y_came, grad_own, grad_came, gain):
    flat, width = residual.shape
    steps = flat // RESIDUAL_TILE
    tile = pl.BlockSpec((RESIDUAL_TILE, width), lambda step: (step, 0))
    sems = pltpu.SemaphoreType.DMA((steps,))
    return pl.pallas_call(
        residual_kernel,
        grid=(steps,),
        in_specs=[tile] * 6 + [pl.BlockSpec((1, width), lambda step: (0, 0))],
        out_specs=[
            tile,
            tile,
            pl.BlockSpec((8, width), lambda step: (0, 0)),
            pl.BlockSpec(memory_space=pl.ANY),
        ],
        out_shape=[
            jax.ShapeDtypeStruct((flat, width), jnp.bfloat16),
            jax.ShapeDtypeStruct((flat, width), jnp.float32),
            jax.ShapeDtypeStruct((8, width), jnp.float32),
            jax.ShapeDtypeStruct((rows, 2 * flat // rows, width), jnp.bfloat16),
        ],
        scratch_shapes=[
            pltpu.VMEM((steps, RESIDUAL_TILE, width), jnp.bfloat16),
            sems,
            sems,
            sems,
        ],
        compiler_params=pltpu.CompilerParams(
            collective_id=3, has_side_effects=True, vmem_limit_bytes=32 * 1024 * 1024
        ),
    )(residual, cot, y_own, y_came, grad_own, grad_came, gain.reshape(1, width))


def following(zed):
    return (2 * zed + 1) % 5


def preceding(zed):
    return (3 * zed + 2) % 5


NORM_TILE = 128


def head_kernel(
    tokens_ref,
    gain_ref,
    cot_ref,
    piece_ref,
    up_ref,
    normed_out,
    cot_out,
    weights_out,
    up_out,
    token_buf,
    normed_buf,
    local_sems,
    send_sems,
    recv_sems,
):
    row, core = lax.axis_index("rows"), lax.axis_index("seq")
    zed, here_y, here_x = row // 4, (row // 2) % 2, row % 2
    rest = row - 4 * zed
    over_x, over_y = row + 1 - 2 * here_x, row + 2 - 4 * here_y
    onward, backward = following(zed) * 4 + rest, preceding(zed) * 4 + rest
    places = [zed]
    for _ in range(3):
        places.append(preceding(places[-1]))
    depth, wide = piece_ref.shape
    half = wide // 2

    barrier = pltpu.get_barrier_semaphore()
    for target in ((onward, core), (backward, core), (over_x, core), (over_y, core), (row, 1 - core)):
        pl.semaphore_signal(
            barrier, inc=1, device_id=target, device_id_type=pl.DeviceIdType.MESH
        )
    load = pltpu.make_async_copy(tokens_ref, token_buf, local_sems.at[0])
    load.start()
    own_rows = pl.ds(pl.multiple_of(row * depth, 16), depth)
    keeps = [
        pltpu.make_async_copy(piece_ref, weights_out.at[own_rows, :], local_sems.at[1]),
        pltpu.make_async_copy(up_ref, up_out.at[zed], local_sems.at[2]),
    ]
    for keep in keeps:
        keep.start()
    pl.semaphore_wait(barrier, 5)

    sent = []

    def send(src, dst, target):
        number = len(sent)
        copy = pltpu.make_async_remote_copy(
            src_ref=src,
            dst_ref=dst,
            send_sem=send_sems.at[number],
            recv_sem=recv_sems.at[number],
            device_id=target,
            device_id_type=pl.DeviceIdType.MESH,
        )
        copy.start()
        sent.append(copy)
        return copy

    def block(place, far_y, far_x, columns):
        at_y = 1 - here_y if far_y else here_y
        at_x = 1 - here_x if far_x else here_x
        index = (place * 2 + at_y) * 2 + at_x
        rows = pl.ds(pl.multiple_of(index * depth, 16), depth)
        return weights_out.at[rows, columns]

    everything, left, right = pl.ds(0, wide), pl.ds(0, half), pl.ds(half, half)

    def source(step, columns):
        if step == 0:
            return piece_ref.at[:, columns]
        return block(places[step], False, False, columns)

    def around(step):
        return send(
            source(step, everything), block(places[step], False, False, everything), (onward, core)
        )

    def around_up(step):
        src = up_ref if step == 0 else up_out.at[places[step]]
        return send(src, up_out.at[places[step]], (onward, core))

    def across(step):
        place = places[step]
        return (
            send(source(step, left), block(place, False, False, left), (over_y, core)),
            send(source(step, right), block(place, False, False, right), (over_x, core)),
            send(source(step, left), block(place, False, False, left), (over_x, core)),
            send(source(step, right), block(place, False, False, right), (over_y, core)),
        )

    def corner(step, crossing):
        place = places[step]
        crossing[0].wait_recv()
        far_left = block(place, True, False, left)
        first = send(far_left, far_left, (over_x, core))
        crossing[1].wait_recv()
        far_right = block(place, False, True, right)
        return first, send(far_right, far_right, (over_y, core))

    ring = around(0)
    crossing = across(0)
    arrivals = [crossing[2], crossing[3]]
    arrivals.append(send(cot_ref, cot_out, (row, 1 - core)))

    load.wait()
    span = token_buf.shape[1]
    for member in range(token_buf.shape[0]):

        def norm_tile(tile, carry, member=member):
            rows = pl.ds(pl.multiple_of(tile * NORM_TILE, NORM_TILE), NORM_TILE)
            unit, _ = norm_stats(token_buf[member, rows, :].astype(jnp.float32))
            normed_buf[member, rows, :] = (unit * gain_ref[...]).astype(jnp.bfloat16)
            return carry

        lax.fori_loop(0, span // NORM_TILE, norm_tile, 0)
    mine = normed_out.at[:, pl.ds(pl.multiple_of(core * span, 16), span), :]
    keeps.append(pltpu.make_async_copy(normed_buf, mine, local_sems.at[3]))
    keeps[-1].start()
    arrivals.append(send(normed_buf, mine, (row, 1 - core)))

    up_ring = None
    for step in range(1, 4):
        ring.wait_recv()
        if step < 3:
            ring = around(step)
        if step == 2:
            up_ring = around_up(0)
        arrivals += corner(step - 1, crossing)
        crossing = across(step)
        arrivals += crossing[2:]
        if step == 3:
            up_ring.wait_recv()
            up_ring = around_up(1)
    arrivals += corner(3, crossing)
    up_ring.wait_recv()
    arrivals.append(around_up(2))
    for copy in arrivals:
        copy.wait_recv()
    for copy in sent:
        copy.wait_send()
    for keep in keeps:
        keep.wait()


def head_call(tokens, gain, cotangent, piece, w_up):
    rows, span, width = tokens.shape
    depth, wide = piece.shape
    anywhere = pl.BlockSpec(memory_space=pl.ANY)
    return pl.pallas_call(
        head_kernel,
        in_specs=[anywhere, pl.BlockSpec(memory_space=pltpu.VMEM)] + [anywhere] * 3,
        out_specs=[anywhere] * 4,
        out_shape=[
            jax.ShapeDtypeStruct((rows, 2 * span, width), jnp.bfloat16),
            jax.ShapeDtypeStruct(cotangent.shape, jnp.bfloat16),
            jax.ShapeDtypeStruct((16 * depth, wide), jnp.bfloat16),
            jax.ShapeDtypeStruct((Z_SIZE,) + w_up.shape, jnp.bfloat16),
        ],
        scratch_shapes=[
            pltpu.VMEM(tokens.shape, jnp.bfloat16),
            pltpu.VMEM(tokens.shape, jnp.bfloat16),
            pltpu.SemaphoreType.DMA((4,)),
            pltpu.SemaphoreType.DMA((32,)),
            pltpu.SemaphoreType.DMA((32,)),
        ],
        compiler_params=pltpu.CompilerParams(
            collective_id=0, has_side_effects=True, vmem_limit_bytes=32 * 1024 * 1024
        ),
    )(tokens, gain.reshape(1, width), cotangent, piece, w_up)


def plus_wide(*terms):
    return sum(term.astype(jnp.float32) for term in terms)


def plus(*terms):
    return plus_wide(*terms).astype(jnp.bfloat16)


TAIL_TILE = 256


def tail_kernel(
    dq_ref,
    dk_ref,
    dv_ref,
    weights_ref,
    query_ref,
    key_ref,
    value_ref,
    tokens_ref,
    residual_ref,
    gain_ref,
    ffn_gain_ref,
    hidden_ref,
    token_out,
    query_out,
    key_out,
    value_out,
    gain_out,
    up_out,
    out_out,
    weight_buf,
    dq_buf,
    dk_buf,
    dv_buf,
    own_buf,
    away_buf,
    came_buf,
    token_buf,
    residual_buf,
    far_buf,
    near_buf,
    turned_buf,
    turned_came,
    sum_buf,
    ring_buf,
    ring_came,
    gain_buf,
    gain_came,
    hidden_buf,
    hidden_came,
    local_sems,
    send_sems,
    recv_sems,
):
    row, core = lax.axis_index("rows"), lax.axis_index("seq")
    zed, here_y, here_x = row // 4, (row // 2) % 2, row % 2
    rest = row - 4 * zed
    over_x, over_y = row + 1 - 2 * here_x, row + 2 - 4 * here_y
    onward, backward = following(zed) * 4 + rest, preceding(zed) * 4 + rest
    beside = (zed + 1 - 2 * (zed % 2)) * 4 + rest
    beyond = (zed + 2 - 4 * (zed // 2)) * 4 + rest
    places = [zed]
    for _ in range(3):
        places.append(preceding(places[-1]))
    depth = query_out.shape[0]
    half_wide = query_ref.shape[1]
    span = own_buf.shape[0] // 2

    barrier = pltpu.get_barrier_semaphore()
    for target in ((onward, core), (backward, core), (over_x, core), (over_y, core), (row, 1 - core)):
        pl.semaphore_signal(
            barrier, inc=1, device_id=target, device_id_type=pl.DeviceIdType.MESH
        )
    loads = [
        pltpu.make_async_copy(
            weights_ref.at[:, pl.ds(0, 3 * half_wide)], weight_buf, local_sems.at[0]
        )
    ]
    for index, (source, target) in enumerate(
        (
            (dq_ref, dq_buf),
            (dk_ref, dk_buf),
            (dv_ref, dv_buf),
            (tokens_ref, token_buf),
            (residual_ref, residual_buf),
        )
    ):
        loads.append(pltpu.make_async_copy(source, target, local_sems.at[1 + index]))
    for load in loads:
        load.start()
    pl.semaphore_wait(barrier, 5)

    sent = []

    def send(src, dst, target):
        number = len(sent)
        copy = pltpu.make_async_remote_copy(
            src_ref=src,
            dst_ref=dst,
            send_sem=send_sems.at[number],
            recv_sem=recv_sems.at[number],
            device_id=target,
            device_id_type=pl.DeviceIdType.MESH,
        )
        copy.start()
        sent.append(copy)
        return copy

    cut = (half_wide // 128 + 1) // 2 * 128
    streams = (
        (query_ref, 0, half_wide, 0, False),
        (key_ref, 0, cut, half_wide, False),
        (key_ref, cut, half_wide - cut, half_wide, True),
        (value_ref, 0, half_wide, 2 * half_wide, True),
    )

    def block_of(step, far_y, far_x):
        at_y = 1 - here_y if far_y else here_y
        at_x = 1 - here_x if far_x else here_x
        index = (places[step] * 2 + at_y) * 2 + at_x
        return pl.ds(pl.multiple_of(index * depth, 16), depth)

    far, near, turned = {}, {}, {}

    def issue(step):
        for which, (grad, column, wide, base, flip) in enumerate(streams):
            columns, place = pl.ds(column, wide), pl.ds(base + column, wide)
            target = (over_y if flip else over_x, core)
            far[step, which] = send(
                grad.at[block_of(step, True, True), columns], far_buf.at[step, :, place], target
            )
        for which, (grad, column, wide, base, flip) in enumerate(streams):
            columns, place = pl.ds(column, wide), pl.ds(base + column, wide)
            target = (over_y if flip else over_x, core)
            near[step, which] = send(
                grad.at[block_of(step, flip, not flip), columns],
                near_buf.at[step, :, place],
                target,
            )

    def turn(step):
        for which, (grad, column, wide, base, flip) in enumerate(streams):
            columns, place = pl.ds(column, wide), pl.ds(base + column, wide)
            far[step, which].wait_recv()
            turned_buf[step, :, place] = plus(
                grad[block_of(step, not flip, flip), columns], far_buf[step, :, place]
            )
            target = (over_x if flip else over_y, core)
            turned[step, which] = send(
                turned_buf.at[step, :, place], turned_came.at[step, :, place], target
            )

    def total(step):
        for which, (grad, column, wide, base, _) in enumerate(streams):
            columns, place = pl.ds(column, wide), pl.ds(base + column, wide)
            near[step, which].wait_recv()
            turned[step, which].wait_recv()
            sum_buf[step, :, place] = plus_wide(
                grad[block_of(step, False, False), columns],
                near_buf[step, :, place],
                turned_came[step, :, place],
            )

    ring = []

    def around(step):
        value = sum_buf[step]
        if step > 1:
            ring[-1].wait_recv()
            value = value + ring_came[step - 2].astype(jnp.float32)
        ring_buf[step - 1] = value.astype(jnp.bfloat16)
        ring.append(send(ring_buf.at[step - 1], ring_came.at[step - 1], (onward, core)))

    hidden_ring = []

    def around_hidden(step):
        value = hidden_ref[places[step]].astype(jnp.float32)
        if step > 1:
            hidden_ring[-1].wait_recv()
            value = value + hidden_came[step - 2].astype(jnp.float32)
        hidden_buf[step - 1] = value.astype(jnp.bfloat16)
        hidden_ring.append(
            send(hidden_buf.at[step - 1], hidden_came.at[step - 1], (onward, core))
        )

    def normed_tile(tile, half):
        first = (tile // 2) * 2 * span + half * span + (tile % 2) * TAIL_TILE
        rows = pl.ds(pl.multiple_of(first, TAIL_TILE), TAIL_TILE)
        part = 0.0
        for index, grad in enumerate((dq_buf, dk_buf, dv_buf)):
            part += lax.dot_general(
                grad[rows, :],
                weight_buf[:, pl.ds(index * half_wide, half_wide)],
                (((1,), (1,)), ((), ())),
                preferred_element_type=jnp.float32,
            )
        return pl.ds(pl.multiple_of(tile * TAIL_TILE, TAIL_TILE), TAIL_TILE), part

    def away_tile(tile, carry):
        rows, part = normed_tile(tile, 1 - core)
        away_buf[rows, :] = part.astype(jnp.bfloat16)
        return carry

    def own_tile(tile, carry):
        rows, part = normed_tile(tile, core)
        own_buf[rows, :] = part
        return carry

    def norm_tile(tile, carry):
        rows = pl.ds(pl.multiple_of(tile * NORM_TILE, NORM_TILE), NORM_TILE)
        grad = own_buf[rows, :] + came_buf[rows, :].astype(jnp.float32)
        unit, scale = norm_stats(token_buf[rows, :].astype(jnp.float32))
        residual_buf[rows, :] += norm_back_rows(unit, scale, gain_ref[...], grad)
        return carry + jnp.sum(grad * unit, 0, keepdims=True)

    tiles = own_buf.shape[0] // TAIL_TILE
    norm_tiles = own_buf.shape[0] // NORM_TILE
    middle, quarter = tiles // 2, norm_tiles // 4
    issue(1)
    around_hidden(1)
    issue(2)
    for load in loads[:4]:
        load.wait()
    lax.fori_loop(0, middle, away_tile, 0)
    turn(1)
    issue(3)
    lax.fori_loop(middle, tiles, away_tile, 0)
    away = send(away_buf, came_buf, (row, 1 - core))
    around_hidden(2)
    lax.fori_loop(0, middle, own_tile, 0)
    turn(2)
    total(1)
    around(1)
    issue(0)
    lax.fori_loop(middle, tiles, own_tile, 0)
    for load in loads[4:]:
        load.wait()
    away.wait_recv()
    gain_part = jnp.zeros((1, own_buf.shape[1]), jnp.float32)
    gain_part = lax.fori_loop(0, quarter, norm_tile, gain_part)
    turn(3)
    around_hidden(3)
    gain_part = lax.fori_loop(quarter, 2 * quarter, norm_tile, gain_part)
    total(2)
    around(2)
    gain_part = lax.fori_loop(2 * quarter, 3 * quarter, norm_tile, gain_part)
    turn(0)
    gain_part = lax.fori_loop(3 * quarter, norm_tiles, norm_tile, gain_part)
    store = pltpu.make_async_copy(residual_buf, token_out, local_sems.at[6])
    store.start()
    gain_buf[0] = jnp.zeros_like(gain_buf[0])
    gain_buf[0, 0:1] = gain_part
    gain_buf[0, 1:2] = ffn_gain_ref[...]

    def exchange(number, target):
        copy = send(gain_buf.at[number], gain_came.at[number], target)
        copy.wait_recv()
        gain_buf[number + 1] = gain_buf[number] + gain_came[number]

    exchange(0, (row, 1 - core))
    exchange(1, (over_x, core))
    total(3)
    around(3)
    exchange(2, (over_y, core))
    exchange(3, (beside, core))
    exchange(4, (beyond, core))
    gain_out[...] = gain_buf[5]
    hidden_ring[-1].wait_recv()
    up_wide = up_out.shape[1]
    for out, columns in ((up_out, pl.ds(0, up_wide)), (out_out, pl.ds(up_wide, half_wide))):
        out[...] = plus_wide(hidden_ref[zed, :, columns], hidden_came[2, :, columns])
    total(0)
    ring[-1].wait_recv()
    for index, out in enumerate((query_out, key_out, value_out)):
        columns = pl.ds(index * half_wide, half_wide)
        out[...] = sum_buf[0, :, columns] + ring_came[2, :, columns].astype(jnp.float32)
    for copy in sent:
        copy.wait_send()
    store.wait()


def tail_call(grads, weights, sums, tokens, grad_residual, gain, ffn_gain, hidden_sums):
    flat, width = grad_residual.shape
    half_wide = sums[0].shape[1]
    depth = sums[0].shape[0] // 16
    anywhere, here = pl.BlockSpec(memory_space=pl.ANY), pl.BlockSpec(memory_space=pltpu.VMEM)
    block = pltpu.VMEM((4, depth, 3 * half_wide), jnp.bfloat16)
    moving = pltpu.VMEM((3, depth, 3 * half_wide), jnp.bfloat16)
    gains = pltpu.VMEM((6, 8, width), jnp.float32)
    sum_shape = jax.ShapeDtypeStruct((depth, half_wide), jnp.float32)
    return pl.pallas_call(
        tail_kernel,
        in_specs=[anywhere] * 4 + [here] * 3 + [anywhere] * 2 + [here] * 3,
        out_specs=[anywhere] + [here] * 6,
        out_shape=[
            jax.ShapeDtypeStruct((flat, width), jnp.float32),
            sum_shape,
            sum_shape,
            sum_shape,
            jax.ShapeDtypeStruct((8, width), jnp.float32),
            jax.ShapeDtypeStruct((depth, hidden_sums.shape[2] - half_wide), jnp.float32),
            sum_shape,
        ],
        scratch_shapes=[pltpu.VMEM((width, 3 * half_wide), jnp.bfloat16)]
        + [pltpu.VMEM((2 * flat, half_wide), jnp.bfloat16)] * 3
        + [
            pltpu.VMEM((flat, width), jnp.float32),
            pltpu.VMEM((flat, width), jnp.bfloat16),
            pltpu.VMEM((flat, width), jnp.bfloat16),
            pltpu.VMEM((flat, width), jnp.bfloat16),
            pltpu.VMEM((flat, width), jnp.float32),
        ]
        + [block] * 4
        + [pltpu.VMEM((4, depth, 3 * half_wide), jnp.float32), moving, moving, gains, gains]
        + [pltpu.VMEM((3,) + hidden_sums.shape[1:], jnp.bfloat16)] * 2
        + [
            pltpu.SemaphoreType.DMA((7,)),
            pltpu.SemaphoreType.DMA((64,)),
            pltpu.SemaphoreType.DMA((64,)),
        ],
        compiler_params=pltpu.CompilerParams(
            collective_id=1, has_side_effects=True, vmem_limit_bytes=60 * 1024 * 1024
        ),
    )(
        *grads,
        weights,
        *sums,
        tokens,
        grad_residual,
        gain.reshape(1, width),
        ffn_gain.reshape(1, width),
        hidden_sums,
    )


def halves_z(stack):
    _, depth, wide = stack.shape
    if depth > 80:
        return stack[:, : depth // 2], stack[:, depth // 2 :]
    cut = (wide // 128 + 1) // 2 * 128
    return stack[:, :, :cut], stack[:, :, cut:]


def gather_first(first, second):
    return jnp.stack([first, swap_y(first)]), jnp.stack([second, swap_x(second)])


def gather_second(first, second):
    return (first, swap_x(first)), (second, swap_y(second))


def dot_low(left_side, right_side):
    return jnp.dot(left_side, right_side, preferred_element_type=jnp.float32)


def outer_low(left_side, right_side):
    return jnp.einsum(
        "tc,te->ce", left_side, right_side, preferred_element_type=jnp.float32
    ).astype(jnp.bfloat16)


class Scatter:

    def __init__(self, first, second, by_rows=False):
        self.parts, self.by_rows = (first, second), by_rows

    def pick(self, which, start_y, start_x, count_y=1, count_x=1):
        picked = []
        for whole, row, depth, column, wide in self.parts[which]:
            planes = Z_SIZE // len(self.parts[which]) if self.by_rows else Z_SIZE
            blocks = whole.reshape(planes, 2, 2, whole.shape[0] // planes // 4, whole.shape[1])
            picked.append(
                lax.dynamic_slice(
                    blocks,
                    (0, start_y, start_x, row, column),
                    (planes, count_y, count_x, depth, wide),
                ).reshape(planes, count_y * count_x, depth, wide)
            )
        axis = 0 if self.by_rows else 3
        return picked[0] if len(picked) == 1 else jnp.concatenate(picked, axis)

    def prepare(self, *after):
        _, here_y, here_x = chip_place()
        here_x, here_y = tie((here_x, here_y), *after)
        self.away = (self.pick(0, 0, 1 - here_x, 2, 1), self.pick(1, 1 - here_y, 0, 1, 2))

    def spread(self):
        self.came = (swap_x(self.away[0]), swap_y(self.away[1]))

    def of_came(self, which, far):
        _, here_y, here_x = chip_place()
        here = here_x if which else here_y
        return lax.dynamic_slice_in_dim(self.came[which], here ^ far, 1, 1)

    def turn(self):
        _, here_y, here_x = chip_place()
        first = plus(self.pick(0, 1 - here_y, here_x), self.of_came(0, 1))
        second = plus(self.pick(1, here_y, 1 - here_x), self.of_came(1, 1))
        self.turning = (first, second)
        self.turned = (swap_y(first), swap_x(second))

    def near_sums(self):
        _, here_y, here_x = chip_place()
        first, second = (
            plus(
                self.pick(which, here_y, here_x), self.of_came(which, 0), self.turned[which]
            ).reshape((Z_SIZE,) + self.turned[which].shape[2:])
            for which in range(2)
        )
        return jnp.concatenate([first, second], 1 if self.by_rows else 2)

    def gather(self):
        self.sums = self.near_sums()
        self.moving = next_z(self.block(1))

    def block(self, back):
        target = (ring_place() - back) % Z_SIZE
        zed = jnp.where(target == 2, 3, jnp.where(target == 3, 2, target))
        if self.by_rows:
            zed = zed ^ (2 * lax.axis_index("seq"))
        return lax.dynamic_index_in_dim(self.sums, zed, 0, keepdims=False)

    def step(self, number):
        self.moving = next_z(plus(self.block(number), self.moving))

    def finish(self):
        return self.block(0).astype(jnp.float32) + self.moving.astype(jnp.float32)

    def hold(self, names, *after):
        for name in names:
            setattr(self, name, tie(getattr(self, name), *after))


def body_pair(
    tokens, segments, gain_attn, w_query, w_key, w_value, w_out, gain_ffn, w_up, w_down, cotangent
):
    core = lax.axis_index("seq")
    rows, span, width = tokens.shape
    flat = rows * span

    def split(flat_rows, axis_width):
        return flat_rows.reshape(rows, 2 * span, axis_width)

    def sharing(values):
        wide = split(values, values.shape[-1])
        return swap_cores(own_half(wide, 1, 1 - core).astype(jnp.bfloat16))

    def shared(values, received):
        wide = split(values, values.shape[-1])
        return (own_half(wide, 1, core) + received.astype(jnp.float32)).reshape(flat, -1)

    attn_piece = jnp.concatenate([w_query, w_key, w_value, w_out], 1)
    half_wide = w_query.shape[1]
    normed, cot_other, attn_weights, up_stack = head_call(
        tokens, gain_attn, cotangent, attn_piece, w_up
    )
    first = core == 0
    tokens_own = tokens.reshape(flat, width).astype(jnp.float32)
    cot_own = cotangent.reshape(flat, width)
    windows = windows_of(segments, QUERY_TILE)
    back_windows = windows_of(segments, BACK_TILE)
    marks = (
        jnp.broadcast_to(segments[:, :, None], segments.shape + (LANES,)),
        jnp.broadcast_to(segments[:, None, :], (rows, 8, 2 * span)),
    )
    normed = normed.reshape(2 * flat, width)
    w_qkv = attn_weights[:, : 3 * half_wide]
    w_q, w_k, w_v = (w_qkv[:, i * half_wide : (i + 1) * half_wide] for i in range(3))

    up_parts = gather_first(*halves_z(up_stack))
    down_steps = [tie(w_down, up_stack)]
    down_steps.append(next_z(down_steps[-1]))
    w_o_half = attn_weights[:, 3 * half_wide :]
    w_o_other = swap_cores(w_o_half)
    qk_rows = dot_low(normed, w_qkv[:, : 2 * half_wide]).astype(jnp.bfloat16)
    normed, w_o_other, down_steps[1], up_parts = tie(
        (normed, w_o_other, down_steps[1], up_parts), qk_rows
    )
    down_steps.append(next_z(down_steps[-1]))
    up_near = up_parts
    up_parts = gather_second(*up_parts)
    normed = tie(normed, up_near)
    value_rows = dot_low(normed, w_qkv[:, 2 * half_wide :]).astype(jnp.bfloat16)
    value_rows, down_steps[2] = tie((value_rows, down_steps[2]))
    down_steps.append(next_z(down_steps[-1]))
    qk_rows, value_rows = split(qk_rows, 2 * half_wide), split(value_rows, half_wide)
    qk_rows = tie(qk_rows, up_near)
    operands = [(qk_rows, 0), (qk_rows, 1), (value_rows, 0)]
    (mixed,) = attention_call(
        attend_kernel, 0, rows, windows, marks, operands, [half_wide], [], half_wide
    )
    mixed, down_steps[3], up_parts = tie((mixed, down_steps[3], up_parts))
    down_first, down_second = halves_z(natural_z(down_steps))
    down_came = swap_y(down_first), swap_x(down_second), swap_x(down_first), swap_y(down_second)
    w_o_other = tie(w_o_other, down_first, down_second)
    w_o = jnp.where(
        first,
        jnp.concatenate([w_o_half, w_o_other], 1),
        jnp.concatenate([w_o_other, w_o_half], 1),
    )
    w_o_rows = own_half(w_o, 0, core)

    mixed_other = swap_cores(own_half(mixed, 1, 1 - core))
    mixed_mine = own_half(mixed, 1, core)
    mixed_own = jnp.where(
        first,
        jnp.concatenate([mixed_mine, mixed_other], 2),
        jnp.concatenate([mixed_other, mixed_mine], 2),
    ).reshape(flat, width)
    mixed_own, w_o, w_o_rows = tie((mixed_own, w_o, w_o_rows))
    residual = tokens_own + dot_low(mixed_own, w_o)
    unit_two, _ = norm_stats(residual)
    normed_two = (unit_two * gain_ffn).astype(jnp.bfloat16)
    cot_other = tie(cot_other, mixed_own)
    cot_all = jnp.concatenate([cot_own, cot_other.reshape(flat, width)], 0)
    normed_two, cot_all, down_came = tie((normed_two, cot_all, down_came))
    first_y, second_x, first_x, second_y = down_came
    down_parts = (down_first, first_y, first_x, down_second, second_x, second_y)
    hidden_low, grad_pre, y_own, grad_two_own, normed_two_all, y_came, grad_two_came = feed_forward(
        normed_two, cot_all, up_parts, down_parts
    )

    down_half = outer_low(hidden_low, cot_all)
    down_away = swap_cores(own_half(down_half, 1, 1 - core))
    layer_out, grad_residual, ffn_gain_rows, grad_attn_all = residual_call(
        rows, residual, cot_own, y_own, y_came, grad_two_own, tie(grad_two_came, down_half), gain_ffn
    )
    ffn_gain_part = ffn_gain_rows[0]
    grad_attn_all = grad_attn_all.reshape(2 * flat, width)
    down_away = tie(down_away, grad_residual)
    depth, wide = w_down.shape
    down_halves = ((down_half, core * wide), (down_away, 0))
    down_sum = Scatter(
        *(
            [(whole, row, depth // 2, column, wide) for whole, column in down_halves]
            for row in (0, depth // 2)
        ),
        True,
    )
    down_sum.prepare()
    down_sum.spread()
    up_whole = outer_low(normed_two_all, tie(grad_pre, *down_sum.away))
    grad_attn_all = tie(grad_attn_all, up_whole)
    out_half = outer_low(mixed.reshape(2 * flat, -1), grad_attn_all)
    out_away = swap_cores(own_half(out_half, 1, 1 - core))
    grad_mixed = split(times_transposed(grad_attn_all, w_o_rows).astype(jnp.bfloat16), width // 2)
    out_away = tie(out_away, grad_mixed)
    out_kept = own_half(out_half, 1, core)
    out_whole = jnp.where(
        first,
        jnp.concatenate([out_kept, out_away], 0),
        jnp.concatenate([out_away, out_kept], 0),
    )
    depth, wide = w_up.shape
    cut = (wide + half_wide) // 256 * 128
    up_sum = Scatter(
        [(up_whole, 0, depth, 0, cut)],
        [(up_whole, 0, depth, cut, wide - cut), (out_whole, 0, depth, 0, half_wide)],
    )
    down_sum.hold(("came",), grad_mixed)
    down_sum.turn()
    up_sum.prepare(*down_sum.turning)
    up_sum.spread()
    grad_mixed = tie(grad_mixed, *up_sum.away, *down_sum.turning)
    scratch = [pltpu.VMEM((2 * span, LANES), jnp.float32)] * 2

    def attend_back(row, grad_rows, begun=()):
        return attention_call(
            attend_back_kernel,
            row,
            1,
            back_windows,
            marks,
            operands + [(grad_rows, 0)],
            [half_wide] * 3,
            scratch,
            LANES,
            begun,
        )

    grads = attend_back(0, grad_mixed)
    down_sum.hold(("turned",), *grads)
    down_sum.gather()
    grads = tie(grads, down_sum.sums)
    for row in range(1, rows):
        grads = attend_back(row, grad_mixed, grads)
    down_sum.hold(("moving",), *grads)
    up_sum.hold(("came",), *grads)
    grads = tie(grads, down_sum.moving, up_sum.came)
    up_sum.turn()
    down_sum.step(2)
    grads = tie(grads, *up_sum.turning)
    grad_queries, grad_keys, grad_values = (grad.reshape(2 * flat, half_wide) for grad in grads)
    query_whole = outer_low(normed, grad_queries)
    key_whole = outer_low(normed, grad_keys)
    down_sum.hold(("moving",), query_whole, key_whole)
    grad_values = tie(grad_values, down_sum.moving)
    down_sum.step(3)
    value_whole = outer_low(normed, grad_values)
    up_sum.hold(("turned",), value_whole)
    sums = tie((query_whole, key_whole, value_whole), down_sum.moving)
    token_grad, query_grad, key_grad, value_grad, gains, up_grad, out_grad = tail_call(
        (grad_queries, grad_keys, grad_values),
        attn_weights,
        sums,
        tokens.reshape(flat, width),
        grad_residual,
        gain_attn,
        ffn_gain_part,
        up_sum.near_sums(),
    )
    gain_attn_grad, gain_ffn_grad = gains[0], gains[1]
    down_grad = down_sum.finish()
    return (
        layer_out.reshape(rows, span, width),
        token_grad.reshape(rows, span, width),
        gain_attn_grad,
        query_grad,
        key_grad,
        value_grad,
        out_grad,
        gain_ffn_grad,
        up_grad,
        down_grad,
    )


def solution(mesh):
    paired = mesh.shape["seq"] == 2 and mesh.shape["rows"] == 16
    program = body_pair if paired else body
    return jax.shard_map(
        program,
        mesh=mesh,
        in_specs=(
            P("rows", "seq", None),
            P("rows", None),
            P(),
            P("rows", "seq"),
            P("rows", "seq"),
            P("rows", "seq"),
            P("rows", "seq"),
            P(),
            P("rows", "seq"),
            P("rows", "seq"),
            P("rows", "seq", None),
        ),
        out_specs=(
            P("rows", "seq", None),
            P("rows", "seq", None),
            P(),
            P("rows", "seq"),
            P("rows", "seq"),
            P("rows", "seq"),
            P("rows", "seq"),
            P(),
            P("rows", "seq"),
            P("rows", "seq"),
        ),
        check_vma=False,
    )
```
